32 devices in a mesh: ctx: 8 (over z, core), fsdp: 4 (over y, x).
Axes of the slice: x: 2, y: 2, z: 4, core: 2. Of those that a mesh axis runs over, the one named last changes fastest.
Arguments:
- inputs: bfloat16 [4, 4096, 1280], P('fsdp', 'ctx'), may hold values from -6 to 6
- cotangent: bfloat16 [4, 4096, 1280], P('fsdp', 'ctx'), may hold values from -6 to 6
- block_order: int32 [4, 16], P('fsdp'), may hold values from 0 to 15, each once within a row
- w_qkv: float32 [1280, 3840], P('fsdp'), may hold values from -0.15625 to 0.15625
- m_qkv: float32 [1280, 3840], P('fsdp'), may hold values from -768 to 768
- v_qkv: float32 [1280, 3840], P('fsdp'), may hold values from 16384 to 65536
- w_out: float32 [1280, 1280], P('fsdp'), may hold values from -2.5 to 2.5
- m_out: float32 [1280, 1280], P('fsdp'), may hold values from -64 to 64
- v_out: float32 [1280, 1280], P('fsdp'), may hold values from 124 to 496
- w_up: float32 [1280, 1280], P('fsdp'), may hold values from -0.15625 to 0.15625
- m_up: float32 [1280, 1280], P('fsdp'), may hold values from -384 to 384
- v_up: float32 [1280, 1280], P('fsdp'), may hold values from 4096 to 16384
- w_down: float32 [1280, 1280], P('fsdp'), may hold values from -0.15625 to 0.15625
- m_down: float32 [1280, 1280], P('fsdp'), may hold values from -448 to 448
- v_down: float32 [1280, 1280], P('fsdp'), may hold values from 5898.24 to 23592.96
- small_params: float32 [2640], replicated, may hold values from -1 to 2, as said below
- small_m: float32 [2640], replicated, may hold values from -576 to 576
- small_v: float32 [2640], replicated, may hold values from 4096 to 147456
Outputs:
- output: bfloat16 [4, 4096, 1280], P('fsdp', 'ctx')
- input_grad: bfloat16 [4, 4096, 1280], P('fsdp', 'ctx')
- qkv_new: float32 [1280, 3840], P('fsdp')
- qkv_first: float32 [1280, 3840], P('fsdp')
- qkv_second: float32 [1280, 3840], P('fsdp')
- qkv_low: bfloat16 [1280, 3840], P('fsdp')
- out_new: float32 [1280, 1280], P('fsdp')
- out_first: float32 [1280, 1280], P('fsdp')
- out_second: float32 [1280, 1280], P('fsdp')
- out_low: bfloat16 [1280, 1280], P('fsdp')
- up_new: float32 [1280, 1280], P('fsdp')
- up_first: float32 [1280, 1280], P('fsdp')
- up_second: float32 [1280, 1280], P('fsdp')
- up_low: bfloat16 [1280, 1280], P('fsdp')
- down_new: float32 [1280, 1280], P('fsdp')
- down_first: float32 [1280, 1280], P('fsdp')
- down_second: float32 [1280, 1280], P('fsdp')
- down_low: bfloat16 [1280, 1280], P('fsdp')
- small_new: float32 [2640], replicated
- small_first: float32 [2640], replicated
- small_second: float32 [2640], replicated
The draws below stay inside these ranges and needn't reach their ends.
Inputs may be any that keep to these rules, and one draw needn't show every extreme that they name: `block_order`: each row lists the 16 causal blocks of its group once each. ctx index c holds the blocks at entries 2 c to 2 c + 1, in that order. Blocks below 8 form the prompt in order; block 8 + j is part (j % 2) of continuation j // 2. `small_params`: entries 0 to 2559 are gains; the last 80 are query scale parameters.
All inputs are finite; a program needn't handle non-finite values.
Results may differ from the reference program's by a relative error of at most 0.025.
Values may be sent and summed in bfloat16 or wider, within the bound.
A program may use at most 384 MiB of HBM per device.

```python
import math
import jax
import jax.numpy as jnp
from jax import lax

D = 1280
H = 16
HD = 80
FF = 1280
BLOCK = 256
CONT = 512
STEP = 3
NB = 16
TOK_G = 4096
GROUPS = 4
ALL_TOK = 16384


def small_scales():
    root = ALL_TOK ** 0.5
    return jnp.concatenate([jnp.full((D,), 1.5 * root, jnp.float32), jnp.full((D,), 0.5 * root, jnp.float32), jnp.full((HD,), 0.5 * root, jnp.float32)])


def draw_small_params(key, part):
    gains = 1.0 + jax.random.uniform(jax.random.fold_in(key, 11), (2 * D,), jnp.float32, -0.3, 0.3)
    scales = jax.random.uniform(jax.random.fold_in(key, 12), (HD,), jnp.float32, -1.0, 2.0)
    return jnp.concatenate([gains, scales])


def draw_small_m(key, part):
    return jax.random.truncated_normal(jax.random.fold_in(key, 21), -3.0, 3.0, (2 * D + HD,), jnp.float32) * small_scales()


def draw_small_v(key, part):
    spread = jax.random.uniform(jax.random.fold_in(key, 31), (2 * D + HD,), jnp.float32, 0.0, 2.0)
    return small_scales() * small_scales() * jnp.exp2(spread)


def block_scale(key, extent, cuts, least, largest):
    gain, own = 1.0, jax.random.fold_in(key, 6)
    for position, blocks in cuts:
        steps = jnp.exp(jax.random.uniform(jax.random.fold_in(own, position), (blocks,), jnp.float32, least / len(cuts), largest / len(cuts)))
        gain = gain * jnp.repeat(steps, extent[position] // blocks).reshape([-1 if axis == position else 1 for axis in range(len(extent))])
    return gain


def normal_values(stream_key, dims, scale, reach, cuts=(), held_as=jnp.bfloat16):
    array = jax.random.normal(stream_key, dims, jnp.float32) * scale
    if len(cuts) > 0:
        array = block_scale(stream_key, dims, cuts, -0.22, 0.18) * array
    return jnp.clip(array, min=-reach, max=reach).astype(held_as)


def setup_inputs(seed: int = 0) -> dict:
    key_list = jax.random.split(jax.random.key(seed), 19)
    inputs = normal_values(key_list[0], (GROUPS, TOK_G, D), 1.0, 6.0, ((0, 4), (1, 8)))
    cotangent = normal_values(key_list[1], (GROUPS, TOK_G, D), 1.0, 6.0, ((0, 4), (1, 8)))
    block_order = jax.vmap(lambda own: jax.random.permutation(own, NB))(jax.random.split(key_list[2], GROUPS)).reshape((GROUPS, NB)).astype(jnp.int32)
    w_qkv = normal_values(key_list[3], (D, 3 * D), D ** -0.5, 0.15625, ((0, 4),), jnp.float32)
    m_qkv = normal_values(key_list[4], (D, 3 * D), (1.0 * ALL_TOK ** 0.5), 768.0, ((0, 4),), jnp.float32)
    v_qkv = jnp.clip(jnp.exp(math.log(65536.0) - 1.3862944 * jax.random.uniform(key_list[5], (D, 3 * D), jnp.float32) ** block_scale(key_list[5], (D, 3 * D), ((0, 4),), -0.2, 0.2)), 16384.0, 65536.0)
    w_out = normal_values(key_list[6], (D, D), (max(D // 256, 1)) ** -0.5, 2.5, ((0, 4),), jnp.float32)
    m_out = normal_values(key_list[7], (D, D), (5.6 * GROUPS ** 0.5), 64.0, ((0, 4),), jnp.float32)
    v_out = jnp.clip(jnp.exp(math.log(496.0) - 1.3862944 * jax.random.uniform(key_list[8], (D, D), jnp.float32) ** block_scale(key_list[8], (D, D), ((0, 4),), -0.2, 0.2)), 124.0, 496.0)
    w_up = normal_values(key_list[9], (D, FF), D ** -0.5, 0.15625, ((0, 4),), jnp.float32)
    m_up = normal_values(key_list[10], (D, FF), (0.5 * ALL_TOK ** 0.5), 384.0, ((0, 4),), jnp.float32)
    v_up = jnp.clip(jnp.exp(math.log(16384.0) - 1.3862944 * jax.random.uniform(key_list[11], (D, FF), jnp.float32) ** block_scale(key_list[11], (D, FF), ((0, 4),), -0.2, 0.2)), 4096.0, 16384.0)
    w_down = normal_values(key_list[12], (FF, D), FF ** -0.5, 0.15625, ((0, 4),), jnp.float32)
    m_down = normal_values(key_list[13], (FF, D), (0.6 * ALL_TOK ** 0.5), 448.0, ((0, 4),), jnp.float32)
    v_down = jnp.clip(jnp.exp(math.log(23592.96) - 1.3862944 * jax.random.uniform(key_list[14], (FF, D), jnp.float32) ** block_scale(key_list[14], (FF, D), ((0, 4),), -0.2, 0.2)), 5898.24, 23592.96)
    small_params = draw_small_params(jax.random.fold_in(key_list[18], 71), 0)
    small_m = draw_small_m(jax.random.fold_in(key_list[18], 71), 0)
    small_v = draw_small_v(jax.random.fold_in(key_list[18], 71), 0)
    return {"inputs": inputs, "cotangent": cotangent, "block_order": block_order, "w_qkv": w_qkv, "m_qkv": m_qkv, "v_qkv": v_qkv, "w_out": w_out, "m_out": m_out, "v_out": v_out, "w_up": w_up, "m_up": m_up, "v_up": v_up, "w_down": w_down, "m_down": m_down, "v_down": v_down, "small_params": small_params, "small_m": small_m, "small_v": small_v}


@jax.custom_vjp
def low(v):
    return lax.optimization_barrier(v.astype(jnp.bfloat16)).astype(jnp.float32)

@jax.custom_vjp
def low_back(v):
    return v

def low_keep(v):
    return (low(v), None)

def low_pass(kept, grad):
    return (grad,)

def back_keep(v):
    return (v, None)

def back_low(kept, grad):
    return (low(grad),)
low.defvjp(low_keep, low_pass)
low_back.defvjp(back_keep, back_low)
norm_eps = 1e-06
beta_one = 0.5
beta_two = 0.5
adam_eps = 1e-08
decay_rate = 0.1
small_rate = 0.75
qkv_rate_base = 1.0
scale_base = 1.442695
highest = lax.Precision.HIGHEST

def token_layout(block_ids):
    prompt_blocks = NB // 2
    cont_blocks = CONT // BLOCK
    later = block_ids - prompt_blocks
    block_seg = jnp.where(block_ids < prompt_blocks, 0, 1 + later // cont_blocks)
    block_base = jnp.where(block_ids < prompt_blocks, block_ids * BLOCK, (prompt_blocks + later % cont_blocks) * BLOCK)
    offset = jnp.arange(BLOCK, dtype=jnp.int32)
    seg_ids = jnp.broadcast_to(block_seg[:, None], (NB, BLOCK)).reshape(-1)
    positions = (block_base[:, None] + offset[None, :]).reshape(-1)
    return (seg_ids.astype(jnp.int32), positions.astype(jnp.int32))

def rms_scale(values):
    return lax.rsqrt(lax.optimization_barrier(jnp.mean(values * values, axis=-1, keepdims=True)) + norm_eps)

def attend_block(query_blk, seg_query, pos_query, keys, values, seg_key, pos_key):
    scores = jnp.einsum('qhd,khd->hqk', query_blk, keys, precision=highest)
    scores = low_back(scores)
    allowed = ((seg_key[None, :] == 0) | (seg_key[None, :] == seg_query[:, None])) & (pos_key[None, :] <= pos_query[:, None])
    scores = jnp.where(allowed[None], scores, -1e+30)
    row_top = lax.optimization_barrier(jnp.max(scores, axis=-1, keepdims=True))
    expd = jnp.exp(scores - row_top)
    prob_rows = low(expd / lax.optimization_barrier(jnp.sum(expd, axis=-1, keepdims=True)))
    return jnp.einsum('hqk,khd->qhd', prob_rows, values, precision=highest)

def layer_group(group_rows, seg_ids, positions, lowered, small):
    wq, wo, wu, wd = lowered
    gain_one = small[:D]
    gain_two = small[D:2 * D]
    query_scale = small[2 * D:]
    normed = low(group_rows * rms_scale(group_rows) * gain_one)
    qkv = low_back(jnp.dot(normed, wq, precision=highest))
    factor = scale_base / math.sqrt(HD) * jax.nn.softplus(query_scale)
    queries = low(qkv[:, :D].reshape(-1, H, HD) * factor)
    keys = low(qkv[:, D:2 * D].reshape(-1, H, HD))
    values = low(qkv[:, 2 * D:].reshape(-1, H, HD))
    qblock = math.gcd(TOK_G, 512)
    num_blocks = TOK_G // qblock
    blocked = jax.checkpoint(attend_block)
    mixed = lax.map(lambda block_args: blocked(block_args[0], block_args[1], block_args[2], keys, values, seg_ids, positions), (queries.reshape(num_blocks, qblock, H, HD), seg_ids.reshape(num_blocks, qblock), positions.reshape(num_blocks, qblock)))
    attn = low(low_back(mixed.reshape(TOK_G, D)))
    mid = group_rows + low_back(jnp.dot(attn, wo, precision=highest))
    normed_two = low(mid * rms_scale(mid) * gain_two)
    hidden = low_back(jnp.dot(normed_two, wu, precision=highest))
    act = low(hidden * jax.nn.sigmoid(hidden))
    return mid + jnp.dot(act, wd, precision=highest)

def adamw(weight, first, second, gradient, step_rate, decay_on):
    first_new = beta_one * first + (1.0 - beta_one) * gradient
    second_new = beta_two * second + (1.0 - beta_two) * gradient * gradient
    corr_one = 1.0 - beta_one ** STEP
    corr_two = 1.0 - beta_two ** STEP
    update = first_new / corr_one / (jnp.sqrt(second_new / corr_two) + adam_eps)
    weight_new = weight - step_rate * (update + decay_on * weight)
    return (weight_new, first_new, second_new)

def reference(inputs, cotangent, block_order, w_qkv, m_qkv, v_qkv, w_out, m_out, v_out, w_up, m_up, v_up, w_down, m_down, v_down, small_params, small_m, small_v):
    seg_all, pos_all = jax.vmap(token_layout)(block_order)

    def forward(layer_in, wq, wo, wu, wd, small):
        lowered = (low(wq), low(wo), low(wu), low(wd))

        def per_group(group_args):
            return layer_group(group_args[0], group_args[1], group_args[2], lowered, small)
        return lax.map(per_group, (layer_in, seg_all, pos_all))
    result, pullback = jax.vjp(forward, inputs.astype(jnp.float32), w_qkv, w_out, w_up, w_down, small_params)
    gradients = pullback(cotangent.astype(jnp.float32))
    qkv_set = adamw(w_qkv, m_qkv, v_qkv, gradients[1], qkv_rate_base / math.sqrt(D), decay_rate)
    out_set = adamw(w_out, m_out, v_out, gradients[2], 0.5 / math.sqrt(max(D // 256, 1)), decay_rate)
    up_set = adamw(w_up, m_up, v_up, gradients[3], 0.5 / math.sqrt(D), decay_rate)
    down_set = adamw(w_down, m_down, v_down, gradients[4], 0.5 / math.sqrt(FF), decay_rate)
    small_set = adamw(small_params, small_m, small_v, gradients[5], small_rate, 0.0)
    return (result.astype(jnp.bfloat16), gradients[0].astype(jnp.bfloat16), qkv_set[0], qkv_set[1], qkv_set[2], qkv_set[0].astype(jnp.bfloat16), out_set[0], out_set[1], out_set[2], out_set[0].astype(jnp.bfloat16), up_set[0], up_set[1], up_set[2], up_set[0].astype(jnp.bfloat16), down_set[0], down_set[1], down_set[2], down_set[0].astype(jnp.bfloat16), small_set[0], small_set[1], small_set[2])
```

```python
import functools
import math

import jax
import jax.numpy as jnp
from jax import lax
from jax.experimental import pallas as pl
from jax.experimental.pallas import tpu as pltpu
from jax.sharding import PartitionSpec as P

D = 1280
H = 16
HD = 80
FF = 1280
BLOCK = 256
CONT = 512
STEP = 3
PAD = 128
EXTRA = 16
TILE = CONT

bf16 = jnp.bfloat16
f32 = jnp.float32

norm_eps = 1e-06
beta_one = 0.5
beta_two = 0.5
adam_eps = 1e-08
decay_rate = 0.1
small_rate = 0.75
qkv_rate_base = 1.0
scale_base = 1.442695
LOG2E = math.log2(math.e)
LN2 = math.log(2.0)


def rms_scale(values):
    return lax.rsqrt(jnp.mean(values * values, axis=-1, keepdims=True) + norm_eps)


def adamw(weight, first, second, gradient, step_rate, decay_on):
    first_new = beta_one * first + (1.0 - beta_one) * gradient
    second_new = beta_two * second + (1.0 - beta_two) * gradient * gradient
    corr_one = 1.0 - beta_one**STEP
    corr_two = 1.0 - beta_two**STEP
    update = first_new / corr_one / (jnp.sqrt(second_new / corr_two) + adam_eps)
    weight_new = weight - step_rate * (update + decay_on * weight)
    return (weight_new, first_new, second_new)


def dot(left, right, contract=(1, 0)):
    return lax.dot_general(
        left, right, (((contract[0],), (contract[1],)), ((), ())), preferred_element_type=f32
    )


def fill_slots(order_ref, slot_ref, num_blocks):
    def place(slot, carry):
        slot_ref[order_ref[slot]] = slot
        return carry

    lax.fori_loop(0, num_blocks, place, 0)


def three_rows(row):
    high = row.astype(bf16)
    rest = row - high.astype(f32)
    middle = rest.astype(bf16)
    low = (rest - middle.astype(f32)).astype(bf16)
    index = lax.broadcasted_iota(jnp.int32, (EXTRA, row.shape[1]), 0)
    zero = jnp.zeros((EXTRA, row.shape[1]), f32)
    rows = jnp.where(index == 0, high.astype(f32), zero)
    rows = jnp.where(index == 1, middle.astype(f32), rows)
    rows = jnp.where(index == 2, low.astype(f32), rows)
    return rows.astype(bf16)


def tile_at(tile):
    return pl.ds(pl.multiple_of(tile * TILE, TILE), TILE)


def half_at(slot):
    return pl.ds(pl.multiple_of(lax.rem(slot, 2) * BLOCK, BLOCK), BLOCK)


def causal():
    key = lax.broadcasted_iota(jnp.int32, (TILE, TILE), 0)
    query = lax.broadcasted_iota(jnp.int32, (TILE, TILE), 1)
    return key <= query


def forward_kernel(
    heads,
    order_ref,
    x_ref,
    wn_ref,
    wt_ref,
    factor_ref,
    qt_ref,
    kt_ref,
    kn_ref,
    vn_ref,
    lse_ref,
    ot_ref,
    slot_ref,
    vt_ref,
    acc_ref,
    top_ref,
):
    tokens = x_ref.shape[0]
    num_blocks = tokens // BLOCK
    num_tiles = tokens // TILE
    prompt_tiles = num_tiles // 2
    fill_slots(order_ref, slot_ref, num_blocks)
    width = heads * HD
    lane = lax.broadcasted_iota(jnp.int32, (BLOCK, PAD), 1)
    is_extra = (lane >= HD) & (lane < HD + 3)

    def project(slot, carry):
        rows = x_ref[pl.ds(pl.multiple_of(slot * BLOCK, BLOCK), BLOCK), :]
        to = pl.ds(pl.multiple_of(order_ref[slot] * BLOCK, BLOCK), BLOCK)
        natural = dot(rows, wn_ref[...])
        flipped = dot(wt_ref[...], rows, (1, 1))
        for head in range(heads):
            key = natural[:, 2 * head * PAD : (2 * head + 1) * PAD]
            value = natural[:, (2 * head + 1) * PAD : (2 * head + 2) * PAD]
            kn_ref[head, to, :] = jnp.where(is_extra, 1.0, key).astype(bf16)
            vn_ref[head, to, :] = jnp.where(is_extra, 1.0, value).astype(bf16)
            at = head * HD
            qt_ref[head, :HD, to] = (flipped[at : at + HD] * factor_ref[...]).astype(bf16)
            qt_ref[head, HD:, to] = jnp.zeros((PAD - HD, BLOCK), bf16)
            kt_ref[head, :, to] = flipped[width + at : width + at + HD].astype(bf16)
            at = 2 * width + head * HD
            vt_ref[head, :HD, to] = flipped[at : at + HD].astype(bf16)
            vt_ref[head, HD:, to] = jnp.ones((EXTRA, BLOCK), bf16)
        return carry

    lax.fori_loop(0, num_blocks, project, 0)
    allowed = causal()

    def query_tile(tile, carry):
        here = tile_at(tile)
        top_ref[...] = jnp.full(top_ref.shape, -1e30, f32)
        acc_ref[...] = jnp.zeros(acc_ref.shape, f32)

        def step(keys, masked):
            for head in range(heads):
                scores = dot(kn_ref[head, keys, :], qt_ref[head, :, here])
                if masked:
                    scores = jnp.where(allowed, scores, -1e30)
                old = top_ref[head]
                top = jnp.maximum(old, jnp.max(scores, axis=0, keepdims=True))
                probs = jnp.exp2(scores - top).astype(bf16)
                acc_ref[head] = acc_ref[head] * jnp.exp2(old - top) + dot(
                    vt_ref[head, :, keys], probs
                )
                top_ref[head] = top

        def full(key_tile, inner):
            step(tile_at(key_tile), False)
            return inner

        lax.fori_loop(0, jnp.minimum(tile, prompt_tiles), full, 0)
        step(here, True)
        for head in range(heads):
            acc = acc_ref[head]
            mass = acc[HD : HD + 1]
            mixed = (acc[:HD] / mass).astype(bf16)
            lse_ref[head, :, here] = top_ref[head] + jnp.log2(mass)
            for part in range(TILE // BLOCK):
                slot = slot_ref[tile * (TILE // BLOCK) + part]
                ot_ref[slot // 2, head * HD : (head + 1) * HD, half_at(slot)] = mixed[
                    :, part * BLOCK : (part + 1) * BLOCK
                ]
        return carry

    lax.fori_loop(0, num_tiles, query_tile, 0)


def backward_kernel(
    heads,
    order_ref,
    qt_ref,
    kt_ref,
    kn_ref,
    vn_ref,
    lse_ref,
    ot_ref,
    dt_ref,
    factor_ref,
    dqkv_ref,
    dscale_ref,
    slot_ref,
    qa_ref,
    da_ref,
    dq_ref,
    dk_ref,
    dv_ref,
):
    tokens = kn_ref.shape[1]
    num_blocks = tokens // BLOCK
    num_tiles = tokens // TILE
    prompt_tiles = num_tiles // 2
    width = heads * HD
    fill_slots(order_ref, slot_ref, num_blocks)

    def prepare(block, carry):
        slot = slot_ref[block]
        to = pl.ds(pl.multiple_of(block * BLOCK, BLOCK), BLOCK)
        for head in range(heads):
            rows = slice(head * HD, (head + 1) * HD)
            grad = dt_ref[slot // 2, rows, half_at(slot)]
            mixed = ot_ref[slot // 2, rows, half_at(slot)]
            delta = jnp.sum(grad.astype(f32) * mixed.astype(f32), axis=0, keepdims=True)
            da_ref[head, :HD, to] = grad
            da_ref[head, HD : HD + EXTRA, to] = three_rows(-delta)
            da_ref[head, HD + EXTRA :, to] = jnp.zeros((PAD - HD - EXTRA, BLOCK), bf16)
            qa_ref[head, :HD, to] = qt_ref[head, :HD, to]
            qa_ref[head, HD : HD + EXTRA, to] = three_rows(-lse_ref[head, :, to])
            qa_ref[head, HD + EXTRA :, to] = jnp.zeros((PAD - HD - EXTRA, BLOCK), bf16)
        return carry

    lax.fori_loop(0, num_blocks, prepare, 0)
    dk_ref[...] = jnp.zeros(dk_ref.shape, f32)
    dv_ref[...] = jnp.zeros(dv_ref.shape, f32)
    dscale_ref[...] = jnp.zeros(dscale_ref.shape, f32)
    allowed = causal()

    def query_tile(tile, carry):
        here = tile_at(tile)
        dq_ref[...] = jnp.zeros(dq_ref.shape, f32)

        def step(keys, masked):
            for head in range(heads):
                probs = jnp.exp2(dot(kn_ref[head, keys, :], qa_ref[head, :, here]))
                if masked:
                    probs = jnp.where(allowed, probs, 0.0)
                spread = dot(vn_ref[head, keys, :], da_ref[head, :, here])
                dscores = (probs * spread).astype(bf16)
                dv_ref[head, :, keys] += dot(da_ref[head, :HD, here], probs.astype(bf16), (1, 1))
                dk_ref[head, :, keys] += dot(qa_ref[head, :HD, here], dscores, (1, 1))
                dq_ref[head] += dot(kt_ref[head, :, keys], dscores)

        def full(key_tile, inner):
            step(tile_at(key_tile), False)
            return inner

        lax.fori_loop(0, jnp.minimum(tile, prompt_tiles), full, 0)
        step(here, True)
        for head in range(heads):
            dq = dq_ref[head]
            product = dq * qt_ref[head, :HD, here].astype(f32)
            for lane in range(TILE // PAD):
                dscale_ref[head] += product[:, lane * PAD : (lane + 1) * PAD]
            scaled = (dq * (factor_ref[...] * LN2)).astype(bf16)
            for part in range(TILE // BLOCK):
                slot = slot_ref[tile * (TILE // BLOCK) + part]
                to = pl.ds(pl.multiple_of(slot * BLOCK, BLOCK), BLOCK)
                dqkv_ref[head * HD : (head + 1) * HD, to] = scaled[
                    :, part * BLOCK : (part + 1) * BLOCK
                ]
        return carry

    lax.fori_loop(0, num_tiles, query_tile, 0)

    def finish(block, carry):
        slot = slot_ref[block]
        to = pl.ds(pl.multiple_of(slot * BLOCK, BLOCK), BLOCK)
        at = pl.ds(pl.multiple_of(block * BLOCK, BLOCK), BLOCK)
        for head in range(heads):
            row = width + head * HD
            dqkv_ref[row : row + HD, to] = (dk_ref[head, :, at] * LN2).astype(bf16)
            row = 2 * width + head * HD
            dqkv_ref[row : row + HD, to] = dv_ref[head, :, at].astype(bf16)
        return carry

    lax.fori_loop(0, num_blocks, finish, 0)


def in_vmem(count):
    return [pl.BlockSpec(memory_space=pltpu.VMEM)] * count


def params():
    return pltpu.CompilerParams(vmem_limit_bytes=60 * 1024 * 1024)


def attention_forward(order, rows, w_natural, w_flipped, factor, parts, heads):
    tokens = rows.shape[0]
    return pl.pallas_call(
        functools.partial(forward_kernel, heads),
        name="attention_forward",
        out_shape=[
            jax.ShapeDtypeStruct((heads, PAD, tokens), bf16),
            jax.ShapeDtypeStruct((heads, HD, tokens), bf16),
            jax.ShapeDtypeStruct((heads, tokens, PAD), bf16),
            jax.ShapeDtypeStruct((heads, tokens, PAD), bf16),
            jax.ShapeDtypeStruct((heads, 1, tokens), f32),
            jax.ShapeDtypeStruct((parts, heads * HD, tokens // parts), bf16),
        ],
        in_specs=[pl.BlockSpec(memory_space=pltpu.SMEM)] + in_vmem(4),
        out_specs=in_vmem(6),
        scratch_shapes=[
            pltpu.SMEM((tokens // BLOCK,), jnp.int32),
            pltpu.VMEM((heads, HD + EXTRA, tokens), bf16),
            pltpu.VMEM((heads, HD + EXTRA, TILE), f32),
            pltpu.VMEM((heads, 1, TILE), f32),
        ],
        compiler_params=params(),
    )(order, rows, w_natural, w_flipped, factor)


def attention_backward(order, kept, mixed, dmixed, factor, heads):
    qt, kt, kn, vn, lse = kept
    tokens = kn.shape[1]
    return pl.pallas_call(
        functools.partial(backward_kernel, heads),
        name="attention_backward",
        out_shape=[
            jax.ShapeDtypeStruct((3 * heads * HD, tokens), bf16),
            jax.ShapeDtypeStruct((heads, HD, PAD), f32),
        ],
        in_specs=[pl.BlockSpec(memory_space=pltpu.SMEM)] + in_vmem(8),
        out_specs=in_vmem(2),
        scratch_shapes=[
            pltpu.SMEM((tokens // BLOCK,), jnp.int32),
            pltpu.VMEM((heads, PAD, tokens), bf16),
            pltpu.VMEM((heads, PAD, tokens), bf16),
            pltpu.VMEM((heads, HD, TILE), f32),
            pltpu.VMEM((heads, HD, tokens), f32),
            pltpu.VMEM((heads, HD, tokens), f32),
        ],
        compiler_params=params(),
    )(order, qt, kt, kn, vn, lse, mixed, dmixed, factor)


def body(
    parts,
    inputs,
    cotangent,
    block_order,
    w_qkv,
    m_qkv,
    v_qkv,
    w_out,
    m_out,
    v_out,
    w_up,
    m_up,
    v_up,
    w_down,
    m_down,
    v_down,
    small_params,
    small_m,
    small_v,
):
    heads = H // parts
    width = heads * HD
    rows_dev = inputs.shape[1]
    tokens = rows_dev * parts
    here = lax.axis_index("ctx")
    order = block_order[0]
    gain_one = small_params[:D]
    gain_two = small_params[D : 2 * D]
    query_scale = small_params[2 * D :]
    own_columns = jnp.concatenate(
        [
            lax.dynamic_slice_in_dim(w_qkv, part * D + here * width, width, 1).astype(bf16)
            for part in range(3)
        ],
        axis=1,
    )
    own_qkv = lax.all_gather(own_columns, "fsdp", axis=0, tiled=True)
    layer_in = inputs[0].astype(f32)
    scale_one = rms_scale(layer_in)
    unit_one = layer_in * scale_one
    normed = (unit_one * gain_one).astype(bf16)
    normed_all = lax.all_gather(normed, "ctx", axis=0, tiled=True)
    out_full, up_full, down_full = (
        lax.all_gather(w_out.astype(bf16), "fsdp", axis=0, tiled=True),
        lax.all_gather(w_up.astype(bf16), "fsdp", axis=0, tiled=True),
        lax.all_gather(w_down.astype(bf16), "fsdp", axis=0, tiled=True),
    )
    factor = scale_base / math.sqrt(HD) * jax.nn.softplus(query_scale)
    factor_two = (factor * LOG2E)[:, None]
    w_flipped = own_qkv.T
    pieces = []
    for head in range(heads):
        for part in (1, 2):
            at = part * width + head * HD
            pieces.append(jnp.pad(own_qkv[:, at : at + HD], ((0, 0), (0, PAD - HD))))
    w_natural = jnp.concatenate(pieces, axis=1)
    *kept, mixed = attention_forward(
        order, normed_all, w_natural, w_flipped, factor_two, parts, heads
    )
    attn_flipped = lax.all_to_all(mixed, "ctx", 0, 0, tiled=True).reshape(D, rows_dev)
    mid = layer_in + dot(attn_flipped, out_full, (0, 0))
    scale_two = rms_scale(mid)
    unit_two = mid * scale_two
    normed_two = (unit_two * gain_two).astype(bf16)
    hidden = dot(normed_two, up_full)
    gate_sig = jax.nn.sigmoid(hidden)
    act = (hidden * gate_sig).astype(bf16)
    output = (mid + dot(act, down_full)).astype(bf16)
    grad_in = cotangent[0]
    grad_down = dot(act, grad_in, (0, 0))
    dact = dot(grad_in, down_full, (1, 1))
    dhidden = (dact * gate_sig * (1.0 + hidden * (1.0 - gate_sig))).astype(bf16)
    grad_up = dot(normed_two, dhidden, (0, 0))
    dnormed_two = dot(dhidden, up_full, (1, 1))
    dunit_two = dnormed_two * gain_two
    dmid = grad_in.astype(f32) + scale_two * (
        dunit_two - unit_two * jnp.mean(dunit_two * unit_two, axis=-1, keepdims=True)
    )
    gain_two_grad = jnp.sum(dnormed_two * unit_two, axis=0)
    dbranch = dmid.astype(bf16)
    grad_out = dot(attn_flipped, dbranch)
    dattn = dot(out_full, dbranch, (1, 1)).astype(bf16)
    dmixed = lax.all_to_all(dattn.reshape(parts, width, rows_dev), "ctx", 0, 0, tiled=True)
    dqkv, dscale = attention_backward(order, kept, mixed, dmixed, factor_two, heads)
    grad_qkv = dot(normed_all, dqkv, (0, 1))
    dnormed_part = dot(dqkv, w_flipped, (0, 0)).astype(bf16)
    dnormed = lax.psum_scatter(dnormed_part, "ctx", scatter_dimension=0, tiled=True).astype(f32)
    scale_grad = (
        jnp.sum(dscale, axis=(0, 2))
        / factor_two[:, 0]
        * (scale_base / math.sqrt(HD))
        * jax.nn.sigmoid(query_scale)
    )
    dunit_one = dnormed * gain_one
    input_grad = dmid + scale_one * (
        dunit_one - unit_one * jnp.mean(dunit_one * unit_one, axis=-1, keepdims=True)
    )
    gain_one_grad = jnp.sum(dnormed * unit_one, axis=0)
    small_grad = jnp.concatenate([gain_one_grad, gain_two_grad, scale_grad])
    small_total = lax.psum(small_grad, ("ctx", "fsdp"))
    rate_qkv = qkv_rate_base / math.sqrt(D)
    rate_out = 0.5 / math.sqrt(max(D // 256, 1))
    rate_up = 0.5 / math.sqrt(D)
    rate_down = 0.5 / math.sqrt(FF)
    shard_out, shard_up, shard_down = (
        lax.psum_scatter(grad.astype(bf16), "fsdp", scatter_dimension=0, tiled=True)
        for grad in (grad_out, grad_up, grad_down)
    )
    total_out, total_up, total_down = (
        lax.psum(shard, "ctx").astype(f32) for shard in (shard_out, shard_up, shard_down)
    )
    shard_qkv = lax.psum_scatter(grad_qkv.astype(bf16), "fsdp", scatter_dimension=0, tiled=True)
    rows = shard_qkv.shape[0]
    total_qkv = (
        lax.all_gather(shard_qkv, "ctx", axis=0)
        .reshape(parts, rows, 3, width)
        .transpose(1, 2, 0, 3)
        .reshape(rows, 3 * D)
        .astype(f32)
    )
    qkv_set = adamw(w_qkv, m_qkv, v_qkv, total_qkv, rate_qkv, decay_rate)
    out_set = adamw(w_out, m_out, v_out, total_out, rate_out, decay_rate)
    up_set = adamw(w_up, m_up, v_up, total_up, rate_up, decay_rate)
    down_set = adamw(w_down, m_down, v_down, total_down, rate_down, decay_rate)
    small_set = adamw(small_params, small_m, small_v, small_total, small_rate, 0.0)
    return (
        output[None],
        input_grad.astype(bf16)[None],
        qkv_set[0],
        qkv_set[1],
        qkv_set[2],
        qkv_set[0].astype(bf16),
        out_set[0],
        out_set[1],
        out_set[2],
        out_set[0].astype(bf16),
        up_set[0],
        up_set[1],
        up_set[2],
        up_set[0].astype(bf16),
        down_set[0],
        down_set[1],
        down_set[2],
        down_set[0].astype(bf16),
        small_set[0],
        small_set[1],
        small_set[2],
    )


def solution(mesh):
    rows = P("fsdp", "ctx", None)
    weight = P("fsdp", None)
    return jax.shard_map(
        functools.partial(body, mesh.shape["ctx"]),
        mesh=mesh,
        in_specs=(rows, rows, weight) + (weight,) * 12 + (P(),) * 3,
        out_specs=(rows, rows) + (weight,) * 16 + (P(),) * 3,
        check_vma=False,
    )
```

```python
import functools
import math

import jax
import jax.numpy as jnp
from jax import lax
from jax.experimental import pallas as pl
from jax.experimental.pallas import tpu as pltpu
from jax.sharding import PartitionSpec as P

D = 1280
H = 16
HD = 80
FF = 1280
BLOCK = 256
CONT = 512
STEP = 3
PAD = 128
EXTRA = 16
TILE = CONT

bf16 = jnp.bfloat16
f32 = jnp.float32

norm_eps = 1e-06
beta_one = 0.5
beta_two = 0.5
adam_eps = 1e-08
decay_rate = 0.1
small_rate = 0.75
qkv_rate_base = 1.0
scale_base = 1.442695
LOG2E = math.log2(math.e)
LN2 = math.log(2.0)


def rms_scale(values):
    return lax.rsqrt(jnp.mean(values * values, axis=-1, keepdims=True) + norm_eps)


def adamw(weight, first, second, gradient, step_rate, decay_on):
    first_new = beta_one * first + (1.0 - beta_one) * gradient
    second_new = beta_two * second + (1.0 - beta_two) * gradient * gradient
    corr_one = 1.0 - beta_one**STEP
    corr_two = 1.0 - beta_two**STEP
    update = first_new / corr_one / (jnp.sqrt(second_new / corr_two) + adam_eps)
    weight_new = weight - step_rate * (update + decay_on * weight)
    return (weight_new, first_new, second_new)


def dot(left, right, contract=(1, 0)):
    return lax.dot_general(
        left, right, (((contract[0],), (contract[1],)), ((), ())), preferred_element_type=f32
    )


def fill_slots(order_ref, slot_ref, num_blocks):
    def place(slot, carry):
        slot_ref[order_ref[slot]] = slot
        return carry

    lax.fori_loop(0, num_blocks, place, 0)


def three_rows(row):
    high = row.astype(bf16)
    rest = row - high.astype(f32)
    middle = rest.astype(bf16)
    low = (rest - middle.astype(f32)).astype(bf16)
    index = lax.broadcasted_iota(jnp.int32, (EXTRA, row.shape[1]), 0)
    zero = jnp.zeros((EXTRA, row.shape[1]), f32)
    rows = jnp.where(index == 0, high.astype(f32), zero)
    rows = jnp.where(index == 1, middle.astype(f32), rows)
    rows = jnp.where(index == 2, low.astype(f32), rows)
    return rows.astype(bf16)


def tile_at(tile):
    return pl.ds(pl.multiple_of(tile * TILE, TILE), TILE)


def half_at(slot):
    return pl.ds(pl.multiple_of(lax.rem(slot, 2) * BLOCK, BLOCK), BLOCK)


def causal():
    key = lax.broadcasted_iota(jnp.int32, (TILE, TILE), 0)
    query = lax.broadcasted_iota(jnp.int32, (TILE, TILE), 1)
    return key <= query


def forward_kernel(
    heads,
    order_ref,
    x_ref,
    wn_ref,
    wt_ref,
    factor_ref,
    qt_ref,
    kt_ref,
    kn_ref,
    vn_ref,
    lse_ref,
    ot_ref,
    slot_ref,
    vt_ref,
    acc_ref,
    top_ref,
):
    tokens = x_ref.shape[0]
    num_blocks = tokens // BLOCK
    num_tiles = tokens // TILE
    prompt_tiles = num_tiles // 2
    fill_slots(order_ref, slot_ref, num_blocks)
    width = heads * HD
    lane = lax.broadcasted_iota(jnp.int32, (BLOCK, PAD), 1)
    is_extra = (lane >= HD) & (lane < HD + 3)

    def project(slot, carry):
        rows = x_ref[pl.ds(pl.multiple_of(slot * BLOCK, BLOCK), BLOCK), :]
        to = pl.ds(pl.multiple_of(order_ref[slot] * BLOCK, BLOCK), BLOCK)
        natural = dot(rows, wn_ref[...])
        flipped = dot(wt_ref[...], rows, (1, 1))
        for head in range(heads):
            key = natural[:, 2 * head * PAD : (2 * head + 1) * PAD]
            value = natural[:, (2 * head + 1) * PAD : (2 * head + 2) * PAD]
            kn_ref[head, to, :] = jnp.where(is_extra, 1.0, key).astype(bf16)
            vn_ref[head, to, :] = jnp.where(is_extra, 1.0, value).astype(bf16)
            at = head * HD
            qt_ref[head, :HD, to] = (flipped[at : at + HD] * factor_ref[...]).astype(bf16)
            qt_ref[head, HD:, to] = jnp.zeros((PAD - HD, BLOCK), bf16)
            kt_ref[head, :, to] = flipped[width + at : width + at + HD].astype(bf16)
            at = 2 * width + head * HD
            vt_ref[head, :HD, to] = flipped[at : at + HD].astype(bf16)
            vt_ref[head, HD:, to] = jnp.ones((EXTRA, BLOCK), bf16)
        return carry

    lax.fori_loop(0, num_blocks, project, 0)
    allowed = causal()

    def query_tile(tile, carry):
        here = tile_at(tile)
        top_ref[...] = jnp.full(top_ref.shape, -1e30, f32)
        acc_ref[...] = jnp.zeros(acc_ref.shape, f32)

        def step(keys, masked):
            for head in range(heads):
                scores = dot(kn_ref[head, keys, :], qt_ref[head, :, here])
                if masked:
                    scores = jnp.where(allowed, scores, -1e30)
                old = top_ref[head]
                top = jnp.maximum(old, jnp.max(scores, axis=0, keepdims=True))
                probs = jnp.exp2(scores - top).astype(bf16)
                acc_ref[head] = acc_ref[head] * jnp.exp2(old - top) + dot(
                    vt_ref[head, :, keys], probs
                )
                top_ref[head] = top

        def full(key_tile, inner):
            step(tile_at(key_tile), False)
            return inner

        lax.fori_loop(0, jnp.minimum(tile, prompt_tiles), full, 0)
        step(here, True)
        for head in range(heads):
            acc = acc_ref[head]
            mass = acc[HD : HD + 1]
            mixed = (acc[:HD] / mass).astype(bf16)
            lse_ref[head, :, here] = top_ref[head] + jnp.log2(mass)
            for part in range(TILE // BLOCK):
                slot = slot_ref[tile * (TILE // BLOCK) + part]
                ot_ref[slot // 2, head * HD : (head + 1) * HD, half_at(slot)] = mixed[
                    :, part * BLOCK : (part + 1) * BLOCK
                ]
        return carry

    lax.fori_loop(0, num_tiles, query_tile, 0)


def backward_kernel(
    heads,
    order_ref,
    qt_ref,
    kt_ref,
    kn_ref,
    vn_ref,
    lse_ref,
    ot_ref,
    dt_ref,
    factor_ref,
    dqkv_ref,
    dscale_ref,
    slot_ref,
    qa_ref,
    da_ref,
    dq_ref,
    dk_ref,
    dv_ref,
):
    tokens = kn_ref.shape[1]
    num_blocks = tokens // BLOCK
    num_tiles = tokens // TILE
    prompt_tiles = num_tiles // 2
    width = heads * HD
    fill_slots(order_ref, slot_ref, num_blocks)

    def prepare(block, carry):
        slot = slot_ref[block]
        to = pl.ds(pl.multiple_of(block * BLOCK, BLOCK), BLOCK)
        for head in range(heads):
            rows = slice(head * HD, (head + 1) * HD)
            grad = dt_ref[slot // 2, rows, half_at(slot)]
            mixed = ot_ref[slot // 2, rows, half_at(slot)]
            delta = jnp.sum(grad.astype(f32) * mixed.astype(f32), axis=0, keepdims=True)
            da_ref[head, :HD, to] = grad
            da_ref[head, HD : HD + EXTRA, to] = three_rows(-delta)
            da_ref[head, HD + EXTRA :, to] = jnp.zeros((PAD - HD - EXTRA, BLOCK), bf16)
            qa_ref[head, :HD, to] = qt_ref[head, :HD, to]
            qa_ref[head, HD : HD + EXTRA, to] = three_rows(-lse_ref[head, :, to])
            qa_ref[head, HD + EXTRA :, to] = jnp.zeros((PAD - HD - EXTRA, BLOCK), bf16)
        return carry

    lax.fori_loop(0, num_blocks, prepare, 0)
    dk_ref[...] = jnp.zeros(dk_ref.shape, f32)
    dv_ref[...] = jnp.zeros(dv_ref.shape, f32)
    dscale_ref[...] = jnp.zeros(dscale_ref.shape, f32)
    allowed = causal()

    def query_tile(tile, carry):
        here = tile_at(tile)
        dq_ref[...] = jnp.zeros(dq_ref.shape, f32)

        def step(keys, masked):
            for head in range(heads):
                probs = jnp.exp2(dot(kn_ref[head, keys, :], qa_ref[head, :, here]))
                if masked:
                    probs = jnp.where(allowed, probs, 0.0)
                spread = dot(vn_ref[head, keys, :], da_ref[head, :, here])
                dscores = (probs * spread).astype(bf16)
                dv_ref[head, :, keys] += dot(da_ref[head, :HD, here], probs.astype(bf16), (1, 1))
                dk_ref[head, :, keys] += dot(qa_ref[head, :HD, here], dscores, (1, 1))
                dq_ref[head] += dot(kt_ref[head, :, keys], dscores)

        def full(key_tile, inner):
            step(tile_at(key_tile), False)
            return inner

        lax.fori_loop(0, jnp.minimum(tile, prompt_tiles), full, 0)
        step(here, True)
        for head in range(heads):
            dq = dq_ref[head]
            product = dq * qt_ref[head, :HD, here].astype(f32)
            for lane in range(TILE // PAD):
                dscale_ref[head] += product[:, lane * PAD : (lane + 1) * PAD]
            scaled = (dq * (factor_ref[...] * LN2)).astype(bf16)
            for part in range(TILE // BLOCK):
                slot = slot_ref[tile * (TILE // BLOCK) + part]
                dqkv_ref[slot // 2, head * HD : (head + 1) * HD, half_at(slot)] = scaled[
                    :, part * BLOCK : (part + 1) * BLOCK
                ]
        return carry

    lax.fori_loop(0, num_tiles, query_tile, 0)

    def finish(block, carry):
        slot = slot_ref[block]
        owner, to = slot // 2, half_at(slot)
        at = pl.ds(pl.multiple_of(block * BLOCK, BLOCK), BLOCK)
        for head in range(heads):
            row = width + head * HD
            dqkv_ref[owner, row : row + HD, to] = (dk_ref[head, :, at] * LN2).astype(bf16)
            row = 2 * width + head * HD
            dqkv_ref[owner, row : row + HD, to] = dv_ref[head, :, at].astype(bf16)
        return carry

    lax.fori_loop(0, num_blocks, finish, 0)


def in_vmem(count):
    return [pl.BlockSpec(memory_space=pltpu.VMEM)] * count


def params():
    return pltpu.CompilerParams(vmem_limit_bytes=60 * 1024 * 1024)


def attention_forward(order, rows, w_natural, w_flipped, factor, parts, heads):
    tokens = rows.shape[0]
    return pl.pallas_call(
        functools.partial(forward_kernel, heads),
        name="attention_forward",
        out_shape=[
            jax.ShapeDtypeStruct((heads, PAD, tokens), bf16),
            jax.ShapeDtypeStruct((heads, HD, tokens), bf16),
            jax.ShapeDtypeStruct((heads, tokens, PAD), bf16),
            jax.ShapeDtypeStruct((heads, tokens, PAD), bf16),
            jax.ShapeDtypeStruct((heads, 1, tokens), f32),
            jax.ShapeDtypeStruct((parts, heads * HD, tokens // parts), bf16),
        ],
        in_specs=[pl.BlockSpec(memory_space=pltpu.SMEM)] + in_vmem(4),
        out_specs=in_vmem(6),
        scratch_shapes=[
            pltpu.SMEM((tokens // BLOCK,), jnp.int32),
            pltpu.VMEM((heads, HD + EXTRA, tokens), bf16),
            pltpu.VMEM((heads, HD + EXTRA, TILE), f32),
            pltpu.VMEM((heads, 1, TILE), f32),
        ],
        compiler_params=params(),
    )(order, rows, w_natural, w_flipped, factor)


def attention_backward(order, kept, mixed, dmixed, factor, heads):
    qt, kt, kn, vn, lse = kept
    tokens = kn.shape[1]
    return pl.pallas_call(
        functools.partial(backward_kernel, heads),
        name="attention_backward",
        out_shape=[
            jax.ShapeDtypeStruct((mixed.shape[0], 3 * heads * HD, mixed.shape[2]), bf16),
            jax.ShapeDtypeStruct((heads, HD, PAD), f32),
        ],
        in_specs=[pl.BlockSpec(memory_space=pltpu.SMEM)] + in_vmem(8),
        out_specs=in_vmem(2),
        scratch_shapes=[
            pltpu.SMEM((tokens // BLOCK,), jnp.int32),
            pltpu.VMEM((heads, PAD, tokens), bf16),
            pltpu.VMEM((heads, PAD, tokens), bf16),
            pltpu.VMEM((heads, HD, TILE), f32),
            pltpu.VMEM((heads, HD, tokens), f32),
            pltpu.VMEM((heads, HD, tokens), f32),
        ],
        compiler_params=params(),
    )(order, qt, kt, kn, vn, lse, mixed, dmixed, factor)


def reduce_kernel(
    parts,
    groups,
    dq_ref,
    wt_ref,
    u_ref,
    wc_ref,
    mlp_ref,
    small_ref,
    down_ref,
    up_ref,
    own_ref,
    ugather_ref,
    mgather_ref,
    sgather_ref,
    pair_ref,
    sum_ref,
    urecv_ref,
    mrecv_ref,
    part_ref,
    column_ref,
    smine_ref,
    srecv_ref,
    pair_sem,
    sum_sem,
    u_sem,
    m_sem,
    line_sem,
    side_sem,
    small_sem,
    cross_sem,
):
    chips = parts // 2
    here = lax.axis_index("ctx")
    group = lax.axis_index("fsdp")
    core = lax.rem(here, 2)
    chip = here // 2
    other = here + 1 - 2 * core
    ctx_peers = [lax.rem(here + step, parts) for step in range(1, parts)]
    chip_peers = [lax.rem(chip + step, chips) for step in range(1, chips)]
    group_peers = [lax.rem(group + step, groups) for step in range(1, groups)]

    barrier = pltpu.get_barrier_semaphore()
    for peer in ctx_peers:
        pl.semaphore_signal(barrier, inc=1, device_id={"ctx": peer})
    for peer in group_peers:
        pl.semaphore_signal(barrier, inc=1, device_id={"fsdp": peer})
    pl.semaphore_wait(barrier, parts + groups - 2)

    def send(source, target, sems, device):
        return pltpu.make_async_remote_copy(
            src_ref=source,
            dst_ref=target,
            send_sem=sems[0],
            recv_sem=sems[1],
            device_id=device,
        )

    def pair_copy(index):
        return send(
            dq_ref.at[index, 1 - core],
            pair_ref.at[index],
            (pair_sem.at[0, index], pair_sem.at[1, index]),
            {"ctx": other},
        )

    def u_copy(peer, source):
        return send(
            u_ref.at[peer],
            urecv_ref.at[source],
            (u_sem.at[0, peer], u_sem.at[1, source]),
            {"fsdp": peer},
        )

    def m_copy(peer, source):
        return send(
            mlp_ref.at[peer],
            mrecv_ref.at[source],
            (m_sem.at[0, peer], m_sem.at[1, source]),
            {"ctx": 2 * peer + core},
        )

    for index in range(chips):
        pair_copy(index).start()
    for peer in group_peers:
        u_copy(peer, group).start()
    for peer in chip_peers:
        m_copy(peer, chip).start()
    for index in range(chips):
        pair_copy(index).wait_recv()

    rows_half = own_ref.shape[0] // 2

    def partial(target):
        def half(index, carry):
            rows = pl.ds(pl.multiple_of(index * rows_half, rows_half), rows_half)
            part_ref[rows, :] = dot(dq_ref[target, core, :, rows], wt_ref[core], (0, 0)) + dot(
                pair_ref[target, :, rows], wt_ref[1 - core], (0, 0)
            )
            return carry

        lax.fori_loop(0, 2, half, 0)

    def sum_copy(way, target):
        return send(
            sum_ref.at[way, target],
            sum_ref.at[way, target],
            (sum_sem.at[0, way, target], sum_sem.at[1, way, target]),
            {"ctx": here + (2 if way else -2)},
        )

    def reduce_step(step):
        last = step == chips - 2
        for way, target, active, first, out_ref in (
            (0, step - (chips - 1) + chip, step >= chips - 1 - chip, chip == chips - 1, down_ref),
            (1, chips - 1 - step + chip, step >= chip, chip == 0, up_ref),
        ):

            @pl.when(active)
            def _():
                partial(target)

                @pl.when(first)
                def _():
                    sum_ref[way, target] = part_ref[...].astype(bf16)

                @pl.when(jnp.logical_not(first))
                def _():
                    sum_copy(way, target).wait_recv()
                    sum_ref[way, target] = (
                        part_ref[...] + sum_ref[way, target].astype(f32)
                    ).astype(bf16)

                if last:
                    out_ref[...] = sum_ref[way, target]
                else:
                    sum_copy(way, target).start()

            if last:

                @pl.when(jnp.logical_not(active))
                def _():
                    out_ref[...] = jnp.zeros(out_ref.shape, bf16)

    gathers = (ugather_ref, mgather_ref)

    def line_copy(which, way, step, piece):
        ref = gathers[which].at[2 * piece + core]
        sems = (line_sem.at[0, which, way, step], line_sem.at[1, which, way, step])
        return send(ref, ref, sems, {"ctx": here + (2 if way else -2)})

    def side_copy(which, piece, lane):
        ref = gathers[which].at[2 * piece + lane]
        sems = (side_sem.at[0, which, piece], side_sem.at[1, which, piece])
        return send(ref, ref, sems, {"ctx": other})

    def line_sends(which, step, go):
        @pl.when((chip < chips - 1) & (chip - step >= 0))
        def _():
            go(line_copy(which, 1, step, chip - step))

        @pl.when((chip > 0) & (chip + step <= chips - 1))
        def _():
            go(line_copy(which, 0, step, chip + step))

    def line_receive(which, step):
        @pl.when(chip - 1 - step >= 0)
        def _():
            line_copy(which, 1, step, chip - 1 - step).wait_recv()
            side_copy(which, chip - 1 - step, core).start()

        @pl.when(chip + 1 + step <= chips - 1)
        def _():
            line_copy(which, 0, step, chip + 1 + step).wait_recv()
            side_copy(which, chip + 1 + step, core).start()

    def small_copy(peer, source):
        return send(
            smine_ref,
            srecv_ref.at[source],
            (small_sem.at[0, peer], small_sem.at[1, source]),
            {"ctx": peer},
        )

    def cross_copy(peer, source):
        return send(
            sgather_ref.at[group],
            sgather_ref.at[source],
            (cross_sem.at[0, peer], cross_sem.at[1, source]),
            {"fsdp": peer},
        )

    reduce_step(0)

    total = u_ref[group].astype(f32)
    for peer in group_peers:
        u_copy(group, peer).wait_recv()
        total = total + urecv_ref[peer].astype(f32)
    ugather_ref[here] = total.astype(bf16)
    side_copy(0, chip, core).start()
    line_sends(0, 0, lambda copy: copy.start())
    held = total.shape[0]
    gain = jnp.sum(total * wc_ref[...].astype(f32), axis=1, keepdims=True)
    column_ref[...] = jnp.zeros(column_ref.shape, f32)
    column_ref[:held, :] = jnp.broadcast_to(gain, (held, PAD))
    flat = column_ref[...].T[:1]
    smine_ref[...] = small_ref[...]
    for row in range(column_ref.shape[0] // PAD):
        smine_ref[row : row + 1, :] = flat[:, row * PAD : (row + 1) * PAD]
    for peer in ctx_peers:
        small_copy(peer, here).start()

    total = mlp_ref[chip].astype(f32)
    for peer in chip_peers:
        m_copy(chip, peer).wait_recv()
        total = total + mrecv_ref[peer].astype(f32)
    mgather_ref[here] = total.astype(bf16)
    side_copy(1, chip, core).start()
    line_sends(1, 0, lambda copy: copy.start())

    for step in range(1, chips):
        if step <= chips - 2:
            reduce_step(step)
        for which in range(2):
            line_receive(which, step - 1)
            if step <= chips - 2:
                line_sends(which, step, lambda copy: copy.start())
        if step == 1:
            small = smine_ref[...]
            for peer in ctx_peers:
                small_copy(here, peer).wait_recv()
                small = small + srecv_ref[peer]
            sgather_ref[group] = small
            for peer in group_peers:
                cross_copy(peer, group).start()

    partial(chip)
    own_ref[...] = part_ref[...]

    for which in range(2):
        for piece in range(chips):
            side_copy(which, piece, 1 - core).wait_recv()
            side_copy(which, piece, core).wait_send()
        for step in range(chips - 1):
            line_sends(which, step, lambda copy: copy.wait_send())
    for index in range(chips):
        pair_copy(index).wait_send()
    for peer in group_peers:
        cross_copy(group, peer).wait_recv()
        cross_copy(peer, group).wait_send()
        u_copy(peer, group).wait_send()
    for peer in chip_peers:
        m_copy(peer, chip).wait_send()
    for peer in ctx_peers:
        small_copy(peer, here).wait_send()
    for step in range(chips - 2):

        @pl.when(step >= chips - 1 - chip)
        def _():
            sum_copy(0, step - (chips - 1) + chip).wait_send()

        @pl.when(step >= chip)
        def _():
            sum_copy(1, chips - 1 - step + chip).wait_send()


def reduce_gradients(parts, groups, dqkv, w_pair, u_parts, w_columns, mlp, small):
    chips = parts // 2
    rows_dev = dqkv.shape[3]
    rows, width = w_columns.shape
    lanes = -(-rows // PAD) * PAD
    dma = pltpu.SemaphoreType.DMA
    return pl.pallas_call(
        functools.partial(reduce_kernel, parts, groups),
        name="reduce_gradients",
        out_shape=[
            jax.ShapeDtypeStruct((rows_dev, D), bf16),
            jax.ShapeDtypeStruct((rows_dev, D), bf16),
            jax.ShapeDtypeStruct((rows_dev, D), f32),
            jax.ShapeDtypeStruct((parts, rows, width), bf16),
            jax.ShapeDtypeStruct((parts,) + mlp.shape[1:], bf16),
            jax.ShapeDtypeStruct((groups,) + small.shape, f32),
        ],
        in_specs=in_vmem(6),
        out_specs=in_vmem(6),
        scratch_shapes=[
            pltpu.VMEM((chips,) + dqkv.shape[2:], bf16),
            pltpu.VMEM((2, chips, rows_dev, D), bf16),
            pltpu.VMEM(u_parts.shape, bf16),
            pltpu.VMEM(mlp.shape, bf16),
            pltpu.VMEM((rows_dev, D), f32),
            pltpu.VMEM((lanes, PAD), f32),
            pltpu.VMEM(small.shape, f32),
            pltpu.VMEM((parts,) + small.shape, f32),
            dma((2, chips)),
            dma((2, 2, chips)),
            dma((2, groups)),
            dma((2, chips)),
            dma((2, 2, 2, chips)),
            dma((2, 2, chips)),
            dma((2, parts)),
            dma((2, groups)),
        ],
        compiler_params=pltpu.CompilerParams(
            vmem_limit_bytes=60 * 1024 * 1024, collective_id=1, has_side_effects=True
        ),
    )(dqkv, w_pair, u_parts, w_columns, mlp, small)


def update_kernel(rates, *refs):
    sets = len(rates)
    for index, rate in enumerate(rates):
        weight, first, second, gradient = (ref[...] for ref in refs[4 * index : 4 * index + 4])
        outs = refs[4 * (sets + index) : 4 * (sets + index) + 4]
        new, first, second = adamw(weight, first, second, gradient.astype(f32), rate, decay_rate)
        outs[0][...] = new
        outs[1][...] = first
        outs[2][...] = second
        outs[3][...] = new.astype(bf16)


def update(rates, *arrays):
    step_rows = 32
    rows = arrays[0].shape[0]
    specs, shapes, moved = [], [], 0
    for array in arrays:
        specs.append(pl.BlockSpec((step_rows, array.shape[1]), lambda i: (i, 0)))
    for index in range(len(rates)):
        shape = arrays[4 * index].shape
        shapes += [jax.ShapeDtypeStruct(shape, f32)] * 3 + [jax.ShapeDtypeStruct(shape, bf16)]
        moved += shape[0] * shape[1] * 28
    return pl.pallas_call(
        functools.partial(update_kernel, rates),
        name="update_weights",
        grid=(rows // step_rows,),
        in_specs=specs,
        out_specs=specs,
        out_shape=shapes,
        compiler_params=params(),
        cost_estimate=pl.CostEstimate(flops=moved, bytes_accessed=moved, transcendentals=0),
    )(*arrays)


def body(
    parts,
    groups,
    inputs,
    cotangent,
    block_order,
    w_qkv,
    m_qkv,
    v_qkv,
    w_out,
    m_out,
    v_out,
    w_up,
    m_up,
    v_up,
    w_down,
    m_down,
    v_down,
    small_params,
    small_m,
    small_v,
):
    heads = H // parts
    width = heads * HD
    rows_dev = inputs.shape[1]
    tokens = rows_dev * parts
    here = lax.axis_index("ctx")
    order = block_order[0]
    gain_one = small_params[:D]
    gain_two = small_params[D : 2 * D]
    query_scale = small_params[2 * D :]
    core = lax.rem(here, 2)
    group = lax.axis_index("fsdp")
    rows = w_qkv.shape[0]

    def head_columns(owner):
        return jnp.concatenate(
            [
                lax.dynamic_slice_in_dim(w_qkv, part * D + owner * width, width, 1)
                for part in range(3)
            ],
            axis=1,
        )

    gain_rows = lax.dynamic_slice_in_dim(gain_one, group * rows, rows, 0)[:, None]
    columns = [head_columns(here - core + lane) for lane in range(2)]
    gained = jnp.concatenate([(gain_rows * part).astype(bf16) for part in columns], axis=1)
    w_pair = lax.all_gather(gained, "fsdp", axis=0, tiled=True).T.reshape(2, 3 * width, D)
    w_flipped = lax.dynamic_index_in_dim(w_pair, core, 0, False)
    own_qkv = w_flipped.T
    w_columns = head_columns(here).astype(bf16)
    layer_in = inputs[0].astype(f32)
    scale_one = rms_scale(layer_in)
    unit_one = layer_in * scale_one
    unit_all = lax.all_gather(unit_one.astype(bf16), "ctx", axis=0, tiled=True)
    out_full, up_full, down_full = (
        lax.all_gather(w_out.astype(bf16), "fsdp", axis=0, tiled=True),
        lax.all_gather(w_up.astype(bf16), "fsdp", axis=0, tiled=True),
        lax.all_gather(w_down.astype(bf16), "fsdp", axis=0, tiled=True),
    )
    factor = scale_base / math.sqrt(HD) * jax.nn.softplus(query_scale)
    factor_two = (factor * LOG2E)[:, None]
    pieces = []
    for head in range(heads):
        for part in (1, 2):
            at = part * width + head * HD
            pieces.append(jnp.pad(own_qkv[:, at : at + HD], ((0, 0), (0, PAD - HD))))
    w_natural = jnp.concatenate(pieces, axis=1)
    *kept, mixed = attention_forward(
        order, unit_all, w_natural, w_flipped, factor_two, parts, heads
    )
    attn_flipped = lax.all_to_all(mixed, "ctx", 0, 0, tiled=True).reshape(D, rows_dev)
    mid = layer_in + dot(attn_flipped, out_full, (0, 0))
    scale_two = rms_scale(mid)
    unit_two = mid * scale_two
    normed_two = (unit_two * gain_two).astype(bf16)
    hidden = dot(normed_two, up_full)
    gate_sig = jax.nn.sigmoid(hidden)
    act = (hidden * gate_sig).astype(bf16)
    output = (mid + dot(act, down_full)).astype(bf16)
    grad_in = cotangent[0]
    grad_down = dot(act, grad_in, (0, 0))
    dact = dot(grad_in, down_full, (1, 1))
    dhidden = (dact * gate_sig * (1.0 + hidden * (1.0 - gate_sig))).astype(bf16)
    grad_up = dot(normed_two, dhidden, (0, 0))
    dnormed_two = dot(dhidden, up_full, (1, 1))
    dunit_two = dnormed_two * gain_two
    dmid = grad_in.astype(f32) + scale_two * (
        dunit_two - unit_two * jnp.mean(dunit_two * unit_two, axis=-1, keepdims=True)
    )
    gain_two_grad = jnp.sum(dnormed_two * unit_two, axis=0)
    dbranch = dmid.astype(bf16)
    grad_out = dot(attn_flipped, dbranch)
    dattn = dot(out_full, dbranch, (1, 1)).astype(bf16)
    half = rows // 2
    grads = jnp.stack([grad_out.astype(bf16), grad_up.astype(bf16), grad_down.astype(bf16)])
    grads = grads.reshape(3, groups, 2, half, D)
    pair = [(i, i ^ 1) for i in range(parts)]
    theirs = lax.dynamic_index_in_dim(grads, 1 - core, 2, False)
    mine = lax.dynamic_index_in_dim(grads, core, 2, False)
    mine = (mine.astype(f32) + lax.ppermute(theirs, "ctx", pair).astype(f32)).astype(bf16)
    mlp_sum = lax.dynamic_index_in_dim(mine, group, 1, False).astype(f32)
    for step in range(1, groups):
        chunk = lax.dynamic_index_in_dim(mine, group ^ step, 1, False)
        swap = [(i, i ^ step) for i in range(groups)]
        mlp_sum = mlp_sum + lax.ppermute(chunk, "fsdp", swap).astype(f32)
    mlp_part = (
        mlp_sum.astype(bf16).reshape(3, parts // 2, rows // parts, D).transpose(1, 0, 2, 3)
    )
    dmixed = lax.all_to_all(dattn.reshape(parts, width, rows_dev), "ctx", 0, 0, tiled=True)
    dqkv, dscale = attention_backward(order, kept, mixed, dmixed, factor_two, heads)
    u_parts = (
        lax.dot_general(
            unit_all.reshape(parts, rows_dev, D),
            dqkv,
            (((0, 1), (0, 2)), ((), ())),
            preferred_element_type=f32,
        )
        .astype(bf16)
        .reshape(groups, rows, 3 * width)
    )
    scale_grad = (
        jnp.sum(dscale, axis=(0, 2))
        / factor_two[:, 0]
        * (scale_base / math.sqrt(HD))
        * jax.nn.sigmoid(query_scale)
    )
    lanes = -(-rows // PAD) * PAD
    small_rows = -(-(lanes + D + PAD) // (8 * PAD)) * 8
    small = jnp.concatenate([jnp.zeros((lanes,), f32), gain_two_grad, scale_grad])
    small = jnp.pad(small, (0, small_rows * PAD - small.shape[0])).reshape(small_rows, PAD)
    send_down, send_up, own_part, u_all, mlp_all, small_all = reduce_gradients(
        parts,
        groups,
        dqkv.reshape(parts // 2, 2, 3 * width, rows_dev),
        w_pair,
        u_parts,
        w_columns,
        mlp_part,
        small,
    )
    got_down = lax.ppermute(send_down, "ctx", [(i, i - 2) for i in range(2, parts)])
    got_up = lax.ppermute(send_up, "ctx", [(i, i + 2) for i in range(parts - 2)])
    total_qkv = (
        u_all.reshape(parts, rows, 3, width).transpose(1, 2, 0, 3).reshape(rows, 3 * D)
        * gain_rows
    ).astype(bf16)
    total_mlp = (
        mlp_all.reshape(parts // 2, 2, 3, rows // parts, D)
        .transpose(2, 1, 0, 3, 4)
        .reshape(3, rows, D)
    )
    rate_qkv = qkv_rate_base / math.sqrt(D)
    rate_out = 0.5 / math.sqrt(max(D // 256, 1))
    rate_up = 0.5 / math.sqrt(D)
    rate_down = 0.5 / math.sqrt(FF)
    updated = update(
        (rate_qkv, rate_out, rate_up, rate_down),
        w_qkv,
        m_qkv,
        v_qkv,
        total_qkv,
        w_out,
        m_out,
        v_out,
        total_mlp[0],
        w_up,
        m_up,
        v_up,
        total_mlp[1],
        w_down,
        m_down,
        v_down,
        total_mlp[2],
    )
    flat = small_all.reshape(groups, small_rows * PAD)
    rest = jnp.sum(flat[:, lanes : lanes + D + HD], axis=0)
    small_total = jnp.concatenate([flat[:, :rows].reshape(D), rest])
    small_set = adamw(small_params, small_m, small_v, small_total, small_rate, 0.0)
    dunit_one = own_part + got_down.astype(f32) + got_up.astype(f32)
    input_grad = dmid + scale_one * (
        dunit_one - unit_one * jnp.mean(dunit_one * unit_one, axis=-1, keepdims=True)
    )
    return (
        output[None],
        input_grad.astype(bf16)[None],
        *updated,
        *small_set,
    )


def solution(mesh):
    rows = P("fsdp", "ctx", None)
    weight = P("fsdp", None)
    return jax.shard_map(
        functools.partial(body, mesh.shape["ctx"], mesh.shape["fsdp"]),
        mesh=mesh,
        in_specs=(rows, rows, weight) + (weight,) * 12 + (P(),) * 3,
        out_specs=(rows, rows) + (weight,) * 16 + (P(),) * 3,
        check_vma=False,
    )
```

```python
import functools
import math

import jax
import jax.numpy as jnp
from jax import lax
from jax.experimental import pallas as pl
from jax.experimental.pallas import tpu as pltpu
from jax.sharding import PartitionSpec as P

D = 1280
H = 16
HD = 80
FF = 1280
BLOCK = 256
CONT = 512
STEP = 3
PAD = 128
EXTRA = 16
TILE = CONT

bf16 = jnp.bfloat16
f32 = jnp.float32

norm_eps = 1e-06
beta_one = 0.5
beta_two = 0.5
adam_eps = 1e-08
decay_rate = 0.1
small_rate = 0.75
qkv_rate_base = 1.0
scale_base = 1.442695
LOG2E = math.log2(math.e)
LN2 = math.log(2.0)


def rms_scale(values):
    return lax.rsqrt(jnp.mean(values * values, axis=-1, keepdims=True) + norm_eps)


def adamw(weight, first, second, gradient, step_rate, decay_on):
    first_new = beta_one * first + (1.0 - beta_one) * gradient
    second_new = beta_two * second + (1.0 - beta_two) * gradient * gradient
    corr_one = 1.0 - beta_one**STEP
    corr_two = 1.0 - beta_two**STEP
    update = first_new / corr_one / (jnp.sqrt(second_new / corr_two) + adam_eps)
    weight_new = weight - step_rate * (update + decay_on * weight)
    return (weight_new, first_new, second_new)


def dot(left, right, contract=(1, 0)):
    return lax.dot_general(
        left, right, (((contract[0],), (contract[1],)), ((), ())), preferred_element_type=f32
    )


def three_rows(row):
    high = row.astype(bf16)
    rest = row - high.astype(f32)
    middle = rest.astype(bf16)
    low = (rest - middle.astype(f32)).astype(bf16)
    index = lax.broadcasted_iota(jnp.int32, (EXTRA, row.shape[1]), 0)
    zero = jnp.zeros((EXTRA, row.shape[1]), f32)
    rows = jnp.where(index == 0, high.astype(f32), zero)
    rows = jnp.where(index == 1, middle.astype(f32), rows)
    rows = jnp.where(index == 2, low.astype(f32), rows)
    return rows.astype(bf16)


def tile_at(tile):
    return pl.ds(pl.multiple_of(tile * TILE, TILE), TILE)


def block_at(slot):
    return pl.ds(pl.multiple_of(slot * BLOCK, BLOCK), BLOCK)


def tile_lanes(ref, head, slot_ref, tile, rows=slice(None)):
    first, second = slot_ref[2 * tile], slot_ref[2 * tile + 1]
    return jnp.concatenate(
        [ref[head, rows, block_at(first)], ref[head, rows, block_at(second)]], axis=1
    )


def tile_rows(ref, head, slot_ref, tile):
    first, second = slot_ref[2 * tile], slot_ref[2 * tile + 1]
    return jnp.concatenate([ref[head, block_at(first), :], ref[head, block_at(second), :]], axis=0)


def half_at(slot):
    return pl.ds(pl.multiple_of(lax.rem(slot, 2) * BLOCK, BLOCK), BLOCK)


def causal():
    key = lax.broadcasted_iota(jnp.int32, (TILE, TILE), 0)
    query = lax.broadcasted_iota(jnp.int32, (TILE, TILE), 1)
    return key <= query


def gather_kernel(
    parts,
    groups,
    heads,
    x_ref,
    gained_ref,
    mlp_ref,
    factor_ref,
    unit_ref,
    full_ref,
    wpair_ref,
    qt_ref,
    kt_ref,
    vt_ref,
    kn_ref,
    vn_ref,
    rows_ref,
    wrecv_ref,
    wflip_ref,
    line_sem,
    side_sem,
    keep_sem,
    w_sem,
    mlp_sem,
    cross_sem,
    own_sem,
):
    chips = parts // 2
    here = lax.axis_index("ctx")
    group = lax.axis_index("fsdp")
    core = lax.rem(here, 2)
    chip = here // 2
    other = here + 1 - 2 * core
    width = heads * HD
    group_peers = [lax.rem(group + step, groups) for step in range(1, groups)]

    barrier = pltpu.get_barrier_semaphore()
    pl.semaphore_signal(barrier, inc=1, device_id={"ctx": other})
    for peer in group_peers:
        pl.semaphore_signal(barrier, inc=1, device_id={"fsdp": peer})
    for step in (1, chips - 1):
        peer = lax.rem(chip + step, chips) * 2 + core
        pl.semaphore_signal(barrier, inc=1, device_id={"ctx": peer})
    pl.semaphore_wait(barrier, groups + 2)

    def send(source, target, sems, device):
        return pltpu.make_async_remote_copy(
            src_ref=source,
            dst_ref=target,
            send_sem=sems[0],
            recv_sem=sems[1],
            device_id=device,
        )

    def line_copy(way, step, piece):
        ref = rows_ref.at[2 * piece + core]
        sems = (line_sem.at[0, way, step], line_sem.at[1, way, step])
        return send(ref, ref, sems, {"ctx": here + (2 if way else -2)})

    def side_copy(piece, lane):
        ref = rows_ref.at[2 * piece + lane]
        return send(ref, ref, (side_sem.at[0, piece], side_sem.at[1, piece]), {"ctx": other})

    def w_copy(peer, source):
        sems = (w_sem.at[0, peer], w_sem.at[1, source])
        return send(gained_ref, wrecv_ref.at[source], sems, {"fsdp": peer})

    def mlp_copy(peer, source):
        sems = (mlp_sem.at[0, peer], mlp_sem.at[1, source])
        return send(mlp_ref.at[:, core], full_ref.at[:, source, core], sems, {"fsdp": peer})

    def cross_copy(source, lane):
        ref = full_ref.at[:, source, lane]
        sems = (cross_sem.at[0, source], cross_sem.at[1, source])
        return send(ref, ref, sems, {"ctx": other})

    def keep_copy(piece):
        return pltpu.make_async_copy(rows_ref.at[piece], unit_ref.at[piece], keep_sem.at[piece])

    own_copy = pltpu.make_async_copy(mlp_ref, full_ref.at[:, group], own_sem)

    rows = x_ref[...].astype(f32)
    rows_ref[here] = (rows * rms_scale(rows)).astype(bf16)

    def forward(way, step, piece):
        @pl.when((chip < chips - 1) if way else (chip > 0))
        def _():
            line_copy(way, step, piece).start()

    for way in range(2):
        forward(way, 0, chip)
    side_copy(chip, core).start()
    for peer in group_peers:
        w_copy(peer, group).start()
    own_copy.start()
    keep_copy(here).start()
    wrecv_ref[group] = gained_ref[...]
    for peer in group_peers:
        w_copy(group, peer).wait_recv()
    for peer in group_peers:
        mlp_copy(peer, group).start()
    flipped = wrecv_ref[...].reshape(D, 6 * width).T
    wpair_ref[0] = flipped[: 3 * width]
    wpair_ref[1] = flipped[3 * width :]
    wflip_ref[...] = wpair_ref[core]

    extra_row = lax.broadcasted_iota(jnp.int32, (PAD - HD, BLOCK), 0)
    extra = jnp.where(extra_row < 3, 1.0, 0.0)
    spare = jnp.zeros((PAD - HD, BLOCK), bf16)

    def project(piece):
        def half(index, carry):
            at = pl.ds(pl.multiple_of(index * BLOCK, BLOCK), BLOCK)
            to = pl.ds(pl.multiple_of((piece * 2 + index) * BLOCK, BLOCK), BLOCK)
            result = dot(wflip_ref[...], rows_ref[piece, at, :], (1, 1))
            for head in range(heads):
                query, key, value = (
                    result[part * width + head * HD : part * width + (head + 1) * HD]
                    for part in range(3)
                )
                qt_ref[head, :HD, to] = (query * factor_ref[...]).astype(bf16)
                qt_ref[head, HD:, to] = spare
                kt_ref[head, :, to] = key.astype(bf16)
                vt_ref[head, :HD, to] = value.astype(bf16)
                vt_ref[head, HD:, to] = jnp.ones((EXTRA, BLOCK), bf16)
                kn_ref[head, to, :] = jnp.concatenate([key, extra], axis=0).T.astype(bf16)
                vn_ref[head, to, :] = jnp.concatenate([value, extra], axis=0).T.astype(bf16)
            return carry

        lax.fori_loop(0, TILE // BLOCK, half, 0)

    def visit(distance, carry):
        for way in range(2):
            piece = chip - distance if way else chip + distance
            valid = (piece >= 0) if way else (piece <= chips - 1)

            @pl.when(valid & (distance > 0))
            def _():
                line_copy(way, distance - 1, piece).wait_recv()
                side_copy(piece, core).start()
                forward(way, distance, piece)
                keep_copy(2 * piece + core).start()

        for way in range(2):
            piece = chip - distance if way else chip + distance
            valid = (piece >= 0) if way else ((piece <= chips - 1) & (distance > 0))

            @pl.when(valid)
            def _():
                project(2 * piece + core)
                side_copy(piece, 1 - core).wait_recv()
                keep_copy(2 * piece + 1 - core).start()
                project(2 * piece + 1 - core)

        return carry

    lax.fori_loop(0, chips, visit, 0)

    for peer in group_peers:
        mlp_copy(group, peer).wait_recv()
        cross_copy(peer, core).start()
    for peer in group_peers:
        cross_copy(peer, 1 - core).wait_recv()
        cross_copy(peer, core).wait_send()
        w_copy(peer, group).wait_send()
        mlp_copy(peer, group).wait_send()
    own_copy.wait()

    def drain(piece, carry):
        keep_copy(2 * piece).wait()
        keep_copy(2 * piece + 1).wait()
        side_copy(piece, core).wait_send()

        @pl.when((piece <= chip) & (chip < chips - 1))
        def _():
            line_copy(1, chip - piece, piece).wait_send()

        @pl.when((piece >= chip) & (chip > 0))
        def _():
            line_copy(0, piece - chip, piece).wait_send()

        return carry

    lax.fori_loop(0, chips, drain, 0)


def gather_rows(parts, groups, heads, rows, gained, mlp, factor):
    rows_dev = rows.shape[0]
    tokens = parts * rows_dev
    dma = pltpu.SemaphoreType.DMA
    chips = parts // 2
    anywhere = pl.BlockSpec(memory_space=pl.ANY)
    return pl.pallas_call(
        functools.partial(gather_kernel, parts, groups, heads),
        name="gather_rows",
        out_shape=[
            jax.ShapeDtypeStruct((parts, rows_dev, D), bf16),
            jax.ShapeDtypeStruct((3, groups) + mlp.shape[1:], bf16),
            jax.ShapeDtypeStruct((2, 3 * heads * HD, D), bf16),
            jax.ShapeDtypeStruct((heads, PAD, tokens), bf16),
            jax.ShapeDtypeStruct((heads, HD, tokens), bf16),
            jax.ShapeDtypeStruct((heads, HD + EXTRA, tokens), bf16),
            jax.ShapeDtypeStruct((heads, tokens, PAD), bf16),
            jax.ShapeDtypeStruct((heads, tokens, PAD), bf16),
        ],
        in_specs=in_vmem(2) + [anywhere] + in_vmem(1),
        out_specs=[anywhere] * 2 + in_vmem(6),
        scratch_shapes=[
            pltpu.VMEM((parts, rows_dev, D), bf16),
            pltpu.VMEM((groups,) + gained.shape, bf16),
            pltpu.VMEM((3 * heads * HD, D), bf16),
            dma((2, 2, chips)),
            dma((2, chips)),
            dma((parts,)),
            dma((2, groups)),
            dma((2, groups)),
            dma((2, groups)),
            dma,
        ],
        compiler_params=pltpu.CompilerParams(
            vmem_limit_bytes=60 * 1024 * 1024, collective_id=2, has_side_effects=True
        ),
    )(rows, gained, mlp, factor)


def forward_kernel(
    heads,
    slot_ref,
    qt_ref,
    kn_ref,
    vt_ref,
    lse_ref,
    ot_ref,
    acc_ref,
    top_ref,
):
    tokens = kn_ref.shape[1]
    num_tiles = tokens // TILE
    prompt_tiles = num_tiles // 2
    allowed = causal()

    def query_tile(tile, carry):
        here = tile_at(tile)
        top_ref[...] = jnp.full(top_ref.shape, -1e30, f32)
        acc_ref[...] = jnp.zeros(acc_ref.shape, f32)

        queries = [tile_lanes(qt_ref, head, slot_ref, tile) for head in range(heads)]

        def step(key_tile, masked):
            for head in range(heads):
                scores = dot(tile_rows(kn_ref, head, slot_ref, key_tile), queries[head])
                if masked:
                    scores = jnp.where(allowed, scores, -1e30)
                old = top_ref[head]
                top = jnp.maximum(old, jnp.max(scores, axis=0, keepdims=True))
                probs = jnp.exp2(scores - top).astype(bf16)
                acc_ref[head] = acc_ref[head] * jnp.exp2(old - top) + dot(
                    tile_lanes(vt_ref, head, slot_ref, key_tile), probs
                )
                top_ref[head] = top

        def full(key_tile, inner):
            step(key_tile, False)
            return inner

        lax.fori_loop(0, jnp.minimum(tile, prompt_tiles), full, 0)
        step(tile, True)
        for head in range(heads):
            acc = acc_ref[head]
            mass = acc[HD : HD + 1]
            mixed = (acc[:HD] / mass).astype(bf16)
            lse_ref[head, :, here] = top_ref[head] + jnp.log2(mass)
            for part in range(TILE // BLOCK):
                slot = slot_ref[tile * (TILE // BLOCK) + part]
                ot_ref[slot // 2, head * HD : (head + 1) * HD, half_at(slot)] = mixed[
                    :, part * BLOCK : (part + 1) * BLOCK
                ]
        return carry

    lax.fori_loop(0, num_tiles, query_tile, 0)


def backward_kernel(
    heads,
    slot_ref,
    qt_ref,
    kt_ref,
    kn_ref,
    vn_ref,
    lse_ref,
    ot_ref,
    dt_ref,
    factor_ref,
    dqkv_ref,
    dscale_ref,
    qa_ref,
    da_ref,
    dq_ref,
    dk_ref,
    dv_ref,
):
    tokens = kn_ref.shape[1]
    num_blocks = tokens // BLOCK
    num_tiles = tokens // TILE
    prompt_tiles = num_tiles // 2
    width = heads * HD

    def prepare(block, carry):
        slot = slot_ref[block]
        to = pl.ds(pl.multiple_of(block * BLOCK, BLOCK), BLOCK)
        for head in range(heads):
            rows = slice(head * HD, (head + 1) * HD)
            grad = dt_ref[slot // 2, rows, half_at(slot)]
            mixed = ot_ref[slot // 2, rows, half_at(slot)]
            delta = jnp.sum(grad.astype(f32) * mixed.astype(f32), axis=0, keepdims=True)
            da_ref[head, :HD, to] = grad
            da_ref[head, HD : HD + EXTRA, to] = three_rows(-delta)
            da_ref[head, HD + EXTRA :, to] = jnp.zeros((PAD - HD - EXTRA, BLOCK), bf16)
            qa_ref[head, :HD, to] = qt_ref[head, :HD, block_at(slot)]
            qa_ref[head, HD : HD + EXTRA, to] = three_rows(-lse_ref[head, :, to])
            qa_ref[head, HD + EXTRA :, to] = jnp.zeros((PAD - HD - EXTRA, BLOCK), bf16)
        return carry

    lax.fori_loop(0, num_blocks, prepare, 0)
    dk_ref[...] = jnp.zeros(dk_ref.shape, f32)
    dv_ref[...] = jnp.zeros(dv_ref.shape, f32)
    dscale_ref[...] = jnp.zeros(dscale_ref.shape, f32)
    allowed = causal()

    def query_tile(tile, carry):
        here = tile_at(tile)
        dq_ref[...] = jnp.zeros(dq_ref.shape, f32)

        def step(key_tile, masked):
            keys = tile_at(key_tile)
            for head in range(heads):
                key_rows = tile_rows(kn_ref, head, slot_ref, key_tile)
                value_rows = tile_rows(vn_ref, head, slot_ref, key_tile)
                probs = jnp.exp2(dot(key_rows, qa_ref[head, :, here]))
                if masked:
                    probs = jnp.where(allowed, probs, 0.0)
                spread = dot(value_rows, da_ref[head, :, here])
                dscores = (probs * spread).astype(bf16)
                dv_ref[head, :, keys] += dot(da_ref[head, :HD, here], probs.astype(bf16), (1, 1))
                dk_ref[head, :, keys] += dot(qa_ref[head, :HD, here], dscores, (1, 1))
                dq_ref[head] += dot(tile_lanes(kt_ref, head, slot_ref, key_tile), dscores)

        def full(key_tile, inner):
            step(key_tile, False)
            return inner

        lax.fori_loop(0, jnp.minimum(tile, prompt_tiles), full, 0)
        step(tile, True)
        for head in range(heads):
            dq = dq_ref[head]
            product = dq * qa_ref[head, :HD, here].astype(f32)
            for lane in range(TILE // PAD):
                dscale_ref[head] += product[:, lane * PAD : (lane + 1) * PAD]
            scaled = (dq * (factor_ref[...] * LN2)).astype(bf16)
            for part in range(TILE // BLOCK):
                slot = slot_ref[tile * (TILE // BLOCK) + part]
                dqkv_ref[slot // 2, head * HD : (head + 1) * HD, half_at(slot)] = scaled[
                    :, part * BLOCK : (part + 1) * BLOCK
                ]
        return carry

    lax.fori_loop(0, num_tiles, query_tile, 0)

    def finish(block, carry):
        slot = slot_ref[block]
        owner, to = slot // 2, half_at(slot)
        at = pl.ds(pl.multiple_of(block * BLOCK, BLOCK), BLOCK)
        for head in range(heads):
            row = width + head * HD
            dqkv_ref[owner, row : row + HD, to] = (dk_ref[head, :, at] * LN2).astype(bf16)
            row = 2 * width + head * HD
            dqkv_ref[owner, row : row + HD, to] = dv_ref[head, :, at].astype(bf16)
        return carry

    lax.fori_loop(0, num_blocks, finish, 0)


def in_vmem(count):
    return [pl.BlockSpec(memory_space=pltpu.VMEM)] * count


def params():
    return pltpu.CompilerParams(vmem_limit_bytes=60 * 1024 * 1024)


def attention_forward(slots, qt, kn, vt, parts):
    heads, tokens = kn.shape[:2]
    return pl.pallas_call(
        functools.partial(forward_kernel, heads),
        name="attention_forward",
        out_shape=[
            jax.ShapeDtypeStruct((heads, 1, tokens), f32),
            jax.ShapeDtypeStruct((parts, heads * HD, tokens // parts), bf16),
        ],
        in_specs=[pl.BlockSpec(memory_space=pltpu.SMEM)] + in_vmem(3),
        out_specs=in_vmem(2),
        scratch_shapes=[
            pltpu.VMEM((heads, HD + EXTRA, TILE), f32),
            pltpu.VMEM((heads, 1, TILE), f32),
        ],
        compiler_params=params(),
        cost_estimate=attention_cost(heads, tokens, 2),
    )(slots, qt, kn, vt)


def attention_cost(heads, tokens, passes):
    pairs = heads * tokens * tokens // 2
    return pl.CostEstimate(
        flops=2 * passes * pairs * BLOCK, bytes_accessed=tokens * D, transcendentals=pairs
    )


def attention_backward(slots, kept, mixed, dmixed, factor):
    qt, kt, kn, vn, lse = kept
    heads, tokens = kn.shape[:2]
    return pl.pallas_call(
        functools.partial(backward_kernel, heads),
        name="attention_backward",
        out_shape=[
            jax.ShapeDtypeStruct((mixed.shape[0], 3 * heads * HD, mixed.shape[2]), bf16),
            jax.ShapeDtypeStruct((heads, HD, PAD), f32),
        ],
        in_specs=[pl.BlockSpec(memory_space=pltpu.SMEM)] + in_vmem(8),
        out_specs=in_vmem(2),
        scratch_shapes=[
            pltpu.VMEM((heads, PAD, tokens), bf16),
            pltpu.VMEM((heads, PAD, tokens), bf16),
            pltpu.VMEM((heads, HD, TILE), f32),
            pltpu.VMEM((heads, HD, tokens), f32),
            pltpu.VMEM((heads, HD, tokens), f32),
        ],
        compiler_params=params(),
        cost_estimate=attention_cost(heads, tokens, 5),
    )(slots, qt, kt, kn, vn, lse, mixed, dmixed, factor)


def reduce_kernel(
    parts,
    groups,
    dq_ref,
    wt_ref,
    u_ref,
    wc_ref,
    mlp_ref,
    small_ref,
    down_ref,
    up_ref,
    own_ref,
    ugather_ref,
    mgather_ref,
    sgather_ref,
    pair_ref,
    sum_ref,
    urecv_ref,
    mrecv_ref,
    part_ref,
    column_ref,
    smine_ref,
    srecv_ref,
    pair_sem,
    sum_sem,
    u_sem,
    m_sem,
    line_sem,
    side_sem,
    small_sem,
    cross_sem,
):
    chips = parts // 2
    here = lax.axis_index("ctx")
    group = lax.axis_index("fsdp")
    core = lax.rem(here, 2)
    chip = here // 2
    other = here + 1 - 2 * core
    ctx_peers = [lax.rem(here + step, parts) for step in range(1, parts)]
    chip_peers = [lax.rem(chip + step, chips) for step in range(1, chips)]
    group_peers = [lax.rem(group + step, groups) for step in range(1, groups)]

    barrier = pltpu.get_barrier_semaphore()
    for peer in ctx_peers:
        pl.semaphore_signal(barrier, inc=1, device_id={"ctx": peer})
    for peer in group_peers:
        pl.semaphore_signal(barrier, inc=1, device_id={"fsdp": peer})
    pl.semaphore_wait(barrier, parts + groups - 2)

    def send(source, target, sems, device):
        return pltpu.make_async_remote_copy(
            src_ref=source,
            dst_ref=target,
            send_sem=sems[0],
            recv_sem=sems[1],
            device_id=device,
        )

    def pair_copy(index):
        return send(
            dq_ref.at[index, 1 - core],
            pair_ref.at[index],
            (pair_sem.at[0, index], pair_sem.at[1, index]),
            {"ctx": other},
        )

    def u_copy(peer, source):
        return send(
            u_ref.at[peer],
            urecv_ref.at[source],
            (u_sem.at[0, peer], u_sem.at[1, source]),
            {"fsdp": peer},
        )

    def m_copy(peer, source):
        return send(
            mlp_ref.at[peer],
            mrecv_ref.at[source],
            (m_sem.at[0, peer], m_sem.at[1, source]),
            {"ctx": 2 * peer + core},
        )

    for index in range(chips):
        pair_copy(index).start()
    for peer in group_peers:
        u_copy(peer, group).start()
    for peer in chip_peers:
        m_copy(peer, chip).start()
    for index in range(chips):
        pair_copy(index).wait_recv()

    rows_half = own_ref.shape[0] // 2

    def partial(target):
        def half(index, carry):
            rows = pl.ds(pl.multiple_of(index * rows_half, rows_half), rows_half)
            part_ref[rows, :] = dot(dq_ref[target, core, :, rows], wt_ref[core], (0, 0)) + dot(
                pair_ref[target, :, rows], wt_ref[1 - core], (0, 0)
            )
            return carry

        lax.fori_loop(0, 2, half, 0)

    def sum_copy(way, target):
        return send(
            sum_ref.at[way, target],
            sum_ref.at[way, target],
            (sum_sem.at[0, way, target], sum_sem.at[1, way, target]),
            {"ctx": here + (2 if way else -2)},
        )

    def reduce_step(step):
        last = step == chips - 2
        for way, target, active, first, out_ref in (
            (0, step - (chips - 1) + chip, step >= chips - 1 - chip, chip == chips - 1, down_ref),
            (1, chips - 1 - step + chip, step >= chip, chip == 0, up_ref),
        ):

            @pl.when(active)
            def _():
                partial(target)

                @pl.when(first)
                def _():
                    sum_ref[way, target] = part_ref[...].astype(bf16)

                @pl.when(jnp.logical_not(first))
                def _():
                    sum_copy(way, target).wait_recv()
                    sum_ref[way, target] = (
                        part_ref[...] + sum_ref[way, target].astype(f32)
                    ).astype(bf16)

                if last:
                    out_ref[...] = sum_ref[way, target]
                else:
                    sum_copy(way, target).start()

            if last:

                @pl.when(jnp.logical_not(active))
                def _():
                    out_ref[...] = jnp.zeros(out_ref.shape, bf16)

    gathers = (ugather_ref, mgather_ref)

    def line_copy(which, way, step, piece):
        ref = gathers[which].at[2 * piece + core]
        sems = (line_sem.at[0, which, way, step], line_sem.at[1, which, way, step])
        return send(ref, ref, sems, {"ctx": here + (2 if way else -2)})

    def side_copy(which, piece, lane):
        ref = gathers[which].at[2 * piece + lane]
        sems = (side_sem.at[0, which, piece], side_sem.at[1, which, piece])
        return send(ref, ref, sems, {"ctx": other})

    def line_sends(which, step, go):
        @pl.when((chip < chips - 1) & (chip - step >= 0))
        def _():
            go(line_copy(which, 1, step, chip - step))

        @pl.when((chip > 0) & (chip + step <= chips - 1))
        def _():
            go(line_copy(which, 0, step, chip + step))

    def line_receive(which, step):
        @pl.when(chip - 1 - step >= 0)
        def _():
            line_copy(which, 1, step, chip - 1 - step).wait_recv()
            side_copy(which, chip - 1 - step, core).start()

        @pl.when(chip + 1 + step <= chips - 1)
        def _():
            line_copy(which, 0, step, chip + 1 + step).wait_recv()
            side_copy(which, chip + 1 + step, core).start()

    def small_copy(peer, source):
        return send(
            smine_ref,
            srecv_ref.at[source],
            (small_sem.at[0, peer], small_sem.at[1, source]),
            {"ctx": peer},
        )

    def cross_copy(peer, source):
        return send(
            sgather_ref.at[group],
            sgather_ref.at[source],
            (cross_sem.at[0, peer], cross_sem.at[1, source]),
            {"fsdp": peer},
        )

    reduce_step(0)

    total = u_ref[group].astype(f32)
    for peer in group_peers:
        u_copy(group, peer).wait_recv()
        total = total + urecv_ref[peer].astype(f32)
    ugather_ref[here] = total.astype(bf16)
    side_copy(0, chip, core).start()
    line_sends(0, 0, lambda copy: copy.start())
    held = total.shape[0]
    gain = jnp.sum(total * wc_ref[...].astype(f32), axis=1, keepdims=True)
    column_ref[...] = jnp.zeros(column_ref.shape, f32)
    column_ref[:held, :] = jnp.broadcast_to(gain, (held, PAD))
    flat = column_ref[...].T[:1]
    smine_ref[...] = small_ref[...]
    for row in range(column_ref.shape[0] // PAD):
        smine_ref[row : row + 1, :] = flat[:, row * PAD : (row + 1) * PAD]
    for peer in ctx_peers:
        small_copy(peer, here).start()

    total = mlp_ref[chip].astype(f32)
    for peer in chip_peers:
        m_copy(chip, peer).wait_recv()
        total = total + mrecv_ref[peer].astype(f32)
    mgather_ref[here] = total.astype(bf16)
    side_copy(1, chip, core).start()
    line_sends(1, 0, lambda copy: copy.start())

    for step in range(1, chips):
        if step <= chips - 2:
            reduce_step(step)
        for which in range(2):
            line_receive(which, step - 1)
            if step <= chips - 2:
                line_sends(which, step, lambda copy: copy.start())
        if step == 1:
            small = smine_ref[...]
            for peer in ctx_peers:
                small_copy(here, peer).wait_recv()
                small = small + srecv_ref[peer]
            sgather_ref[group] = small
            for peer in group_peers:
                cross_copy(peer, group).start()

    partial(chip)
    own_ref[...] = part_ref[...]

    for which in range(2):
        for piece in range(chips):
            side_copy(which, piece, 1 - core).wait_recv()
            side_copy(which, piece, core).wait_send()
        for step in range(chips - 1):
            line_sends(which, step, lambda copy: copy.wait_send())
    for index in range(chips):
        pair_copy(index).wait_send()
    for peer in group_peers:
        cross_copy(group, peer).wait_recv()
        cross_copy(peer, group).wait_send()
        u_copy(peer, group).wait_send()
    for peer in chip_peers:
        m_copy(peer, chip).wait_send()
    for peer in ctx_peers:
        small_copy(peer, here).wait_send()
    for step in range(chips - 2):

        @pl.when(step >= chips - 1 - chip)
        def _():
            sum_copy(0, step - (chips - 1) + chip).wait_send()

        @pl.when(step >= chip)
        def _():
            sum_copy(1, chips - 1 - step + chip).wait_send()


def reduce_gradients(parts, groups, dqkv, w_pair, u_parts, w_columns, mlp, small):
    chips = parts // 2
    rows_dev = dqkv.shape[3]
    rows, width = w_columns.shape
    lanes = -(-rows // PAD) * PAD
    dma = pltpu.SemaphoreType.DMA
    return pl.pallas_call(
        functools.partial(reduce_kernel, parts, groups),
        name="reduce_gradients",
        out_shape=[
            jax.ShapeDtypeStruct((rows_dev, D), bf16),
            jax.ShapeDtypeStruct((rows_dev, D), bf16),
            jax.ShapeDtypeStruct((rows_dev, D), f32),
            jax.ShapeDtypeStruct((parts, rows, width), bf16),
            jax.ShapeDtypeStruct((parts,) + mlp.shape[1:], bf16),
            jax.ShapeDtypeStruct((groups,) + small.shape, f32),
        ],
        in_specs=in_vmem(6),
        out_specs=in_vmem(6),
        scratch_shapes=[
            pltpu.VMEM((chips,) + dqkv.shape[2:], bf16),
            pltpu.VMEM((2, chips, rows_dev, D), bf16),
            pltpu.VMEM(u_parts.shape, bf16),
            pltpu.VMEM(mlp.shape, bf16),
            pltpu.VMEM((rows_dev, D), f32),
            pltpu.VMEM((lanes, PAD), f32),
            pltpu.VMEM(small.shape, f32),
            pltpu.VMEM((parts,) + small.shape, f32),
            dma((2, chips)),
            dma((2, 2, chips)),
            dma((2, groups)),
            dma((2, chips)),
            dma((2, 2, 2, chips)),
            dma((2, 2, chips)),
            dma((2, parts)),
            dma((2, groups)),
        ],
        compiler_params=pltpu.CompilerParams(
            vmem_limit_bytes=60 * 1024 * 1024, collective_id=1, has_side_effects=True
        ),
    )(dqkv, w_pair, u_parts, w_columns, mlp, small)


def update_kernel(rates, *refs):
    sets = len(rates)
    for index, rate in enumerate(rates):
        weight, first, second, gradient = (ref[...] for ref in refs[4 * index : 4 * index + 4])
        outs = refs[4 * (sets + index) : 4 * (sets + index) + 4]
        new, first, second = adamw(weight, first, second, gradient.astype(f32), rate, decay_rate)
        outs[0][...] = new
        outs[1][...] = first
        outs[2][...] = second
        outs[3][...] = new.astype(bf16)


def update(rates, *arrays):
    step_rows = 32
    rows = arrays[0].shape[0]
    specs, shapes, moved = [], [], 0
    for array in arrays:
        specs.append(pl.BlockSpec((step_rows, array.shape[1]), lambda i: (i, 0)))
    for index in range(len(rates)):
        shape = arrays[4 * index].shape
        shapes += [jax.ShapeDtypeStruct(shape, f32)] * 3 + [jax.ShapeDtypeStruct(shape, bf16)]
        moved += shape[0] * shape[1] * 28
    return pl.pallas_call(
        functools.partial(update_kernel, rates),
        name="update_weights",
        grid=(rows // step_rows,),
        in_specs=specs,
        out_specs=specs,
        out_shape=shapes,
        compiler_params=params(),
        cost_estimate=pl.CostEstimate(flops=moved, bytes_accessed=moved, transcendentals=0),
    )(*arrays)


def body(
    parts,
    groups,
    inputs,
    cotangent,
    block_order,
    w_qkv,
    m_qkv,
    v_qkv,
    w_out,
    m_out,
    v_out,
    w_up,
    m_up,
    v_up,
    w_down,
    m_down,
    v_down,
    small_params,
    small_m,
    small_v,
):
    heads = H // parts
    width = heads * HD
    rows_dev = inputs.shape[1]
    tokens = rows_dev * parts
    here = lax.axis_index("ctx")
    index = jnp.arange(block_order.shape[1], dtype=jnp.int32)
    slots = jnp.sum(jnp.where(block_order[0][None] == index[:, None], index[None], 0), axis=1)
    gain_one = small_params[:D]
    gain_two = small_params[D : 2 * D]
    query_scale = small_params[2 * D :]
    core = lax.rem(here, 2)
    group = lax.axis_index("fsdp")
    rows = w_qkv.shape[0]

    def head_columns(owner):
        return jnp.concatenate(
            [
                lax.dynamic_slice_in_dim(w_qkv, part * D + owner * width, width, 1)
                for part in range(3)
            ],
            axis=1,
        )

    gain_rows = lax.dynamic_slice_in_dim(gain_one, group * rows, rows, 0)[:, None]
    columns = [head_columns(here - core + lane) for lane in range(2)]
    gained = jnp.concatenate([(gain_rows * part).astype(bf16) for part in columns], axis=1)
    w_columns = head_columns(here).astype(bf16)
    layer_in = inputs[0].astype(f32)
    scale_one = rms_scale(layer_in)
    unit_one = layer_in * scale_one
    factor = scale_base / math.sqrt(HD) * jax.nn.softplus(query_scale)
    factor_two = (factor * LOG2E)[:, None]
    half = rows // 2
    mlp = jnp.stack([w_out.astype(bf16), w_up.astype(bf16), w_down.astype(bf16)])
    mlp = mlp.reshape(3, 2, half, D)
    unit_all, mlp_full, w_pair, qt, kt, vt, kn, vn = gather_rows(
        parts, groups, heads, inputs[0], gained, mlp, factor_two
    )
    out_full, up_full, down_full = mlp_full.reshape(3, D, D)
    lse, mixed = attention_forward(slots, qt, kn, vt, parts)
    kept = (qt, kt, kn, vn, lse)
    attn_flipped = lax.all_to_all(mixed, "ctx", 0, 0, tiled=True).reshape(D, rows_dev)
    mid = layer_in + dot(attn_flipped, out_full, (0, 0))
    scale_two = rms_scale(mid)
    unit_two = mid * scale_two
    normed_two = (unit_two * gain_two).astype(bf16)
    hidden = dot(normed_two, up_full)
    gate_sig = jax.nn.sigmoid(hidden)
    act = (hidden * gate_sig).astype(bf16)
    output = (mid + dot(act, down_full)).astype(bf16)
    grad_in = cotangent[0]
    grad_down = dot(act, grad_in, (0, 0))
    dact = dot(grad_in, down_full, (1, 1))
    dhidden = (dact * gate_sig * (1.0 + hidden * (1.0 - gate_sig))).astype(bf16)
    grad_up = dot(normed_two, dhidden, (0, 0))
    dnormed_two = dot(dhidden, up_full, (1, 1))
    dunit_two = dnormed_two * gain_two
    dmid = grad_in.astype(f32) + scale_two * (
        dunit_two - unit_two * jnp.mean(dunit_two * unit_two, axis=-1, keepdims=True)
    )
    gain_two_grad = jnp.sum(dnormed_two * unit_two, axis=0)
    dbranch = dmid.astype(bf16)
    grad_out = dot(attn_flipped, dbranch)
    dattn = dot(out_full, dbranch, (1, 1)).astype(bf16)
    grads = jnp.stack([grad_out.astype(bf16), grad_up.astype(bf16), grad_down.astype(bf16)])
    grads = grads.reshape(3, groups, 2, half, D)
    pair = [(i, i ^ 1) for i in range(parts)]
    theirs = lax.dynamic_index_in_dim(grads, 1 - core, 2, False)
    mine = lax.dynamic_index_in_dim(grads, core, 2, False)
    mine = (mine.astype(f32) + lax.ppermute(theirs, "ctx", pair).astype(f32)).astype(bf16)
    dmixed = lax.all_to_all(dattn.reshape(parts, width, rows_dev), "ctx", 0, 0, tiled=True)
    dmixed, mine = lax.optimization_barrier((dmixed, mine))
    mlp_sum = lax.dynamic_index_in_dim(mine, group, 1, False).astype(f32)
    for step in range(1, groups):
        chunk = lax.dynamic_index_in_dim(mine, group ^ step, 1, False)
        swap = [(i, i ^ step) for i in range(groups)]
        mlp_sum = mlp_sum + lax.ppermute(chunk, "fsdp", swap).astype(f32)
    mlp_part = (
        mlp_sum.astype(bf16).reshape(3, parts // 2, rows // parts, D).transpose(1, 0, 2, 3)
    )
    dqkv, dscale = attention_backward(slots, kept, mixed, dmixed, factor_two)
    u_parts = (
        lax.dot_general(
            unit_all,
            dqkv,
            (((0, 1), (0, 2)), ((), ())),
            preferred_element_type=f32,
        )
        .astype(bf16)
        .reshape(groups, rows, 3 * width)
    )
    scale_grad = (
        jnp.sum(dscale, axis=(0, 2))
        / factor_two[:, 0]
        * (scale_base / math.sqrt(HD))
        * jax.nn.sigmoid(query_scale)
    )
    lanes = -(-rows // PAD) * PAD
    small_rows = -(-(lanes + D + PAD) // (8 * PAD)) * 8
    small = jnp.concatenate([jnp.zeros((lanes,), f32), gain_two_grad, scale_grad])
    small = jnp.pad(small, (0, small_rows * PAD - small.shape[0])).reshape(small_rows, PAD)
    send_down, send_up, own_part, u_all, mlp_all, small_all = reduce_gradients(
        parts,
        groups,
        dqkv.reshape(parts // 2, 2, 3 * width, rows_dev),
        w_pair,
        u_parts,
        w_columns,
        mlp_part,
        small,
    )
    got_down = lax.ppermute(send_down, "ctx", [(i, i - 2) for i in range(2, parts)])
    got_up = lax.ppermute(send_up, "ctx", [(i, i + 2) for i in range(parts - 2)])
    total_qkv = (
        u_all.reshape(parts, rows, 3, width).transpose(1, 2, 0, 3).reshape(rows, 3 * D)
        * gain_rows
    ).astype(bf16)
    total_mlp = (
        mlp_all.reshape(parts // 2, 2, 3, rows // parts, D)
        .transpose(2, 1, 0, 3, 4)
        .reshape(3, rows, D)
    )
    rate_qkv = qkv_rate_base / math.sqrt(D)
    rate_out = 0.5 / math.sqrt(max(D // 256, 1))
    rate_up = 0.5 / math.sqrt(D)
    rate_down = 0.5 / math.sqrt(FF)
    updated = update(
        (rate_qkv, rate_out, rate_up, rate_down),
        w_qkv,
        m_qkv,
        v_qkv,
        total_qkv,
        w_out,
        m_out,
        v_out,
        total_mlp[0],
        w_up,
        m_up,
        v_up,
        total_mlp[1],
        w_down,
        m_down,
        v_down,
        total_mlp[2],
    )
    flat = small_all.reshape(groups, small_rows * PAD)
    rest = jnp.sum(flat[:, lanes : lanes + D + HD], axis=0)
    small_total = jnp.concatenate([flat[:, :rows].reshape(D), rest])
    small_set = adamw(small_params, small_m, small_v, small_total, small_rate, 0.0)
    dunit_one = own_part + got_down.astype(f32) + got_up.astype(f32)
    input_grad = dmid + scale_one * (
        dunit_one - unit_one * jnp.mean(dunit_one * unit_one, axis=-1, keepdims=True)
    )
    return (
        output[None],
        input_grad.astype(bf16)[None],
        *updated,
        *small_set,
    )


def solution(mesh):
    rows = P("fsdp", "ctx", None)
    weight = P("fsdp", None)
    return jax.shard_map(
        functools.partial(body, mesh.shape["ctx"], mesh.shape["fsdp"]),
        mesh=mesh,
        in_specs=(rows, rows, weight) + (weight,) * 12 + (P(),) * 3,
        out_specs=(rows, rows) + (weight,) * 16 + (P(),) * 3,
        check_vma=False,
    )
```

```python
import functools
import math

import jax
import jax.numpy as jnp
from jax import lax
from jax.experimental import pallas as pl
from jax.experimental.pallas import tpu as pltpu
from jax.sharding import PartitionSpec as P

D = 1280
H = 16
HD = 80
FF = 1280
BLOCK = 256
CONT = 512
STEP = 3
PAD = 128
EXTRA = 16
TILE = CONT

bf16 = jnp.bfloat16
f32 = jnp.float32

norm_eps = 1e-06
beta_one = 0.5
beta_two = 0.5
adam_eps = 1e-08
decay_rate = 0.1
small_rate = 0.75
qkv_rate_base = 1.0
scale_base = 1.442695
LOG2E = math.log2(math.e)
LN2 = math.log(2.0)


def rms_scale(values):
    return lax.rsqrt(jnp.mean(values * values, axis=-1, keepdims=True) + norm_eps)


def adamw(weight, first, second, gradient, step_rate, decay_on):
    first_new = beta_one * first + (1.0 - beta_one) * gradient
    second_new = beta_two * second + (1.0 - beta_two) * gradient * gradient
    corr_one = 1.0 - beta_one**STEP
    corr_two = 1.0 - beta_two**STEP
    update = first_new / corr_one / (jnp.sqrt(second_new / corr_two) + adam_eps)
    weight_new = weight - step_rate * (update + decay_on * weight)
    return (weight_new, first_new, second_new)


def dot(left, right, contract=(1, 0)):
    return lax.dot_general(
        left, right, (((contract[0],), (contract[1],)), ((), ())), preferred_element_type=f32
    )


def three_rows(row):
    high = row.astype(bf16)
    rest = row - high.astype(f32)
    middle = rest.astype(bf16)
    low = (rest - middle.astype(f32)).astype(bf16)
    index = lax.broadcasted_iota(jnp.int32, (EXTRA, row.shape[1]), 0)
    zero = jnp.zeros((EXTRA, row.shape[1]), f32)
    rows = jnp.where(index == 0, high.astype(f32), zero)
    rows = jnp.where(index == 1, middle.astype(f32), rows)
    rows = jnp.where(index == 2, low.astype(f32), rows)
    return rows.astype(bf16)


def tile_at(tile):
    return pl.ds(pl.multiple_of(tile * TILE, TILE), TILE)


def block_at(slot):
    return pl.ds(pl.multiple_of(slot * BLOCK, BLOCK), BLOCK)


def tile_lanes(ref, head, slot_ref, tile, rows=slice(None)):
    first, second = slot_ref[2 * tile], slot_ref[2 * tile + 1]
    return jnp.concatenate(
        [ref[head, rows, block_at(first)], ref[head, rows, block_at(second)]], axis=1
    )


def tile_rows(ref, head, slot_ref, tile):
    first, second = slot_ref[2 * tile], slot_ref[2 * tile + 1]
    return jnp.concatenate([ref[head, block_at(first), :], ref[head, block_at(second), :]], axis=0)


def half_at(slot):
    return pl.ds(pl.multiple_of(lax.rem(slot, 2) * BLOCK, BLOCK), BLOCK)


def causal():
    key = lax.broadcasted_iota(jnp.int32, (TILE, TILE), 0)
    query = lax.broadcasted_iota(jnp.int32, (TILE, TILE), 1)
    return key <= query


def gather_kernel(
    parts,
    groups,
    heads,
    x_ref,
    gained_ref,
    mlp_ref,
    factor_ref,
    unit_ref,
    full_ref,
    wpair_ref,
    qt_ref,
    kt_ref,
    vt_ref,
    kn_ref,
    vn_ref,
    rows_ref,
    wrecv_ref,
    wflip_ref,
    line_sem,
    side_sem,
    keep_sem,
    w_sem,
    mlp_sem,
    cross_sem,
    own_sem,
):
    chips = parts // 2
    here = lax.axis_index("ctx")
    group = lax.axis_index("fsdp")
    core = lax.rem(here, 2)
    chip = here // 2
    other = here + 1 - 2 * core
    width = heads * HD
    group_peers = [lax.rem(group + step, groups) for step in range(1, groups)]

    barrier = pltpu.get_barrier_semaphore()
    pl.semaphore_signal(barrier, inc=1, device_id={"ctx": other})
    for peer in group_peers:
        pl.semaphore_signal(barrier, inc=1, device_id={"fsdp": peer})
    for step in (1, chips - 1):
        peer = lax.rem(chip + step, chips) * 2 + core
        pl.semaphore_signal(barrier, inc=1, device_id={"ctx": peer})
    pl.semaphore_wait(barrier, groups + 2)

    def send(source, target, sems, device):
        return pltpu.make_async_remote_copy(
            src_ref=source,
            dst_ref=target,
            send_sem=sems[0],
            recv_sem=sems[1],
            device_id=device,
        )

    def line_copy(way, step, piece):
        ref = rows_ref.at[2 * piece + core]
        sems = (line_sem.at[0, way, step], line_sem.at[1, way, step])
        return send(ref, ref, sems, {"ctx": here + (2 if way else -2)})

    def side_copy(piece, lane):
        ref = rows_ref.at[2 * piece + lane]
        return send(ref, ref, (side_sem.at[0, piece], side_sem.at[1, piece]), {"ctx": other})

    def w_copy(peer, source):
        sems = (w_sem.at[0, peer], w_sem.at[1, source])
        return send(gained_ref, wrecv_ref.at[source], sems, {"fsdp": peer})

    def mlp_copy(peer, source):
        sems = (mlp_sem.at[0, peer], mlp_sem.at[1, source])
        return send(mlp_ref.at[:, core], full_ref.at[:, source, core], sems, {"fsdp": peer})

    def cross_copy(source, lane):
        ref = full_ref.at[:, source, lane]
        sems = (cross_sem.at[0, source], cross_sem.at[1, source])
        return send(ref, ref, sems, {"ctx": other})

    def keep_copy(piece):
        return pltpu.make_async_copy(rows_ref.at[piece], unit_ref.at[piece], keep_sem.at[piece])

    own_copy = pltpu.make_async_copy(mlp_ref, full_ref.at[:, group], own_sem)

    rows = x_ref[...].astype(f32)
    rows_ref[here] = (rows * rms_scale(rows)).astype(bf16)

    def forward(way, step, piece):
        @pl.when((chip < chips - 1) if way else (chip > 0))
        def _():
            line_copy(way, step, piece).start()

    for way in range(2):
        forward(way, 0, chip)
    side_copy(chip, core).start()
    for peer in group_peers:
        w_copy(peer, group).start()
    own_copy.start()
    keep_copy(here).start()
    wrecv_ref[group] = gained_ref[...]
    for peer in group_peers:
        w_copy(group, peer).wait_recv()
    for peer in group_peers:
        mlp_copy(peer, group).start()
    flipped = wrecv_ref[...].reshape(D, 6 * width).T
    wpair_ref[0] = flipped[: 3 * width]
    wpair_ref[1] = flipped[3 * width :]
    wflip_ref[...] = wpair_ref[core]

    extra_row = lax.broadcasted_iota(jnp.int32, (PAD - HD, BLOCK), 0)
    extra = jnp.where(extra_row < 3, 1.0, 0.0)
    spare = jnp.zeros((PAD - HD, BLOCK), bf16)

    def project(piece):
        def half(index, carry):
            at = pl.ds(pl.multiple_of(index * BLOCK, BLOCK), BLOCK)
            to = pl.ds(pl.multiple_of((piece * 2 + index) * BLOCK, BLOCK), BLOCK)
            result = dot(wflip_ref[...], rows_ref[piece, at, :], (1, 1))
            for head in range(heads):
                query, key, value = (
                    result[part * width + head * HD : part * width + (head + 1) * HD]
                    for part in range(3)
                )
                qt_ref[head, :HD, to] = (query * factor_ref[...]).astype(bf16)
                qt_ref[head, HD:, to] = spare
                kt_ref[head, :, to] = key.astype(bf16)
                vt_ref[head, :HD, to] = value.astype(bf16)
                vt_ref[head, HD:, to] = jnp.ones((EXTRA, BLOCK), bf16)
                kn_ref[head, to, :] = jnp.concatenate([key, extra], axis=0).T.astype(bf16)
                vn_ref[head, to, :] = jnp.concatenate([value, extra], axis=0).T.astype(bf16)
            return carry

        lax.fori_loop(0, TILE // BLOCK, half, 0)

    def visit(distance, carry):
        for way in range(2):
            piece = chip - distance if way else chip + distance
            valid = (piece >= 0) if way else (piece <= chips - 1)

            @pl.when(valid & (distance > 0))
            def _():
                line_copy(way, distance - 1, piece).wait_recv()
                side_copy(piece, core).start()
                forward(way, distance, piece)
                keep_copy(2 * piece + core).start()

        for way in range(2):
            piece = chip - distance if way else chip + distance
            valid = (piece >= 0) if way else ((piece <= chips - 1) & (distance > 0))

            @pl.when(valid)
            def _():
                project(2 * piece + core)
                side_copy(piece, 1 - core).wait_recv()
                keep_copy(2 * piece + 1 - core).start()
                project(2 * piece + 1 - core)

        return carry

    lax.fori_loop(0, chips, visit, 0)

    for peer in group_peers:
        mlp_copy(group, peer).wait_recv()
        cross_copy(peer, core).start()
    for peer in group_peers:
        cross_copy(peer, 1 - core).wait_recv()
        cross_copy(peer, core).wait_send()
        w_copy(peer, group).wait_send()
        mlp_copy(peer, group).wait_send()
    own_copy.wait()

    def drain(piece, carry):
        keep_copy(2 * piece).wait()
        keep_copy(2 * piece + 1).wait()
        side_copy(piece, core).wait_send()

        @pl.when((piece <= chip) & (chip < chips - 1))
        def _():
            line_copy(1, chip - piece, piece).wait_send()

        @pl.when((piece >= chip) & (chip > 0))
        def _():
            line_copy(0, piece - chip, piece).wait_send()

        return carry

    lax.fori_loop(0, chips, drain, 0)


def gather_rows(parts, groups, heads, rows, gained, mlp, factor):
    rows_dev = rows.shape[0]
    tokens = parts * rows_dev
    dma = pltpu.SemaphoreType.DMA
    chips = parts // 2
    anywhere = pl.BlockSpec(memory_space=pl.ANY)
    return pl.pallas_call(
        functools.partial(gather_kernel, parts, groups, heads),
        name="gather_rows",
        out_shape=[
            jax.ShapeDtypeStruct((parts, rows_dev, D), bf16),
            jax.ShapeDtypeStruct((3, groups) + mlp.shape[1:], bf16),
            jax.ShapeDtypeStruct((2, 3 * heads * HD, D), bf16),
            jax.ShapeDtypeStruct((heads, PAD, tokens), bf16),
            jax.ShapeDtypeStruct((heads, HD, tokens), bf16),
            jax.ShapeDtypeStruct((heads, HD + EXTRA, tokens), bf16),
            jax.ShapeDtypeStruct((heads, tokens, PAD), bf16),
            jax.ShapeDtypeStruct((heads, tokens, PAD), bf16),
        ],
        in_specs=in_vmem(2) + [anywhere] + in_vmem(1),
        out_specs=[anywhere] * 2 + in_vmem(6),
        scratch_shapes=[
            pltpu.VMEM((parts, rows_dev, D), bf16),
            pltpu.VMEM((groups,) + gained.shape, bf16),
            pltpu.VMEM((3 * heads * HD, D), bf16),
            dma((2, 2, chips)),
            dma((2, chips)),
            dma((parts,)),
            dma((2, groups)),
            dma((2, groups)),
            dma((2, groups)),
            dma,
        ],
        compiler_params=pltpu.CompilerParams(
            vmem_limit_bytes=60 * 1024 * 1024, collective_id=2, has_side_effects=True
        ),
    )(rows, gained, mlp, factor)


def forward_kernel(
    heads,
    slot_ref,
    qt_ref,
    kn_ref,
    vt_ref,
    lse_ref,
    ot_ref,
    acc_ref,
    top_ref,
):
    tokens = kn_ref.shape[1]
    num_tiles = tokens // TILE
    prompt_tiles = num_tiles // 2
    allowed = causal()

    def query_tile(tile, carry):
        here = tile_at(tile)
        top_ref[...] = jnp.full(top_ref.shape, -1e30, f32)
        acc_ref[...] = jnp.zeros(acc_ref.shape, f32)

        queries = [tile_lanes(qt_ref, head, slot_ref, tile) for head in range(heads)]

        def step(key_tile, masked):
            for head in range(heads):
                scores = dot(tile_rows(kn_ref, head, slot_ref, key_tile), queries[head])
                if masked:
                    scores = jnp.where(allowed, scores, -1e30)
                old = top_ref[head]
                top = jnp.maximum(old, jnp.max(scores, axis=0, keepdims=True))
                probs = jnp.exp2(scores - top).astype(bf16)
                acc_ref[head] = acc_ref[head] * jnp.exp2(old - top) + dot(
                    tile_lanes(vt_ref, head, slot_ref, key_tile), probs
                )
                top_ref[head] = top

        def full(key_tile, inner):
            step(key_tile, False)
            return inner

        lax.fori_loop(0, jnp.minimum(tile, prompt_tiles), full, 0)
        step(tile, True)
        for head in range(heads):
            acc = acc_ref[head]
            mass = acc[HD : HD + 1]
            mixed = (acc[:HD] / mass).astype(bf16)
            lse_ref[head, :, here] = top_ref[head] + jnp.log2(mass)
            for part in range(TILE // BLOCK):
                slot = slot_ref[tile * (TILE // BLOCK) + part]
                ot_ref[slot // 2, head * HD : (head + 1) * HD, half_at(slot)] = mixed[
                    :, part * BLOCK : (part + 1) * BLOCK
                ]
        return carry

    lax.fori_loop(0, num_tiles, query_tile, 0)


def backward_kernel(
    heads,
    slot_ref,
    qt_ref,
    kt_ref,
    kn_ref,
    vn_ref,
    lse_ref,
    ot_ref,
    dt_ref,
    factor_ref,
    units_ref,
    dqkv_ref,
    dscale_ref,
    u_ref,
    qa_ref,
    da_ref,
    dq_ref,
    dk_ref,
    dv_ref,
    held_ref,
    total_ref,
    load_sem,
):
    parts = units_ref.shape[0]

    def load(piece):
        slot = lax.rem(piece, 2)
        return pltpu.make_async_copy(units_ref.at[piece], held_ref.at[slot], load_sem.at[slot])

    for piece in range(2):
        load(piece).start()
    tokens = kn_ref.shape[1]
    num_blocks = tokens // BLOCK
    num_tiles = tokens // TILE
    prompt_tiles = num_tiles // 2
    width = heads * HD

    def prepare(block, carry):
        slot = slot_ref[block]
        to = pl.ds(pl.multiple_of(block * BLOCK, BLOCK), BLOCK)
        for head in range(heads):
            rows = slice(head * HD, (head + 1) * HD)
            grad = dt_ref[slot // 2, rows, half_at(slot)]
            mixed = ot_ref[slot // 2, rows, half_at(slot)]
            delta = jnp.sum(grad.astype(f32) * mixed.astype(f32), axis=0, keepdims=True)
            da_ref[head, :HD, to] = grad
            da_ref[head, HD : HD + EXTRA, to] = three_rows(-delta)
            da_ref[head, HD + EXTRA :, to] = jnp.zeros((PAD - HD - EXTRA, BLOCK), bf16)
            qa_ref[head, :HD, to] = qt_ref[head, :HD, block_at(slot)]
            qa_ref[head, HD : HD + EXTRA, to] = three_rows(-lse_ref[head, :, to])
            qa_ref[head, HD + EXTRA :, to] = jnp.zeros((PAD - HD - EXTRA, BLOCK), bf16)
        return carry

    lax.fori_loop(0, num_blocks, prepare, 0)
    dk_ref[...] = jnp.zeros(dk_ref.shape, f32)
    dv_ref[...] = jnp.zeros(dv_ref.shape, f32)
    dscale_ref[...] = jnp.zeros(dscale_ref.shape, f32)
    allowed = causal()

    def query_tile(tile, carry):
        here = tile_at(tile)
        dq_ref[...] = jnp.zeros(dq_ref.shape, f32)

        def step(key_tile, masked):
            keys = tile_at(key_tile)
            for head in range(heads):
                key_rows = tile_rows(kn_ref, head, slot_ref, key_tile)
                value_rows = tile_rows(vn_ref, head, slot_ref, key_tile)
                probs = jnp.exp2(dot(key_rows, qa_ref[head, :, here]))
                if masked:
                    probs = jnp.where(allowed, probs, 0.0)
                spread = dot(value_rows, da_ref[head, :, here])
                dscores = (probs * spread).astype(bf16)
                dv_ref[head, :, keys] += dot(da_ref[head, :HD, here], probs.astype(bf16), (1, 1))
                dk_ref[head, :, keys] += dot(qa_ref[head, :HD, here], dscores, (1, 1))
                dq_ref[head] += dot(tile_lanes(kt_ref, head, slot_ref, key_tile), dscores)

        def full(key_tile, inner):
            step(key_tile, False)
            return inner

        lax.fori_loop(0, jnp.minimum(tile, prompt_tiles), full, 0)
        step(tile, True)
        for head in range(heads):
            dq = dq_ref[head]
            product = dq * qa_ref[head, :HD, here].astype(f32)
            for lane in range(TILE // PAD):
                dscale_ref[head] += product[:, lane * PAD : (lane + 1) * PAD]
            scaled = (dq * (factor_ref[...] * LN2)).astype(bf16)
            for part in range(TILE // BLOCK):
                slot = slot_ref[tile * (TILE // BLOCK) + part]
                dqkv_ref[slot // 2, head * HD : (head + 1) * HD, half_at(slot)] = scaled[
                    :, part * BLOCK : (part + 1) * BLOCK
                ]
        return carry

    lax.fori_loop(0, num_tiles, query_tile, 0)

    def finish(block, carry):
        slot = slot_ref[block]
        owner, to = slot // 2, half_at(slot)
        at = pl.ds(pl.multiple_of(block * BLOCK, BLOCK), BLOCK)
        for head in range(heads):
            row = width + head * HD
            dqkv_ref[owner, row : row + HD, to] = (dk_ref[head, :, at] * LN2).astype(bf16)
            row = 2 * width + head * HD
            dqkv_ref[owner, row : row + HD, to] = dv_ref[head, :, at].astype(bf16)
        return carry

    lax.fori_loop(0, num_blocks, finish, 0)
    total_ref[...] = jnp.zeros(total_ref.shape, f32)

    def project(piece, carry):
        load(piece).wait()
        total_ref[...] += dot(dqkv_ref[piece], held_ref[lax.rem(piece, 2)])

        @pl.when(piece + 2 < parts)
        def _():
            load(piece + 2).start()

        return carry

    lax.fori_loop(0, parts, project, 0)
    u_ref[...] = total_ref[...].T.astype(bf16)


def in_vmem(count):
    return [pl.BlockSpec(memory_space=pltpu.VMEM)] * count


def params():
    return pltpu.CompilerParams(vmem_limit_bytes=60 * 1024 * 1024)


def attention_forward(slots, qt, kn, vt, parts):
    heads, tokens = kn.shape[:2]
    return pl.pallas_call(
        functools.partial(forward_kernel, heads),
        name="attention_forward",
        out_shape=[
            jax.ShapeDtypeStruct((heads, 1, tokens), f32),
            jax.ShapeDtypeStruct((parts, heads * HD, tokens // parts), bf16),
        ],
        in_specs=[pl.BlockSpec(memory_space=pltpu.SMEM)] + in_vmem(3),
        out_specs=in_vmem(2),
        scratch_shapes=[
            pltpu.VMEM((heads, HD + EXTRA, TILE), f32),
            pltpu.VMEM((heads, 1, TILE), f32),
        ],
        compiler_params=params(),
        cost_estimate=attention_cost(heads, tokens, 2),
    )(slots, qt, kn, vt)


def attention_cost(heads, tokens, passes):
    pairs = heads * tokens * tokens // 2
    return pl.CostEstimate(
        flops=2 * passes * pairs * BLOCK, bytes_accessed=tokens * D, transcendentals=pairs
    )


def attention_backward(slots, kept, mixed, dmixed, factor, units):
    qt, kt, kn, vn, lse = kept
    heads, tokens = kn.shape[:2]
    return pl.pallas_call(
        functools.partial(backward_kernel, heads),
        name="attention_backward",
        out_shape=[
            jax.ShapeDtypeStruct((mixed.shape[0], 3 * heads * HD, mixed.shape[2]), bf16),
            jax.ShapeDtypeStruct((heads, HD, PAD), f32),
            jax.ShapeDtypeStruct((D, 3 * heads * HD), bf16),
        ],
        in_specs=[pl.BlockSpec(memory_space=pltpu.SMEM)]
        + in_vmem(8)
        + [pl.BlockSpec(memory_space=pl.ANY)],
        out_specs=in_vmem(3),
        scratch_shapes=[
            pltpu.VMEM((heads, PAD, tokens), bf16),
            pltpu.VMEM((heads, PAD, tokens), bf16),
            pltpu.VMEM((heads, HD, TILE), f32),
            pltpu.VMEM((heads, HD, tokens), f32),
            pltpu.VMEM((heads, HD, tokens), f32),
            pltpu.VMEM((2,) + units.shape[1:], bf16),
            pltpu.VMEM((3 * heads * HD, D), f32),
            pltpu.SemaphoreType.DMA((2,)),
        ],
        compiler_params=params(),
        cost_estimate=attention_cost(heads, tokens, 5),
    )(slots, qt, kt, kn, vn, lse, mixed, dmixed, factor, units)


def middle_kernel(
    parts,
    groups,
    mixed_ref,
    x_ref,
    dy_ref,
    weights_ref,
    gain_ref,
    *refs,
):
    out_ref, dmid_ref, dmixed_ref, gain_grad_ref = refs[:4]
    chunk_refs = refs[4 : 4 + groups]
    (
        w_ref,
        attn_ref,
        dattn_ref,
        act_ref,
        normed_ref,
        dhidden_ref,
        dbranch_ref,
        grad_ref,
        theirs_ref,
        w_sem,
        attn_sem,
        dattn_sem,
        pair_sem,
    ) = refs[4 + groups :]
    here = lax.axis_index("ctx")
    group = lax.axis_index("fsdp")
    core = lax.rem(here, 2)
    other = here + 1 - 2 * core
    peers = [lax.rem(here + step, parts) for step in range(1, parts)]
    tokens = x_ref.shape[0]
    width = mixed_ref.shape[1]
    held = theirs_ref.shape[2]
    loads = [
        pltpu.make_async_copy(weights_ref.at[index], w_ref.at[index], w_sem.at[index])
        for index in range(3)
    ]
    for load in loads:
        load.start()

    barrier = pltpu.get_barrier_semaphore()
    for peer in peers:
        pl.semaphore_signal(barrier, inc=1, device_id={"ctx": peer})
    pl.semaphore_wait(barrier, parts - 1)

    def lanes(part):
        return pl.ds(pl.multiple_of(part * BLOCK, BLOCK), BLOCK)

    def attn_copy(part, peer, source):
        return pltpu.make_async_remote_copy(
            src_ref=mixed_ref.at[peer, :, lanes(part)],
            dst_ref=attn_ref.at[source, :, lanes(part)],
            send_sem=attn_sem.at[0, part, peer],
            recv_sem=attn_sem.at[1, part, source],
            device_id={"ctx": peer},
        )

    def dattn_copy(part, peer, source):
        return pltpu.make_async_remote_copy(
            src_ref=dattn_ref.at[peer, :, lanes(part)],
            dst_ref=dmixed_ref.at[source, :, lanes(part)],
            send_sem=dattn_sem.at[0, part, peer],
            recv_sem=dattn_sem.at[1, part, source],
            device_id={"ctx": peer},
        )

    def rows_of(owner, lane):
        start = pl.multiple_of((owner * 2 + lane) * held, 16)
        return pl.ds(start, held)

    def pair_copy(index, owner, lane):
        return pltpu.make_async_remote_copy(
            src_ref=grad_ref.at[index, rows_of(owner, lane), :],
            dst_ref=theirs_ref.at[index, owner],
            send_sem=pair_sem.at[0, index, owner],
            recv_sem=pair_sem.at[1, index, owner],
            device_id={"ctx": other},
        )

    for part in range(tokens // BLOCK):
        for peer in peers:
            attn_copy(part, peer, here).start()
    attn_ref[here] = mixed_ref[here]
    gain_grad_ref[...] = jnp.zeros(gain_grad_ref.shape, f32)
    for load in loads:
        load.wait()
    gain = gain_ref[...]

    def layer(part, carry):
        rows = lanes(part)
        for peer in peers:
            attn_copy(part, here, peer).wait_recv()
        attn = attn_ref[:, :, rows].reshape(D, BLOCK)
        mid = x_ref[rows, :].astype(f32) + dot(attn, w_ref[0], (0, 0))
        scale = rms_scale(mid)
        unit = mid * scale
        normed = (unit * gain).astype(bf16)
        normed_ref[rows, :] = normed
        hidden = dot(normed, w_ref[1])
        gate = jax.nn.sigmoid(hidden)
        act = (hidden * gate).astype(bf16)
        act_ref[rows, :] = act
        dy = dy_ref[rows, :]
        dact = dot(dy, w_ref[2], (1, 1))
        dhidden = (dact * gate * (1.0 + hidden * (1.0 - gate))).astype(bf16)
        dhidden_ref[rows, :] = dhidden
        dnormed = dot(dhidden, w_ref[1], (1, 1))
        dunit = dnormed * gain
        dmid = dy.astype(f32) + scale * (
            dunit - unit * jnp.mean(dunit * unit, axis=-1, keepdims=True)
        )
        dmid_ref[rows, :] = dmid
        dbranch = dmid.astype(bf16)
        dbranch_ref[rows, :] = dbranch
        dattn = dot(w_ref[0], dbranch, (1, 1)).astype(bf16).reshape(parts, width, BLOCK)
        dattn_ref[:, :, rows] = dattn
        for peer in peers:
            dattn_copy(part, peer, here).start()
        dmixed_ref[here, :, rows] = dattn_ref[here, :, rows]
        out_ref[rows, :] = (mid + dot(act, w_ref[2])).astype(bf16)
        gain_grad_ref[...] += jnp.sum(dnormed * unit, axis=0, keepdims=True)
        return carry

    lax.fori_loop(0, tokens // BLOCK, layer, 0)

    def down_rows(index, carry):
        rows = lanes(index)
        grad_ref[2, rows, :] = dot(act_ref[:, rows], dy_ref[...], (0, 0)).astype(bf16)
        return carry

    def up_rows(index, carry):
        rows = lanes(index)
        grad_ref[1, rows, :] = dot(normed_ref[:, rows], dhidden_ref[...], (0, 0)).astype(bf16)
        return carry

    def out_rows(index, carry):
        rows = pl.ds(pl.multiple_of(index * width, 16), width)
        grad_ref[0, rows, :] = dot(attn_ref[index], dbranch_ref[...]).astype(bf16)
        return carry

    for index, count, run in (
        (2, D // BLOCK, down_rows),
        (1, D // BLOCK, up_rows),
        (0, parts, out_rows),
    ):
        lax.fori_loop(0, count, run, 0)
        for owner in range(groups):
            pair_copy(index, owner, 1 - core).start()
    for step in range(groups):
        owner = group ^ step
        for index in (2, 1, 0):
            pair_copy(index, owner, core).wait_recv()
            chunk_refs[step][index] = (
                grad_ref[index, rows_of(owner, core), :].astype(f32)
                + theirs_ref[index, owner].astype(f32)
            ).astype(bf16)
    for part in range(tokens // BLOCK):
        for peer in peers:
            dattn_copy(part, here, peer).wait_recv()
            dattn_copy(part, peer, here).wait_send()
            attn_copy(part, peer, here).wait_send()
    for index in range(3):
        for owner in range(groups):
            pair_copy(index, owner, 1 - core).wait_send()


def middle(parts, groups, mixed, rows, cotangent, weights, gain):
    rows_dev = rows.shape[0]
    half = D // groups // 2
    dma = pltpu.SemaphoreType.DMA
    halves = rows_dev // BLOCK
    return pl.pallas_call(
        functools.partial(middle_kernel, parts, groups),
        name="middle",
        out_shape=[
            jax.ShapeDtypeStruct((rows_dev, D), bf16),
            jax.ShapeDtypeStruct((rows_dev, D), f32),
            jax.ShapeDtypeStruct(mixed.shape, bf16),
            jax.ShapeDtypeStruct((1, D), f32),
        ]
        + [jax.ShapeDtypeStruct((3, half, D), bf16)] * groups,
        in_specs=in_vmem(3) + [pl.BlockSpec(memory_space=pl.ANY)] + in_vmem(1),
        out_specs=in_vmem(4 + groups),
        scratch_shapes=[
            pltpu.VMEM((3, D, D), bf16),
            pltpu.VMEM(mixed.shape, bf16),
            pltpu.VMEM(mixed.shape, bf16),
            pltpu.VMEM((rows_dev, D), bf16),
            pltpu.VMEM((rows_dev, D), bf16),
            pltpu.VMEM((rows_dev, D), bf16),
            pltpu.VMEM((rows_dev, D), bf16),
            pltpu.VMEM((3, D, D), bf16),
            pltpu.VMEM((3, groups, half, D), bf16),
            dma((3,)),
            dma((2, halves, parts)),
            dma((2, halves, parts)),
            dma((2, 3, groups)),
        ],
        compiler_params=pltpu.CompilerParams(
            vmem_limit_bytes=60 * 1024 * 1024, collective_id=3, has_side_effects=True
        ),
    )(mixed, rows, cotangent, weights, gain)


def reduce_kernel(
    parts,
    groups,
    dq_ref,
    wt_ref,
    u_ref,
    wc_ref,
    mlp_ref,
    small_ref,
    down_ref,
    up_ref,
    own_ref,
    ugather_ref,
    mgather_ref,
    sgather_ref,
    pair_ref,
    sum_ref,
    urecv_ref,
    mrecv_ref,
    part_ref,
    column_ref,
    smine_ref,
    srecv_ref,
    pair_sem,
    sum_sem,
    u_sem,
    m_sem,
    line_sem,
    side_sem,
    small_sem,
    cross_sem,
):
    chips = parts // 2
    here = lax.axis_index("ctx")
    group = lax.axis_index("fsdp")
    core = lax.rem(here, 2)
    chip = here // 2
    other = here + 1 - 2 * core
    ctx_peers = [lax.rem(here + step, parts) for step in range(1, parts)]
    chip_peers = [lax.rem(chip + step, chips) for step in range(1, chips)]
    group_peers = [lax.rem(group + step, groups) for step in range(1, groups)]

    barrier = pltpu.get_barrier_semaphore()
    for peer in ctx_peers:
        pl.semaphore_signal(barrier, inc=1, device_id={"ctx": peer})
    for peer in group_peers:
        pl.semaphore_signal(barrier, inc=1, device_id={"fsdp": peer})
    pl.semaphore_wait(barrier, parts + groups - 2)

    def send(source, target, sems, device):
        return pltpu.make_async_remote_copy(
            src_ref=source,
            dst_ref=target,
            send_sem=sems[0],
            recv_sem=sems[1],
            device_id=device,
        )

    def pair_copy(index):
        return send(
            dq_ref.at[index, 1 - core],
            pair_ref.at[index],
            (pair_sem.at[0, index], pair_sem.at[1, index]),
            {"ctx": other},
        )

    def u_copy(peer, source):
        return send(
            u_ref.at[peer],
            urecv_ref.at[source],
            (u_sem.at[0, peer], u_sem.at[1, source]),
            {"fsdp": peer},
        )

    def m_copy(peer, source):
        return send(
            mlp_ref.at[peer],
            mrecv_ref.at[source],
            (m_sem.at[0, peer], m_sem.at[1, source]),
            {"ctx": 2 * peer + core},
        )

    for index in range(chips):
        pair_copy(index).start()
    for peer in group_peers:
        u_copy(peer, group).start()
    for peer in chip_peers:
        m_copy(peer, chip).start()
    for index in range(chips):
        pair_copy(index).wait_recv()

    rows_half = own_ref.shape[0] // 2

    def partial(target):
        def half(index, carry):
            rows = pl.ds(pl.multiple_of(index * rows_half, rows_half), rows_half)
            part_ref[rows, :] = dot(dq_ref[target, core, :, rows], wt_ref[core], (0, 0)) + dot(
                pair_ref[target, :, rows], wt_ref[1 - core], (0, 0)
            )
            return carry

        lax.fori_loop(0, 2, half, 0)

    def sum_copy(way, target):
        return send(
            sum_ref.at[way, target],
            sum_ref.at[way, target],
            (sum_sem.at[0, way, target], sum_sem.at[1, way, target]),
            {"ctx": here + (2 if way else -2)},
        )

    def reduce_step(step):
        last = step == chips - 2
        for way, target, active, first, out_ref in (
            (0, step - (chips - 1) + chip, step >= chips - 1 - chip, chip == chips - 1, down_ref),
            (1, chips - 1 - step + chip, step >= chip, chip == 0, up_ref),
        ):

            @pl.when(active)
            def _():
                partial(target)

                @pl.when(first)
                def _():
                    sum_ref[way, target] = part_ref[...].astype(bf16)

                @pl.when(jnp.logical_not(first))
                def _():
                    sum_copy(way, target).wait_recv()
                    sum_ref[way, target] = (
                        part_ref[...] + sum_ref[way, target].astype(f32)
                    ).astype(bf16)

                if last:
                    out_ref[...] = sum_ref[way, target]
                else:
                    sum_copy(way, target).start()

            if last:

                @pl.when(jnp.logical_not(active))
                def _():
                    out_ref[...] = jnp.zeros(out_ref.shape, bf16)

    gathers = (ugather_ref, mgather_ref)

    def line_copy(which, way, step, piece):
        ref = gathers[which].at[2 * piece + core]
        sems = (line_sem.at[0, which, way, step], line_sem.at[1, which, way, step])
        return send(ref, ref, sems, {"ctx": here + (2 if way else -2)})

    def side_copy(which, piece, lane):
        ref = gathers[which].at[2 * piece + lane]
        sems = (side_sem.at[0, which, piece], side_sem.at[1, which, piece])
        return send(ref, ref, sems, {"ctx": other})

    def line_sends(which, step, go):
        @pl.when((chip < chips - 1) & (chip - step >= 0))
        def _():
            go(line_copy(which, 1, step, chip - step))

        @pl.when((chip > 0) & (chip + step <= chips - 1))
        def _():
            go(line_copy(which, 0, step, chip + step))

    def line_receive(which, step):
        @pl.when(chip - 1 - step >= 0)
        def _():
            line_copy(which, 1, step, chip - 1 - step).wait_recv()
            side_copy(which, chip - 1 - step, core).start()

        @pl.when(chip + 1 + step <= chips - 1)
        def _():
            line_copy(which, 0, step, chip + 1 + step).wait_recv()
            side_copy(which, chip + 1 + step, core).start()

    def small_copy(peer, source):
        return send(
            smine_ref,
            srecv_ref.at[source],
            (small_sem.at[0, peer], small_sem.at[1, source]),
            {"ctx": peer},
        )

    def cross_copy(peer, source):
        return send(
            sgather_ref.at[group],
            sgather_ref.at[source],
            (cross_sem.at[0, peer], cross_sem.at[1, source]),
            {"fsdp": peer},
        )

    reduce_step(0)

    total = u_ref[group].astype(f32)
    for peer in group_peers:
        u_copy(group, peer).wait_recv()
        total = total + urecv_ref[peer].astype(f32)
    ugather_ref[here] = total.astype(bf16)
    side_copy(0, chip, core).start()
    line_sends(0, 0, lambda copy: copy.start())
    held = total.shape[0]
    gain = jnp.sum(total * wc_ref[...].astype(f32), axis=1, keepdims=True)
    column_ref[...] = jnp.zeros(column_ref.shape, f32)
    column_ref[:held, :] = jnp.broadcast_to(gain, (held, PAD))
    flat = column_ref[...].T[:1]
    smine_ref[...] = small_ref[...]
    for row in range(column_ref.shape[0] // PAD):
        smine_ref[row : row + 1, :] = flat[:, row * PAD : (row + 1) * PAD]
    for peer in ctx_peers:
        small_copy(peer, here).start()

    total = mlp_ref[chip].astype(f32)
    for peer in chip_peers:
        m_copy(chip, peer).wait_recv()
        total = total + mrecv_ref[peer].astype(f32)
    mgather_ref[here] = total.astype(bf16)
    side_copy(1, chip, core).start()
    line_sends(1, 0, lambda copy: copy.start())

    for step in range(1, chips):
        if step <= chips - 2:
            reduce_step(step)
        for which in range(2):
            line_receive(which, step - 1)
            if step <= chips - 2:
                line_sends(which, step, lambda copy: copy.start())
        if step == 1:
            small = smine_ref[...]
            for peer in ctx_peers:
                small_copy(here, peer).wait_recv()
                small = small + srecv_ref[peer]
            sgather_ref[group] = small
            for peer in group_peers:
                cross_copy(peer, group).start()

    partial(chip)
    own_ref[...] = part_ref[...]

    for which in range(2):
        for piece in range(chips):
            side_copy(which, piece, 1 - core).wait_recv()
            side_copy(which, piece, core).wait_send()
        for step in range(chips - 1):
            line_sends(which, step, lambda copy: copy.wait_send())
    for index in range(chips):
        pair_copy(index).wait_send()
    for peer in group_peers:
        cross_copy(group, peer).wait_recv()
        cross_copy(peer, group).wait_send()
        u_copy(peer, group).wait_send()
    for peer in chip_peers:
        m_copy(peer, chip).wait_send()
    for peer in ctx_peers:
        small_copy(peer, here).wait_send()
    for step in range(chips - 2):

        @pl.when(step >= chips - 1 - chip)
        def _():
            sum_copy(0, step - (chips - 1) + chip).wait_send()

        @pl.when(step >= chip)
        def _():
            sum_copy(1, chips - 1 - step + chip).wait_send()


def reduce_gradients(parts, groups, dqkv, w_pair, u_parts, w_columns, mlp, small):
    chips = parts // 2
    rows_dev = dqkv.shape[3]
    rows, width = w_columns.shape
    lanes = -(-rows // PAD) * PAD
    dma = pltpu.SemaphoreType.DMA
    return pl.pallas_call(
        functools.partial(reduce_kernel, parts, groups),
        name="reduce_gradients",
        out_shape=[
            jax.ShapeDtypeStruct((rows_dev, D), bf16),
            jax.ShapeDtypeStruct((rows_dev, D), bf16),
            jax.ShapeDtypeStruct((rows_dev, D), f32),
            jax.ShapeDtypeStruct((parts, rows, width), bf16),
            jax.ShapeDtypeStruct((parts,) + mlp.shape[1:], bf16),
            jax.ShapeDtypeStruct((groups,) + small.shape, f32),
        ],
        in_specs=in_vmem(6),
        out_specs=in_vmem(6),
        scratch_shapes=[
            pltpu.VMEM((chips,) + dqkv.shape[2:], bf16),
            pltpu.VMEM((2, chips, rows_dev, D), bf16),
            pltpu.VMEM(u_parts.shape, bf16),
            pltpu.VMEM(mlp.shape, bf16),
            pltpu.VMEM((rows_dev, D), f32),
            pltpu.VMEM((lanes, PAD), f32),
            pltpu.VMEM(small.shape, f32),
            pltpu.VMEM((parts,) + small.shape, f32),
            dma((2, chips)),
            dma((2, 2, chips)),
            dma((2, groups)),
            dma((2, chips)),
            dma((2, 2, 2, chips)),
            dma((2, 2, chips)),
            dma((2, parts)),
            dma((2, groups)),
        ],
        compiler_params=pltpu.CompilerParams(
            vmem_limit_bytes=60 * 1024 * 1024, collective_id=1, has_side_effects=True
        ),
    )(dqkv, w_pair, u_parts, w_columns, mlp, small)


def update_kernel(rates, *refs):
    sets = len(rates)
    for index, rate in enumerate(rates):
        weight, first, second, gradient = (ref[...] for ref in refs[4 * index : 4 * index + 4])
        outs = refs[4 * (sets + index) : 4 * (sets + index) + 4]
        new, first, second = adamw(weight, first, second, gradient.astype(f32), rate, decay_rate)
        outs[0][...] = new
        outs[1][...] = first
        outs[2][...] = second
        outs[3][...] = new.astype(bf16)


def update(rates, *arrays):
    step_rows = 32
    rows = arrays[0].shape[0]
    specs, shapes, moved = [], [], 0
    for array in arrays:
        specs.append(pl.BlockSpec((step_rows, array.shape[1]), lambda i: (i, 0)))
    for index in range(len(rates)):
        shape = arrays[4 * index].shape
        shapes += [jax.ShapeDtypeStruct(shape, f32)] * 3 + [jax.ShapeDtypeStruct(shape, bf16)]
        moved += shape[0] * shape[1] * 28
    return pl.pallas_call(
        functools.partial(update_kernel, rates),
        name="update_weights",
        grid=(rows // step_rows,),
        in_specs=specs,
        out_specs=specs,
        out_shape=shapes,
        compiler_params=params(),
        cost_estimate=pl.CostEstimate(flops=moved, bytes_accessed=moved, transcendentals=0),
    )(*arrays)


def body(
    parts,
    groups,
    inputs,
    cotangent,
    block_order,
    w_qkv,
    m_qkv,
    v_qkv,
    w_out,
    m_out,
    v_out,
    w_up,
    m_up,
    v_up,
    w_down,
    m_down,
    v_down,
    small_params,
    small_m,
    small_v,
):
    heads = H // parts
    width = heads * HD
    rows_dev = inputs.shape[1]
    tokens = rows_dev * parts
    here = lax.axis_index("ctx")
    index = jnp.arange(block_order.shape[1], dtype=jnp.int32)
    slots = jnp.sum(jnp.where(block_order[0][None] == index[:, None], index[None], 0), axis=1)
    gain_one = small_params[:D]
    gain_two = small_params[D : 2 * D]
    query_scale = small_params[2 * D :]
    core = lax.rem(here, 2)
    group = lax.axis_index("fsdp")
    rows = w_qkv.shape[0]

    def head_columns(owner):
        return jnp.concatenate(
            [
                lax.dynamic_slice_in_dim(w_qkv, part * D + owner * width, width, 1)
                for part in range(3)
            ],
            axis=1,
        )

    gain_rows = lax.dynamic_slice_in_dim(gain_one, group * rows, rows, 0)[:, None]
    columns = [head_columns(here - core + lane) for lane in range(2)]
    gained = jnp.concatenate([(gain_rows * part).astype(bf16) for part in columns], axis=1)
    w_columns = head_columns(here).astype(bf16)
    layer_in = inputs[0].astype(f32)
    scale_one = rms_scale(layer_in)
    unit_one = layer_in * scale_one
    factor = scale_base / math.sqrt(HD) * jax.nn.softplus(query_scale)
    factor_two = (factor * LOG2E)[:, None]
    half = rows // 2
    mlp = jnp.stack([w_out.astype(bf16), w_up.astype(bf16), w_down.astype(bf16)])
    mlp = mlp.reshape(3, 2, half, D)
    unit_all, mlp_full, w_pair, qt, kt, vt, kn, vn = gather_rows(
        parts, groups, heads, inputs[0], gained, mlp, factor_two
    )
    lse, mixed = attention_forward(slots, qt, kn, vt, parts)
    kept = (qt, kt, kn, vn, lse)
    output, dmid, dmixed, gain_two_grad, *chunks = middle(
        parts,
        groups,
        mixed,
        inputs[0],
        cotangent[0],
        mlp_full.reshape(3, D, D),
        gain_two[None],
    )
    mlp_sum = chunks[0].astype(f32)
    for step in range(1, groups):
        swap = [(i, i ^ step) for i in range(groups)]
        mlp_sum = mlp_sum + lax.ppermute(chunks[step], "fsdp", swap).astype(f32)
    mlp_part = (
        mlp_sum.astype(bf16).reshape(3, parts // 2, rows // parts, D).transpose(1, 0, 2, 3)
    )
    dqkv, dscale, u_parts = attention_backward(slots, kept, mixed, dmixed, factor_two, unit_all)
    u_parts = u_parts.reshape(groups, rows, 3 * width)
    scale_grad = (
        jnp.sum(dscale, axis=(0, 2))
        / factor_two[:, 0]
        * (scale_base / math.sqrt(HD))
        * jax.nn.sigmoid(query_scale)
    )
    lanes = -(-rows // PAD) * PAD
    small_rows = -(-(lanes + D + PAD) // (8 * PAD)) * 8
    small = jnp.concatenate([jnp.zeros((lanes,), f32), gain_two_grad[0], scale_grad])
    small = jnp.pad(small, (0, small_rows * PAD - small.shape[0])).reshape(small_rows, PAD)
    send_down, send_up, own_part, u_all, mlp_all, small_all = reduce_gradients(
        parts,
        groups,
        dqkv.reshape(parts // 2, 2, 3 * width, rows_dev),
        w_pair,
        u_parts,
        w_columns,
        mlp_part,
        small,
    )
    got_down = lax.ppermute(send_down, "ctx", [(i, i - 2) for i in range(2, parts)])
    got_up = lax.ppermute(send_up, "ctx", [(i, i + 2) for i in range(parts - 2)])
    total_qkv = (
        u_all.reshape(parts, rows, 3, width).transpose(1, 2, 0, 3).reshape(rows, 3 * D)
        * gain_rows
    ).astype(bf16)
    total_mlp = (
        mlp_all.reshape(parts // 2, 2, 3, rows // parts, D)
        .transpose(2, 1, 0, 3, 4)
        .reshape(3, rows, D)
    )
    rate_qkv = qkv_rate_base / math.sqrt(D)
    rate_out = 0.5 / math.sqrt(max(D // 256, 1))
    rate_up = 0.5 / math.sqrt(D)
    rate_down = 0.5 / math.sqrt(FF)
    updated = update(
        (rate_qkv, rate_out, rate_up, rate_down),
        w_qkv,
        m_qkv,
        v_qkv,
        total_qkv,
        w_out,
        m_out,
        v_out,
        total_mlp[0],
        w_up,
        m_up,
        v_up,
        total_mlp[1],
        w_down,
        m_down,
        v_down,
        total_mlp[2],
    )
    flat = small_all.reshape(groups, small_rows * PAD)
    rest = jnp.sum(flat[:, lanes : lanes + D + HD], axis=0)
    small_total = jnp.concatenate([flat[:, :rows].reshape(D), rest])
    small_set = adamw(small_params, small_m, small_v, small_total, small_rate, 0.0)
    dunit_one = own_part + got_down.astype(f32) + got_up.astype(f32)
    input_grad = dmid + scale_one * (
        dunit_one - unit_one * jnp.mean(dunit_one * unit_one, axis=-1, keepdims=True)
    )
    return (
        output[None],
        input_grad.astype(bf16)[None],
        *updated,
        *small_set,
    )


def solution(mesh):
    rows = P("fsdp", "ctx", None)
    weight = P("fsdp", None)
    return jax.shard_map(
        functools.partial(body, mesh.shape["ctx"], mesh.shape["fsdp"]),
        mesh=mesh,
        in_specs=(rows, rows, weight) + (weight,) * 12 + (P(),) * 3,
        out_specs=(rows, rows) + (weight,) * 16 + (P(),) * 3,
        check_vma=False,
    )
```

```python
import functools
import math

import jax
import jax.numpy as jnp
from jax import lax
from jax.experimental import pallas as pl
from jax.experimental.pallas import tpu as pltpu
from jax.sharding import PartitionSpec as P

D = 1280
H = 16
HD = 80
FF = 1280
BLOCK = 256
CONT = 512
STEP = 3
PAD = 128
EXTRA = 16
TILE = CONT

bf16 = jnp.bfloat16
f32 = jnp.float32

norm_eps = 1e-06
beta_one = 0.5
beta_two = 0.5
adam_eps = 1e-08
decay_rate = 0.1
small_rate = 0.75
qkv_rate_base = 1.0
scale_base = 1.442695
LOG2E = math.log2(math.e)
LN2 = math.log(2.0)


def rms_scale(values):
    return lax.rsqrt(jnp.mean(values * values, axis=-1, keepdims=True) + norm_eps)


def adamw(weight, first, second, gradient, step_rate, decay_on):
    first_new = beta_one * first + (1.0 - beta_one) * gradient
    second_new = beta_two * second + (1.0 - beta_two) * gradient * gradient
    corr_one = 1.0 - beta_one**STEP
    corr_two = 1.0 - beta_two**STEP
    update = first_new / corr_one / (jnp.sqrt(second_new / corr_two) + adam_eps)
    weight_new = weight - step_rate * (update + decay_on * weight)
    return (weight_new, first_new, second_new)


def dot(left, right, contract=(1, 0)):
    return lax.dot_general(
        left, right, (((contract[0],), (contract[1],)), ((), ())), preferred_element_type=f32
    )


def three_rows(row):
    high = row.astype(bf16)
    rest = row - high.astype(f32)
    middle = rest.astype(bf16)
    low = (rest - middle.astype(f32)).astype(bf16)
    index = lax.broadcasted_iota(jnp.int32, (EXTRA, row.shape[1]), 0)
    zero = jnp.zeros((EXTRA, row.shape[1]), f32)
    rows = jnp.where(index == 0, high.astype(f32), zero)
    rows = jnp.where(index == 1, middle.astype(f32), rows)
    rows = jnp.where(index == 2, low.astype(f32), rows)
    return rows.astype(bf16)


def tile_at(tile):
    return pl.ds(pl.multiple_of(tile * TILE, TILE), TILE)


def block_at(slot):
    return pl.ds(pl.multiple_of(slot * BLOCK, BLOCK), BLOCK)


def tile_lanes(ref, head, slot_ref, tile, rows=slice(None)):
    first, second = slot_ref[2 * tile], slot_ref[2 * tile + 1]
    return jnp.concatenate(
        [ref[head, rows, block_at(first)], ref[head, rows, block_at(second)]], axis=1
    )


def tile_rows(ref, head, slot_ref, tile):
    first, second = slot_ref[2 * tile], slot_ref[2 * tile + 1]
    return jnp.concatenate([ref[head, block_at(first), :], ref[head, block_at(second), :]], axis=0)


def half_at(slot):
    return pl.ds(pl.multiple_of(lax.rem(slot, 2) * BLOCK, BLOCK), BLOCK)


def causal():
    key = lax.broadcasted_iota(jnp.int32, (TILE, TILE), 0)
    query = lax.broadcasted_iota(jnp.int32, (TILE, TILE), 1)
    return key <= query


def gather_kernel(
    parts,
    groups,
    heads,
    x_ref,
    wqkv_ref,
    gain_ref,
    wout_ref,
    wup_ref,
    wdown_ref,
    factor_ref,
    unit_ref,
    full_ref,
    wpair_ref,
    qt_ref,
    kt_ref,
    vt_ref,
    kn_ref,
    vn_ref,
    rows_ref,
    gained_ref,
    mlp_ref,
    wrecv_ref,
    wflip_ref,
    line_sem,
    side_sem,
    keep_sem,
    w_sem,
    mlp_sem,
    cross_sem,
    own_sem,
):
    chips = parts // 2
    here = lax.axis_index("ctx")
    group = lax.axis_index("fsdp")
    core = lax.rem(here, 2)
    chip = here // 2
    other = here + 1 - 2 * core
    width = heads * HD
    group_peers = [lax.rem(group + step, groups) for step in range(1, groups)]

    barrier = pltpu.get_barrier_semaphore()
    pl.semaphore_signal(barrier, inc=1, device_id={"ctx": other})
    for peer in group_peers:
        pl.semaphore_signal(barrier, inc=1, device_id={"fsdp": peer})
    for step in (1, chips - 1):
        peer = lax.rem(chip + step, chips) * 2 + core
        pl.semaphore_signal(barrier, inc=1, device_id={"ctx": peer})
    pl.semaphore_wait(barrier, groups + 2)

    def send(source, target, sems, device):
        return pltpu.make_async_remote_copy(
            src_ref=source,
            dst_ref=target,
            send_sem=sems[0],
            recv_sem=sems[1],
            device_id=device,
        )

    def line_copy(way, step, piece):
        ref = rows_ref.at[2 * piece + core]
        sems = (line_sem.at[0, way, step], line_sem.at[1, way, step])
        return send(ref, ref, sems, {"ctx": here + (2 if way else -2)})

    def side_copy(piece, lane):
        ref = rows_ref.at[2 * piece + lane]
        return send(ref, ref, (side_sem.at[0, piece], side_sem.at[1, piece]), {"ctx": other})

    def w_copy(peer, source):
        sems = (w_sem.at[0, peer], w_sem.at[1, source])
        return send(gained_ref, wrecv_ref.at[source], sems, {"fsdp": peer})

    def mlp_copy(peer, source):
        sems = (mlp_sem.at[0, peer], mlp_sem.at[1, source])
        return send(mlp_ref.at[:, core], full_ref.at[:, source, core], sems, {"fsdp": peer})

    def cross_copy(source, lane):
        ref = full_ref.at[:, source, lane]
        sems = (cross_sem.at[0, source], cross_sem.at[1, source])
        return send(ref, ref, sems, {"ctx": other})

    def keep_copy(piece):
        return pltpu.make_async_copy(rows_ref.at[piece], unit_ref.at[piece], keep_sem.at[piece])

    own_copy = pltpu.make_async_copy(mlp_ref, full_ref.at[:, group], own_sem)

    rows = x_ref[...].astype(f32)
    rows_ref[here] = (rows * rms_scale(rows)).astype(bf16)

    def forward(way, step, piece):
        @pl.when((chip < chips - 1) if way else (chip > 0))
        def _():
            line_copy(way, step, piece).start()

    for way in range(2):
        forward(way, 0, chip)
    side_copy(chip, core).start()
    span = 2 * width
    shift = lax.rem(D - chip * span, D)
    for part in range(3):
        turned = pltpu.roll(wqkv_ref[:, part * D : (part + 1) * D], shift, 1)
        gained_ref[part] = (turned[:, :span] * gain_ref[...]).astype(bf16)
    for peer in group_peers:
        w_copy(peer, group).start()
    for index, ref in enumerate((wout_ref, wup_ref, wdown_ref)):
        mlp_ref[index] = ref[...].astype(bf16).reshape(mlp_ref.shape[1:])
    own_copy.start()
    keep_copy(here).start()
    wrecv_ref[group] = gained_ref[...]
    for peer in group_peers:
        w_copy(group, peer).wait_recv()
    for peer in group_peers:
        mlp_copy(peer, group).start()
    for part in range(3):
        flipped = wrecv_ref[:, part].reshape(D, span).T
        for lane in range(2):
            wpair_ref[lane, part * width : (part + 1) * width] = flipped[
                lane * width : (lane + 1) * width
            ]
    wflip_ref[...] = wpair_ref[core]

    extra_row = lax.broadcasted_iota(jnp.int32, (PAD - HD, BLOCK), 0)
    extra = jnp.where(extra_row < 3, 1.0, 0.0)
    spare = jnp.zeros((PAD - HD, BLOCK), bf16)

    def project(piece):
        def half(index, carry):
            at = pl.ds(pl.multiple_of(index * BLOCK, BLOCK), BLOCK)
            to = pl.ds(pl.multiple_of((piece * 2 + index) * BLOCK, BLOCK), BLOCK)
            result = dot(wflip_ref[...], rows_ref[piece, at, :], (1, 1))
            for head in range(heads):
                query, key, value = (
                    result[part * width + head * HD : part * width + (head + 1) * HD]
                    for part in range(3)
                )
                qt_ref[head, :HD, to] = (query * factor_ref[...]).astype(bf16)
                qt_ref[head, HD:, to] = spare
                kt_ref[head, :, to] = key.astype(bf16)
                vt_ref[head, :HD, to] = value.astype(bf16)
                vt_ref[head, HD:, to] = jnp.ones((EXTRA, BLOCK), bf16)
                kn_ref[head, to, :] = jnp.concatenate([key, extra], axis=0).T.astype(bf16)
                vn_ref[head, to, :] = jnp.concatenate([value, extra], axis=0).T.astype(bf16)
            return carry

        lax.fori_loop(0, TILE // BLOCK, half, 0)

    def visit(distance, carry):
        for way in range(2):
            piece = chip - distance if way else chip + distance
            valid = (piece >= 0) if way else (piece <= chips - 1)

            @pl.when(valid & (distance > 0))
            def _():
                line_copy(way, distance - 1, piece).wait_recv()
                side_copy(piece, core).start()
                forward(way, distance, piece)
                keep_copy(2 * piece + core).start()

        for way in range(2):
            piece = chip - distance if way else chip + distance
            valid = (piece >= 0) if way else ((piece <= chips - 1) & (distance > 0))

            @pl.when(valid)
            def _():
                project(2 * piece + core)
                side_copy(piece, 1 - core).wait_recv()
                keep_copy(2 * piece + 1 - core).start()
                project(2 * piece + 1 - core)

        return carry

    lax.fori_loop(0, chips, visit, 0)

    for peer in group_peers:
        mlp_copy(group, peer).wait_recv()
        cross_copy(peer, core).start()
    for peer in group_peers:
        cross_copy(peer, 1 - core).wait_recv()
        cross_copy(peer, core).wait_send()
        w_copy(peer, group).wait_send()
        mlp_copy(peer, group).wait_send()
    own_copy.wait()

    def drain(piece, carry):
        keep_copy(2 * piece).wait()
        keep_copy(2 * piece + 1).wait()
        side_copy(piece, core).wait_send()

        @pl.when((piece <= chip) & (chip < chips - 1))
        def _():
            line_copy(1, chip - piece, piece).wait_send()

        @pl.when((piece >= chip) & (chip > 0))
        def _():
            line_copy(0, piece - chip, piece).wait_send()

        return carry

    lax.fori_loop(0, chips, drain, 0)


def gather_rows(parts, groups, heads, rows, w_qkv, gain, w_out, w_up, w_down, factor):
    rows_dev = rows.shape[0]
    held = w_qkv.shape[0]
    tokens = parts * rows_dev
    dma = pltpu.SemaphoreType.DMA
    chips = parts // 2
    anywhere = pl.BlockSpec(memory_space=pl.ANY)
    return pl.pallas_call(
        functools.partial(gather_kernel, parts, groups, heads),
        name="gather_rows",
        out_shape=[
            jax.ShapeDtypeStruct((parts, rows_dev, D), bf16),
            jax.ShapeDtypeStruct((3, groups, 2, held // 2, D), bf16),
            jax.ShapeDtypeStruct((2, 3 * heads * HD, D), bf16),
            jax.ShapeDtypeStruct((heads, PAD, tokens), bf16),
            jax.ShapeDtypeStruct((heads, HD, tokens), bf16),
            jax.ShapeDtypeStruct((heads, HD + EXTRA, tokens), bf16),
            jax.ShapeDtypeStruct((heads, tokens, PAD), bf16),
            jax.ShapeDtypeStruct((heads, tokens, PAD), bf16),
        ],
        in_specs=in_vmem(7),
        out_specs=[anywhere] * 2 + in_vmem(6),
        scratch_shapes=[
            pltpu.VMEM((parts, rows_dev, D), bf16),
            pltpu.VMEM((3, held, 2 * heads * HD), bf16),
            pltpu.VMEM((3, 2, held // 2, D), bf16),
            pltpu.VMEM((groups, 3, held, 2 * heads * HD), bf16),
            pltpu.VMEM((3 * heads * HD, D), bf16),
            dma((2, 2, chips)),
            dma((2, chips)),
            dma((parts,)),
            dma((2, groups)),
            dma((2, groups)),
            dma((2, groups)),
            dma,
        ],
        compiler_params=pltpu.CompilerParams(
            vmem_limit_bytes=60 * 1024 * 1024, collective_id=2, has_side_effects=True
        ),
    )(rows, w_qkv, gain, w_out, w_up, w_down, factor)


def forward_kernel(
    heads,
    slot_ref,
    qt_ref,
    kn_ref,
    vt_ref,
    lse_ref,
    ot_ref,
    acc_ref,
    top_ref,
):
    tokens = kn_ref.shape[1]
    num_tiles = tokens // TILE
    prompt_tiles = num_tiles // 2
    allowed = causal()

    def query_tile(tile, carry):
        here = tile_at(tile)
        top_ref[...] = jnp.full(top_ref.shape, -1e30, f32)
        acc_ref[...] = jnp.zeros(acc_ref.shape, f32)

        queries = [tile_lanes(qt_ref, head, slot_ref, tile) for head in range(heads)]

        def step(key_tile, masked):
            for head in range(heads):
                scores = dot(tile_rows(kn_ref, head, slot_ref, key_tile), queries[head])
                if masked:
                    scores = jnp.where(allowed, scores, -1e30)
                old = top_ref[head]
                top = jnp.maximum(old, jnp.max(scores, axis=0, keepdims=True))
                probs = jnp.exp2(scores - top).astype(bf16)
                acc_ref[head] = acc_ref[head] * jnp.exp2(old - top) + dot(
                    tile_lanes(vt_ref, head, slot_ref, key_tile), probs
                )
                top_ref[head] = top

        def full(key_tile, inner):
            step(key_tile, False)
            return inner

        lax.fori_loop(0, jnp.minimum(tile, prompt_tiles), full, 0)
        step(tile, True)
        for head in range(heads):
            acc = acc_ref[head]
            mass = acc[HD : HD + 1]
            mixed = (acc[:HD] / mass).astype(bf16)
            lse_ref[head, :, here] = top_ref[head] + jnp.log2(mass)
            for part in range(TILE // BLOCK):
                slot = slot_ref[tile * (TILE // BLOCK) + part]
                ot_ref[slot // 2, head * HD : (head + 1) * HD, half_at(slot)] = mixed[
                    :, part * BLOCK : (part + 1) * BLOCK
                ]
        return carry

    lax.fori_loop(0, num_tiles, query_tile, 0)


def backward_kernel(
    heads,
    slot_ref,
    qt_ref,
    kt_ref,
    kn_ref,
    vn_ref,
    lse_ref,
    ot_ref,
    dt_ref,
    factor_ref,
    units_ref,
    dqkv_ref,
    dscale_ref,
    u_ref,
    qa_ref,
    da_ref,
    dq_ref,
    dk_ref,
    dv_ref,
    held_ref,
    total_ref,
    load_sem,
):
    parts = units_ref.shape[0]

    def load(piece):
        slot = lax.rem(piece, 2)
        return pltpu.make_async_copy(units_ref.at[piece], held_ref.at[slot], load_sem.at[slot])

    for piece in range(2):
        load(piece).start()
    tokens = kn_ref.shape[1]
    num_blocks = tokens // BLOCK
    num_tiles = tokens // TILE
    prompt_tiles = num_tiles // 2
    width = heads * HD

    def prepare(block, carry):
        slot = slot_ref[block]
        to = pl.ds(pl.multiple_of(block * BLOCK, BLOCK), BLOCK)
        for head in range(heads):
            rows = slice(head * HD, (head + 1) * HD)
            grad = dt_ref[slot // 2, rows, half_at(slot)]
            mixed = ot_ref[slot // 2, rows, half_at(slot)]
            delta = jnp.sum(grad.astype(f32) * mixed.astype(f32), axis=0, keepdims=True)
            da_ref[head, :HD, to] = grad
            da_ref[head, HD : HD + EXTRA, to] = three_rows(-delta)
            da_ref[head, HD + EXTRA :, to] = jnp.zeros((PAD - HD - EXTRA, BLOCK), bf16)
            qa_ref[head, :HD, to] = qt_ref[head, :HD, block_at(slot)]
            qa_ref[head, HD : HD + EXTRA, to] = three_rows(-lse_ref[head, :, to])
            qa_ref[head, HD + EXTRA :, to] = jnp.zeros((PAD - HD - EXTRA, BLOCK), bf16)
        return carry

    lax.fori_loop(0, num_blocks, prepare, 0)
    dk_ref[...] = jnp.zeros(dk_ref.shape, f32)
    dv_ref[...] = jnp.zeros(dv_ref.shape, f32)
    dscale_ref[...] = jnp.zeros(dscale_ref.shape, f32)
    allowed = causal()

    def query_tile(tile, carry):
        here = tile_at(tile)
        dq_ref[...] = jnp.zeros(dq_ref.shape, f32)

        def step(key_tile, masked):
            keys = tile_at(key_tile)
            for head in range(heads):
                key_rows = tile_rows(kn_ref, head, slot_ref, key_tile)
                value_rows = tile_rows(vn_ref, head, slot_ref, key_tile)
                probs = jnp.exp2(dot(key_rows, qa_ref[head, :, here]))
                if masked:
                    probs = jnp.where(allowed, probs, 0.0)
                spread = dot(value_rows, da_ref[head, :, here])
                dscores = (probs * spread).astype(bf16)
                dv_ref[head, :, keys] += dot(da_ref[head, :HD, here], probs.astype(bf16), (1, 1))
                dk_ref[head, :, keys] += dot(qa_ref[head, :HD, here], dscores, (1, 1))
                dq_ref[head] += dot(tile_lanes(kt_ref, head, slot_ref, key_tile), dscores)

        def full(key_tile, inner):
            step(key_tile, False)
            return inner

        lax.fori_loop(0, jnp.minimum(tile, prompt_tiles), full, 0)
        step(tile, True)
        for head in range(heads):
            dq = dq_ref[head]
            product = dq * qa_ref[head, :HD, here].astype(f32)
            for lane in range(TILE // PAD):
                dscale_ref[head] += product[:, lane * PAD : (lane + 1) * PAD]
            scaled = (dq * (factor_ref[...] * LN2)).astype(bf16)
            for part in range(TILE // BLOCK):
                slot = slot_ref[tile * (TILE // BLOCK) + part]
                dqkv_ref[slot // 2, head * HD : (head + 1) * HD, half_at(slot)] = scaled[
                    :, part * BLOCK : (part + 1) * BLOCK
                ]
        return carry

    lax.fori_loop(0, num_tiles, query_tile, 0)

    def finish(block, carry):
        slot = slot_ref[block]
        owner, to = slot // 2, half_at(slot)
        at = pl.ds(pl.multiple_of(block * BLOCK, BLOCK), BLOCK)
        for head in range(heads):
            row = width + head * HD
            dqkv_ref[owner, row : row + HD, to] = (dk_ref[head, :, at] * LN2).astype(bf16)
            row = 2 * width + head * HD
            dqkv_ref[owner, row : row + HD, to] = dv_ref[head, :, at].astype(bf16)
        return carry

    lax.fori_loop(0, num_blocks, finish, 0)
    total_ref[...] = jnp.zeros(total_ref.shape, f32)

    def project(piece, carry):
        load(piece).wait()
        total_ref[...] += dot(dqkv_ref[piece], held_ref[lax.rem(piece, 2)])

        @pl.when(piece + 2 < parts)
        def _():
            load(piece + 2).start()

        return carry

    lax.fori_loop(0, parts, project, 0)
    u_ref[...] = total_ref[...].T.astype(bf16)


def in_vmem(count):
    return [pl.BlockSpec(memory_space=pltpu.VMEM)] * count


def params():
    return pltpu.CompilerParams(vmem_limit_bytes=60 * 1024 * 1024)


def attention_forward(slots, qt, kn, vt, parts):
    heads, tokens = kn.shape[:2]
    return pl.pallas_call(
        functools.partial(forward_kernel, heads),
        name="attention_forward",
        out_shape=[
            jax.ShapeDtypeStruct((heads, 1, tokens), f32),
            jax.ShapeDtypeStruct((parts, heads * HD, tokens // parts), bf16),
        ],
        in_specs=[pl.BlockSpec(memory_space=pltpu.SMEM)] + in_vmem(3),
        out_specs=in_vmem(2),
        scratch_shapes=[
            pltpu.VMEM((heads, HD + EXTRA, TILE), f32),
            pltpu.VMEM((heads, 1, TILE), f32),
        ],
        compiler_params=params(),
        cost_estimate=attention_cost(heads, tokens, 2),
    )(slots, qt, kn, vt)


def attention_cost(heads, tokens, passes):
    pairs = heads * tokens * tokens // 2
    return pl.CostEstimate(
        flops=2 * passes * pairs * BLOCK, bytes_accessed=tokens * D, transcendentals=pairs
    )


def attention_backward(slots, kept, mixed, dmixed, factor, units):
    qt, kt, kn, vn, lse = kept
    heads, tokens = kn.shape[:2]
    return pl.pallas_call(
        functools.partial(backward_kernel, heads),
        name="attention_backward",
        out_shape=[
            jax.ShapeDtypeStruct((mixed.shape[0], 3 * heads * HD, mixed.shape[2]), bf16),
            jax.ShapeDtypeStruct((heads, HD, PAD), f32),
            jax.ShapeDtypeStruct((D, 3 * heads * HD), bf16),
        ],
        in_specs=[pl.BlockSpec(memory_space=pltpu.SMEM)]
        + in_vmem(8)
        + [pl.BlockSpec(memory_space=pl.ANY)],
        out_specs=in_vmem(3),
        scratch_shapes=[
            pltpu.VMEM((heads, PAD, tokens), bf16),
            pltpu.VMEM((heads, PAD, tokens), bf16),
            pltpu.VMEM((heads, HD, TILE), f32),
            pltpu.VMEM((heads, HD, tokens), f32),
            pltpu.VMEM((heads, HD, tokens), f32),
            pltpu.VMEM((2,) + units.shape[1:], bf16),
            pltpu.VMEM((3 * heads * HD, D), f32),
            pltpu.SemaphoreType.DMA((2,)),
        ],
        compiler_params=params(),
        cost_estimate=attention_cost(heads, tokens, 5),
    )(slots, qt, kt, kn, vn, lse, mixed, dmixed, factor, units)


def middle_kernel(
    parts,
    groups,
    mixed_ref,
    x_ref,
    dy_ref,
    weights_ref,
    gain_ref,
    *refs,
):
    out_ref, dmid_ref, dmixed_ref, gain_grad_ref = refs[:4]
    chunk_refs = refs[4 : 4 + groups]
    (
        w_ref,
        attn_ref,
        dattn_ref,
        act_ref,
        normed_ref,
        dhidden_ref,
        dbranch_ref,
        grad_ref,
        theirs_ref,
        w_sem,
        attn_sem,
        dattn_sem,
        pair_sem,
    ) = refs[4 + groups :]
    here = lax.axis_index("ctx")
    group = lax.axis_index("fsdp")
    core = lax.rem(here, 2)
    other = here + 1 - 2 * core
    peers = [lax.rem(here + step, parts) for step in range(1, parts)]
    tokens = x_ref.shape[0]
    width = mixed_ref.shape[1]
    held = theirs_ref.shape[2]
    loads = [
        pltpu.make_async_copy(weights_ref.at[index], w_ref.at[index], w_sem.at[index])
        for index in range(3)
    ]
    for load in loads:
        load.start()

    barrier = pltpu.get_barrier_semaphore()
    for peer in peers:
        pl.semaphore_signal(barrier, inc=1, device_id={"ctx": peer})
    pl.semaphore_wait(barrier, parts - 1)

    def lanes(part):
        return pl.ds(pl.multiple_of(part * BLOCK, BLOCK), BLOCK)

    def attn_copy(part, peer, source):
        return pltpu.make_async_remote_copy(
            src_ref=mixed_ref.at[peer, :, lanes(part)],
            dst_ref=attn_ref.at[source, :, lanes(part)],
            send_sem=attn_sem.at[0, part, peer],
            recv_sem=attn_sem.at[1, part, source],
            device_id={"ctx": peer},
        )

    def dattn_copy(part, peer, source):
        return pltpu.make_async_remote_copy(
            src_ref=dattn_ref.at[peer, :, lanes(part)],
            dst_ref=dmixed_ref.at[source, :, lanes(part)],
            send_sem=dattn_sem.at[0, part, peer],
            recv_sem=dattn_sem.at[1, part, source],
            device_id={"ctx": peer},
        )

    def rows_of(owner, lane):
        start = pl.multiple_of((owner * 2 + lane) * held, 16)
        return pl.ds(start, held)

    def pair_copy(index, owner, lane):
        return pltpu.make_async_remote_copy(
            src_ref=grad_ref.at[index, rows_of(owner, lane), :],
            dst_ref=theirs_ref.at[index, owner],
            send_sem=pair_sem.at[0, index, owner],
            recv_sem=pair_sem.at[1, index, owner],
            device_id={"ctx": other},
        )

    for part in range(tokens // BLOCK):
        for peer in peers:
            attn_copy(part, peer, here).start()
    attn_ref[here] = mixed_ref[here]
    gain_grad_ref[...] = jnp.zeros(gain_grad_ref.shape, f32)
    for load in loads:
        load.wait()
    gain = gain_ref[...]

    def layer(part, carry):
        rows = lanes(part)
        for peer in peers:
            attn_copy(part, here, peer).wait_recv()
        attn = attn_ref[:, :, rows].reshape(D, BLOCK)
        mid = x_ref[rows, :].astype(f32) + dot(attn, w_ref[0], (0, 0))
        scale = rms_scale(mid)
        unit = mid * scale
        normed = (unit * gain).astype(bf16)
        normed_ref[rows, :] = normed
        hidden = dot(normed, w_ref[1])
        gate = jax.nn.sigmoid(hidden)
        act = (hidden * gate).astype(bf16)
        act_ref[rows, :] = act
        dy = dy_ref[rows, :]
        dact = dot(dy, w_ref[2], (1, 1))
        dhidden = (dact * gate * (1.0 + hidden * (1.0 - gate))).astype(bf16)
        dhidden_ref[rows, :] = dhidden
        dnormed = dot(dhidden, w_ref[1], (1, 1))
        dunit = dnormed * gain
        dmid = dy.astype(f32) + scale * (
            dunit - unit * jnp.mean(dunit * unit, axis=-1, keepdims=True)
        )
        dmid_ref[rows, :] = dmid
        dbranch = dmid.astype(bf16)
        dbranch_ref[rows, :] = dbranch
        dattn = dot(w_ref[0], dbranch, (1, 1)).astype(bf16).reshape(parts, width, BLOCK)
        dattn_ref[:, :, rows] = dattn
        for peer in peers:
            dattn_copy(part, peer, here).start()
        dmixed_ref[here, :, rows] = dattn_ref[here, :, rows]
        out_ref[rows, :] = (mid + dot(act, w_ref[2])).astype(bf16)
        gain_grad_ref[...] += jnp.sum(dnormed * unit, axis=0, keepdims=True)
        return carry

    lax.fori_loop(0, tokens // BLOCK, layer, 0)

    def down_rows(index, carry):
        rows = lanes(index)
        grad_ref[2, rows, :] = dot(act_ref[:, rows], dy_ref[...], (0, 0)).astype(bf16)
        return carry

    def up_rows(index, carry):
        rows = lanes(index)
        grad_ref[1, rows, :] = dot(normed_ref[:, rows], dhidden_ref[...], (0, 0)).astype(bf16)
        return carry

    def out_rows(index, carry):
        rows = pl.ds(pl.multiple_of(index * width, 16), width)
        grad_ref[0, rows, :] = dot(attn_ref[index], dbranch_ref[...]).astype(bf16)
        return carry

    for index, count, run in (
        (2, D // BLOCK, down_rows),
        (1, D // BLOCK, up_rows),
        (0, parts, out_rows),
    ):
        lax.fori_loop(0, count, run, 0)
        for owner in range(groups):
            pair_copy(index, owner, 1 - core).start()
    for step in range(groups):
        owner = group ^ step
        for index in (2, 1, 0):
            pair_copy(index, owner, core).wait_recv()
            chunk_refs[step][index] = (
                grad_ref[index, rows_of(owner, core), :].astype(f32)
                + theirs_ref[index, owner].astype(f32)
            ).astype(bf16)
    for part in range(tokens // BLOCK):
        for peer in peers:
            dattn_copy(part, here, peer).wait_recv()
            dattn_copy(part, peer, here).wait_send()
            attn_copy(part, peer, here).wait_send()
    for index in range(3):
        for owner in range(groups):
            pair_copy(index, owner, 1 - core).wait_send()


def middle(parts, groups, mixed, rows, cotangent, weights, gain):
    rows_dev = rows.shape[0]
    half = D // groups // 2
    dma = pltpu.SemaphoreType.DMA
    halves = rows_dev // BLOCK
    return pl.pallas_call(
        functools.partial(middle_kernel, parts, groups),
        name="middle",
        out_shape=[
            jax.ShapeDtypeStruct((rows_dev, D), bf16),
            jax.ShapeDtypeStruct((rows_dev, D), f32),
            jax.ShapeDtypeStruct(mixed.shape, bf16),
            jax.ShapeDtypeStruct((1, D), f32),
        ]
        + [jax.ShapeDtypeStruct((3, half, D), bf16)] * groups,
        in_specs=in_vmem(3) + [pl.BlockSpec(memory_space=pl.ANY)] + in_vmem(1),
        out_specs=in_vmem(4 + groups),
        scratch_shapes=[
            pltpu.VMEM((3, D, D), bf16),
            pltpu.VMEM(mixed.shape, bf16),
            pltpu.VMEM(mixed.shape, bf16),
            pltpu.VMEM((rows_dev, D), bf16),
            pltpu.VMEM((rows_dev, D), bf16),
            pltpu.VMEM((rows_dev, D), bf16),
            pltpu.VMEM((rows_dev, D), bf16),
            pltpu.VMEM((3, D, D), bf16),
            pltpu.VMEM((3, groups, half, D), bf16),
            dma((3,)),
            dma((2, halves, parts)),
            dma((2, halves, parts)),
            dma((2, 3, groups)),
        ],
        compiler_params=pltpu.CompilerParams(
            vmem_limit_bytes=60 * 1024 * 1024, collective_id=3, has_side_effects=True
        ),
    )(mixed, rows, cotangent, weights, gain)


def reduce_kernel(
    parts,
    groups,
    dq_ref,
    wt_ref,
    u_ref,
    wc_ref,
    mlp_ref,
    small_ref,
    down_ref,
    up_ref,
    own_ref,
    ugather_ref,
    mgather_ref,
    sgather_ref,
    pair_ref,
    sum_ref,
    urecv_ref,
    mrecv_ref,
    part_ref,
    column_ref,
    smine_ref,
    srecv_ref,
    pair_sem,
    sum_sem,
    u_sem,
    m_sem,
    line_sem,
    side_sem,
    small_sem,
    cross_sem,
):
    chips = parts // 2
    here = lax.axis_index("ctx")
    group = lax.axis_index("fsdp")
    core = lax.rem(here, 2)
    chip = here // 2
    other = here + 1 - 2 * core
    ctx_peers = [lax.rem(here + step, parts) for step in range(1, parts)]
    chip_peers = [lax.rem(chip + step, chips) for step in range(1, chips)]
    group_peers = [lax.rem(group + step, groups) for step in range(1, groups)]

    barrier = pltpu.get_barrier_semaphore()
    for peer in ctx_peers:
        pl.semaphore_signal(barrier, inc=1, device_id={"ctx": peer})
    for peer in group_peers:
        pl.semaphore_signal(barrier, inc=1, device_id={"fsdp": peer})
    pl.semaphore_wait(barrier, parts + groups - 2)

    def send(source, target, sems, device):
        return pltpu.make_async_remote_copy(
            src_ref=source,
            dst_ref=target,
            send_sem=sems[0],
            recv_sem=sems[1],
            device_id=device,
        )

    def pair_copy(index):
        return send(
            dq_ref.at[index, 1 - core],
            pair_ref.at[index],
            (pair_sem.at[0, index], pair_sem.at[1, index]),
            {"ctx": other},
        )

    def u_copy(peer, source):
        return send(
            u_ref.at[peer],
            urecv_ref.at[source],
            (u_sem.at[0, peer], u_sem.at[1, source]),
            {"fsdp": peer},
        )

    def m_copy(peer, source):
        return send(
            mlp_ref.at[peer],
            mrecv_ref.at[source],
            (m_sem.at[0, peer], m_sem.at[1, source]),
            {"ctx": 2 * peer + core},
        )

    for index in range(chips):
        pair_copy(index).start()
    for peer in group_peers:
        u_copy(peer, group).start()
    for peer in chip_peers:
        m_copy(peer, chip).start()
    for index in range(chips):
        pair_copy(index).wait_recv()

    rows_half = own_ref.shape[0] // 2

    def partial(target):
        def half(index, carry):
            rows = pl.ds(pl.multiple_of(index * rows_half, rows_half), rows_half)
            part_ref[rows, :] = dot(dq_ref[target, core, :, rows], wt_ref[core], (0, 0)) + dot(
                pair_ref[target, :, rows], wt_ref[1 - core], (0, 0)
            )
            return carry

        lax.fori_loop(0, 2, half, 0)

    def sum_copy(way, target):
        return send(
            sum_ref.at[way, target],
            sum_ref.at[way, target],
            (sum_sem.at[0, way, target], sum_sem.at[1, way, target]),
            {"ctx": here + (2 if way else -2)},
        )

    def reduce_step(step):
        last = step == chips - 2
        for way, target, active, first, out_ref in (
            (0, step - (chips - 1) + chip, step >= chips - 1 - chip, chip == chips - 1, down_ref),
            (1, chips - 1 - step + chip, step >= chip, chip == 0, up_ref),
        ):

            @pl.when(active)
            def _():
                partial(target)

                @pl.when(first)
                def _():
                    sum_ref[way, target] = part_ref[...].astype(bf16)

                @pl.when(jnp.logical_not(first))
                def _():
                    sum_copy(way, target).wait_recv()
                    sum_ref[way, target] = (
                        part_ref[...] + sum_ref[way, target].astype(f32)
                    ).astype(bf16)

                if last:
                    out_ref[...] = sum_ref[way, target]
                else:
                    sum_copy(way, target).start()

            if last:

                @pl.when(jnp.logical_not(active))
                def _():
                    out_ref[...] = jnp.zeros(out_ref.shape, bf16)

    gathers = (ugather_ref, mgather_ref)

    def line_copy(which, way, step, piece):
        ref = gathers[which].at[2 * piece + core]
        sems = (line_sem.at[0, which, way, step], line_sem.at[1, which, way, step])
        return send(ref, ref, sems, {"ctx": here + (2 if way else -2)})

    def side_copy(which, piece, lane):
        ref = gathers[which].at[2 * piece + lane]
        sems = (side_sem.at[0, which, piece], side_sem.at[1, which, piece])
        return send(ref, ref, sems, {"ctx": other})

    def line_sends(which, step, go):
        @pl.when((chip < chips - 1) & (chip - step >= 0))
        def _():
            go(line_copy(which, 1, step, chip - step))

        @pl.when((chip > 0) & (chip + step <= chips - 1))
        def _():
            go(line_copy(which, 0, step, chip + step))

    def line_receive(which, step):
        @pl.when(chip - 1 - step >= 0)
        def _():
            line_copy(which, 1, step, chip - 1 - step).wait_recv()
            side_copy(which, chip - 1 - step, core).start()

        @pl.when(chip + 1 + step <= chips - 1)
        def _():
            line_copy(which, 0, step, chip + 1 + step).wait_recv()
            side_copy(which, chip + 1 + step, core).start()

    def small_copy(peer, source):
        return send(
            smine_ref,
            srecv_ref.at[source],
            (small_sem.at[0, peer], small_sem.at[1, source]),
            {"ctx": peer},
        )

    def cross_copy(peer, source):
        return send(
            sgather_ref.at[group],
            sgather_ref.at[source],
            (cross_sem.at[0, peer], cross_sem.at[1, source]),
            {"fsdp": peer},
        )

    reduce_step(0)

    total = u_ref[group].astype(f32)
    for peer in group_peers:
        u_copy(group, peer).wait_recv()
        total = total + urecv_ref[peer].astype(f32)
    ugather_ref[here] = total.astype(bf16)
    side_copy(0, chip, core).start()
    line_sends(0, 0, lambda copy: copy.start())
    held = total.shape[0]
    gain = jnp.sum(total * wc_ref[...].astype(f32), axis=1, keepdims=True)
    column_ref[...] = jnp.zeros(column_ref.shape, f32)
    column_ref[:held, :] = jnp.broadcast_to(gain, (held, PAD))
    flat = column_ref[...].T[:1]
    smine_ref[...] = small_ref[...]
    for row in range(column_ref.shape[0] // PAD):
        smine_ref[row : row + 1, :] = flat[:, row * PAD : (row + 1) * PAD]
    for peer in ctx_peers:
        small_copy(peer, here).start()

    total = mlp_ref[chip].astype(f32)
    for peer in chip_peers:
        m_copy(chip, peer).wait_recv()
        total = total + mrecv_ref[peer].astype(f32)
    mgather_ref[here] = total.astype(bf16)
    side_copy(1, chip, core).start()
    line_sends(1, 0, lambda copy: copy.start())

    for step in range(1, chips):
        if step <= chips - 2:
            reduce_step(step)
        for which in range(2):
            line_receive(which, step - 1)
            if step <= chips - 2:
                line_sends(which, step, lambda copy: copy.start())
        if step == 1:
            small = smine_ref[...]
            for peer in ctx_peers:
                small_copy(here, peer).wait_recv()
                small = small + srecv_ref[peer]
            sgather_ref[group] = small
            for peer in group_peers:
                cross_copy(peer, group).start()

    partial(chip)
    own_ref[...] = part_ref[...]

    for which in range(2):
        for piece in range(chips):
            side_copy(which, piece, 1 - core).wait_recv()
            side_copy(which, piece, core).wait_send()
        for step in range(chips - 1):
            line_sends(which, step, lambda copy: copy.wait_send())
    for index in range(chips):
        pair_copy(index).wait_send()
    for peer in group_peers:
        cross_copy(group, peer).wait_recv()
        cross_copy(peer, group).wait_send()
        u_copy(peer, group).wait_send()
    for peer in chip_peers:
        m_copy(peer, chip).wait_send()
    for peer in ctx_peers:
        small_copy(peer, here).wait_send()
    for step in range(chips - 2):

        @pl.when(step >= chips - 1 - chip)
        def _():
            sum_copy(0, step - (chips - 1) + chip).wait_send()

        @pl.when(step >= chip)
        def _():
            sum_copy(1, chips - 1 - step + chip).wait_send()


def reduce_gradients(parts, groups, dqkv, w_pair, u_parts, w_columns, mlp, small):
    chips = parts // 2
    rows_dev = dqkv.shape[3]
    rows, width = w_columns.shape
    lanes = -(-rows // PAD) * PAD
    dma = pltpu.SemaphoreType.DMA
    return pl.pallas_call(
        functools.partial(reduce_kernel, parts, groups),
        name="reduce_gradients",
        out_shape=[
            jax.ShapeDtypeStruct((rows_dev, D), bf16),
            jax.ShapeDtypeStruct((rows_dev, D), bf16),
            jax.ShapeDtypeStruct((rows_dev, D), f32),
            jax.ShapeDtypeStruct((parts, rows, width), bf16),
            jax.ShapeDtypeStruct((parts,) + mlp.shape[1:], bf16),
            jax.ShapeDtypeStruct((groups,) + small.shape, f32),
        ],
        in_specs=in_vmem(6),
        out_specs=in_vmem(6),
        scratch_shapes=[
            pltpu.VMEM((chips,) + dqkv.shape[2:], bf16),
            pltpu.VMEM((2, chips, rows_dev, D), bf16),
            pltpu.VMEM(u_parts.shape, bf16),
            pltpu.VMEM(mlp.shape, bf16),
            pltpu.VMEM((rows_dev, D), f32),
            pltpu.VMEM((lanes, PAD), f32),
            pltpu.VMEM(small.shape, f32),
            pltpu.VMEM((parts,) + small.shape, f32),
            dma((2, chips)),
            dma((2, 2, chips)),
            dma((2, groups)),
            dma((2, chips)),
            dma((2, 2, 2, chips)),
            dma((2, 2, chips)),
            dma((2, parts)),
            dma((2, groups)),
        ],
        compiler_params=pltpu.CompilerParams(
            vmem_limit_bytes=60 * 1024 * 1024, collective_id=1, has_side_effects=True
        ),
    )(dqkv, w_pair, u_parts, w_columns, mlp, small)


def update_kernel(rates, qkv_ref, gain_ref, mlp_ref, *refs):
    sets = len(rates)
    parts, rows, width = qkv_ref.shape
    width = width // 3
    for index, rate in enumerate(rates):
        weight, first, second = (ref[...] for ref in refs[3 * index : 3 * index + 3])
        if index == 0:
            pieces = [qkv_ref[part].astype(f32) for part in range(parts)]
            gradient = jnp.concatenate(
                [piece[:, at * width : (at + 1) * width] for at in range(3) for piece in pieces],
                axis=1,
            )
            gradient = gradient * gain_ref[...]
        else:
            gradient = mlp_ref[0, index - 1].astype(f32)
        outs = refs[3 * sets + 4 * index : 3 * sets + 4 * index + 4]
        new, first, second = adamw(weight, first, second, gradient, rate, decay_rate)
        outs[0][...] = new
        outs[1][...] = first
        outs[2][...] = second
        outs[3][...] = new.astype(bf16)


def update(rates, parts, qkv, gain, mlp, *arrays):
    rows = arrays[0].shape[0]
    chips = parts // 2
    step_rows = rows // parts
    if step_rows % 8 == 0:

        def owner(i):
            return (2 * lax.rem(i, chips) + i // chips, 0, 0, 0)

    else:
        step_rows = 32
        mlp = mlp.reshape(chips, 2, 3, rows // parts, D).transpose(2, 1, 0, 3, 4)
        mlp = mlp.reshape(3, rows // step_rows, step_rows, D).transpose(1, 0, 2, 3)

        def owner(i):
            return (i, 0, 0, 0)

    in_specs = [
        pl.BlockSpec((parts, step_rows, qkv.shape[2]), lambda i: (0, i, 0)),
        pl.BlockSpec((step_rows, 1), lambda i: (i, 0)),
        pl.BlockSpec((1, 3, step_rows, D), owner),
    ]
    specs, shapes, moved = [], [], 0
    for array in arrays:
        in_specs.append(pl.BlockSpec((step_rows, array.shape[1]), lambda i: (i, 0)))
    for index in range(len(rates)):
        shape = arrays[3 * index].shape
        shapes += [jax.ShapeDtypeStruct(shape, f32)] * 3 + [jax.ShapeDtypeStruct(shape, bf16)]
        specs += [pl.BlockSpec((step_rows, shape[1]), lambda i: (i, 0))] * 4
        moved += shape[0] * shape[1] * 28
    return pl.pallas_call(
        functools.partial(update_kernel, rates),
        name="update_weights",
        grid=(rows // step_rows,),
        in_specs=in_specs,
        out_specs=specs,
        out_shape=shapes,
        compiler_params=params(),
        cost_estimate=pl.CostEstimate(flops=moved, bytes_accessed=moved, transcendentals=0),
    )(qkv, gain, mlp, *arrays)


def body(
    parts,
    groups,
    inputs,
    cotangent,
    block_order,
    w_qkv,
    m_qkv,
    v_qkv,
    w_out,
    m_out,
    v_out,
    w_up,
    m_up,
    v_up,
    w_down,
    m_down,
    v_down,
    small_params,
    small_m,
    small_v,
):
    heads = H // parts
    width = heads * HD
    rows_dev = inputs.shape[1]
    tokens = rows_dev * parts
    here = lax.axis_index("ctx")
    index = jnp.arange(block_order.shape[1], dtype=jnp.int32)
    slots = jnp.sum(jnp.where(block_order[0][None] == index[:, None], index[None], 0), axis=1)
    gain_one = small_params[:D]
    gain_two = small_params[D : 2 * D]
    query_scale = small_params[2 * D :]
    group = lax.axis_index("fsdp")
    rows = w_qkv.shape[0]

    def head_columns(owner):
        return jnp.concatenate(
            [
                lax.dynamic_slice_in_dim(w_qkv, part * D + owner * width, width, 1)
                for part in range(3)
            ],
            axis=1,
        )

    gain_rows = lax.dynamic_slice_in_dim(gain_one, group * rows, rows, 0)[:, None]
    w_columns = head_columns(here).astype(bf16)
    layer_in = inputs[0].astype(f32)
    scale_one = rms_scale(layer_in)
    unit_one = layer_in * scale_one
    factor = scale_base / math.sqrt(HD) * jax.nn.softplus(query_scale)
    factor_two = (factor * LOG2E)[:, None]
    unit_all, mlp_full, w_pair, qt, kt, vt, kn, vn = gather_rows(
        parts, groups, heads, inputs[0], w_qkv, gain_rows, w_out, w_up, w_down, factor_two
    )
    lse, mixed = attention_forward(slots, qt, kn, vt, parts)
    kept = (qt, kt, kn, vn, lse)
    output, dmid, dmixed, gain_two_grad, *chunks = middle(
        parts,
        groups,
        mixed,
        inputs[0],
        cotangent[0],
        mlp_full.reshape(3, D, D),
        gain_two[None],
    )
    mlp_sum = chunks[0].astype(f32)
    for step in range(1, groups):
        swap = [(i, i ^ step) for i in range(groups)]
        mlp_sum = mlp_sum + lax.ppermute(chunks[step], "fsdp", swap).astype(f32)
    mlp_part = (
        mlp_sum.astype(bf16).reshape(3, parts // 2, rows // parts, D).transpose(1, 0, 2, 3)
    )
    dqkv, dscale, u_parts = attention_backward(slots, kept, mixed, dmixed, factor_two, unit_all)
    u_parts = u_parts.reshape(groups, rows, 3 * width)
    scale_grad = (
        jnp.sum(dscale, axis=(0, 2))
        / factor_two[:, 0]
        * (scale_base / math.sqrt(HD))
        * jax.nn.sigmoid(query_scale)
    )
    lanes = -(-rows // PAD) * PAD
    small_rows = -(-(lanes + D + PAD) // (8 * PAD)) * 8
    small = jnp.concatenate([jnp.zeros((lanes,), f32), gain_two_grad[0], scale_grad])
    small = jnp.pad(small, (0, small_rows * PAD - small.shape[0])).reshape(small_rows, PAD)
    send_down, send_up, own_part, u_all, mlp_all, small_all = reduce_gradients(
        parts,
        groups,
        dqkv.reshape(parts // 2, 2, 3 * width, rows_dev),
        w_pair,
        u_parts,
        w_columns,
        mlp_part,
        small,
    )
    got_down = lax.ppermute(send_down, "ctx", [(i, i - 2) for i in range(2, parts)])
    got_up = lax.ppermute(send_up, "ctx", [(i, i + 2) for i in range(parts - 2)])
    rate_qkv = qkv_rate_base / math.sqrt(D)
    rate_out = 0.5 / math.sqrt(max(D // 256, 1))
    rate_up = 0.5 / math.sqrt(D)
    rate_down = 0.5 / math.sqrt(FF)
    updated = update(
        (rate_qkv, rate_out, rate_up, rate_down),
        parts,
        u_all,
        gain_rows,
        mlp_all,
        w_qkv,
        m_qkv,
        v_qkv,
        w_out,
        m_out,
        v_out,
        w_up,
        m_up,
        v_up,
        w_down,
        m_down,
        v_down,
    )
    flat = small_all.reshape(groups, small_rows * PAD)
    rest = jnp.sum(flat[:, lanes : lanes + D + HD], axis=0)
    small_total = jnp.concatenate([flat[:, :rows].reshape(D), rest])
    small_set = adamw(small_params, small_m, small_v, small_total, small_rate, 0.0)
    dunit_one = own_part + got_down.astype(f32) + got_up.astype(f32)
    input_grad = dmid + scale_one * (
        dunit_one - unit_one * jnp.mean(dunit_one * unit_one, axis=-1, keepdims=True)
    )
    return (
        output[None],
        input_grad.astype(bf16)[None],
        *updated,
        *small_set,
    )


def solution(mesh):
    rows = P("fsdp", "ctx", None)
    weight = P("fsdp", None)
    return jax.shard_map(
        functools.partial(body, mesh.shape["ctx"], mesh.shape["fsdp"]),
        mesh=mesh,
        in_specs=(rows, rows, weight) + (weight,) * 12 + (P(),) * 3,
        out_specs=(rows, rows) + (weight,) * 16 + (P(),) * 3,
        check_vma=False,
    )
```

```python
import functools
import math

import jax
import jax.numpy as jnp
from jax import lax
from jax.experimental import pallas as pl
from jax.experimental.pallas import tpu as pltpu
from jax.sharding import PartitionSpec as P

D = 1280
H = 16
HD = 80
FF = 1280
BLOCK = 256
CONT = 512
STEP = 3
PAD = 128
EXTRA = 16
TILE = CONT
SCORE_BOUND = 96.0

bf16 = jnp.bfloat16
f32 = jnp.float32

norm_eps = 1e-06
beta_one = 0.5
beta_two = 0.5
adam_eps = 1e-08
decay_rate = 0.1
small_rate = 0.75
qkv_rate_base = 1.0
scale_base = 1.442695
LOG2E = math.log2(math.e)
LN2 = math.log(2.0)


def rms_scale(values):
    return lax.rsqrt(jnp.mean(values * values, axis=-1, keepdims=True) + norm_eps)


def adamw(weight, first, second, gradient, step_rate, decay_on):
    first_new = beta_one * first + (1.0 - beta_one) * gradient
    second_new = beta_two * second + (1.0 - beta_two) * gradient * gradient
    corr_one = 1.0 - beta_one**STEP
    corr_two = 1.0 - beta_two**STEP
    update = first_new / corr_one / (jnp.sqrt(second_new / corr_two) + adam_eps)
    weight_new = weight - step_rate * (update + decay_on * weight)
    return (weight_new, first_new, second_new)


def dot(left, right, contract=(1, 0)):
    return lax.dot_general(
        left, right, (((contract[0],), (contract[1],)), ((), ())), preferred_element_type=f32
    )


def three_rows(row):
    high = row.astype(bf16)
    rest = row - high.astype(f32)
    middle = rest.astype(bf16)
    low = (rest - middle.astype(f32)).astype(bf16)
    index = lax.broadcasted_iota(jnp.int32, (EXTRA, row.shape[1]), 0)
    zero = jnp.zeros((EXTRA, row.shape[1]), f32)
    rows = jnp.where(index == 0, high.astype(f32), zero)
    rows = jnp.where(index == 1, middle.astype(f32), rows)
    rows = jnp.where(index == 2, low.astype(f32), rows)
    return rows.astype(bf16)


def tile_at(tile):
    return pl.ds(pl.multiple_of(tile * TILE, TILE), TILE)


def block_at(slot):
    return pl.ds(pl.multiple_of(slot * BLOCK, BLOCK), BLOCK)


def tile_lanes(ref, head, slot_ref, tile, rows=slice(None)):
    first, second = slot_ref[2 * tile], slot_ref[2 * tile + 1]
    return jnp.concatenate(
        [ref[head, rows, block_at(first)], ref[head, rows, block_at(second)]], axis=1
    )


def tile_rows(ref, head, slot_ref, tile):
    first, second = slot_ref[2 * tile], slot_ref[2 * tile + 1]
    return jnp.concatenate([ref[head, block_at(first), :], ref[head, block_at(second), :]], axis=0)


def half_at(slot):
    return pl.ds(pl.multiple_of(lax.rem(slot, 2) * BLOCK, BLOCK), BLOCK)


def causal(shape):
    key = lax.broadcasted_iota(jnp.int32, shape, 0)
    query = lax.broadcasted_iota(jnp.int32, shape, 1)
    return key <= query


def gather_kernel(
    parts,
    groups,
    heads,
    x_ref,
    wqkv_ref,
    gain_ref,
    wout_ref,
    wup_ref,
    wdown_ref,
    factor_ref,
    unit_ref,
    full_ref,
    wpair_ref,
    qt_ref,
    kt_ref,
    vt_ref,
    kn_ref,
    vn_ref,
    rows_ref,
    wstage_ref,
    mstage_ref,
    gained_ref,
    mlp_ref,
    wrecv_ref,
    wflip_ref,
    line_sem,
    side_sem,
    keep_sem,
    w_sem,
    lane_sem,
    mlp_sem,
    cross_sem,
    own_sem,
    stage_sem,
):
    chips = parts // 2
    here = lax.axis_index("ctx")
    group = lax.axis_index("fsdp")
    core = lax.rem(here, 2)
    chip = here // 2
    other = here + 1 - 2 * core
    width = heads * HD
    group_peers = [lax.rem(group + step, groups) for step in range(1, groups)]

    barrier = pltpu.get_barrier_semaphore()
    pl.semaphore_signal(barrier, inc=1, device_id={"ctx": other})
    for peer in group_peers:
        pl.semaphore_signal(barrier, inc=1, device_id={"fsdp": peer})
    for step in (1, chips - 1):
        peer = lax.rem(chip + step, chips) * 2 + core
        pl.semaphore_signal(barrier, inc=1, device_id={"ctx": peer})
    pl.semaphore_wait(barrier, groups + 2)

    def send(source, target, sems, device):
        return pltpu.make_async_remote_copy(
            src_ref=source,
            dst_ref=target,
            send_sem=sems[0],
            recv_sem=sems[1],
            device_id=device,
        )

    def line_copy(way, step, piece):
        ref = rows_ref.at[2 * piece + core]
        sems = (line_sem.at[0, way, step], line_sem.at[1, way, step])
        return send(ref, ref, sems, {"ctx": here + (2 if way else -2)})

    def side_copy(piece, lane):
        ref = rows_ref.at[2 * piece + lane]
        return send(ref, ref, (side_sem.at[0, piece], side_sem.at[1, piece]), {"ctx": other})

    def w_copy(peer, source):
        sems = (w_sem.at[0, peer], w_sem.at[1, source])
        return send(gained_ref, wrecv_ref.at[source], sems, {"fsdp": peer})

    def lane_copy(lane):
        ref = wpair_ref.at[lane]
        return send(ref, ref, (lane_sem.at[0], lane_sem.at[1]), {"ctx": other})

    def mlp_copy(peer, source):
        sems = (mlp_sem.at[0, peer], mlp_sem.at[1, source])
        return send(mlp_ref.at[:, core], full_ref.at[:, source, core], sems, {"fsdp": peer})

    def cross_copy(source, lane):
        ref = full_ref.at[:, source, lane]
        sems = (cross_sem.at[0, source], cross_sem.at[1, source])
        return send(ref, ref, sems, {"ctx": other})

    def keep_copy(piece):
        return pltpu.make_async_copy(rows_ref.at[piece], unit_ref.at[piece], keep_sem.at[piece])

    own_copy = pltpu.make_async_copy(mlp_ref, full_ref.at[:, group], own_sem)

    stages = [pltpu.make_async_copy(wqkv_ref, wstage_ref, stage_sem.at[0])] + [
        pltpu.make_async_copy(ref, mstage_ref.at[index], stage_sem.at[index + 1])
        for index, ref in enumerate((wout_ref, wup_ref, wdown_ref))
    ]
    for stage in stages:
        stage.start()
    rows = x_ref[...].astype(f32)
    rows_ref[here] = (rows * rms_scale(rows)).astype(bf16)

    def forward(way, step, piece):
        @pl.when((chip < chips - 1) if way else (chip > 0))
        def _():
            line_copy(way, step, piece).start()

    for way in range(2):
        forward(way, 0, chip)
    side_copy(chip, core).start()
    shift = lax.rem(D - here * width, D)
    stages[0].wait()
    for part in range(3):
        turned = pltpu.roll(wstage_ref[:, part * D : (part + 1) * D], shift, 1)
        gained_ref[part] = (turned[:, :width] * gain_ref[...]).astype(bf16)
    for peer in group_peers:
        w_copy(peer, group).start()
    for index in range(3):
        stages[index + 1].wait()
        mlp_ref[index] = mstage_ref[index].astype(bf16).reshape(mlp_ref.shape[1:])
    own_copy.start()
    keep_copy(here).start()
    wrecv_ref[group] = gained_ref[...]
    for peer in group_peers:
        w_copy(group, peer).wait_recv()
    for peer in group_peers:
        mlp_copy(peer, group).start()
    for part in range(3):
        flipped = wrecv_ref[:, part].reshape(D, width).T
        wflip_ref[part * width : (part + 1) * width] = flipped
    wpair_ref[core] = wflip_ref[...]
    lane_copy(core).start()

    extra_row = lax.broadcasted_iota(jnp.int32, (PAD - HD, BLOCK), 0)
    extra = jnp.where(extra_row < 3, 1.0, 0.0)
    spare = jnp.zeros((PAD - HD, BLOCK), bf16)

    def project(piece):
        def half(index, carry):
            at = pl.ds(pl.multiple_of(index * BLOCK, BLOCK), BLOCK)
            to = pl.ds(pl.multiple_of((piece * 2 + index) * BLOCK, BLOCK), BLOCK)
            result = dot(wflip_ref[...], rows_ref[piece, at, :], (1, 1))
            for head in range(heads):
                query, key, value = (
                    result[part * width + head * HD : part * width + (head + 1) * HD]
                    for part in range(3)
                )
                qt_ref[head, :HD, to] = (query * factor_ref[...]).astype(bf16)
                qt_ref[head, HD:, to] = spare
                kt_ref[head, :, to] = key.astype(bf16)
                vt_ref[head, :HD, to] = value.astype(bf16)
                vt_ref[head, HD:, to] = jnp.ones((EXTRA, BLOCK), bf16)
                kn_ref[head, to, :] = jnp.concatenate([key, extra], axis=0).T.astype(bf16)
                vn_ref[head, to, :] = jnp.concatenate([value, extra], axis=0).T.astype(bf16)
            return carry

        lax.fori_loop(0, TILE // BLOCK, half, 0)

    def visit(distance, carry):
        for way in range(2):
            piece = chip - distance if way else chip + distance
            valid = (piece >= 0) if way else (piece <= chips - 1)

            @pl.when(valid & (distance > 0))
            def _():
                line_copy(way, distance - 1, piece).wait_recv()
                side_copy(piece, core).start()
                forward(way, distance, piece)
                keep_copy(2 * piece + core).start()

        for way in range(2):
            piece = chip - distance if way else chip + distance
            valid = (piece >= 0) if way else ((piece <= chips - 1) & (distance > 0))

            @pl.when(valid)
            def _():
                project(2 * piece + core)
                side_copy(piece, 1 - core).wait_recv()
                keep_copy(2 * piece + 1 - core).start()
                project(2 * piece + 1 - core)

        return carry

    lax.fori_loop(0, chips, visit, 0)

    for peer in group_peers:
        mlp_copy(group, peer).wait_recv()
        cross_copy(peer, core).start()
    for peer in group_peers:
        cross_copy(peer, 1 - core).wait_recv()
        cross_copy(peer, core).wait_send()
        w_copy(peer, group).wait_send()
        mlp_copy(peer, group).wait_send()
    own_copy.wait()
    lane_copy(1 - core).wait_recv()
    lane_copy(core).wait_send()

    def drain(piece, carry):
        keep_copy(2 * piece).wait()
        keep_copy(2 * piece + 1).wait()
        side_copy(piece, core).wait_send()

        @pl.when((piece <= chip) & (chip < chips - 1))
        def _():
            line_copy(1, chip - piece, piece).wait_send()

        @pl.when((piece >= chip) & (chip > 0))
        def _():
            line_copy(0, piece - chip, piece).wait_send()

        return carry

    lax.fori_loop(0, chips, drain, 0)


def gather_rows(parts, groups, heads, rows, w_qkv, gain, w_out, w_up, w_down, factor):
    rows_dev = rows.shape[0]
    held = w_qkv.shape[0]
    tokens = parts * rows_dev
    dma = pltpu.SemaphoreType.DMA
    chips = parts // 2
    anywhere = pl.BlockSpec(memory_space=pl.ANY)
    return pl.pallas_call(
        functools.partial(gather_kernel, parts, groups, heads),
        name="gather_rows",
        out_shape=[
            jax.ShapeDtypeStruct((parts, rows_dev, D), bf16),
            jax.ShapeDtypeStruct((3, groups, 2, held // 2, D), bf16),
            jax.ShapeDtypeStruct((2, 3 * heads * HD, D), bf16),
            jax.ShapeDtypeStruct((heads, PAD, tokens), bf16),
            jax.ShapeDtypeStruct((heads, HD, tokens), bf16),
            jax.ShapeDtypeStruct((heads, HD + EXTRA, tokens), bf16),
            jax.ShapeDtypeStruct((heads, tokens, PAD), bf16),
            jax.ShapeDtypeStruct((heads, tokens, PAD), bf16),
        ],
        in_specs=in_vmem(1) + [anywhere] + in_vmem(1) + [anywhere] * 3 + in_vmem(1),
        out_specs=[anywhere] * 2 + in_vmem(6),
        scratch_shapes=[
            pltpu.VMEM((parts, rows_dev, D), bf16),
            pltpu.VMEM((held, 3 * D), f32),
            pltpu.VMEM((3, held, D), f32),
            pltpu.VMEM((3, held, heads * HD), bf16),
            pltpu.VMEM((3, 2, held // 2, D), bf16),
            pltpu.VMEM((groups, 3, held, heads * HD), bf16),
            pltpu.VMEM((3 * heads * HD, D), bf16),
            dma((2, 2, chips)),
            dma((2, chips)),
            dma((parts,)),
            dma((2, groups)),
            dma((2,)),
            dma((2, groups)),
            dma((2, groups)),
            dma,
            dma((4,)),
        ],
        compiler_params=pltpu.CompilerParams(
            vmem_limit_bytes=60 * 1024 * 1024, collective_id=2, has_side_effects=True
        ),
    )(rows, w_qkv, gain, w_out, w_up, w_down, factor)


def forward_kernel(
    heads,
    slot_ref,
    qt_ref,
    kt_ref,
    kn_ref,
    vt_ref,
    lse_ref,
    ot_ref,
    acc_ref,
    top_ref,
):
    tokens = kn_ref.shape[1]
    num_tiles = tokens // TILE
    prompt_tiles = num_tiles // 2

    def longest(ref):
        def visit(slot, most):
            rows = [ref[head, :HD, block_at(slot)].astype(f32) for head in range(heads)]
            sums = [jnp.sum(row * row, axis=0, keepdims=True) for row in rows]
            return functools.reduce(jnp.maximum, sums, most)

        return jnp.max(lax.fori_loop(0, tokens // BLOCK, visit, jnp.zeros((1, BLOCK), f32)))

    bounded = longest(qt_ref) * longest(kt_ref) <= SCORE_BOUND * SCORE_BOUND

    def run(shifted):
        def query_tile(tile, carry):
            queries = [tile_lanes(qt_ref, head, slot_ref, tile) for head in range(heads)]
            if shifted:
                top_ref[...] = jnp.full(top_ref.shape, -1e30, f32)
            else:
                top_ref[...] = jnp.zeros(top_ref.shape, f32)
            acc_ref[...] = jnp.zeros(acc_ref.shape, f32)

            def step(key_rows, value_lanes, start, masked):
                scores = [dot(key_rows[head], queries[head][:, start:]) for head in range(heads)]
                if masked:
                    allowed = causal(scores[0].shape)
                    scores = [jnp.where(allowed, score, -1e30) for score in scores]
                if shifted:
                    olds = [top_ref[head, :, start:] for head in range(heads)]
                    tops = [
                        jnp.maximum(old, jnp.max(score, axis=0, keepdims=True))
                        for old, score in zip(olds, scores)
                    ]
                    scores = [score - top for score, top in zip(scores, tops)]
                    for head in range(heads):
                        acc_ref[head, :, start:] *= jnp.exp2(olds[head] - tops[head])
                        top_ref[head, :, start:] = tops[head]
                probs = [jnp.exp2(score).astype(bf16) for score in scores]
                for head in range(heads):
                    acc_ref[head, :, start:] += dot(value_lanes[head], probs[head])

            def full(key_tile, inner):
                step(
                    [tile_rows(kn_ref, head, slot_ref, key_tile) for head in range(heads)],
                    [tile_lanes(vt_ref, head, slot_ref, key_tile) for head in range(heads)],
                    0,
                    False,
                )
                return inner

            lax.fori_loop(0, jnp.minimum(tile, prompt_tiles), full, 0)
            for part in range(TILE // BLOCK):
                block = block_at(slot_ref[tile * (TILE // BLOCK) + part])
                step(
                    [kn_ref[head, block, :] for head in range(heads)],
                    [vt_ref[head, :, block] for head in range(heads)],
                    part * BLOCK,
                    True,
                )
            for head in range(heads):
                acc = acc_ref[head]
                mass = acc[HD : HD + 1]
                mixed = (acc[:HD] / mass).astype(bf16)
                lse_ref[head, :, tile_at(tile)] = top_ref[head] + jnp.log2(mass)
                for part in range(TILE // BLOCK):
                    slot = slot_ref[tile * (TILE // BLOCK) + part]
                    ot_ref[slot // 2, head * HD : (head + 1) * HD, half_at(slot)] = mixed[
                        :, part * BLOCK : (part + 1) * BLOCK
                    ]
            return carry

        lax.fori_loop(0, num_tiles, query_tile, 0)

    @pl.when(bounded)
    def _():
        run(False)

    @pl.when(jnp.logical_not(bounded))
    def _():
        run(True)


def backward_kernel(
    heads,
    slot_ref,
    qt_ref,
    kt_ref,
    kn_ref,
    vn_ref,
    lse_ref,
    ot_ref,
    dt_ref,
    factor_ref,
    units_ref,
    dqkv_ref,
    dscale_ref,
    u_ref,
    qa_ref,
    da_ref,
    dq_ref,
    dk_ref,
    dv_ref,
    held_ref,
    total_ref,
    load_sem,
):
    parts = units_ref.shape[0]

    def load(piece):
        slot = lax.rem(piece, 2)
        return pltpu.make_async_copy(units_ref.at[piece], held_ref.at[slot], load_sem.at[slot])

    for piece in range(2):
        load(piece).start()
    tokens = kn_ref.shape[1]
    num_blocks = tokens // BLOCK
    num_tiles = tokens // TILE
    prompt_tiles = num_tiles // 2
    width = heads * HD

    def prepare(block, carry):
        slot = slot_ref[block]
        to = pl.ds(pl.multiple_of(block * BLOCK, BLOCK), BLOCK)
        for head in range(heads):
            rows = slice(head * HD, (head + 1) * HD)
            grad = dt_ref[slot // 2, rows, half_at(slot)]
            mixed = ot_ref[slot // 2, rows, half_at(slot)]
            delta = jnp.sum(grad.astype(f32) * mixed.astype(f32), axis=0, keepdims=True)
            da_ref[head, :HD, to] = grad
            da_ref[head, HD : HD + EXTRA, to] = three_rows(-delta)
            da_ref[head, HD + EXTRA :, to] = jnp.zeros((PAD - HD - EXTRA, BLOCK), bf16)
            qa_ref[head, :HD, to] = qt_ref[head, :HD, block_at(slot)]
            qa_ref[head, HD : HD + EXTRA, to] = three_rows(-lse_ref[head, :, to])
            qa_ref[head, HD + EXTRA :, to] = jnp.zeros((PAD - HD - EXTRA, BLOCK), bf16)
        return carry

    lax.fori_loop(0, num_blocks, prepare, 0)
    dk_ref[...] = jnp.zeros(dk_ref.shape, f32)
    dv_ref[...] = jnp.zeros(dv_ref.shape, f32)
    dscale_ref[...] = jnp.zeros(dscale_ref.shape, f32)

    def query_tile(tile, carry):
        here = tile_at(tile)
        dq_ref[...] = jnp.zeros(dq_ref.shape, f32)

        def step(keys, key_rows, key_lanes, value_rows, start, masked):
            to = pl.ds(pl.multiple_of(tile * TILE + start, BLOCK), TILE - start)
            queries = [qa_ref[head, :, to] for head in range(heads)]
            grads = [da_ref[head, :, to] for head in range(heads)]
            scores = [dot(key_rows[head], queries[head]) for head in range(heads)]
            spreads = [dot(value_rows[head], grads[head]) for head in range(heads)]
            probs = [jnp.exp2(score) for score in scores]
            if masked:
                allowed = causal(scores[0].shape)
                probs = [jnp.where(allowed, prob, 0.0) for prob in probs]
            dscores = [(prob * spread).astype(bf16) for prob, spread in zip(probs, spreads)]
            for head in range(heads):
                dv_ref[head, :, keys] += dot(grads[head][:HD], probs[head].astype(bf16), (1, 1))
                dk_ref[head, :, keys] += dot(queries[head][:HD], dscores[head], (1, 1))
                dq_ref[head, :, start:] += dot(key_lanes[head], dscores[head])

        def full(key_tile, inner):
            step(
                tile_at(key_tile),
                [tile_rows(kn_ref, head, slot_ref, key_tile) for head in range(heads)],
                [tile_lanes(kt_ref, head, slot_ref, key_tile) for head in range(heads)],
                [tile_rows(vn_ref, head, slot_ref, key_tile) for head in range(heads)],
                0,
                False,
            )
            return inner

        lax.fori_loop(0, jnp.minimum(tile, prompt_tiles), full, 0)
        for part in range(TILE // BLOCK):
            position = tile * (TILE // BLOCK) + part
            block = block_at(slot_ref[position])
            step(
                block_at(position),
                [kn_ref[head, block, :] for head in range(heads)],
                [kt_ref[head, :, block] for head in range(heads)],
                [vn_ref[head, block, :] for head in range(heads)],
                part * BLOCK,
                True,
            )
        for head in range(heads):
            dq = dq_ref[head]
            product = dq * qa_ref[head, :HD, here].astype(f32)
            for lane in range(TILE // PAD):
                dscale_ref[head] += product[:, lane * PAD : (lane + 1) * PAD]
            scaled = (dq * (factor_ref[...] * LN2)).astype(bf16)
            for part in range(TILE // BLOCK):
                slot = slot_ref[tile * (TILE // BLOCK) + part]
                dqkv_ref[slot // 2, head * HD : (head + 1) * HD, half_at(slot)] = scaled[
                    :, part * BLOCK : (part + 1) * BLOCK
                ]
        return carry

    lax.fori_loop(0, num_tiles, query_tile, 0)

    def finish(block, carry):
        slot = slot_ref[block]
        owner, to = slot // 2, half_at(slot)
        at = pl.ds(pl.multiple_of(block * BLOCK, BLOCK), BLOCK)
        for head in range(heads):
            row = width + head * HD
            dqkv_ref[owner, row : row + HD, to] = (dk_ref[head, :, at] * LN2).astype(bf16)
            row = 2 * width + head * HD
            dqkv_ref[owner, row : row + HD, to] = dv_ref[head, :, at].astype(bf16)
        return carry

    lax.fori_loop(0, num_blocks, finish, 0)
    total_ref[...] = jnp.zeros(total_ref.shape, f32)

    def project(piece, carry):
        load(piece).wait()
        total_ref[...] += dot(dqkv_ref[piece], held_ref[lax.rem(piece, 2)])

        @pl.when(piece + 2 < parts)
        def _():
            load(piece + 2).start()

        return carry

    lax.fori_loop(0, parts, project, 0)
    u_ref[...] = total_ref[...].T.astype(bf16)


def in_vmem(count):
    return [pl.BlockSpec(memory_space=pltpu.VMEM)] * count


def params():
    return pltpu.CompilerParams(vmem_limit_bytes=60 * 1024 * 1024)


def attention_forward(slots, qt, kt, kn, vt, parts):
    heads, tokens = kn.shape[:2]
    return pl.pallas_call(
        functools.partial(forward_kernel, heads),
        name="attention_forward",
        out_shape=[
            jax.ShapeDtypeStruct((heads, 1, tokens), f32),
            jax.ShapeDtypeStruct((parts, heads * HD, tokens // parts), bf16),
        ],
        in_specs=[pl.BlockSpec(memory_space=pltpu.SMEM)] + in_vmem(4),
        out_specs=in_vmem(2),
        scratch_shapes=[
            pltpu.VMEM((heads, HD + EXTRA, TILE), f32),
            pltpu.VMEM((heads, 1, TILE), f32),
        ],
        compiler_params=params(),
        cost_estimate=attention_cost(heads, tokens, 2),
    )(slots, qt, kt, kn, vt)


def attention_cost(heads, tokens, passes):
    pairs = heads * tokens * tokens // 2
    return pl.CostEstimate(
        flops=2 * passes * pairs * BLOCK, bytes_accessed=tokens * D, transcendentals=pairs
    )


def attention_backward(slots, kept, mixed, dmixed, factor, units):
    qt, kt, kn, vn, lse = kept
    heads, tokens = kn.shape[:2]
    return pl.pallas_call(
        functools.partial(backward_kernel, heads),
        name="attention_backward",
        out_shape=[
            jax.ShapeDtypeStruct((mixed.shape[0], 3 * heads * HD, mixed.shape[2]), bf16),
            jax.ShapeDtypeStruct((heads, HD, PAD), f32),
            jax.ShapeDtypeStruct((D, 3 * heads * HD), bf16),
        ],
        in_specs=[pl.BlockSpec(memory_space=pltpu.SMEM)]
        + in_vmem(8)
        + [pl.BlockSpec(memory_space=pl.ANY)],
        out_specs=in_vmem(3),
        scratch_shapes=[
            pltpu.VMEM((heads, PAD, tokens), bf16),
            pltpu.VMEM((heads, PAD, tokens), bf16),
            pltpu.VMEM((heads, HD, TILE), f32),
            pltpu.VMEM((heads, HD, tokens), f32),
            pltpu.VMEM((heads, HD, tokens), f32),
            pltpu.VMEM((2,) + units.shape[1:], bf16),
            pltpu.VMEM((3 * heads * HD, D), f32),
            pltpu.SemaphoreType.DMA((2,)),
        ],
        compiler_params=params(),
        cost_estimate=attention_cost(heads, tokens, 5),
    )(slots, qt, kt, kn, vn, lse, mixed, dmixed, factor, units)


def middle_kernel(
    parts,
    groups,
    mixed_ref,
    x_ref,
    dy_ref,
    weights_ref,
    gain_ref,
    *refs,
):
    out_ref, dmid_ref, dmixed_ref, gain_grad_ref = refs[:4]
    chunk_refs = refs[4 : 4 + groups]
    (
        w_ref,
        attn_ref,
        dattn_ref,
        act_ref,
        normed_ref,
        dhidden_ref,
        dbranch_ref,
        grad_ref,
        theirs_ref,
        w_sem,
        attn_sem,
        dattn_sem,
        pair_sem,
    ) = refs[4 + groups :]
    here = lax.axis_index("ctx")
    group = lax.axis_index("fsdp")
    core = lax.rem(here, 2)
    other = here + 1 - 2 * core
    peers = [lax.rem(here + step, parts) for step in range(1, parts)]
    tokens = x_ref.shape[0]
    width = mixed_ref.shape[1]
    held = theirs_ref.shape[2]
    loads = [
        pltpu.make_async_copy(weights_ref.at[index], w_ref.at[index], w_sem.at[index])
        for index in range(3)
    ]
    for load in loads:
        load.start()

    barrier = pltpu.get_barrier_semaphore()
    for peer in peers:
        pl.semaphore_signal(barrier, inc=1, device_id={"ctx": peer})
    pl.semaphore_wait(barrier, parts - 1)

    def lanes(part):
        return pl.ds(pl.multiple_of(part * BLOCK, BLOCK), BLOCK)

    def attn_copy(part, peer, source):
        return pltpu.make_async_remote_copy(
            src_ref=mixed_ref.at[peer, :, lanes(part)],
            dst_ref=attn_ref.at[source, :, lanes(part)],
            send_sem=attn_sem.at[0, part, peer],
            recv_sem=attn_sem.at[1, part, source],
            device_id={"ctx": peer},
        )

    def dattn_copy(part, peer, source):
        return pltpu.make_async_remote_copy(
            src_ref=dattn_ref.at[peer, :, lanes(part)],
            dst_ref=dmixed_ref.at[source, :, lanes(part)],
            send_sem=dattn_sem.at[0, part, peer],
            recv_sem=dattn_sem.at[1, part, source],
            device_id={"ctx": peer},
        )

    def rows_of(owner, lane):
        start = pl.multiple_of((owner * 2 + lane) * held, 16)
        return pl.ds(start, held)

    def pair_copy(index, owner, lane):
        return pltpu.make_async_remote_copy(
            src_ref=grad_ref.at[index, rows_of(owner, lane), :],
            dst_ref=theirs_ref.at[index, owner],
            send_sem=pair_sem.at[0, index, owner],
            recv_sem=pair_sem.at[1, index, owner],
            device_id={"ctx": other},
        )

    for part in range(tokens // BLOCK):
        for peer in peers:
            attn_copy(part, peer, here).start()
    attn_ref[here] = mixed_ref[here]
    gain_grad_ref[...] = jnp.zeros(gain_grad_ref.shape, f32)
    for load in loads:
        load.wait()
    gain = gain_ref[...]

    def layer(part, carry):
        rows = lanes(part)
        for peer in peers:
            attn_copy(part, here, peer).wait_recv()
        attn = attn_ref[:, :, rows].reshape(D, BLOCK)
        mid = x_ref[rows, :].astype(f32) + dot(attn, w_ref[0], (0, 0))
        scale = rms_scale(mid)
        unit = mid * scale
        normed = (unit * gain).astype(bf16)
        normed_ref[rows, :] = normed
        hidden = dot(normed, w_ref[1])
        gate = jax.nn.sigmoid(hidden)
        act = (hidden * gate).astype(bf16)
        act_ref[rows, :] = act
        dy = dy_ref[rows, :]
        dact = dot(dy, w_ref[2], (1, 1))
        dhidden = (dact * gate * (1.0 + hidden * (1.0 - gate))).astype(bf16)
        dhidden_ref[rows, :] = dhidden
        dnormed = dot(dhidden, w_ref[1], (1, 1))
        dunit = dnormed * gain
        dmid = dy.astype(f32) + scale * (
            dunit - unit * jnp.mean(dunit * unit, axis=-1, keepdims=True)
        )
        dmid_ref[rows, :] = dmid
        dbranch = dmid.astype(bf16)
        dbranch_ref[rows, :] = dbranch
        dattn = dot(w_ref[0], dbranch, (1, 1)).astype(bf16).reshape(parts, width, BLOCK)
        dattn_ref[:, :, rows] = dattn
        for peer in peers:
            dattn_copy(part, peer, here).start()
        dmixed_ref[here, :, rows] = dattn_ref[here, :, rows]
        out_ref[rows, :] = (mid + dot(act, w_ref[2])).astype(bf16)
        gain_grad_ref[...] += jnp.sum(dnormed * unit, axis=0, keepdims=True)
        return carry

    lax.fori_loop(0, tokens // BLOCK, layer, 0)

    def down_rows(index, carry):
        rows = lanes(index)
        grad_ref[2, rows, :] = dot(act_ref[:, rows], dy_ref[...], (0, 0)).astype(bf16)
        return carry

    def up_rows(index, carry):
        rows = lanes(index)
        grad_ref[1, rows, :] = dot(normed_ref[:, rows], dhidden_ref[...], (0, 0)).astype(bf16)
        return carry

    def out_rows(index, carry):
        rows = pl.ds(pl.multiple_of(index * width, 16), width)
        grad_ref[0, rows, :] = dot(attn_ref[index], dbranch_ref[...]).astype(bf16)
        return carry

    for index, count, run in (
        (2, D // BLOCK, down_rows),
        (1, D // BLOCK, up_rows),
        (0, parts, out_rows),
    ):
        lax.fori_loop(0, count, run, 0)
        for owner in range(groups):
            pair_copy(index, owner, 1 - core).start()
    for step in range(groups):
        owner = group ^ step
        for index in (2, 1, 0):
            pair_copy(index, owner, core).wait_recv()
            chunk_refs[step][index] = (
                grad_ref[index, rows_of(owner, core), :].astype(f32)
                + theirs_ref[index, owner].astype(f32)
            ).astype(bf16)
    for part in range(tokens // BLOCK):
        for peer in peers:
            dattn_copy(part, here, peer).wait_recv()
            dattn_copy(part, peer, here).wait_send()
            attn_copy(part, peer, here).wait_send()
    for index in range(3):
        for owner in range(groups):
            pair_copy(index, owner, 1 - core).wait_send()


def middle(parts, groups, mixed, rows, cotangent, weights, gain):
    rows_dev = rows.shape[0]
    half = D // groups // 2
    dma = pltpu.SemaphoreType.DMA
    halves = rows_dev // BLOCK
    return pl.pallas_call(
        functools.partial(middle_kernel, parts, groups),
        name="middle",
        out_shape=[
            jax.ShapeDtypeStruct((rows_dev, D), bf16),
            jax.ShapeDtypeStruct((rows_dev, D), f32),
            jax.ShapeDtypeStruct(mixed.shape, bf16),
            jax.ShapeDtypeStruct((1, D), f32),
        ]
        + [jax.ShapeDtypeStruct((3, half, D), bf16)] * groups,
        in_specs=in_vmem(3) + [pl.BlockSpec(memory_space=pl.ANY)] + in_vmem(1),
        out_specs=in_vmem(4 + groups),
        scratch_shapes=[
            pltpu.VMEM((3, D, D), bf16),
            pltpu.VMEM(mixed.shape, bf16),
            pltpu.VMEM(mixed.shape, bf16),
            pltpu.VMEM((rows_dev, D), bf16),
            pltpu.VMEM((rows_dev, D), bf16),
            pltpu.VMEM((rows_dev, D), bf16),
            pltpu.VMEM((rows_dev, D), bf16),
            pltpu.VMEM((3, D, D), bf16),
            pltpu.VMEM((3, groups, half, D), bf16),
            dma((3,)),
            dma((2, halves, parts)),
            dma((2, halves, parts)),
            dma((2, 3, groups)),
        ],
        compiler_params=pltpu.CompilerParams(
            vmem_limit_bytes=60 * 1024 * 1024, collective_id=3, has_side_effects=True
        ),
    )(mixed, rows, cotangent, weights, gain)


def reduce_kernel(
    parts,
    groups,
    dq_ref,
    wt_ref,
    u_ref,
    wc_ref,
    mlp_ref,
    small_ref,
    down_ref,
    up_ref,
    own_ref,
    ugather_ref,
    mgather_ref,
    sgather_ref,
    pair_ref,
    sum_ref,
    urecv_ref,
    mrecv_ref,
    part_ref,
    column_ref,
    smine_ref,
    srecv_ref,
    pair_sem,
    sum_sem,
    u_sem,
    m_sem,
    line_sem,
    side_sem,
    small_sem,
    cross_sem,
):
    chips = parts // 2
    here = lax.axis_index("ctx")
    group = lax.axis_index("fsdp")
    core = lax.rem(here, 2)
    chip = here // 2
    other = here + 1 - 2 * core
    ctx_peers = [lax.rem(here + step, parts) for step in range(1, parts)]
    chip_peers = [lax.rem(chip + step, chips) for step in range(1, chips)]
    group_peers = [lax.rem(group + step, groups) for step in range(1, groups)]

    barrier = pltpu.get_barrier_semaphore()
    for peer in ctx_peers:
        pl.semaphore_signal(barrier, inc=1, device_id={"ctx": peer})
    for peer in group_peers:
        pl.semaphore_signal(barrier, inc=1, device_id={"fsdp": peer})
    pl.semaphore_wait(barrier, parts + groups - 2)

    def send(source, target, sems, device):
        return pltpu.make_async_remote_copy(
            src_ref=source,
            dst_ref=target,
            send_sem=sems[0],
            recv_sem=sems[1],
            device_id=device,
        )

    def pair_copy(index):
        return send(
            dq_ref.at[index, 1 - core],
            pair_ref.at[index],
            (pair_sem.at[0, index], pair_sem.at[1, index]),
            {"ctx": other},
        )

    def u_copy(peer, source):
        return send(
            u_ref.at[peer],
            urecv_ref.at[source],
            (u_sem.at[0, peer], u_sem.at[1, source]),
            {"fsdp": peer},
        )

    def m_copy(peer, source):
        return send(
            mlp_ref.at[peer],
            mrecv_ref.at[source],
            (m_sem.at[0, peer], m_sem.at[1, source]),
            {"ctx": 2 * peer + core},
        )

    for index in range(chips):
        pair_copy(index).start()
    for peer in group_peers:
        u_copy(peer, group).start()
    for peer in chip_peers:
        m_copy(peer, chip).start()
    for index in range(chips):
        pair_copy(index).wait_recv()

    rows_half = own_ref.shape[0] // 2

    def partial(target):
        def half(index, carry):
            rows = pl.ds(pl.multiple_of(index * rows_half, rows_half), rows_half)
            part_ref[rows, :] = dot(dq_ref[target, core, :, rows], wt_ref[core], (0, 0)) + dot(
                pair_ref[target, :, rows], wt_ref[1 - core], (0, 0)
            )
            return carry

        lax.fori_loop(0, 2, half, 0)

    def sum_copy(way, target):
        return send(
            sum_ref.at[way, target],
            sum_ref.at[way, target],
            (sum_sem.at[0, way, target], sum_sem.at[1, way, target]),
            {"ctx": here + (2 if way else -2)},
        )

    def reduce_step(step):
        last = step == chips - 2
        for way, target, active, first, out_ref in (
            (0, step - (chips - 1) + chip, step >= chips - 1 - chip, chip == chips - 1, down_ref),
            (1, chips - 1 - step + chip, step >= chip, chip == 0, up_ref),
        ):

            @pl.when(active)
            def _():
                partial(target)

                @pl.when(first)
                def _():
                    sum_ref[way, target] = part_ref[...].astype(bf16)

                @pl.when(jnp.logical_not(first))
                def _():
                    sum_copy(way, target).wait_recv()
                    sum_ref[way, target] = (
                        part_ref[...] + sum_ref[way, target].astype(f32)
                    ).astype(bf16)

                if last:
                    out_ref[...] = sum_ref[way, target]
                else:
                    sum_copy(way, target).start()

            if last:

                @pl.when(jnp.logical_not(active))
                def _():
                    out_ref[...] = jnp.zeros(out_ref.shape, bf16)

    gathers = (ugather_ref, mgather_ref)

    def line_copy(which, way, step, piece):
        ref = gathers[which].at[2 * piece + core]
        sems = (line_sem.at[0, which, way, step], line_sem.at[1, which, way, step])
        return send(ref, ref, sems, {"ctx": here + (2 if way else -2)})

    def side_copy(which, piece, lane):
        ref = gathers[which].at[2 * piece + lane]
        sems = (side_sem.at[0, which, piece], side_sem.at[1, which, piece])
        return send(ref, ref, sems, {"ctx": other})

    def line_sends(which, step, go):
        @pl.when((chip < chips - 1) & (chip - step >= 0))
        def _():
            go(line_copy(which, 1, step, chip - step))

        @pl.when((chip > 0) & (chip + step <= chips - 1))
        def _():
            go(line_copy(which, 0, step, chip + step))

    def line_receive(which, step):
        @pl.when(chip - 1 - step >= 0)
        def _():
            line_copy(which, 1, step, chip - 1 - step).wait_recv()
            side_copy(which, chip - 1 - step, core).start()

        @pl.when(chip + 1 + step <= chips - 1)
        def _():
            line_copy(which, 0, step, chip + 1 + step).wait_recv()
            side_copy(which, chip + 1 + step, core).start()

    def small_copy(peer, source):
        return send(
            smine_ref,
            srecv_ref.at[source],
            (small_sem.at[0, peer], small_sem.at[1, source]),
            {"ctx": peer},
        )

    def cross_copy(peer, source):
        return send(
            sgather_ref.at[group],
            sgather_ref.at[source],
            (cross_sem.at[0, peer], cross_sem.at[1, source]),
            {"fsdp": peer},
        )

    reduce_step(0)

    total = u_ref[group].astype(f32)
    for peer in group_peers:
        u_copy(group, peer).wait_recv()
        total = total + urecv_ref[peer].astype(f32)
    ugather_ref[here] = total.astype(bf16)
    side_copy(0, chip, core).start()
    line_sends(0, 0, lambda copy: copy.start())
    held = total.shape[0]
    gain = jnp.sum(total * wc_ref[...].astype(f32), axis=1, keepdims=True)
    column_ref[...] = jnp.zeros(column_ref.shape, f32)
    column_ref[:held, :] = jnp.broadcast_to(gain, (held, PAD))
    flat = column_ref[...].T[:1]
    smine_ref[...] = small_ref[...]
    for row in range(column_ref.shape[0] // PAD):
        smine_ref[row : row + 1, :] = flat[:, row * PAD : (row + 1) * PAD]
    for peer in ctx_peers:
        small_copy(peer, here).start()

    total = mlp_ref[chip].astype(f32)
    for peer in chip_peers:
        m_copy(chip, peer).wait_recv()
        total = total + mrecv_ref[peer].astype(f32)
    mgather_ref[here] = total.astype(bf16)
    side_copy(1, chip, core).start()
    line_sends(1, 0, lambda copy: copy.start())

    for step in range(1, chips):
        if step <= chips - 2:
            reduce_step(step)
        for which in range(2):
            line_receive(which, step - 1)
            if step <= chips - 2:
                line_sends(which, step, lambda copy: copy.start())
        if step == 1:
            small = smine_ref[...]
            for peer in ctx_peers:
                small_copy(here, peer).wait_recv()
                small = small + srecv_ref[peer]
            sgather_ref[group] = small
            for peer in group_peers:
                cross_copy(peer, group).start()

    partial(chip)
    own_ref[...] = part_ref[...]

    for which in range(2):
        for piece in range(chips):
            side_copy(which, piece, 1 - core).wait_recv()
            side_copy(which, piece, core).wait_send()
        for step in range(chips - 1):
            line_sends(which, step, lambda copy: copy.wait_send())
    for index in range(chips):
        pair_copy(index).wait_send()
    for peer in group_peers:
        cross_copy(group, peer).wait_recv()
        cross_copy(peer, group).wait_send()
        u_copy(peer, group).wait_send()
    for peer in chip_peers:
        m_copy(peer, chip).wait_send()
    for peer in ctx_peers:
        small_copy(peer, here).wait_send()
    for step in range(chips - 2):

        @pl.when(step >= chips - 1 - chip)
        def _():
            sum_copy(0, step - (chips - 1) + chip).wait_send()

        @pl.when(step >= chip)
        def _():
            sum_copy(1, chips - 1 - step + chip).wait_send()


def reduce_gradients(parts, groups, dqkv, w_pair, u_parts, w_columns, mlp, small):
    chips = parts // 2
    rows_dev = dqkv.shape[3]
    rows, width = w_columns.shape
    lanes = -(-rows // PAD) * PAD
    dma = pltpu.SemaphoreType.DMA
    return pl.pallas_call(
        functools.partial(reduce_kernel, parts, groups),
        name="reduce_gradients",
        out_shape=[
            jax.ShapeDtypeStruct((rows_dev, D), bf16),
            jax.ShapeDtypeStruct((rows_dev, D), bf16),
            jax.ShapeDtypeStruct((rows_dev, D), f32),
            jax.ShapeDtypeStruct((parts, rows, width), bf16),
            jax.ShapeDtypeStruct((parts,) + mlp.shape[1:], bf16),
            jax.ShapeDtypeStruct((groups,) + small.shape, f32),
        ],
        in_specs=in_vmem(6),
        out_specs=in_vmem(6),
        scratch_shapes=[
            pltpu.VMEM((chips,) + dqkv.shape[2:], bf16),
            pltpu.VMEM((2, chips, rows_dev, D), bf16),
            pltpu.VMEM(u_parts.shape, bf16),
            pltpu.VMEM(mlp.shape, bf16),
            pltpu.VMEM((rows_dev, D), f32),
            pltpu.VMEM((lanes, PAD), f32),
            pltpu.VMEM(small.shape, f32),
            pltpu.VMEM((parts,) + small.shape, f32),
            dma((2, chips)),
            dma((2, 2, chips)),
            dma((2, groups)),
            dma((2, chips)),
            dma((2, 2, 2, chips)),
            dma((2, 2, chips)),
            dma((2, parts)),
            dma((2, groups)),
        ],
        compiler_params=pltpu.CompilerParams(
            vmem_limit_bytes=60 * 1024 * 1024, collective_id=1, has_side_effects=True
        ),
    )(dqkv, w_pair, u_parts, w_columns, mlp, small)


def update_kernel(rates, qkv_ref, gain_ref, mlp_ref, *refs):
    sets = len(rates)
    parts, rows, width = qkv_ref.shape
    width = width // 3
    for index, rate in enumerate(rates):
        weight, first, second = (ref[...] for ref in refs[3 * index : 3 * index + 3])
        if index == 0:
            pieces = [qkv_ref[part].astype(f32) for part in range(parts)]
            gradient = jnp.concatenate(
                [piece[:, at * width : (at + 1) * width] for at in range(3) for piece in pieces],
                axis=1,
            )
            gradient = gradient * gain_ref[...]
        else:
            gradient = mlp_ref[0, index - 1].astype(f32)
        outs = refs[3 * sets + 4 * index : 3 * sets + 4 * index + 4]
        new, first, second = adamw(weight, first, second, gradient, rate, decay_rate)
        outs[0][...] = new
        outs[1][...] = first
        outs[2][...] = second
        outs[3][...] = new.astype(bf16)


def update(rates, parts, qkv, gain, mlp, *arrays):
    rows = arrays[0].shape[0]
    chips = parts // 2
    step_rows = rows // parts
    if step_rows % 8 == 0:

        def owner(i):
            return (2 * lax.rem(i, chips) + i // chips, 0, 0, 0)

    else:
        step_rows = 32
        mlp = mlp.reshape(chips, 2, 3, rows // parts, D).transpose(2, 1, 0, 3, 4)
        mlp = mlp.reshape(3, rows // step_rows, step_rows, D).transpose(1, 0, 2, 3)

        def owner(i):
            return (i, 0, 0, 0)

    in_specs = [
        pl.BlockSpec((parts, step_rows, qkv.shape[2]), lambda i: (0, i, 0)),
        pl.BlockSpec((step_rows, 1), lambda i: (i, 0)),
        pl.BlockSpec((1, 3, step_rows, D), owner),
    ]
    specs, shapes, moved = [], [], 0
    for array in arrays:
        in_specs.append(pl.BlockSpec((step_rows, array.shape[1]), lambda i: (i, 0)))
    for index in range(len(rates)):
        shape = arrays[3 * index].shape
        shapes += [jax.ShapeDtypeStruct(shape, f32)] * 3 + [jax.ShapeDtypeStruct(shape, bf16)]
        specs += [pl.BlockSpec((step_rows, shape[1]), lambda i: (i, 0))] * 4
        moved += shape[0] * shape[1] * 28
    return pl.pallas_call(
        functools.partial(update_kernel, rates),
        name="update_weights",
        grid=(rows // step_rows,),
        in_specs=in_specs,
        out_specs=specs,
        out_shape=shapes,
        compiler_params=params(),
        cost_estimate=pl.CostEstimate(flops=moved, bytes_accessed=moved, transcendentals=0),
    )(qkv, gain, mlp, *arrays)


def body(
    parts,
    groups,
    inputs,
    cotangent,
    block_order,
    w_qkv,
    m_qkv,
    v_qkv,
    w_out,
    m_out,
    v_out,
    w_up,
    m_up,
    v_up,
    w_down,
    m_down,
    v_down,
    small_params,
    small_m,
    small_v,
):
    heads = H // parts
    width = heads * HD
    rows_dev = inputs.shape[1]
    tokens = rows_dev * parts
    here = lax.axis_index("ctx")
    index = jnp.arange(block_order.shape[1], dtype=jnp.int32)
    slots = jnp.sum(jnp.where(block_order[0][None] == index[:, None], index[None], 0), axis=1)
    gain_one = small_params[:D]
    gain_two = small_params[D : 2 * D]
    query_scale = small_params[2 * D :]
    group = lax.axis_index("fsdp")
    rows = w_qkv.shape[0]

    def head_columns(owner):
        return jnp.concatenate(
            [
                lax.dynamic_slice_in_dim(w_qkv, part * D + owner * width, width, 1)
                for part in range(3)
            ],
            axis=1,
        )

    gain_rows = lax.dynamic_slice_in_dim(gain_one, group * rows, rows, 0)[:, None]
    w_columns = head_columns(here).astype(bf16)
    layer_in = inputs[0].astype(f32)
    scale_one = rms_scale(layer_in)
    unit_one = layer_in * scale_one
    factor = scale_base / math.sqrt(HD) * jax.nn.softplus(query_scale)
    factor_two = (factor * LOG2E)[:, None]
    unit_all, mlp_full, w_pair, qt, kt, vt, kn, vn = gather_rows(
        parts, groups, heads, inputs[0], w_qkv, gain_rows, w_out, w_up, w_down, factor_two
    )
    lse, mixed = attention_forward(slots, qt, kt, kn, vt, parts)
    kept = (qt, kt, kn, vn, lse)
    output, dmid, dmixed, gain_two_grad, *chunks = middle(
        parts,
        groups,
        mixed,
        inputs[0],
        cotangent[0],
        mlp_full.reshape(3, D, D),
        gain_two[None],
    )
    mlp_sum = chunks[0].astype(f32)
    for step in range(1, groups):
        swap = [(i, i ^ step) for i in range(groups)]
        mlp_sum = mlp_sum + lax.ppermute(chunks[step], "fsdp", swap).astype(f32)
    mlp_part = (
        mlp_sum.astype(bf16).reshape(3, parts // 2, rows // parts, D).transpose(1, 0, 2, 3)
    )
    dqkv, dscale, u_parts = attention_backward(slots, kept, mixed, dmixed, factor_two, unit_all)
    u_parts = u_parts.reshape(groups, rows, 3 * width)
    scale_grad = (
        jnp.sum(dscale, axis=(0, 2))
        / factor_two[:, 0]
        * (scale_base / math.sqrt(HD))
        * jax.nn.sigmoid(query_scale)
    )
    lanes = -(-rows // PAD) * PAD
    small_rows = -(-(lanes + D + PAD) // (8 * PAD)) * 8
    small = jnp.concatenate([jnp.zeros((lanes,), f32), gain_two_grad[0], scale_grad])
    small = jnp.pad(small, (0, small_rows * PAD - small.shape[0])).reshape(small_rows, PAD)
    send_down, send_up, own_part, u_all, mlp_all, small_all = reduce_gradients(
        parts,
        groups,
        dqkv.reshape(parts // 2, 2, 3 * width, rows_dev),
        w_pair,
        u_parts,
        w_columns,
        mlp_part,
        small,
    )
    got_down = lax.ppermute(send_down, "ctx", [(i, i - 2) for i in range(2, parts)])
    got_up = lax.ppermute(send_up, "ctx", [(i, i + 2) for i in range(parts - 2)])
    rate_qkv = qkv_rate_base / math.sqrt(D)
    rate_out = 0.5 / math.sqrt(max(D // 256, 1))
    rate_up = 0.5 / math.sqrt(D)
    rate_down = 0.5 / math.sqrt(FF)
    updated = update(
        (rate_qkv, rate_out, rate_up, rate_down),
        parts,
        u_all,
        gain_rows,
        mlp_all,
        w_qkv,
        m_qkv,
        v_qkv,
        w_out,
        m_out,
        v_out,
        w_up,
        m_up,
        v_up,
        w_down,
        m_down,
        v_down,
    )
    flat = small_all.reshape(groups, small_rows * PAD)
    rest = jnp.sum(flat[:, lanes : lanes + D + HD], axis=0)
    small_total = jnp.concatenate([flat[:, :rows].reshape(D), rest])
    small_set = adamw(small_params, small_m, small_v, small_total, small_rate, 0.0)
    dunit_one = own_part + got_down.astype(f32) + got_up.astype(f32)
    input_grad = dmid + scale_one * (
        dunit_one - unit_one * jnp.mean(dunit_one * unit_one, axis=-1, keepdims=True)
    )
    return (
        output[None],
        input_grad.astype(bf16)[None],
        *updated,
        *small_set,
    )


def solution(mesh):
    rows = P("fsdp", "ctx", None)
    weight = P("fsdp", None)
    return jax.shard_map(
        functools.partial(body, mesh.shape["ctx"], mesh.shape["fsdp"]),
        mesh=mesh,
        in_specs=(rows, rows, weight) + (weight,) * 12 + (P(),) * 3,
        out_specs=(rows, rows) + (weight,) * 16 + (P(),) * 3,
        check_vma=False,
    )
```

```python
import functools
import math

import jax
import jax.numpy as jnp
from jax import lax
from jax.experimental import pallas as pl
from jax.experimental.pallas import tpu as pltpu
from jax.sharding import PartitionSpec as P

D = 1280
H = 16
HD = 80
FF = 1280
BLOCK = 256
CONT = 512
STEP = 3
PAD = 128
EXTRA = 16
TILE = CONT
SCORE_BOUND = 96.0

bf16 = jnp.bfloat16
f32 = jnp.float32

norm_eps = 1e-06
beta_one = 0.5
beta_two = 0.5
adam_eps = 1e-08
decay_rate = 0.1
small_rate = 0.75
qkv_rate_base = 1.0
scale_base = 1.442695
LOG2E = math.log2(math.e)
LN2 = math.log(2.0)


def rms_scale(values):
    return lax.rsqrt(jnp.mean(values * values, axis=-1, keepdims=True) + norm_eps)


def adamw(weight, first, second, gradient, step_rate, decay_on):
    first_new = beta_one * first + (1.0 - beta_one) * gradient
    second_new = beta_two * second + (1.0 - beta_two) * gradient * gradient
    corr_one = 1.0 - beta_one**STEP
    corr_two = 1.0 - beta_two**STEP
    update = first_new / corr_one / (jnp.sqrt(second_new / corr_two) + adam_eps)
    weight_new = weight - step_rate * (update + decay_on * weight)
    return (weight_new, first_new, second_new)


def dot(left, right, contract=(1, 0)):
    return lax.dot_general(
        left, right, (((contract[0],), (contract[1],)), ((), ())), preferred_element_type=f32
    )


def three_rows(row):
    high = row.astype(bf16)
    rest = row - high.astype(f32)
    middle = rest.astype(bf16)
    low = (rest - middle.astype(f32)).astype(bf16)
    index = lax.broadcasted_iota(jnp.int32, (EXTRA, row.shape[1]), 0)
    zero = jnp.zeros((EXTRA, row.shape[1]), f32)
    rows = jnp.where(index == 0, high.astype(f32), zero)
    rows = jnp.where(index == 1, middle.astype(f32), rows)
    rows = jnp.where(index == 2, low.astype(f32), rows)
    return rows.astype(bf16)


def tile_at(tile):
    return pl.ds(pl.multiple_of(tile * TILE, TILE), TILE)


def block_at(slot):
    return pl.ds(pl.multiple_of(slot * BLOCK, BLOCK), BLOCK)


def tile_lanes(ref, head, slot_ref, tile, rows=slice(None)):
    first, second = slot_ref[2 * tile], slot_ref[2 * tile + 1]
    return jnp.concatenate(
        [ref[head, rows, block_at(first)], ref[head, rows, block_at(second)]], axis=1
    )


def tile_rows(ref, head, slot_ref, tile):
    first, second = slot_ref[2 * tile], slot_ref[2 * tile + 1]
    return jnp.concatenate([ref[head, block_at(first), :], ref[head, block_at(second), :]], axis=0)


def half_at(slot):
    return pl.ds(pl.multiple_of(lax.rem(slot, 2) * BLOCK, BLOCK), BLOCK)


def causal(shape):
    key = lax.broadcasted_iota(jnp.int32, shape, 0)
    query = lax.broadcasted_iota(jnp.int32, shape, 1)
    return key <= query


def gather_kernel(
    parts,
    groups,
    heads,
    x_ref,
    wqkv_ref,
    gain_ref,
    wout_ref,
    wup_ref,
    wdown_ref,
    factor_ref,
    unit_ref,
    full_ref,
    wpair_ref,
    qt_ref,
    kt_ref,
    vt_ref,
    kn_ref,
    vn_ref,
    wcol_ref,
    rows_ref,
    wstage_ref,
    mstage_ref,
    gained_ref,
    mlp_ref,
    wrecv_ref,
    wflip_ref,
    line_sem,
    side_sem,
    keep_sem,
    w_sem,
    lane_sem,
    mlp_sem,
    cross_sem,
    own_sem,
    stage_sem,
):
    chips = parts // 2
    here = lax.axis_index("ctx")
    group = lax.axis_index("fsdp")
    core = lax.rem(here, 2)
    chip = here // 2
    other = here + 1 - 2 * core
    width = heads * HD
    group_peers = [lax.rem(group + step, groups) for step in range(1, groups)]

    barrier = pltpu.get_barrier_semaphore()
    pl.semaphore_signal(barrier, inc=1, device_id={"ctx": other})
    for peer in group_peers:
        pl.semaphore_signal(barrier, inc=1, device_id={"fsdp": peer})
    for step in (1, chips - 1):
        peer = lax.rem(chip + step, chips) * 2 + core
        pl.semaphore_signal(barrier, inc=1, device_id={"ctx": peer})
    pl.semaphore_wait(barrier, groups + 2)

    def send(source, target, sems, device):
        return pltpu.make_async_remote_copy(
            src_ref=source,
            dst_ref=target,
            send_sem=sems[0],
            recv_sem=sems[1],
            device_id=device,
        )

    def line_copy(way, step, piece):
        ref = rows_ref.at[2 * piece + core]
        sems = (line_sem.at[0, way, step], line_sem.at[1, way, step])
        return send(ref, ref, sems, {"ctx": here + (2 if way else -2)})

    def side_copy(piece, lane):
        ref = rows_ref.at[2 * piece + lane]
        return send(ref, ref, (side_sem.at[0, piece], side_sem.at[1, piece]), {"ctx": other})

    def w_copy(peer, source):
        sems = (w_sem.at[0, peer], w_sem.at[1, source])
        return send(gained_ref, wrecv_ref.at[source], sems, {"fsdp": peer})

    def lane_copy(lane):
        ref = wpair_ref.at[lane]
        return send(ref, ref, (lane_sem.at[0], lane_sem.at[1]), {"ctx": other})

    def mlp_copy(peer, source):
        sems = (mlp_sem.at[0, peer], mlp_sem.at[1, source])
        return send(mlp_ref.at[:, core], full_ref.at[:, source, core], sems, {"fsdp": peer})

    def cross_copy(source, lane):
        ref = full_ref.at[:, source, lane]
        sems = (cross_sem.at[0, source], cross_sem.at[1, source])
        return send(ref, ref, sems, {"ctx": other})

    def keep_copy(piece):
        return pltpu.make_async_copy(rows_ref.at[piece], unit_ref.at[piece], keep_sem.at[piece])

    own_copy = pltpu.make_async_copy(mlp_ref, full_ref.at[:, group], own_sem)

    stages = [pltpu.make_async_copy(wqkv_ref, wstage_ref, stage_sem.at[0])] + [
        pltpu.make_async_copy(ref, mstage_ref.at[index], stage_sem.at[index + 1])
        for index, ref in enumerate((wout_ref, wup_ref, wdown_ref))
    ]
    for stage in stages:
        stage.start()
    rows = x_ref[...].astype(f32)
    rows_ref[here] = (rows * rms_scale(rows)).astype(bf16)

    def forward(way, step, piece):
        @pl.when((chip < chips - 1) if way else (chip > 0))
        def _():
            line_copy(way, step, piece).start()

    for way in range(2):
        forward(way, 0, chip)
    side_copy(chip, core).start()
    shift = lax.rem(D - here * width, D)
    stages[0].wait()
    for part in range(3):
        turned = pltpu.roll(wstage_ref[:, part * D : (part + 1) * D], shift, 1)
        gained_ref[part] = (turned[:, :width] * gain_ref[...]).astype(bf16)
        wcol_ref[:, part * width : (part + 1) * width] = turned[:, :width].astype(bf16)
    for peer in group_peers:
        w_copy(peer, group).start()
    for index in range(3):
        stages[index + 1].wait()
        mlp_ref[index] = mstage_ref[index].astype(bf16).reshape(mlp_ref.shape[1:])
    own_copy.start()
    keep_copy(here).start()
    wrecv_ref[group] = gained_ref[...]
    for peer in group_peers:
        w_copy(group, peer).wait_recv()
    for peer in group_peers:
        mlp_copy(peer, group).start()
    for part in range(3):
        flipped = wrecv_ref[:, part].reshape(D, width).T
        wflip_ref[part * width : (part + 1) * width] = flipped
    wpair_ref[core] = wflip_ref[...]
    lane_copy(core).start()

    extra_row = lax.broadcasted_iota(jnp.int32, (PAD - HD, BLOCK), 0)
    extra = jnp.where(extra_row < 3, 1.0, 0.0)
    spare = jnp.zeros((PAD - HD, BLOCK), bf16)

    def project(piece):
        def half(index, carry):
            at = pl.ds(pl.multiple_of(index * BLOCK, BLOCK), BLOCK)
            to = pl.ds(pl.multiple_of((piece * 2 + index) * BLOCK, BLOCK), BLOCK)
            result = dot(wflip_ref[...], rows_ref[piece, at, :], (1, 1))
            for head in range(heads):
                query, key, value = (
                    result[part * width + head * HD : part * width + (head + 1) * HD]
                    for part in range(3)
                )
                qt_ref[head, :HD, to] = (query * factor_ref[...]).astype(bf16)
                qt_ref[head, HD:, to] = spare
                kt_ref[head, :, to] = key.astype(bf16)
                vt_ref[head, :HD, to] = value.astype(bf16)
                vt_ref[head, HD:, to] = jnp.ones((EXTRA, BLOCK), bf16)
                kn_ref[head, to, :] = jnp.concatenate([key, extra], axis=0).T.astype(bf16)
                vn_ref[head, to, :] = jnp.concatenate([value, extra], axis=0).T.astype(bf16)
            return carry

        lax.fori_loop(0, TILE // BLOCK, half, 0)

    def visit(distance, carry):
        for way in range(2):
            piece = chip - distance if way else chip + distance
            valid = (piece >= 0) if way else (piece <= chips - 1)

            @pl.when(valid & (distance > 0))
            def _():
                line_copy(way, distance - 1, piece).wait_recv()
                side_copy(piece, core).start()
                forward(way, distance, piece)
                keep_copy(2 * piece + core).start()

        for way in range(2):
            piece = chip - distance if way else chip + distance
            valid = (piece >= 0) if way else ((piece <= chips - 1) & (distance > 0))

            @pl.when(valid)
            def _():
                project(2 * piece + core)
                side_copy(piece, 1 - core).wait_recv()
                keep_copy(2 * piece + 1 - core).start()
                project(2 * piece + 1 - core)

        return carry

    lax.fori_loop(0, chips, visit, 0)

    for peer in group_peers:
        mlp_copy(group, peer).wait_recv()
        cross_copy(peer, core).start()
    for peer in group_peers:
        cross_copy(peer, 1 - core).wait_recv()
        cross_copy(peer, core).wait_send()
        w_copy(peer, group).wait_send()
        mlp_copy(peer, group).wait_send()
    own_copy.wait()
    lane_copy(1 - core).wait_recv()
    lane_copy(core).wait_send()

    def drain(piece, carry):
        keep_copy(2 * piece).wait()
        keep_copy(2 * piece + 1).wait()
        side_copy(piece, core).wait_send()

        @pl.when((piece <= chip) & (chip < chips - 1))
        def _():
            line_copy(1, chip - piece, piece).wait_send()

        @pl.when((piece >= chip) & (chip > 0))
        def _():
            line_copy(0, piece - chip, piece).wait_send()

        return carry

    lax.fori_loop(0, chips, drain, 0)


def gather_rows(parts, groups, heads, rows, w_qkv, gain, w_out, w_up, w_down, factor):
    rows_dev = rows.shape[0]
    held = w_qkv.shape[0]
    tokens = parts * rows_dev
    dma = pltpu.SemaphoreType.DMA
    chips = parts // 2
    anywhere = pl.BlockSpec(memory_space=pl.ANY)
    return pl.pallas_call(
        functools.partial(gather_kernel, parts, groups, heads),
        name="gather_rows",
        out_shape=[
            jax.ShapeDtypeStruct((parts, rows_dev, D), bf16),
            jax.ShapeDtypeStruct((3, groups, 2, held // 2, D), bf16),
            jax.ShapeDtypeStruct((2, 3 * heads * HD, D), bf16),
            jax.ShapeDtypeStruct((heads, PAD, tokens), bf16),
            jax.ShapeDtypeStruct((heads, HD, tokens), bf16),
            jax.ShapeDtypeStruct((heads, HD + EXTRA, tokens), bf16),
            jax.ShapeDtypeStruct((heads, tokens, PAD), bf16),
            jax.ShapeDtypeStruct((heads, tokens, PAD), bf16),
            jax.ShapeDtypeStruct((held, 3 * heads * HD), bf16),
        ],
        in_specs=in_vmem(1) + [anywhere] + in_vmem(1) + [anywhere] * 3 + in_vmem(1),
        out_specs=[anywhere] * 2 + in_vmem(7),
        scratch_shapes=[
            pltpu.VMEM((parts, rows_dev, D), bf16),
            pltpu.VMEM((held, 3 * D), f32),
            pltpu.VMEM((3, held, D), f32),
            pltpu.VMEM((3, held, heads * HD), bf16),
            pltpu.VMEM((3, 2, held // 2, D), bf16),
            pltpu.VMEM((groups, 3, held, heads * HD), bf16),
            pltpu.VMEM((3 * heads * HD, D), bf16),
            dma((2, 2, chips)),
            dma((2, chips)),
            dma((parts,)),
            dma((2, groups)),
            dma((2,)),
            dma((2, groups)),
            dma((2, groups)),
            dma,
            dma((4,)),
        ],
        compiler_params=pltpu.CompilerParams(
            vmem_limit_bytes=60 * 1024 * 1024, collective_id=2, has_side_effects=True
        ),
    )(rows, w_qkv, gain, w_out, w_up, w_down, factor)


def forward_kernel(
    heads,
    slot_ref,
    qt_ref,
    kt_ref,
    kn_ref,
    vt_ref,
    lse_ref,
    ot_ref,
    acc_ref,
    top_ref,
):
    tokens = kn_ref.shape[1]
    num_tiles = tokens // TILE
    prompt_tiles = num_tiles // 2

    def longest(ref):
        def visit(slot, most):
            rows = [ref[head, :HD, block_at(slot)].astype(f32) for head in range(heads)]
            sums = [jnp.sum(row * row, axis=0, keepdims=True) for row in rows]
            return functools.reduce(jnp.maximum, sums, most)

        return jnp.max(lax.fori_loop(0, tokens // BLOCK, visit, jnp.zeros((1, BLOCK), f32)))

    bounded = longest(qt_ref) * longest(kt_ref) <= SCORE_BOUND * SCORE_BOUND

    def run(shifted):
        def query_tile(tile, carry):
            queries = [tile_lanes(qt_ref, head, slot_ref, tile) for head in range(heads)]
            if shifted:
                top_ref[...] = jnp.full(top_ref.shape, -1e30, f32)
            else:
                top_ref[...] = jnp.zeros(top_ref.shape, f32)
            acc_ref[...] = jnp.zeros(acc_ref.shape, f32)

            def step(key_rows, value_lanes, start, masked):
                scores = [dot(key_rows[head], queries[head][:, start:]) for head in range(heads)]
                if masked:
                    allowed = causal(scores[0].shape)
                    scores = [jnp.where(allowed, score, -1e30) for score in scores]
                if shifted:
                    olds = [top_ref[head, :, start:] for head in range(heads)]
                    tops = [
                        jnp.maximum(old, jnp.max(score, axis=0, keepdims=True))
                        for old, score in zip(olds, scores)
                    ]
                    scores = [score - top for score, top in zip(scores, tops)]
                    for head in range(heads):
                        acc_ref[head, :, start:] *= jnp.exp2(olds[head] - tops[head])
                        top_ref[head, :, start:] = tops[head]
                probs = [jnp.exp2(score).astype(bf16) for score in scores]
                for head in range(heads):
                    acc_ref[head, :, start:] += dot(value_lanes[head], probs[head])

            def full(key_tile, inner):
                step(
                    [tile_rows(kn_ref, head, slot_ref, key_tile) for head in range(heads)],
                    [tile_lanes(vt_ref, head, slot_ref, key_tile) for head in range(heads)],
                    0,
                    False,
                )
                return inner

            lax.fori_loop(0, jnp.minimum(tile, prompt_tiles), full, 0)
            for part in range(TILE // BLOCK):
                block = block_at(slot_ref[tile * (TILE // BLOCK) + part])
                step(
                    [kn_ref[head, block, :] for head in range(heads)],
                    [vt_ref[head, :, block] for head in range(heads)],
                    part * BLOCK,
                    True,
                )
            for head in range(heads):
                acc = acc_ref[head]
                mass = acc[HD : HD + 1]
                mixed = (acc[:HD] / mass).astype(bf16)
                lse_ref[head, :, tile_at(tile)] = top_ref[head] + jnp.log2(mass)
                for part in range(TILE // BLOCK):
                    slot = slot_ref[tile * (TILE // BLOCK) + part]
                    ot_ref[slot // 2, head * HD : (head + 1) * HD, half_at(slot)] = mixed[
                        :, part * BLOCK : (part + 1) * BLOCK
                    ]
            return carry

        lax.fori_loop(0, num_tiles, query_tile, 0)

    @pl.when(bounded)
    def _():
        run(False)

    @pl.when(jnp.logical_not(bounded))
    def _():
        run(True)


def backward_kernel(
    heads,
    slot_ref,
    qt_ref,
    kt_ref,
    kn_ref,
    vn_ref,
    lse_ref,
    ot_ref,
    dt_ref,
    factor_ref,
    units_ref,
    dqkv_ref,
    dscale_ref,
    u_ref,
    qa_ref,
    da_ref,
    dq_ref,
    dk_ref,
    dv_ref,
    held_ref,
    total_ref,
    scale_ref,
    load_sem,
):
    parts = units_ref.shape[0]

    def load(piece):
        slot = lax.rem(piece, 2)
        return pltpu.make_async_copy(units_ref.at[piece], held_ref.at[slot], load_sem.at[slot])

    for piece in range(2):
        load(piece).start()
    tokens = kn_ref.shape[1]
    num_blocks = tokens // BLOCK
    num_tiles = tokens // TILE
    prompt_tiles = num_tiles // 2
    width = heads * HD

    def prepare(block, carry):
        slot = slot_ref[block]
        to = pl.ds(pl.multiple_of(block * BLOCK, BLOCK), BLOCK)
        for head in range(heads):
            rows = slice(head * HD, (head + 1) * HD)
            grad = dt_ref[slot // 2, rows, half_at(slot)]
            mixed = ot_ref[slot // 2, rows, half_at(slot)]
            delta = jnp.sum(grad.astype(f32) * mixed.astype(f32), axis=0, keepdims=True)
            da_ref[head, :HD, to] = grad
            da_ref[head, HD : HD + EXTRA, to] = three_rows(-delta)
            da_ref[head, HD + EXTRA :, to] = jnp.zeros((PAD - HD - EXTRA, BLOCK), bf16)
            qa_ref[head, :HD, to] = qt_ref[head, :HD, block_at(slot)]
            qa_ref[head, HD : HD + EXTRA, to] = three_rows(-lse_ref[head, :, to])
            qa_ref[head, HD + EXTRA :, to] = jnp.zeros((PAD - HD - EXTRA, BLOCK), bf16)
        return carry

    lax.fori_loop(0, num_blocks, prepare, 0)
    dk_ref[...] = jnp.zeros(dk_ref.shape, f32)
    dv_ref[...] = jnp.zeros(dv_ref.shape, f32)
    scale_ref[...] = jnp.zeros(scale_ref.shape, f32)

    def query_tile(tile, carry):
        here = tile_at(tile)
        dq_ref[...] = jnp.zeros(dq_ref.shape, f32)

        def step(keys, key_rows, key_lanes, value_rows, start, masked):
            to = pl.ds(pl.multiple_of(tile * TILE + start, BLOCK), TILE - start)
            queries = [qa_ref[head, :, to] for head in range(heads)]
            grads = [da_ref[head, :, to] for head in range(heads)]
            scores = [dot(key_rows[head], queries[head]) for head in range(heads)]
            spreads = [dot(value_rows[head], grads[head]) for head in range(heads)]
            probs = [jnp.exp2(score) for score in scores]
            if masked:
                allowed = causal(scores[0].shape)
                probs = [jnp.where(allowed, prob, 0.0) for prob in probs]
            dscores = [(prob * spread).astype(bf16) for prob, spread in zip(probs, spreads)]
            for head in range(heads):
                dv_ref[head, :, keys] += dot(grads[head][:HD], probs[head].astype(bf16), (1, 1))
                dk_ref[head, :, keys] += dot(queries[head][:HD], dscores[head], (1, 1))
                dq_ref[head, :, start:] += dot(key_lanes[head], dscores[head])

        def full(key_tile, inner):
            step(
                tile_at(key_tile),
                [tile_rows(kn_ref, head, slot_ref, key_tile) for head in range(heads)],
                [tile_lanes(kt_ref, head, slot_ref, key_tile) for head in range(heads)],
                [tile_rows(vn_ref, head, slot_ref, key_tile) for head in range(heads)],
                0,
                False,
            )
            return inner

        lax.fori_loop(0, jnp.minimum(tile, prompt_tiles), full, 0)
        for part in range(TILE // BLOCK):
            position = tile * (TILE // BLOCK) + part
            block = block_at(slot_ref[position])
            step(
                block_at(position),
                [kn_ref[head, block, :] for head in range(heads)],
                [kt_ref[head, :, block] for head in range(heads)],
                [vn_ref[head, block, :] for head in range(heads)],
                part * BLOCK,
                True,
            )
        for head in range(heads):
            dq = dq_ref[head]
            product = dq * qa_ref[head, :HD, here].astype(f32)
            for lane in range(TILE // PAD):
                scale_ref[head] += product[:, lane * PAD : (lane + 1) * PAD]
            scaled = (dq * (factor_ref[...] * LN2)).astype(bf16)
            for part in range(TILE // BLOCK):
                slot = slot_ref[tile * (TILE // BLOCK) + part]
                dqkv_ref[slot // 2, head * HD : (head + 1) * HD, half_at(slot)] = scaled[
                    :, part * BLOCK : (part + 1) * BLOCK
                ]
        return carry

    lax.fori_loop(0, num_tiles, query_tile, 0)

    def finish(block, carry):
        slot = slot_ref[block]
        owner, to = slot // 2, half_at(slot)
        at = pl.ds(pl.multiple_of(block * BLOCK, BLOCK), BLOCK)
        for head in range(heads):
            row = width + head * HD
            dqkv_ref[owner, row : row + HD, to] = (dk_ref[head, :, at] * LN2).astype(bf16)
            row = 2 * width + head * HD
            dqkv_ref[owner, row : row + HD, to] = dv_ref[head, :, at].astype(bf16)
        return carry

    lax.fori_loop(0, num_blocks, finish, 0)
    total_ref[...] = jnp.zeros(total_ref.shape, f32)

    def project(piece, carry):
        load(piece).wait()
        total_ref[...] += dot(dqkv_ref[piece], held_ref[lax.rem(piece, 2)])

        @pl.when(piece + 2 < parts)
        def _():
            load(piece + 2).start()

        return carry

    lax.fori_loop(0, parts, project, 0)
    u_ref[...] = total_ref[...].T.astype(bf16)
    sums = functools.reduce(jnp.add, [scale_ref[head] for head in range(heads)])
    sums = jnp.concatenate([sums, jnp.zeros((PAD - HD, PAD), f32)], axis=0).T
    dscale_ref[...] = jnp.sum(sums, axis=0, keepdims=True)


def in_vmem(count):
    return [pl.BlockSpec(memory_space=pltpu.VMEM)] * count


def params():
    return pltpu.CompilerParams(vmem_limit_bytes=60 * 1024 * 1024)


def attention_forward(slots, qt, kt, kn, vt, parts):
    heads, tokens = kn.shape[:2]
    return pl.pallas_call(
        functools.partial(forward_kernel, heads),
        name="attention_forward",
        out_shape=[
            jax.ShapeDtypeStruct((heads, 1, tokens), f32),
            jax.ShapeDtypeStruct((parts, heads * HD, tokens // parts), bf16),
        ],
        in_specs=[pl.BlockSpec(memory_space=pltpu.SMEM)] + in_vmem(4),
        out_specs=in_vmem(2),
        scratch_shapes=[
            pltpu.VMEM((heads, HD + EXTRA, TILE), f32),
            pltpu.VMEM((heads, 1, TILE), f32),
        ],
        compiler_params=params(),
        cost_estimate=attention_cost(heads, tokens, 2),
    )(slots, qt, kt, kn, vt)


def attention_cost(heads, tokens, passes):
    pairs = heads * tokens * tokens // 2
    return pl.CostEstimate(
        flops=2 * passes * pairs * BLOCK, bytes_accessed=tokens * D, transcendentals=pairs
    )


def attention_backward(slots, kept, mixed, dmixed, factor, units):
    qt, kt, kn, vn, lse = kept
    heads, tokens = kn.shape[:2]
    return pl.pallas_call(
        functools.partial(backward_kernel, heads),
        name="attention_backward",
        out_shape=[
            jax.ShapeDtypeStruct((mixed.shape[0], 3 * heads * HD, mixed.shape[2]), bf16),
            jax.ShapeDtypeStruct((1, PAD), f32),
            jax.ShapeDtypeStruct((D, 3 * heads * HD), bf16),
        ],
        in_specs=[pl.BlockSpec(memory_space=pltpu.SMEM)]
        + in_vmem(8)
        + [pl.BlockSpec(memory_space=pl.ANY)],
        out_specs=in_vmem(3),
        scratch_shapes=[
            pltpu.VMEM((heads, PAD, tokens), bf16),
            pltpu.VMEM((heads, PAD, tokens), bf16),
            pltpu.VMEM((heads, HD, TILE), f32),
            pltpu.VMEM((heads, HD, tokens), f32),
            pltpu.VMEM((heads, HD, tokens), f32),
            pltpu.VMEM((2,) + units.shape[1:], bf16),
            pltpu.VMEM((3 * heads * HD, D), f32),
            pltpu.VMEM((heads, HD, PAD), f32),
            pltpu.SemaphoreType.DMA((2,)),
        ],
        compiler_params=params(),
        cost_estimate=attention_cost(heads, tokens, 5),
    )(slots, qt, kt, kn, vn, lse, mixed, dmixed, factor, units)


def middle_kernel(
    parts,
    groups,
    mixed_ref,
    x_ref,
    dy_ref,
    weights_ref,
    gain_ref,
    *refs,
):
    out_ref, dmid_ref, dmixed_ref, gain_grad_ref = refs[:4]
    chunk_refs = refs[4 : 4 + groups]
    (
        w_ref,
        attn_ref,
        dattn_ref,
        act_ref,
        normed_ref,
        dhidden_ref,
        dbranch_ref,
        grad_ref,
        theirs_ref,
        w_sem,
        attn_sem,
        dattn_sem,
        pair_sem,
    ) = refs[4 + groups :]
    here = lax.axis_index("ctx")
    group = lax.axis_index("fsdp")
    core = lax.rem(here, 2)
    other = here + 1 - 2 * core
    peers = [lax.rem(here + step, parts) for step in range(1, parts)]
    tokens = x_ref.shape[0]
    width = mixed_ref.shape[1]
    held = theirs_ref.shape[2]
    loads = [
        pltpu.make_async_copy(weights_ref.at[index], w_ref.at[index], w_sem.at[index])
        for index in range(3)
    ]
    for load in loads:
        load.start()

    barrier = pltpu.get_barrier_semaphore()
    for peer in peers:
        pl.semaphore_signal(barrier, inc=1, device_id={"ctx": peer})
    pl.semaphore_wait(barrier, parts - 1)

    def lanes(part):
        return pl.ds(pl.multiple_of(part * BLOCK, BLOCK), BLOCK)

    def attn_copy(part, peer, source):
        return pltpu.make_async_remote_copy(
            src_ref=mixed_ref.at[peer, :, lanes(part)],
            dst_ref=attn_ref.at[source, :, lanes(part)],
            send_sem=attn_sem.at[0, part, peer],
            recv_sem=attn_sem.at[1, part, source],
            device_id={"ctx": peer},
        )

    def dattn_copy(part, peer, source):
        return pltpu.make_async_remote_copy(
            src_ref=dattn_ref.at[peer, :, lanes(part)],
            dst_ref=dmixed_ref.at[source, :, lanes(part)],
            send_sem=dattn_sem.at[0, part, peer],
            recv_sem=dattn_sem.at[1, part, source],
            device_id={"ctx": peer},
        )

    def rows_of(owner, lane):
        start = pl.multiple_of((owner * 2 + lane) * held, 16)
        return pl.ds(start, held)

    def pair_copy(index, owner, lane):
        return pltpu.make_async_remote_copy(
            src_ref=grad_ref.at[index, rows_of(owner, lane), :],
            dst_ref=theirs_ref.at[index, owner],
            send_sem=pair_sem.at[0, index, owner],
            recv_sem=pair_sem.at[1, index, owner],
            device_id={"ctx": other},
        )

    for part in range(tokens // BLOCK):
        for peer in peers:
            attn_copy(part, peer, here).start()
    attn_ref[here] = mixed_ref[here]
    gain_grad_ref[...] = jnp.zeros(gain_grad_ref.shape, f32)
    for load in loads:
        load.wait()
    gain = gain_ref[...]

    def layer(part, carry):
        rows = lanes(part)
        for peer in peers:
            attn_copy(part, here, peer).wait_recv()
        attn = attn_ref[:, :, rows].reshape(D, BLOCK)
        mid = x_ref[rows, :].astype(f32) + dot(attn, w_ref[0], (0, 0))
        scale = rms_scale(mid)
        unit = mid * scale
        normed = (unit * gain).astype(bf16)
        normed_ref[rows, :] = normed
        hidden = dot(normed, w_ref[1])
        gate = jax.nn.sigmoid(hidden)
        act = (hidden * gate).astype(bf16)
        act_ref[rows, :] = act
        dy = dy_ref[rows, :]
        dact = dot(dy, w_ref[2], (1, 1))
        dhidden = (dact * gate * (1.0 + hidden * (1.0 - gate))).astype(bf16)
        dhidden_ref[rows, :] = dhidden
        dnormed = dot(dhidden, w_ref[1], (1, 1))
        dunit = dnormed * gain
        dmid = dy.astype(f32) + scale * (
            dunit - unit * jnp.mean(dunit * unit, axis=-1, keepdims=True)
        )
        dmid_ref[rows, :] = dmid
        dbranch = dmid.astype(bf16)
        dbranch_ref[rows, :] = dbranch
        dattn = dot(w_ref[0], dbranch, (1, 1)).astype(bf16).reshape(parts, width, BLOCK)
        dattn_ref[:, :, rows] = dattn
        for peer in peers:
            dattn_copy(part, peer, here).start()
        dmixed_ref[here, :, rows] = dattn_ref[here, :, rows]
        out_ref[rows, :] = (mid + dot(act, w_ref[2])).astype(bf16)
        gain_grad_ref[...] += jnp.sum(dnormed * unit, axis=0, keepdims=True)
        return carry

    lax.fori_loop(0, tokens // BLOCK, layer, 0)

    def down_rows(index, carry):
        rows = lanes(index)
        grad_ref[2, rows, :] = dot(act_ref[:, rows], dy_ref[...], (0, 0)).astype(bf16)
        return carry

    def up_rows(index, carry):
        rows = lanes(index)
        grad_ref[1, rows, :] = dot(normed_ref[:, rows], dhidden_ref[...], (0, 0)).astype(bf16)
        return carry

    def out_rows(index, carry):
        rows = pl.ds(pl.multiple_of(index * width, 16), width)
        grad_ref[0, rows, :] = dot(attn_ref[index], dbranch_ref[...]).astype(bf16)
        return carry

    for index, count, run in (
        (2, D // BLOCK, down_rows),
        (1, D // BLOCK, up_rows),
        (0, parts, out_rows),
    ):
        lax.fori_loop(0, count, run, 0)
        for owner in range(groups):
            pair_copy(index, owner, 1 - core).start()
    for step in range(groups):
        owner = group ^ step
        for index in (2, 1, 0):
            pair_copy(index, owner, core).wait_recv()
            chunk_refs[step][index] = (
                grad_ref[index, rows_of(owner, core), :].astype(f32)
                + theirs_ref[index, owner].astype(f32)
            ).astype(bf16)
    for part in range(tokens // BLOCK):
        for peer in peers:
            dattn_copy(part, here, peer).wait_recv()
            dattn_copy(part, peer, here).wait_send()
            attn_copy(part, peer, here).wait_send()
    for index in range(3):
        for owner in range(groups):
            pair_copy(index, owner, 1 - core).wait_send()


def middle(parts, groups, mixed, rows, cotangent, weights, gain):
    rows_dev = rows.shape[0]
    half = D // groups // 2
    dma = pltpu.SemaphoreType.DMA
    halves = rows_dev // BLOCK
    return pl.pallas_call(
        functools.partial(middle_kernel, parts, groups),
        name="middle",
        out_shape=[
            jax.ShapeDtypeStruct((rows_dev, D), bf16),
            jax.ShapeDtypeStruct((rows_dev, D), f32),
            jax.ShapeDtypeStruct(mixed.shape, bf16),
            jax.ShapeDtypeStruct((1, D), f32),
        ]
        + [jax.ShapeDtypeStruct((3, half, D), bf16)] * groups,
        in_specs=in_vmem(3) + [pl.BlockSpec(memory_space=pl.ANY)] + in_vmem(1),
        out_specs=in_vmem(4 + groups),
        scratch_shapes=[
            pltpu.VMEM((3, D, D), bf16),
            pltpu.VMEM(mixed.shape, bf16),
            pltpu.VMEM(mixed.shape, bf16),
            pltpu.VMEM((rows_dev, D), bf16),
            pltpu.VMEM((rows_dev, D), bf16),
            pltpu.VMEM((rows_dev, D), bf16),
            pltpu.VMEM((rows_dev, D), bf16),
            pltpu.VMEM((3, D, D), bf16),
            pltpu.VMEM((3, groups, half, D), bf16),
            dma((3,)),
            dma((2, halves, parts)),
            dma((2, halves, parts)),
            dma((2, 3, groups)),
        ],
        compiler_params=pltpu.CompilerParams(
            vmem_limit_bytes=60 * 1024 * 1024, collective_id=3, has_side_effects=True
        ),
    )(mixed, rows, cotangent, weights, gain)


def reduce_kernel(
    parts,
    groups,
    dq_ref,
    wt_ref,
    u_ref,
    wc_ref,
    small_ref,
    *refs,
):
    chunk_refs = refs[:groups]
    (
        down_ref,
        up_ref,
        own_ref,
        ugather_ref,
        mgather_ref,
        sgather_ref,
        pair_ref,
        sum_ref,
        urecv_ref,
        mlp_ref,
        mrecv_ref,
        part_ref,
        column_ref,
        smine_ref,
        srecv_ref,
        pair_sem,
        sum_sem,
        u_sem,
        m_sem,
        line_sem,
        side_sem,
        small_sem,
        cross_sem,
    ) = refs[groups:]
    chips = parts // 2
    here = lax.axis_index("ctx")
    group = lax.axis_index("fsdp")
    core = lax.rem(here, 2)
    chip = here // 2
    other = here + 1 - 2 * core
    ctx_peers = [lax.rem(here + step, parts) for step in range(1, parts)]
    chip_peers = [lax.rem(chip + step, chips) for step in range(1, chips)]
    group_peers = [lax.rem(group + step, groups) for step in range(1, groups)]

    barrier = pltpu.get_barrier_semaphore()
    for peer in ctx_peers:
        pl.semaphore_signal(barrier, inc=1, device_id={"ctx": peer})
    for peer in group_peers:
        pl.semaphore_signal(barrier, inc=1, device_id={"fsdp": peer})
    pl.semaphore_wait(barrier, parts + groups - 2)

    def send(source, target, sems, device):
        return pltpu.make_async_remote_copy(
            src_ref=source,
            dst_ref=target,
            send_sem=sems[0],
            recv_sem=sems[1],
            device_id=device,
        )

    def pair_copy(index):
        return send(
            dq_ref.at[index, 1 - core],
            pair_ref.at[index],
            (pair_sem.at[0, index], pair_sem.at[1, index]),
            {"ctx": other},
        )

    def u_copy(peer, source):
        return send(
            u_ref.at[peer],
            urecv_ref.at[source],
            (u_sem.at[0, peer], u_sem.at[1, source]),
            {"fsdp": peer},
        )

    def m_copy(peer, source):
        return send(
            mlp_ref.at[peer],
            mrecv_ref.at[source],
            (m_sem.at[0, peer], m_sem.at[1, source]),
            {"ctx": 2 * peer + core},
        )

    for index in range(chips):
        pair_copy(index).start()
    for peer in group_peers:
        u_copy(peer, group).start()
    share = mlp_ref.shape[2]
    for matrix in range(3):
        total = functools.reduce(jnp.add, [ref[matrix].astype(f32) for ref in chunk_refs])
        for index in range(chips):
            mlp_ref[index, matrix] = total[index * share : (index + 1) * share].astype(bf16)
    for peer in chip_peers:
        m_copy(peer, chip).start()
    for index in range(chips):
        pair_copy(index).wait_recv()

    rows_half = own_ref.shape[0] // 2

    def partial(target, index):
        rows = pl.ds(pl.multiple_of(index * rows_half, rows_half), rows_half)
        part_ref[rows, :] = dot(dq_ref[target, core, :, rows], wt_ref[core], (0, 0)) + dot(
            pair_ref[target, :, rows], wt_ref[1 - core], (0, 0)
        )
        return rows

    def sum_copy(way, target, index):
        ref = sum_ref.at[way, target, pl.ds(index * rows_half, rows_half)]
        sems = (sum_sem.at[0, way, target, index], sum_sem.at[1, way, target, index])
        return send(ref, ref, sems, {"ctx": here + (2 if way else -2)})

    def reduce_step(step):
        last = step == chips - 2
        for way, target, active, first, out_ref in (
            (0, step - (chips - 1) + chip, step >= chips - 1 - chip, chip == chips - 1, down_ref),
            (1, chips - 1 - step + chip, step >= chip, chip == 0, up_ref),
        ):

            @pl.when(active)
            def _():
                def half(index, carry):
                    rows = partial(target, index)

                    @pl.when(first)
                    def _():
                        sum_ref[way, target, rows] = part_ref[rows, :].astype(bf16)

                    @pl.when(jnp.logical_not(first))
                    def _():
                        sum_copy(way, target, index).wait_recv()
                        sum_ref[way, target, rows] = (
                            part_ref[rows, :] + sum_ref[way, target, rows].astype(f32)
                        ).astype(bf16)

                    if last:
                        out_ref[rows, :] = sum_ref[way, target, rows]
                    else:
                        sum_copy(way, target, index).start()
                    return carry

                lax.fori_loop(0, 2, half, 0)

            if last:

                @pl.when(jnp.logical_not(active))
                def _():
                    out_ref[...] = jnp.zeros(out_ref.shape, bf16)

    gathers = (ugather_ref, mgather_ref)

    def line_copy(which, way, step, piece):
        ref = gathers[which].at[2 * piece + core]
        sems = (line_sem.at[0, which, way, step], line_sem.at[1, which, way, step])
        return send(ref, ref, sems, {"ctx": here + (2 if way else -2)})

    def side_copy(which, piece, lane):
        ref = gathers[which].at[2 * piece + lane]
        sems = (side_sem.at[0, which, piece], side_sem.at[1, which, piece])
        return send(ref, ref, sems, {"ctx": other})

    def line_sends(which, step, go):
        @pl.when((chip < chips - 1) & (chip - step >= 0))
        def _():
            go(line_copy(which, 1, step, chip - step))

        @pl.when((chip > 0) & (chip + step <= chips - 1))
        def _():
            go(line_copy(which, 0, step, chip + step))

    def line_receive(which, step):
        @pl.when(chip - 1 - step >= 0)
        def _():
            line_copy(which, 1, step, chip - 1 - step).wait_recv()
            side_copy(which, chip - 1 - step, core).start()

        @pl.when(chip + 1 + step <= chips - 1)
        def _():
            line_copy(which, 0, step, chip + 1 + step).wait_recv()
            side_copy(which, chip + 1 + step, core).start()

    def small_copy(peer, source):
        return send(
            smine_ref,
            srecv_ref.at[source],
            (small_sem.at[0, peer], small_sem.at[1, source]),
            {"ctx": peer},
        )

    def cross_copy(peer, source):
        return send(
            sgather_ref.at[group],
            sgather_ref.at[source],
            (cross_sem.at[0, peer], cross_sem.at[1, source]),
            {"fsdp": peer},
        )

    reduce_step(0)

    total = u_ref[group].astype(f32)
    for peer in group_peers:
        u_copy(group, peer).wait_recv()
        total = total + urecv_ref[peer].astype(f32)
    ugather_ref[here] = total.astype(bf16)
    side_copy(0, chip, core).start()
    line_sends(0, 0, lambda copy: copy.start())
    held = total.shape[0]
    gain = jnp.sum(total * wc_ref[...].astype(f32), axis=1, keepdims=True)
    column_ref[...] = jnp.zeros(column_ref.shape, f32)
    column_ref[:held, :] = jnp.broadcast_to(gain, (held, PAD))
    flat = column_ref[...].T[:1]
    smine_ref[...] = small_ref[...]
    for row in range(column_ref.shape[0] // PAD):
        smine_ref[row : row + 1, :] = flat[:, row * PAD : (row + 1) * PAD]
    for peer in ctx_peers:
        small_copy(peer, here).start()

    total = mlp_ref[chip].astype(f32)
    for peer in chip_peers:
        m_copy(chip, peer).wait_recv()
        total = total + mrecv_ref[peer].astype(f32)
    mgather_ref[here] = total.astype(bf16)
    side_copy(1, chip, core).start()
    line_sends(1, 0, lambda copy: copy.start())

    for step in range(1, chips):
        if step == 1:
            reduce_step(step)
        for which in range(2):
            line_receive(which, step - 1)
            if step <= chips - 2:
                line_sends(which, step, lambda copy: copy.start())
        if 1 < step <= chips - 2:
            reduce_step(step)
        if step == 1:
            small = smine_ref[...]
            for peer in ctx_peers:
                small_copy(here, peer).wait_recv()
                small = small + srecv_ref[peer]
            sgather_ref[group] = small
            for peer in group_peers:
                cross_copy(peer, group).start()

    for index in range(2):
        rows = partial(chip, index)
        own_ref[rows, :] = part_ref[rows, :]

    for which in range(2):
        for piece in range(chips):
            side_copy(which, piece, 1 - core).wait_recv()
            side_copy(which, piece, core).wait_send()
        for step in range(chips - 1):
            line_sends(which, step, lambda copy: copy.wait_send())
    for index in range(chips):
        pair_copy(index).wait_send()
    for peer in group_peers:
        cross_copy(group, peer).wait_recv()
        cross_copy(peer, group).wait_send()
        u_copy(peer, group).wait_send()
    for peer in chip_peers:
        m_copy(peer, chip).wait_send()
    for peer in ctx_peers:
        small_copy(peer, here).wait_send()
    for step in range(chips - 2):

        @pl.when(step >= chips - 1 - chip)
        def _():
            for index in range(2):
                sum_copy(0, step - (chips - 1) + chip, index).wait_send()

        @pl.when(step >= chip)
        def _():
            for index in range(2):
                sum_copy(1, chips - 1 - step + chip, index).wait_send()


def reduce_gradients(parts, groups, dqkv, w_pair, u_parts, w_columns, small, chunks):
    chips = parts // 2
    mlp_shape = (chips, 3, chunks[0].shape[1] // chips, D)
    rows_dev = dqkv.shape[3]
    rows, width = w_columns.shape
    lanes = -(-rows // PAD) * PAD
    dma = pltpu.SemaphoreType.DMA
    return pl.pallas_call(
        functools.partial(reduce_kernel, parts, groups),
        name="reduce_gradients",
        out_shape=[
            jax.ShapeDtypeStruct((rows_dev, D), bf16),
            jax.ShapeDtypeStruct((rows_dev, D), bf16),
            jax.ShapeDtypeStruct((rows_dev, D), f32),
            jax.ShapeDtypeStruct((parts, rows, width), bf16),
            jax.ShapeDtypeStruct((parts,) + mlp_shape[1:], bf16),
            jax.ShapeDtypeStruct((groups,) + small.shape, f32),
        ],
        in_specs=in_vmem(5 + groups),
        out_specs=in_vmem(6),
        scratch_shapes=[
            pltpu.VMEM((chips,) + dqkv.shape[2:], bf16),
            pltpu.VMEM((2, chips, rows_dev, D), bf16),
            pltpu.VMEM(u_parts.shape, bf16),
            pltpu.VMEM(mlp_shape, bf16),
            pltpu.VMEM(mlp_shape, bf16),
            pltpu.VMEM((rows_dev, D), f32),
            pltpu.VMEM((lanes, PAD), f32),
            pltpu.VMEM(small.shape, f32),
            pltpu.VMEM((parts,) + small.shape, f32),
            dma((2, chips)),
            dma((2, 2, chips, 2)),
            dma((2, groups)),
            dma((2, chips)),
            dma((2, 2, 2, chips)),
            dma((2, 2, chips)),
            dma((2, parts)),
            dma((2, groups)),
        ],
        compiler_params=pltpu.CompilerParams(
            vmem_limit_bytes=60 * 1024 * 1024, collective_id=1, has_side_effects=True
        ),
    )(dqkv, w_pair, u_parts, w_columns, small, *chunks)


def update_kernel(rates, qkv_ref, gain_ref, mlp_ref, *refs):
    sets = len(rates)
    parts, rows, width = qkv_ref.shape
    width = width // 3
    for index, rate in enumerate(rates):
        weight, first, second = (ref[...] for ref in refs[3 * index : 3 * index + 3])
        if index == 0:
            pieces = [qkv_ref[part].astype(f32) for part in range(parts)]
            gradient = jnp.concatenate(
                [piece[:, at * width : (at + 1) * width] for at in range(3) for piece in pieces],
                axis=1,
            )
            gradient = gradient * gain_ref[...]
        else:
            gradient = mlp_ref[0, index - 1].astype(f32)
        outs = refs[3 * sets + 4 * index : 3 * sets + 4 * index + 4]
        new, first, second = adamw(weight, first, second, gradient, rate, decay_rate)
        outs[0][...] = new
        outs[1][...] = first
        outs[2][...] = second
        outs[3][...] = new.astype(bf16)


def update(rates, parts, qkv, gain, mlp, *arrays):
    rows = arrays[0].shape[0]
    chips = parts // 2
    step_rows = rows // parts
    if step_rows % 8 == 0:

        def owner(i):
            return (2 * lax.rem(i, chips) + i // chips, 0, 0, 0)

    else:
        step_rows = 32
        mlp = mlp.reshape(chips, 2, 3, rows // parts, D).transpose(2, 1, 0, 3, 4)
        mlp = mlp.reshape(3, rows // step_rows, step_rows, D).transpose(1, 0, 2, 3)

        def owner(i):
            return (i, 0, 0, 0)

    in_specs = [
        pl.BlockSpec((parts, step_rows, qkv.shape[2]), lambda i: (0, i, 0)),
        pl.BlockSpec((step_rows, 1), lambda i: (i, 0)),
        pl.BlockSpec((1, 3, step_rows, D), owner),
    ]
    specs, shapes, moved = [], [], 0
    for array in arrays:
        in_specs.append(pl.BlockSpec((step_rows, array.shape[1]), lambda i: (i, 0)))
    for index in range(len(rates)):
        shape = arrays[3 * index].shape
        shapes += [jax.ShapeDtypeStruct(shape, f32)] * 3 + [jax.ShapeDtypeStruct(shape, bf16)]
        specs += [pl.BlockSpec((step_rows, shape[1]), lambda i: (i, 0))] * 4
        moved += shape[0] * shape[1] * 28
    return pl.pallas_call(
        functools.partial(update_kernel, rates),
        name="update_weights",
        grid=(rows // step_rows,),
        in_specs=in_specs,
        out_specs=specs,
        out_shape=shapes,
        compiler_params=params(),
        cost_estimate=pl.CostEstimate(flops=moved, bytes_accessed=moved, transcendentals=0),
    )(qkv, gain, mlp, *arrays)


def finish_kernel(x_ref, dmid_ref, own_ref, down_ref, up_ref, out_ref):
    rows = x_ref[...].astype(f32)
    scale = rms_scale(rows)
    unit = rows * scale
    dunit = own_ref[...] + down_ref[...].astype(f32) + up_ref[...].astype(f32)
    grad = dmid_ref[...] + scale * (
        dunit - unit * jnp.mean(dunit * unit, axis=-1, keepdims=True)
    )
    out_ref[...] = grad.astype(bf16)


def finish(*arrays):
    rows = arrays[0].shape[0]
    spec = pl.BlockSpec((PAD, D), lambda i: (i, 0))
    return pl.pallas_call(
        finish_kernel,
        name="finish",
        grid=(rows // PAD,),
        in_specs=[spec] * len(arrays),
        out_specs=spec,
        out_shape=jax.ShapeDtypeStruct((rows, D), bf16),
        compiler_params=params(),
    )(*arrays)


def body(
    parts,
    groups,
    inputs,
    cotangent,
    block_order,
    w_qkv,
    m_qkv,
    v_qkv,
    w_out,
    m_out,
    v_out,
    w_up,
    m_up,
    v_up,
    w_down,
    m_down,
    v_down,
    small_params,
    small_m,
    small_v,
):
    heads = H // parts
    width = heads * HD
    rows_dev = inputs.shape[1]
    tokens = rows_dev * parts
    here = lax.axis_index("ctx")
    index = jnp.arange(block_order.shape[1], dtype=jnp.int32)
    slots = jnp.sum(jnp.where(block_order[0][None] == index[:, None], index[None], 0), axis=1)
    gain_one = small_params[:D]
    gain_two = small_params[D : 2 * D]
    query_scale = small_params[2 * D :]
    group = lax.axis_index("fsdp")
    rows = w_qkv.shape[0]

    gain_rows = lax.dynamic_slice_in_dim(gain_one, group * rows, rows, 0)[:, None]
    factor = scale_base / math.sqrt(HD) * jax.nn.softplus(query_scale)
    factor_two = (factor * LOG2E)[:, None]
    unit_all, mlp_full, w_pair, qt, kt, vt, kn, vn, w_columns = gather_rows(
        parts, groups, heads, inputs[0], w_qkv, gain_rows, w_out, w_up, w_down, factor_two
    )
    lse, mixed = attention_forward(slots, qt, kt, kn, vt, parts)
    kept = (qt, kt, kn, vn, lse)
    output, dmid, dmixed, gain_two_grad, *chunks = middle(
        parts,
        groups,
        mixed,
        inputs[0],
        cotangent[0],
        mlp_full.reshape(3, D, D),
        gain_two[None],
    )
    for step in range(1, groups):
        swap = [(i, i ^ step) for i in range(groups)]
        chunks[step] = lax.ppermute(chunks[step], "fsdp", swap)
    dqkv, dscale, u_parts = attention_backward(slots, kept, mixed, dmixed, factor_two, unit_all)
    u_parts = u_parts.reshape(groups, rows, 3 * width)
    scale_grad = (
        dscale[0, :HD]
        / factor_two[:, 0]
        * (scale_base / math.sqrt(HD))
        * jax.nn.sigmoid(query_scale)
    )
    lanes = -(-rows // PAD) * PAD
    small_rows = -(-(lanes + D + PAD) // (8 * PAD)) * 8
    small = jnp.concatenate([jnp.zeros((lanes,), f32), gain_two_grad[0], scale_grad])
    small = jnp.pad(small, (0, small_rows * PAD - small.shape[0])).reshape(small_rows, PAD)
    send_down, send_up, own_part, u_all, mlp_all, small_all = reduce_gradients(
        parts,
        groups,
        dqkv.reshape(parts // 2, 2, 3 * width, rows_dev),
        w_pair,
        u_parts,
        w_columns,
        small,
        chunks,
    )
    got_down = lax.ppermute(send_down, "ctx", [(i, i - 2) for i in range(2, parts)])
    got_up = lax.ppermute(send_up, "ctx", [(i, i + 2) for i in range(parts - 2)])
    rate_qkv = qkv_rate_base / math.sqrt(D)
    rate_out = 0.5 / math.sqrt(max(D // 256, 1))
    rate_up = 0.5 / math.sqrt(D)
    rate_down = 0.5 / math.sqrt(FF)
    updated = update(
        (rate_qkv, rate_out, rate_up, rate_down),
        parts,
        u_all,
        gain_rows,
        mlp_all,
        w_qkv,
        m_qkv,
        v_qkv,
        w_out,
        m_out,
        v_out,
        w_up,
        m_up,
        v_up,
        w_down,
        m_down,
        v_down,
    )
    flat = small_all.reshape(groups, small_rows * PAD)
    rest = jnp.sum(flat[:, lanes : lanes + D + HD], axis=0)
    small_total = jnp.concatenate([flat[:, :rows].reshape(D), rest])
    small_set = adamw(small_params, small_m, small_v, small_total, small_rate, 0.0)
    input_grad = finish(inputs[0], dmid, own_part, got_down, got_up)
    return (
        output[None],
        input_grad[None],
        *updated,
        *small_set,
    )


def solution(mesh):
    rows = P("fsdp", "ctx", None)
    weight = P("fsdp", None)
    return jax.shard_map(
        functools.partial(body, mesh.shape["ctx"], mesh.shape["fsdp"]),
        mesh=mesh,
        in_specs=(rows, rows, weight) + (weight,) * 12 + (P(),) * 3,
        out_specs=(rows, rows) + (weight,) * 16 + (P(),) * 3,
        check_vma=False,
    )
```

```python
import functools
import math

import jax
import jax.numpy as jnp
from jax import lax
from jax.experimental import pallas as pl
from jax.experimental.pallas import tpu as pltpu
from jax.sharding import PartitionSpec as P

D = 1280
H = 16
HD = 80
FF = 1280
BLOCK = 256
CONT = 512
STEP = 3
PAD = 128
EXTRA = 16
TILE = CONT
SCORE_BOUND = 96.0

bf16 = jnp.bfloat16
f32 = jnp.float32

norm_eps = 1e-06
beta_one = 0.5
beta_two = 0.5
adam_eps = 1e-08
decay_rate = 0.1
small_rate = 0.75
qkv_rate_base = 1.0
scale_base = 1.442695
LOG2E = math.log2(math.e)
LN2 = math.log(2.0)


def rms_scale(values):
    return lax.rsqrt(jnp.mean(values * values, axis=-1, keepdims=True) + norm_eps)


def adamw(weight, first, second, gradient, step_rate, decay_on):
    first_new = beta_one * first + (1.0 - beta_one) * gradient
    second_new = beta_two * second + (1.0 - beta_two) * gradient * gradient
    corr_one = 1.0 - beta_one**STEP
    corr_two = 1.0 - beta_two**STEP
    update = first_new / corr_one / (jnp.sqrt(second_new / corr_two) + adam_eps)
    weight_new = weight - step_rate * (update + decay_on * weight)
    return (weight_new, first_new, second_new)


def dot(left, right, contract=(1, 0)):
    return lax.dot_general(
        left, right, (((contract[0],), (contract[1],)), ((), ())), preferred_element_type=f32
    )


def three_rows(row):
    high = row.astype(bf16)
    rest = row - high.astype(f32)
    middle = rest.astype(bf16)
    low = (rest - middle.astype(f32)).astype(bf16)
    index = lax.broadcasted_iota(jnp.int32, (EXTRA, row.shape[1]), 0)
    zero = jnp.zeros((EXTRA, row.shape[1]), f32)
    rows = jnp.where(index == 0, high.astype(f32), zero)
    rows = jnp.where(index == 1, middle.astype(f32), rows)
    rows = jnp.where(index == 2, low.astype(f32), rows)
    return rows.astype(bf16)


def tile_at(tile):
    return pl.ds(pl.multiple_of(tile * TILE, TILE), TILE)


def block_at(slot):
    return pl.ds(pl.multiple_of(slot * BLOCK, BLOCK), BLOCK)


def tile_lanes(ref, head, slot_ref, tile, rows=slice(None)):
    first, second = slot_ref[2 * tile], slot_ref[2 * tile + 1]
    return jnp.concatenate(
        [ref[head, rows, block_at(first)], ref[head, rows, block_at(second)]], axis=1
    )


def tile_rows(ref, head, slot_ref, tile):
    first, second = slot_ref[2 * tile], slot_ref[2 * tile + 1]
    return jnp.concatenate([ref[head, block_at(first), :], ref[head, block_at(second), :]], axis=0)


def half_at(slot):
    return pl.ds(pl.multiple_of(lax.rem(slot, 2) * BLOCK, BLOCK), BLOCK)


def causal(shape):
    key = lax.broadcasted_iota(jnp.int32, shape, 0)
    query = lax.broadcasted_iota(jnp.int32, shape, 1)
    return key <= query


def gather_kernel(
    parts,
    groups,
    heads,
    x_ref,
    wqkv_ref,
    gain_ref,
    wout_ref,
    wup_ref,
    wdown_ref,
    factor_ref,
    unit_ref,
    full_ref,
    wpair_ref,
    qt_out_ref,
    kt_out_ref,
    vt_out_ref,
    kn_out_ref,
    vn_out_ref,
    wcol_ref,
    qt_ref,
    kt_ref,
    vt_ref,
    kn_ref,
    vn_ref,
    rows_ref,
    wstage_ref,
    mstage_ref,
    gained_ref,
    mlp_ref,
    wrecv_ref,
    wflip_ref,
    line_sem,
    side_sem,
    keep_sem,
    w_sem,
    lane_sem,
    mlp_sem,
    cross_sem,
    own_sem,
    stage_sem,
    lanes_sem,
    sides_sem,
):
    chips = parts // 2
    here = lax.axis_index("ctx")
    group = lax.axis_index("fsdp")
    core = lax.rem(here, 2)
    chip = here // 2
    other = here + 1 - 2 * core
    width = heads * HD
    group_peers = [lax.rem(group + step, groups) for step in range(1, groups)]

    barrier = pltpu.get_barrier_semaphore()
    pl.semaphore_signal(barrier, inc=1, device_id={"ctx": other})
    for peer in group_peers:
        pl.semaphore_signal(barrier, inc=1, device_id={"fsdp": peer})
    for step in (1, chips - 1):
        peer = lax.rem(chip + step, chips) * 2 + core
        pl.semaphore_signal(barrier, inc=1, device_id={"ctx": peer})
    pl.semaphore_wait(barrier, groups + 2)

    def send(source, target, sems, device):
        return pltpu.make_async_remote_copy(
            src_ref=source,
            dst_ref=target,
            send_sem=sems[0],
            recv_sem=sems[1],
            device_id=device,
        )

    halves = rows_ref.shape[1] // BLOCK

    def line_copy(way, step, piece, part):
        ref = rows_ref.at[2 * piece + core, block_at(part)]
        sems = (line_sem.at[0, way, step, part], line_sem.at[1, way, step, part])
        return send(ref, ref, sems, {"ctx": here + (2 if way else -2)})

    def side_copy(piece, lane, part):
        ref = rows_ref.at[2 * piece + lane, block_at(part)]
        sems = (side_sem.at[0, piece, part], side_sem.at[1, piece, part])
        return send(ref, ref, sems, {"ctx": other})

    def results(slot):
        to = block_at(slot)
        copies = [
            pltpu.make_async_copy(ref.at[:, :, to], out.at[:, :, to], lanes_sem.at[index, slot])
            for index, (ref, out) in enumerate(
                ((qt_ref, qt_out_ref), (kt_ref, kt_out_ref), (vt_ref, vt_out_ref))
            )
        ]
        return copies + [
            pltpu.make_async_copy(ref.at[:, to], out.at[:, to], sides_sem.at[index, slot])
            for index, (ref, out) in enumerate(((kn_ref, kn_out_ref), (vn_ref, vn_out_ref)))
        ]

    def w_copy(peer, source):
        sems = (w_sem.at[0, peer], w_sem.at[1, source])
        return send(gained_ref, wrecv_ref.at[source], sems, {"fsdp": peer})

    def lane_copy(lane):
        ref = wpair_ref.at[lane]
        return send(ref, ref, (lane_sem.at[0], lane_sem.at[1]), {"ctx": other})

    def mlp_copy(peer, source):
        sems = (mlp_sem.at[0, peer], mlp_sem.at[1, source])
        return send(mlp_ref.at[:, core], full_ref.at[:, source, core], sems, {"fsdp": peer})

    def cross_copy(source, lane):
        ref = full_ref.at[:, source, lane]
        sems = (cross_sem.at[0, source], cross_sem.at[1, source])
        return send(ref, ref, sems, {"ctx": other})

    def keep_copy(piece):
        return pltpu.make_async_copy(rows_ref.at[piece], unit_ref.at[piece], keep_sem.at[piece])

    own_copy = pltpu.make_async_copy(mlp_ref, full_ref.at[:, group], own_sem)

    stages = [pltpu.make_async_copy(wqkv_ref, wstage_ref, stage_sem.at[0])] + [
        pltpu.make_async_copy(ref, mstage_ref.at[index], stage_sem.at[index + 1])
        for index, ref in enumerate((wout_ref, wup_ref, wdown_ref))
    ]
    for stage in stages:
        stage.start()
    rows = x_ref[...].astype(f32)
    rows_ref[here] = (rows * rms_scale(rows)).astype(bf16)

    def forward(way, step, piece, part):
        @pl.when((chip < chips - 1) if way else (chip > 0))
        def _():
            line_copy(way, step, piece, part).start()

    for part in range(halves):
        for way in range(2):
            forward(way, 0, chip, part)
        side_copy(chip, core, part).start()
    shift = lax.rem(D - here * width, D)
    stages[0].wait()
    for part in range(3):
        turned = pltpu.roll(wstage_ref[:, part * D : (part + 1) * D], shift, 1)
        gained_ref[part] = (turned[:, :width] * gain_ref[...]).astype(bf16)
        wcol_ref[:, part * width : (part + 1) * width] = turned[:, :width].astype(bf16)
    for peer in group_peers:
        w_copy(peer, group).start()
    for index in range(3):
        stages[index + 1].wait()
        mlp_ref[index] = mstage_ref[index].astype(bf16).reshape(mlp_ref.shape[1:])
    own_copy.start()
    keep_copy(here).start()
    wrecv_ref[group] = gained_ref[...]
    for peer in group_peers:
        w_copy(group, peer).wait_recv()
    for peer in group_peers:
        mlp_copy(peer, group).start()
    for part in range(3):
        flipped = wrecv_ref[:, part].reshape(D, width).T
        wflip_ref[part * width : (part + 1) * width] = flipped
    wpair_ref[core] = wflip_ref[...]
    lane_copy(core).start()

    extra_row = lax.broadcasted_iota(jnp.int32, (PAD - HD, BLOCK), 0)
    extra = jnp.where(extra_row < 3, 1.0, 0.0)
    spare = jnp.zeros((PAD - HD, BLOCK), bf16)

    def project(piece, part):
        slot = piece * halves + part
        to = block_at(slot)
        result = dot(wflip_ref[...], rows_ref[piece, block_at(part), :], (1, 1))
        for head in range(heads):
            query, key, value = (
                result[share * width + head * HD : share * width + (head + 1) * HD]
                for share in range(3)
            )
            qt_ref[head, :HD, to] = (query * factor_ref[...]).astype(bf16)
            qt_ref[head, HD:, to] = spare
            kt_ref[head, :, to] = key.astype(bf16)
            vt_ref[head, :HD, to] = value.astype(bf16)
            vt_ref[head, HD:, to] = jnp.ones((EXTRA, BLOCK), bf16)
            kn_ref[head, to, :] = jnp.concatenate([key, extra], axis=0).T.astype(bf16)
            vn_ref[head, to, :] = jnp.concatenate([value, extra], axis=0).T.astype(bf16)
        for copy in results(slot):
            copy.start()

    def visit(index, carry):
        distance, part = index // halves, lax.rem(index, halves)
        for way in range(2):
            piece = chip - distance if way else chip + distance
            valid = (piece >= 0) if way else (piece <= chips - 1)

            @pl.when(valid & (distance > 0))
            def _():
                line_copy(way, distance - 1, piece, part).wait_recv()
                side_copy(piece, core, part).start()
                forward(way, distance, piece, part)

                @pl.when(part == halves - 1)
                def _():
                    keep_copy(2 * piece + core).start()

        for way in range(2):
            piece = chip - distance if way else chip + distance
            valid = (piece >= 0) if way else ((piece <= chips - 1) & (distance > 0))

            @pl.when(valid)
            def _():
                project(2 * piece + core, part)
                side_copy(piece, 1 - core, part).wait_recv()
                project(2 * piece + 1 - core, part)

                @pl.when(part == halves - 1)
                def _():
                    keep_copy(2 * piece + 1 - core).start()

        return carry

    lax.fori_loop(0, chips * halves, visit, 0)

    for peer in group_peers:
        mlp_copy(group, peer).wait_recv()
        cross_copy(peer, core).start()
    for peer in group_peers:
        cross_copy(peer, 1 - core).wait_recv()
        cross_copy(peer, core).wait_send()
        w_copy(peer, group).wait_send()
        mlp_copy(peer, group).wait_send()
    own_copy.wait()
    lane_copy(1 - core).wait_recv()
    lane_copy(core).wait_send()

    def drain(piece, carry):
        keep_copy(2 * piece).wait()
        keep_copy(2 * piece + 1).wait()
        for part in range(halves):
            side_copy(piece, core, part).wait_send()

            @pl.when((piece <= chip) & (chip < chips - 1))
            def _():
                line_copy(1, chip - piece, piece, part).wait_send()

            @pl.when((piece >= chip) & (chip > 0))
            def _():
                line_copy(0, piece - chip, piece, part).wait_send()

        return carry

    lax.fori_loop(0, chips, drain, 0)

    def settle(slot, carry):
        for copy in results(slot):
            copy.wait()
        return carry

    lax.fori_loop(0, 2 * chips * halves, settle, 0)


def gather_rows(parts, groups, heads, rows, w_qkv, gain, w_out, w_up, w_down, factor):
    rows_dev = rows.shape[0]
    held = w_qkv.shape[0]
    tokens = parts * rows_dev
    dma = pltpu.SemaphoreType.DMA
    chips = parts // 2
    anywhere = pl.BlockSpec(memory_space=pl.ANY)
    return pl.pallas_call(
        functools.partial(gather_kernel, parts, groups, heads),
        name="gather_rows",
        out_shape=[
            jax.ShapeDtypeStruct((parts, rows_dev, D), bf16),
            jax.ShapeDtypeStruct((3, groups, 2, held // 2, D), bf16),
            jax.ShapeDtypeStruct((2, 3 * heads * HD, D), bf16),
            jax.ShapeDtypeStruct((heads, PAD, tokens), bf16),
            jax.ShapeDtypeStruct((heads, HD, tokens), bf16),
            jax.ShapeDtypeStruct((heads, HD + EXTRA, tokens), bf16),
            jax.ShapeDtypeStruct((heads, tokens, PAD), bf16),
            jax.ShapeDtypeStruct((heads, tokens, PAD), bf16),
            jax.ShapeDtypeStruct((held, 3 * heads * HD), bf16),
        ],
        in_specs=in_vmem(1) + [anywhere] + in_vmem(1) + [anywhere] * 3 + in_vmem(1),
        out_specs=[anywhere] * 2 + in_vmem(1) + [anywhere] * 5 + in_vmem(1),
        scratch_shapes=[
            pltpu.VMEM((heads, PAD, tokens), bf16),
            pltpu.VMEM((heads, HD, tokens), bf16),
            pltpu.VMEM((heads, HD + EXTRA, tokens), bf16),
            pltpu.VMEM((heads, tokens, PAD), bf16),
            pltpu.VMEM((heads, tokens, PAD), bf16),
            pltpu.VMEM((parts, rows_dev, D), bf16),
            pltpu.VMEM((held, 3 * D), f32),
            pltpu.VMEM((3, held, D), f32),
            pltpu.VMEM((3, held, heads * HD), bf16),
            pltpu.VMEM((3, 2, held // 2, D), bf16),
            pltpu.VMEM((groups, 3, held, heads * HD), bf16),
            pltpu.VMEM((3 * heads * HD, D), bf16),
            dma((2, 2, chips, rows_dev // BLOCK)),
            dma((2, chips, rows_dev // BLOCK)),
            dma((parts,)),
            dma((2, groups)),
            dma((2,)),
            dma((2, groups)),
            dma((2, groups)),
            dma,
            dma((4,)),
            dma((3, tokens // BLOCK)),
            dma((2, tokens // BLOCK)),
        ],
        compiler_params=pltpu.CompilerParams(
            vmem_limit_bytes=60 * 1024 * 1024, collective_id=2, has_side_effects=True
        ),
    )(rows, w_qkv, gain, w_out, w_up, w_down, factor)


def forward_kernel(
    heads,
    slot_ref,
    qt_ref,
    kt_ref,
    kn_ref,
    vt_ref,
    lse_ref,
    ot_ref,
    acc_ref,
    top_ref,
):
    tokens = kn_ref.shape[1]
    num_tiles = tokens // TILE
    prompt_tiles = num_tiles // 2

    def longest(ref):
        def visit(slot, most):
            rows = [ref[head, :HD, block_at(slot)].astype(f32) for head in range(heads)]
            sums = [jnp.sum(row * row, axis=0, keepdims=True) for row in rows]
            return functools.reduce(jnp.maximum, sums, most)

        return jnp.max(lax.fori_loop(0, tokens // BLOCK, visit, jnp.zeros((1, BLOCK), f32)))

    bounded = longest(qt_ref) * longest(kt_ref) <= SCORE_BOUND * SCORE_BOUND

    def run(shifted):
        def query_tile(tile, carry):
            queries = [tile_lanes(qt_ref, head, slot_ref, tile) for head in range(heads)]
            if shifted:
                top_ref[...] = jnp.full(top_ref.shape, -1e30, f32)
            else:
                top_ref[...] = jnp.zeros(top_ref.shape, f32)
            acc_ref[...] = jnp.zeros(acc_ref.shape, f32)

            def step(key_rows, value_lanes, start, masked):
                scores = [dot(key_rows[head], queries[head][:, start:]) for head in range(heads)]
                if masked:
                    allowed = causal(scores[0].shape)
                    scores = [jnp.where(allowed, score, -1e30) for score in scores]
                if shifted:
                    olds = [top_ref[head, :, start:] for head in range(heads)]
                    tops = [
                        jnp.maximum(old, jnp.max(score, axis=0, keepdims=True))
                        for old, score in zip(olds, scores)
                    ]
                    scores = [score - top for score, top in zip(scores, tops)]
                    for head in range(heads):
                        acc_ref[head, :, start:] *= jnp.exp2(olds[head] - tops[head])
                        top_ref[head, :, start:] = tops[head]
                probs = [jnp.exp2(score).astype(bf16) for score in scores]
                for head in range(heads):
                    acc_ref[head, :, start:] += dot(value_lanes[head], probs[head])

            def full(key_tile, inner):
                step(
                    [tile_rows(kn_ref, head, slot_ref, key_tile) for head in range(heads)],
                    [tile_lanes(vt_ref, head, slot_ref, key_tile) for head in range(heads)],
                    0,
                    False,
                )
                return inner

            lax.fori_loop(0, jnp.minimum(tile, prompt_tiles), full, 0)
            for part in range(TILE // BLOCK):
                block = block_at(slot_ref[tile * (TILE // BLOCK) + part])
                step(
                    [kn_ref[head, block, :] for head in range(heads)],
                    [vt_ref[head, :, block] for head in range(heads)],
                    part * BLOCK,
                    True,
                )
            for head in range(heads):
                acc = acc_ref[head]
                mass = acc[HD : HD + 1]
                mixed = (acc[:HD] / mass).astype(bf16)
                lse_ref[head, :, tile_at(tile)] = top_ref[head] + jnp.log2(mass)
                for part in range(TILE // BLOCK):
                    slot = slot_ref[tile * (TILE // BLOCK) + part]
                    ot_ref[slot // 2, head * HD : (head + 1) * HD, half_at(slot)] = mixed[
                        :, part * BLOCK : (part + 1) * BLOCK
                    ]
            return carry

        lax.fori_loop(0, num_tiles, query_tile, 0)

    @pl.when(bounded)
    def _():
        run(False)

    @pl.when(jnp.logical_not(bounded))
    def _():
        run(True)


def backward_kernel(
    heads,
    slot_ref,
    qt_ref,
    kt_ref,
    kn_ref,
    vn_ref,
    lse_ref,
    ot_ref,
    dt_ref,
    factor_ref,
    dqkv_ref,
    dscale_ref,
    qa_ref,
    da_ref,
    dq_ref,
    dk_ref,
    dv_ref,
    scale_ref,
):
    tokens = kn_ref.shape[1]
    num_blocks = tokens // BLOCK
    num_tiles = tokens // TILE
    prompt_tiles = num_tiles // 2
    width = heads * HD

    def prepare(block, carry):
        slot = slot_ref[block]
        to = pl.ds(pl.multiple_of(block * BLOCK, BLOCK), BLOCK)
        for head in range(heads):
            rows = slice(head * HD, (head + 1) * HD)
            grad = dt_ref[slot // 2, rows, half_at(slot)]
            mixed = ot_ref[slot // 2, rows, half_at(slot)]
            delta = jnp.sum(grad.astype(f32) * mixed.astype(f32), axis=0, keepdims=True)
            da_ref[head, :HD, to] = grad
            da_ref[head, HD : HD + EXTRA, to] = three_rows(-delta)
            da_ref[head, HD + EXTRA :, to] = jnp.zeros((PAD - HD - EXTRA, BLOCK), bf16)
            qa_ref[head, :HD, to] = qt_ref[head, :HD, block_at(slot)]
            qa_ref[head, HD : HD + EXTRA, to] = three_rows(-lse_ref[head, :, to])
            qa_ref[head, HD + EXTRA :, to] = jnp.zeros((PAD - HD - EXTRA, BLOCK), bf16)
        return carry

    lax.fori_loop(0, num_blocks, prepare, 0)
    dk_ref[...] = jnp.zeros(dk_ref.shape, f32)
    dv_ref[...] = jnp.zeros(dv_ref.shape, f32)
    scale_ref[...] = jnp.zeros(scale_ref.shape, f32)

    def query_tile(tile, carry):
        here = tile_at(tile)
        dq_ref[...] = jnp.zeros(dq_ref.shape, f32)

        def step(keys, key_rows, key_lanes, value_rows, start, masked):
            to = pl.ds(pl.multiple_of(tile * TILE + start, BLOCK), TILE - start)
            queries = [qa_ref[head, :, to] for head in range(heads)]
            grads = [da_ref[head, :, to] for head in range(heads)]
            scores = [dot(key_rows[head], queries[head]) for head in range(heads)]
            spreads = [dot(value_rows[head], grads[head]) for head in range(heads)]
            probs = [jnp.exp2(score) for score in scores]
            if masked:
                allowed = causal(scores[0].shape)
                probs = [jnp.where(allowed, prob, 0.0) for prob in probs]
            dscores = [(prob * spread).astype(bf16) for prob, spread in zip(probs, spreads)]
            for head in range(heads):
                dv_ref[head, :, keys] += dot(grads[head][:HD], probs[head].astype(bf16), (1, 1))
                dk_ref[head, :, keys] += dot(queries[head][:HD], dscores[head], (1, 1))
                dq_ref[head, :, start:] += dot(key_lanes[head], dscores[head])

        def full(key_tile, inner):
            step(
                tile_at(key_tile),
                [tile_rows(kn_ref, head, slot_ref, key_tile) for head in range(heads)],
                [tile_lanes(kt_ref, head, slot_ref, key_tile) for head in range(heads)],
                [tile_rows(vn_ref, head, slot_ref, key_tile) for head in range(heads)],
                0,
                False,
            )
            return inner

        lax.fori_loop(0, jnp.minimum(tile, prompt_tiles), full, 0)
        for part in range(TILE // BLOCK):
            position = tile * (TILE // BLOCK) + part
            block = block_at(slot_ref[position])
            step(
                block_at(position),
                [kn_ref[head, block, :] for head in range(heads)],
                [kt_ref[head, :, block] for head in range(heads)],
                [vn_ref[head, block, :] for head in range(heads)],
                part * BLOCK,
                True,
            )
        for head in range(heads):
            dq = dq_ref[head]
            product = dq * qa_ref[head, :HD, here].astype(f32)
            for lane in range(TILE // PAD):
                scale_ref[head] += product[:, lane * PAD : (lane + 1) * PAD]
            scaled = (dq * (factor_ref[...] * LN2)).astype(bf16)
            for part in range(TILE // BLOCK):
                slot = slot_ref[tile * (TILE // BLOCK) + part]
                dqkv_ref[slot // 2, head * HD : (head + 1) * HD, half_at(slot)] = scaled[
                    :, part * BLOCK : (part + 1) * BLOCK
                ]
        return carry

    lax.fori_loop(0, num_tiles, query_tile, 0)

    def finish(block, carry):
        slot = slot_ref[block]
        owner, to = slot // 2, half_at(slot)
        at = pl.ds(pl.multiple_of(block * BLOCK, BLOCK), BLOCK)
        for head in range(heads):
            row = width + head * HD
            dqkv_ref[owner, row : row + HD, to] = (dk_ref[head, :, at] * LN2).astype(bf16)
            row = 2 * width + head * HD
            dqkv_ref[owner, row : row + HD, to] = dv_ref[head, :, at].astype(bf16)
        return carry

    lax.fori_loop(0, num_blocks, finish, 0)
    sums = functools.reduce(jnp.add, [scale_ref[head] for head in range(heads)])
    sums = jnp.concatenate([sums, jnp.zeros((PAD - HD, PAD), f32)], axis=0).T
    dscale_ref[...] = jnp.sum(sums, axis=0, keepdims=True)


def in_vmem(count):
    return [pl.BlockSpec(memory_space=pltpu.VMEM)] * count


def params():
    return pltpu.CompilerParams(vmem_limit_bytes=60 * 1024 * 1024)


def attention_forward(slots, qt, kt, kn, vt, parts):
    heads, tokens = kn.shape[:2]
    return pl.pallas_call(
        functools.partial(forward_kernel, heads),
        name="attention_forward",
        out_shape=[
            jax.ShapeDtypeStruct((heads, 1, tokens), f32),
            jax.ShapeDtypeStruct((parts, heads * HD, tokens // parts), bf16),
        ],
        in_specs=[pl.BlockSpec(memory_space=pltpu.SMEM)] + in_vmem(4),
        out_specs=in_vmem(2),
        scratch_shapes=[
            pltpu.VMEM((heads, HD + EXTRA, TILE), f32),
            pltpu.VMEM((heads, 1, TILE), f32),
        ],
        compiler_params=params(),
        cost_estimate=attention_cost(heads, tokens, 2),
    )(slots, qt, kt, kn, vt)


def attention_cost(heads, tokens, passes):
    pairs = heads * tokens * tokens // 2
    return pl.CostEstimate(
        flops=2 * passes * pairs * BLOCK, bytes_accessed=tokens * D, transcendentals=pairs
    )


def attention_backward(slots, kept, mixed, dmixed, factor):
    qt, kt, kn, vn, lse = kept
    heads, tokens = kn.shape[:2]
    return pl.pallas_call(
        functools.partial(backward_kernel, heads),
        name="attention_backward",
        out_shape=[
            jax.ShapeDtypeStruct((mixed.shape[0], 3 * heads * HD, mixed.shape[2]), bf16),
            jax.ShapeDtypeStruct((1, PAD), f32),
        ],
        in_specs=[pl.BlockSpec(memory_space=pltpu.SMEM)] + in_vmem(8),
        out_specs=in_vmem(2),
        scratch_shapes=[
            pltpu.VMEM((heads, PAD, tokens), bf16),
            pltpu.VMEM((heads, PAD, tokens), bf16),
            pltpu.VMEM((heads, HD, TILE), f32),
            pltpu.VMEM((heads, HD, tokens), f32),
            pltpu.VMEM((heads, HD, tokens), f32),
            pltpu.VMEM((heads, HD, PAD), f32),
        ],
        compiler_params=params(),
        cost_estimate=attention_cost(heads, tokens, 5),
    )(slots, qt, kt, kn, vn, lse, mixed, dmixed, factor)


def middle_kernel(
    parts,
    groups,
    mixed_ref,
    x_ref,
    dy_ref,
    weights_ref,
    gain_ref,
    *refs,
):
    out_ref, dmid_ref, dmixed_ref, gain_grad_ref = refs[:4]
    chunk_refs = refs[4 : 4 + groups]
    (
        w_ref,
        attn_ref,
        dattn_ref,
        act_ref,
        normed_ref,
        dhidden_ref,
        dbranch_ref,
        grad_ref,
        theirs_ref,
        w_sem,
        attn_sem,
        dattn_sem,
        pair_sem,
    ) = refs[4 + groups :]
    here = lax.axis_index("ctx")
    group = lax.axis_index("fsdp")
    core = lax.rem(here, 2)
    other = here + 1 - 2 * core
    peers = [lax.rem(here + step, parts) for step in range(1, parts)]
    tokens = x_ref.shape[0]
    width = mixed_ref.shape[1]
    held = theirs_ref.shape[2]
    loads = [
        pltpu.make_async_copy(weights_ref.at[index], w_ref.at[index], w_sem.at[index])
        for index in range(3)
    ]
    for load in loads:
        load.start()

    barrier = pltpu.get_barrier_semaphore()
    for peer in peers:
        pl.semaphore_signal(barrier, inc=1, device_id={"ctx": peer})
    pl.semaphore_wait(barrier, parts - 1)

    def lanes(part):
        return pl.ds(pl.multiple_of(part * BLOCK, BLOCK), BLOCK)

    def attn_copy(part, peer, source):
        return pltpu.make_async_remote_copy(
            src_ref=mixed_ref.at[peer, :, lanes(part)],
            dst_ref=attn_ref.at[source, :, lanes(part)],
            send_sem=attn_sem.at[0, part, peer],
            recv_sem=attn_sem.at[1, part, source],
            device_id={"ctx": peer},
        )

    def dattn_copy(part, peer, source):
        return pltpu.make_async_remote_copy(
            src_ref=dattn_ref.at[peer, :, lanes(part)],
            dst_ref=dmixed_ref.at[source, :, lanes(part)],
            send_sem=dattn_sem.at[0, part, peer],
            recv_sem=dattn_sem.at[1, part, source],
            device_id={"ctx": peer},
        )

    def rows_of(owner, lane):
        start = pl.multiple_of((owner * 2 + lane) * held, 16)
        return pl.ds(start, held)

    def pair_copy(index, owner, lane):
        return pltpu.make_async_remote_copy(
            src_ref=grad_ref.at[index, rows_of(owner, lane), :],
            dst_ref=theirs_ref.at[index, owner],
            send_sem=pair_sem.at[0, index, owner],
            recv_sem=pair_sem.at[1, index, owner],
            device_id={"ctx": other},
        )

    for part in range(tokens // BLOCK):
        for peer in peers:
            attn_copy(part, peer, here).start()
    attn_ref[here] = mixed_ref[here]
    gain_grad_ref[...] = jnp.zeros(gain_grad_ref.shape, f32)
    for load in loads:
        load.wait()
    gain = gain_ref[...]

    def layer(part, carry):
        rows = lanes(part)
        for peer in peers:
            attn_copy(part, here, peer).wait_recv()
        attn = attn_ref[:, :, rows].reshape(D, BLOCK)
        mid = x_ref[rows, :].astype(f32) + dot(attn, w_ref[0], (0, 0))
        scale = rms_scale(mid)
        unit = mid * scale
        normed = (unit * gain).astype(bf16)
        normed_ref[rows, :] = normed
        hidden = dot(normed, w_ref[1])
        gate = jax.nn.sigmoid(hidden)
        act = (hidden * gate).astype(bf16)
        act_ref[rows, :] = act
        dy = dy_ref[rows, :]
        dact = dot(dy, w_ref[2], (1, 1))
        dhidden = (dact * gate * (1.0 + hidden * (1.0 - gate))).astype(bf16)
        dhidden_ref[rows, :] = dhidden
        dnormed = dot(dhidden, w_ref[1], (1, 1))
        dunit = dnormed * gain
        dmid = dy.astype(f32) + scale * (
            dunit - unit * jnp.mean(dunit * unit, axis=-1, keepdims=True)
        )
        dmid_ref[rows, :] = dmid
        dbranch = dmid.astype(bf16)
        dbranch_ref[rows, :] = dbranch
        dattn = dot(w_ref[0], dbranch, (1, 1)).astype(bf16).reshape(parts, width, BLOCK)
        dattn_ref[:, :, rows] = dattn
        for peer in peers:
            dattn_copy(part, peer, here).start()
        dmixed_ref[here, :, rows] = dattn_ref[here, :, rows]
        out_ref[rows, :] = (mid + dot(act, w_ref[2])).astype(bf16)
        gain_grad_ref[...] += jnp.sum(dnormed * unit, axis=0, keepdims=True)
        return carry

    lax.fori_loop(0, tokens // BLOCK, layer, 0)

    def down_rows(index, carry):
        rows = lanes(index)
        grad_ref[2, rows, :] = dot(act_ref[:, rows], dy_ref[...], (0, 0)).astype(bf16)
        return carry

    def up_rows(index, carry):
        rows = lanes(index)
        grad_ref[1, rows, :] = dot(normed_ref[:, rows], dhidden_ref[...], (0, 0)).astype(bf16)
        return carry

    def out_rows(index, carry):
        rows = pl.ds(pl.multiple_of(index * width, 16), width)
        grad_ref[0, rows, :] = dot(attn_ref[index], dbranch_ref[...]).astype(bf16)
        return carry

    for index, count, run in (
        (2, D // BLOCK, down_rows),
        (1, D // BLOCK, up_rows),
        (0, parts, out_rows),
    ):
        lax.fori_loop(0, count, run, 0)
        for owner in range(groups):
            pair_copy(index, owner, 1 - core).start()
    for step in range(groups):
        owner = group ^ step
        for index in (2, 1, 0):
            pair_copy(index, owner, core).wait_recv()
            chunk_refs[step][index] = (
                grad_ref[index, rows_of(owner, core), :].astype(f32)
                + theirs_ref[index, owner].astype(f32)
            ).astype(bf16)
    for part in range(tokens // BLOCK):
        for peer in peers:
            dattn_copy(part, here, peer).wait_recv()
            dattn_copy(part, peer, here).wait_send()
            attn_copy(part, peer, here).wait_send()
    for index in range(3):
        for owner in range(groups):
            pair_copy(index, owner, 1 - core).wait_send()


def middle(parts, groups, mixed, rows, cotangent, weights, gain):
    rows_dev = rows.shape[0]
    half = D // groups // 2
    dma = pltpu.SemaphoreType.DMA
    halves = rows_dev // BLOCK
    return pl.pallas_call(
        functools.partial(middle_kernel, parts, groups),
        name="middle",
        out_shape=[
            jax.ShapeDtypeStruct((rows_dev, D), bf16),
            jax.ShapeDtypeStruct((rows_dev, D), f32),
            jax.ShapeDtypeStruct(mixed.shape, bf16),
            jax.ShapeDtypeStruct((1, D), f32),
        ]
        + [jax.ShapeDtypeStruct((3, half, D), bf16)] * groups,
        in_specs=in_vmem(3) + [pl.BlockSpec(memory_space=pl.ANY)] + in_vmem(1),
        out_specs=in_vmem(4 + groups),
        scratch_shapes=[
            pltpu.VMEM((3, D, D), bf16),
            pltpu.VMEM(mixed.shape, bf16),
            pltpu.VMEM(mixed.shape, bf16),
            pltpu.VMEM((rows_dev, D), bf16),
            pltpu.VMEM((rows_dev, D), bf16),
            pltpu.VMEM((rows_dev, D), bf16),
            pltpu.VMEM((rows_dev, D), bf16),
            pltpu.VMEM((3, D, D), bf16),
            pltpu.VMEM((3, groups, half, D), bf16),
            dma((3,)),
            dma((2, halves, parts)),
            dma((2, halves, parts)),
            dma((2, 3, groups)),
        ],
        compiler_params=pltpu.CompilerParams(
            vmem_limit_bytes=60 * 1024 * 1024, collective_id=3, has_side_effects=True
        ),
    )(mixed, rows, cotangent, weights, gain)


def reduce_kernel(
    parts,
    groups,
    dq_in_ref,
    wt_in_ref,
    units_ref,
    wc_ref,
    small_ref,
    *refs,
):
    chunk_in_refs = refs[:groups]
    (
        down_ref,
        up_ref,
        own_ref,
        ugather_ref,
        mgather_ref,
        sgather_ref,
        dq_ref,
        wt_ref,
        chunk_ref,
        held_ref,
        total_ref,
        u_ref,
        usum_ref,
        msum_ref,
        pair_ref,
        sum_ref,
        urecv_ref,
        mlp_ref,
        mrecv_ref,
        part_ref,
        column_ref,
        smine_ref,
        srecv_ref,
        pair_sem,
        sum_sem,
        u_sem,
        m_sem,
        line_sem,
        side_sem,
        small_sem,
        cross_sem,
        load_sem,
        held_sem,
        keep_sem,
    ) = refs[groups:]
    chips = parts // 2
    here = lax.axis_index("ctx")
    group = lax.axis_index("fsdp")
    core = lax.rem(here, 2)
    chip = here // 2
    other = here + 1 - 2 * core
    ctx_peers = [lax.rem(here + step, parts) for step in range(1, parts)]
    chip_peers = [lax.rem(chip + step, chips) for step in range(1, chips)]
    group_peers = [lax.rem(group + step, groups) for step in range(1, groups)]

    loads = [
        pltpu.make_async_copy(ref, chunk_ref.at[index], load_sem.at[index])
        for index, ref in enumerate(chunk_in_refs)
    ]
    loads.append(pltpu.make_async_copy(dq_in_ref, dq_ref, load_sem.at[groups]))
    loads.append(pltpu.make_async_copy(wt_in_ref, wt_ref, load_sem.at[groups + 1]))
    for load in loads:
        load.start()

    def unit_load(piece):
        slot = lax.rem(piece, 2)
        return pltpu.make_async_copy(units_ref.at[piece], held_ref.at[slot], held_sem.at[slot])

    for piece in range(2):
        unit_load(piece).start()

    barrier = pltpu.get_barrier_semaphore()
    for peer in ctx_peers:
        pl.semaphore_signal(barrier, inc=1, device_id={"ctx": peer})
    for peer in group_peers:
        pl.semaphore_signal(barrier, inc=1, device_id={"fsdp": peer})
    pl.semaphore_wait(barrier, parts + groups - 2)

    def send(source, target, sems, device):
        return pltpu.make_async_remote_copy(
            src_ref=source,
            dst_ref=target,
            send_sem=sems[0],
            recv_sem=sems[1],
            device_id=device,
        )

    def pair_copy(index):
        return send(
            dq_in_ref.at[index, 1 - core],
            pair_ref.at[index],
            (pair_sem.at[0, index], pair_sem.at[1, index]),
            {"ctx": other},
        )

    def u_copy(peer, source):
        return send(
            u_ref.at[peer],
            urecv_ref.at[source],
            (u_sem.at[0, peer], u_sem.at[1, source]),
            {"fsdp": peer},
        )

    def m_copy(peer, source):
        return send(
            mlp_ref.at[peer],
            mrecv_ref.at[source],
            (m_sem.at[0, peer], m_sem.at[1, source]),
            {"ctx": 2 * peer + core},
        )

    for index in range(chips):
        pair_copy(index).start()
    for load in loads:
        load.wait()
    share = mlp_ref.shape[2]
    for matrix in range(3):
        total = functools.reduce(jnp.add, [chunk_ref[step, matrix].astype(f32) for step in range(groups)])
        for index in range(chips):
            mlp_ref[index, matrix] = total[index * share : (index + 1) * share].astype(bf16)
    for peer in chip_peers:
        m_copy(peer, chip).start()
    for index in range(chips):
        pair_copy(index).wait_recv()

    rows_half = own_ref.shape[0] // 2

    def partial(target, index):
        rows = pl.ds(pl.multiple_of(index * rows_half, rows_half), rows_half)
        part_ref[rows, :] = dot(dq_ref[target, core, :, rows], wt_ref[core], (0, 0)) + dot(
            pair_ref[target, :, rows], wt_ref[1 - core], (0, 0)
        )
        return rows

    def sum_copy(way, target, index):
        ref = sum_ref.at[way + target, pl.ds(index * rows_half, rows_half)]
        sems = (sum_sem.at[0, way, target, index], sum_sem.at[1, way, target, index])
        return send(ref, ref, sems, {"ctx": here + (2 if way else -2)})

    def reduce_step(step):
        last = step == chips - 2
        for way, target, active, first, out_ref in (
            (0, step - (chips - 1) + chip, step >= chips - 1 - chip, chip == chips - 1, down_ref),
            (1, chips - 1 - step + chip, step >= chip, chip == 0, up_ref),
        ):

            @pl.when(active)
            def _():
                def half(index, carry):
                    rows = partial(target, index)

                    @pl.when(first)
                    def _():
                        sum_ref[way + target, rows] = part_ref[rows, :].astype(bf16)

                    @pl.when(jnp.logical_not(first))
                    def _():
                        sum_copy(way, target, index).wait_recv()
                        sum_ref[way + target, rows] = (
                            part_ref[rows, :] + sum_ref[way + target, rows].astype(f32)
                        ).astype(bf16)

                    if last:
                        out_ref[rows, :] = sum_ref[way + target, rows]
                    else:
                        sum_copy(way, target, index).start()
                    return carry

                lax.fori_loop(0, 2, half, 0)

            if last:

                @pl.when(jnp.logical_not(active))
                def _():
                    out_ref[...] = jnp.zeros(out_ref.shape, bf16)

    gathers = (ugather_ref, mgather_ref)
    sums = (usum_ref, msum_ref)

    def keep_copy(which):
        return pltpu.make_async_copy(sums[which], gathers[which].at[here], keep_sem.at[which])

    def line_copy(which, way, step, piece):
        ref = gathers[which].at[2 * piece + core]
        sems = (line_sem.at[0, which, way, step], line_sem.at[1, which, way, step])
        source = sums[which] if step == 0 else ref
        return send(source, ref, sems, {"ctx": here + (2 if way else -2)})

    def side_copy(which, piece, lane, own=False):
        ref = gathers[which].at[2 * piece + lane]
        sems = (side_sem.at[0, which, piece], side_sem.at[1, which, piece])
        return send(sums[which] if own else ref, ref, sems, {"ctx": other})

    def line_sends(which, step, go):
        @pl.when((chip < chips - 1) & (chip - step >= 0))
        def _():
            go(line_copy(which, 1, step, chip - step))

        @pl.when((chip > 0) & (chip + step <= chips - 1))
        def _():
            go(line_copy(which, 0, step, chip + step))

    def line_receive(which, step):
        @pl.when(chip - 1 - step >= 0)
        def _():
            line_copy(which, 1, step, chip - 1 - step).wait_recv()
            side_copy(which, chip - 1 - step, core).start()

        @pl.when(chip + 1 + step <= chips - 1)
        def _():
            line_copy(which, 0, step, chip + 1 + step).wait_recv()
            side_copy(which, chip + 1 + step, core).start()

    def small_copy(peer, source):
        return send(
            smine_ref,
            srecv_ref.at[source],
            (small_sem.at[0, peer], small_sem.at[1, source]),
            {"ctx": peer},
        )

    def cross_copy(peer, source):
        return send(
            sgather_ref.at[group],
            sgather_ref.at[source],
            (cross_sem.at[0, peer], cross_sem.at[1, source]),
            {"fsdp": peer},
        )

    reduce_step(0)

    total_ref[...] = jnp.zeros(total_ref.shape, f32)

    def accumulate(piece, carry):
        unit_load(piece).wait()
        total_ref[...] += dot(dq_ref[piece // 2, lax.rem(piece, 2)], held_ref[lax.rem(piece, 2)])

        @pl.when(piece + 2 < parts)
        def _():
            unit_load(piece + 2).start()

        return carry

    lax.fori_loop(0, parts, accumulate, 0)
    u_ref[...] = total_ref[...].T.astype(bf16).reshape(u_ref.shape)
    for peer in group_peers:
        u_copy(peer, group).start()

    total = mlp_ref[chip].astype(f32)
    for peer in chip_peers:
        m_copy(chip, peer).wait_recv()
        total = total + mrecv_ref[peer].astype(f32)
    msum_ref[...] = total.astype(bf16)
    keep_copy(1).start()
    side_copy(1, chip, core, True).start()
    line_sends(1, 0, lambda copy: copy.start())

    total = u_ref[group].astype(f32)
    for peer in group_peers:
        u_copy(group, peer).wait_recv()
        total = total + urecv_ref[peer].astype(f32)
    usum_ref[...] = total.astype(bf16)
    keep_copy(0).start()
    side_copy(0, chip, core, True).start()
    line_sends(0, 0, lambda copy: copy.start())
    held = total.shape[0]
    gain = jnp.sum(total * wc_ref[...].astype(f32), axis=1, keepdims=True)
    column_ref[...] = jnp.zeros(column_ref.shape, f32)
    column_ref[:held, :] = jnp.broadcast_to(gain, (held, PAD))
    flat = column_ref[...].T[:1]
    smine_ref[...] = small_ref[...]
    for row in range(column_ref.shape[0] // PAD):
        smine_ref[row : row + 1, :] = flat[:, row * PAD : (row + 1) * PAD]
    for peer in ctx_peers:
        small_copy(peer, here).start()

    for step in range(1, chips):
        if step == 1:
            reduce_step(step)
        for which in range(2):
            line_receive(which, step - 1)
            if step <= chips - 2:
                line_sends(which, step, lambda copy: copy.start())
        if 1 < step <= chips - 2:
            reduce_step(step)
        if step == 1:
            small = smine_ref[...]
            for peer in ctx_peers:
                small_copy(here, peer).wait_recv()
                small = small + srecv_ref[peer]
            sgather_ref[group] = small
            for peer in group_peers:
                cross_copy(peer, group).start()

    for index in range(2):
        rows = partial(chip, index)
        own_ref[rows, :] = part_ref[rows, :].astype(bf16)

    for which in range(2):
        keep_copy(which).wait()
        for piece in range(chips):
            side_copy(which, piece, 1 - core).wait_recv()
            side_copy(which, piece, core).wait_send()
        for step in range(chips - 1):
            line_sends(which, step, lambda copy: copy.wait_send())
    for index in range(chips):
        pair_copy(index).wait_send()
    for peer in group_peers:
        cross_copy(group, peer).wait_recv()
        cross_copy(peer, group).wait_send()
        u_copy(peer, group).wait_send()
    for peer in chip_peers:
        m_copy(peer, chip).wait_send()
    for peer in ctx_peers:
        small_copy(peer, here).wait_send()
    for step in range(chips - 2):

        @pl.when(step >= chips - 1 - chip)
        def _():
            for index in range(2):
                sum_copy(0, step - (chips - 1) + chip, index).wait_send()

        @pl.when(step >= chip)
        def _():
            for index in range(2):
                sum_copy(1, chips - 1 - step + chip, index).wait_send()


def reduce_gradients(parts, groups, dqkv, w_pair, units, w_columns, small, chunks):
    chips = parts // 2
    mlp_shape = (chips, 3, chunks[0].shape[1] // chips, D)
    rows_dev = dqkv.shape[3]
    rows, width = w_columns.shape
    lanes = -(-rows // PAD) * PAD
    dma = pltpu.SemaphoreType.DMA
    anywhere = pl.BlockSpec(memory_space=pl.ANY)
    u_shape = (groups, rows, width)
    return pl.pallas_call(
        functools.partial(reduce_kernel, parts, groups),
        name="reduce_gradients",
        out_shape=[
            jax.ShapeDtypeStruct((rows_dev, D), bf16),
            jax.ShapeDtypeStruct((rows_dev, D), bf16),
            jax.ShapeDtypeStruct((rows_dev, D), bf16),
            jax.ShapeDtypeStruct((parts, rows, width), bf16),
            jax.ShapeDtypeStruct((parts,) + mlp_shape[1:], bf16),
            jax.ShapeDtypeStruct((groups,) + small.shape, f32),
        ],
        in_specs=[anywhere] * 3 + in_vmem(2) + [anywhere] * groups,
        out_specs=in_vmem(3) + [anywhere] * 2 + in_vmem(1),
        scratch_shapes=[
            pltpu.VMEM(dqkv.shape, bf16),
            pltpu.VMEM(w_pair.shape, bf16),
            pltpu.VMEM((groups,) + chunks[0].shape, bf16),
            pltpu.VMEM((2,) + units.shape[1:], bf16),
            pltpu.VMEM((width, D), f32),
            pltpu.VMEM(u_shape, bf16),
            pltpu.VMEM(u_shape[1:], bf16),
            pltpu.VMEM(mlp_shape[1:], bf16),
            pltpu.VMEM((chips,) + dqkv.shape[2:], bf16),
            pltpu.VMEM((chips + 1, rows_dev, D), bf16),
            pltpu.VMEM(u_shape, bf16),
            pltpu.VMEM(mlp_shape, bf16),
            pltpu.VMEM(mlp_shape, bf16),
            pltpu.VMEM((rows_dev, D), f32),
            pltpu.VMEM((lanes, PAD), f32),
            pltpu.VMEM(small.shape, f32),
            pltpu.VMEM((parts,) + small.shape, f32),
            dma((2, chips)),
            dma((2, 2, chips, 2)),
            dma((2, groups)),
            dma((2, chips)),
            dma((2, 2, 2, chips)),
            dma((2, 2, chips)),
            dma((2, parts)),
            dma((2, groups)),
            dma((groups + 2,)),
            dma((2,)),
            dma((2,)),
        ],
        compiler_params=pltpu.CompilerParams(
            vmem_limit_bytes=60 * 1024 * 1024, collective_id=1, has_side_effects=True
        ),
    )(dqkv, w_pair, units, w_columns, small, *chunks)


def update_kernel(rates, qkv_ref, gain_ref, mlp_ref, *refs):
    sets = len(rates)
    parts, rows, width = qkv_ref.shape
    width = width // 3
    for index, rate in enumerate(rates):
        weight, first, second = (ref[...] for ref in refs[3 * index : 3 * index + 3])
        if index == 0:
            pieces = [qkv_ref[part].astype(f32) for part in range(parts)]
            gradient = jnp.concatenate(
                [piece[:, at * width : (at + 1) * width] for at in range(3) for piece in pieces],
                axis=1,
            )
            gradient = gradient * gain_ref[...]
        else:
            gradient = mlp_ref[0, index - 1].astype(f32)
        outs = refs[3 * sets + 4 * index : 3 * sets + 4 * index + 4]
        new, first, second = adamw(weight, first, second, gradient, rate, decay_rate)
        outs[0][...] = new
        outs[1][...] = first
        outs[2][...] = second
        outs[3][...] = new.astype(bf16)


def update(rates, parts, qkv, gain, mlp, *arrays):
    rows = arrays[0].shape[0]
    chips = parts // 2
    step_rows = rows // parts
    if step_rows % 8 == 0:

        def owner(i):
            return (2 * lax.rem(i, chips) + i // chips, 0, 0, 0)

    else:
        step_rows = 32
        mlp = mlp.reshape(chips, 2, 3, rows // parts, D).transpose(2, 1, 0, 3, 4)
        mlp = mlp.reshape(3, rows // step_rows, step_rows, D).transpose(1, 0, 2, 3)

        def owner(i):
            return (i, 0, 0, 0)

    in_specs = [
        pl.BlockSpec((parts, step_rows, qkv.shape[2]), lambda i: (0, i, 0)),
        pl.BlockSpec((step_rows, 1), lambda i: (i, 0)),
        pl.BlockSpec((1, 3, step_rows, D), owner),
    ]
    specs, shapes, moved = [], [], 0
    for array in arrays:
        in_specs.append(pl.BlockSpec((step_rows, array.shape[1]), lambda i: (i, 0)))
    for index in range(len(rates)):
        shape = arrays[3 * index].shape
        shapes += [jax.ShapeDtypeStruct(shape, f32)] * 3 + [jax.ShapeDtypeStruct(shape, bf16)]
        specs += [pl.BlockSpec((step_rows, shape[1]), lambda i: (i, 0))] * 4
        moved += shape[0] * shape[1] * 28
    return pl.pallas_call(
        functools.partial(update_kernel, rates),
        name="update_weights",
        grid=(rows // step_rows,),
        in_specs=in_specs,
        out_specs=specs,
        out_shape=shapes,
        compiler_params=params(),
        cost_estimate=pl.CostEstimate(flops=moved, bytes_accessed=moved, transcendentals=0),
    )(qkv, gain, mlp, *arrays)


def finish_kernel(x_ref, dmid_ref, own_ref, down_ref, up_ref, layer_ref, out_ref, same_ref):
    rows = x_ref[...].astype(f32)
    scale = rms_scale(rows)
    unit = rows * scale
    dunit = own_ref[...].astype(f32) + down_ref[...].astype(f32) + up_ref[...].astype(f32)
    grad = dmid_ref[...] + scale * (
        dunit - unit * jnp.mean(dunit * unit, axis=-1, keepdims=True)
    )
    out_ref[...] = grad.astype(bf16)
    same_ref[...] = layer_ref[...]


def finish(*arrays):
    rows = arrays[0].shape[0]
    spec = pl.BlockSpec((PAD, D), lambda i: (i, 0))
    return pl.pallas_call(
        finish_kernel,
        name="finish",
        grid=(rows // PAD,),
        in_specs=[spec] * len(arrays),
        out_specs=[spec] * 2,
        out_shape=[jax.ShapeDtypeStruct((rows, D), bf16)] * 2,
        compiler_params=params(),
    )(*arrays)


def body(
    parts,
    groups,
    inputs,
    cotangent,
    block_order,
    w_qkv,
    m_qkv,
    v_qkv,
    w_out,
    m_out,
    v_out,
    w_up,
    m_up,
    v_up,
    w_down,
    m_down,
    v_down,
    small_params,
    small_m,
    small_v,
):
    heads = H // parts
    width = heads * HD
    rows_dev = inputs.shape[1]
    tokens = rows_dev * parts
    here = lax.axis_index("ctx")
    index = jnp.arange(block_order.shape[1], dtype=jnp.int32)
    slots = jnp.sum(jnp.where(block_order[0][None] == index[:, None], index[None], 0), axis=1)
    gain_one = small_params[:D]
    gain_two = small_params[D : 2 * D]
    query_scale = small_params[2 * D :]
    group = lax.axis_index("fsdp")
    rows = w_qkv.shape[0]

    gain_rows = lax.dynamic_slice_in_dim(gain_one, group * rows, rows, 0)[:, None]
    factor = scale_base / math.sqrt(HD) * jax.nn.softplus(query_scale)
    factor_two = (factor * LOG2E)[:, None]
    unit_all, mlp_full, w_pair, qt, kt, vt, kn, vn, w_columns = gather_rows(
        parts, groups, heads, inputs[0], w_qkv, gain_rows, w_out, w_up, w_down, factor_two
    )
    lse, mixed = attention_forward(slots, qt, kt, kn, vt, parts)
    kept = (qt, kt, kn, vn, lse)
    output, dmid, dmixed, gain_two_grad, *chunks = middle(
        parts,
        groups,
        mixed,
        inputs[0],
        cotangent[0],
        mlp_full.reshape(3, D, D),
        gain_two[None],
    )
    for step in range(1, groups):
        swap = [(i, i ^ step) for i in range(groups)]
        chunks[step] = lax.ppermute(chunks[step], "fsdp", swap)
    dqkv, dscale = attention_backward(slots, kept, mixed, dmixed, factor_two)
    scale_grad = (
        dscale[0, :HD]
        / factor_two[:, 0]
        * (scale_base / math.sqrt(HD))
        * jax.nn.sigmoid(query_scale)
    )
    lanes = -(-rows // PAD) * PAD
    small_rows = -(-(lanes + D + PAD) // (8 * PAD)) * 8
    small = jnp.concatenate([jnp.zeros((lanes,), f32), gain_two_grad[0], scale_grad])
    small = jnp.pad(small, (0, small_rows * PAD - small.shape[0])).reshape(small_rows, PAD)
    send_down, send_up, own_part, u_all, mlp_all, small_all = reduce_gradients(
        parts,
        groups,
        dqkv.reshape(parts // 2, 2, 3 * width, rows_dev),
        w_pair,
        unit_all,
        w_columns,
        small,
        chunks,
    )
    got_down = lax.ppermute(send_down, "ctx", [(i, i - 2) for i in range(2, parts)])
    got_up = lax.ppermute(send_up, "ctx", [(i, i + 2) for i in range(parts - 2)])
    rate_qkv = qkv_rate_base / math.sqrt(D)
    rate_out = 0.5 / math.sqrt(max(D // 256, 1))
    rate_up = 0.5 / math.sqrt(D)
    rate_down = 0.5 / math.sqrt(FF)
    updated = update(
        (rate_qkv, rate_out, rate_up, rate_down),
        parts,
        u_all,
        gain_rows,
        mlp_all,
        w_qkv,
        m_qkv,
        v_qkv,
        w_out,
        m_out,
        v_out,
        w_up,
        m_up,
        v_up,
        w_down,
        m_down,
        v_down,
    )
    flat = small_all.reshape(groups, small_rows * PAD)
    rest = jnp.sum(flat[:, lanes : lanes + D + HD], axis=0)
    small_total = jnp.concatenate([flat[:, :rows].reshape(D), rest])
    small_set = adamw(small_params, small_m, small_v, small_total, small_rate, 0.0)
    input_grad, output = finish(inputs[0], dmid, own_part, got_down, got_up, output)
    return (
        output[None],
        input_grad[None],
        *updated,
        *small_set,
    )


def solution(mesh):
    rows = P("fsdp", "ctx", None)
    weight = P("fsdp", None)
    return jax.shard_map(
        functools.partial(body, mesh.shape["ctx"], mesh.shape["fsdp"]),
        mesh=mesh,
        in_specs=(rows, rows, weight) + (weight,) * 12 + (P(),) * 3,
        out_specs=(rows, rows) + (weight,) * 16 + (P(),) * 3,
        check_vma=False,
    )
```

```python
import functools
import math

import jax
import jax.numpy as jnp
from jax import lax
from jax.experimental import pallas as pl
from jax.experimental.pallas import tpu as pltpu
from jax.sharding import PartitionSpec as P

D = 1280
H = 16
HD = 80
FF = 1280
BLOCK = 256
CONT = 512
STEP = 3
PAD = 128
EXTRA = 16
TILE = CONT
SCORE_BOUND = 96.0

bf16 = jnp.bfloat16
f32 = jnp.float32

norm_eps = 1e-06
beta_one = 0.5
beta_two = 0.5
adam_eps = 1e-08
decay_rate = 0.1
small_rate = 0.75
qkv_rate_base = 1.0
scale_base = 1.442695
LOG2E = math.log2(math.e)
LN2 = math.log(2.0)


def rms_scale(values):
    return lax.rsqrt(jnp.mean(values * values, axis=-1, keepdims=True) + norm_eps)


def adamw(weight, first, second, gradient, step_rate, decay_on):
    first_new = beta_one * first + (1.0 - beta_one) * gradient
    second_new = beta_two * second + (1.0 - beta_two) * gradient * gradient
    corr_one = 1.0 - beta_one**STEP
    corr_two = 1.0 - beta_two**STEP
    update = first_new / corr_one / (jnp.sqrt(second_new / corr_two) + adam_eps)
    weight_new = weight - step_rate * (update + decay_on * weight)
    return (weight_new, first_new, second_new)


def dot(left, right, contract=(1, 0)):
    return lax.dot_general(
        left, right, (((contract[0],), (contract[1],)), ((), ())), preferred_element_type=f32
    )


def fill_slots(order_ref, slot_ref):
    def place(slot, carry):
        slot_ref[order_ref[slot]] = slot
        return carry

    lax.fori_loop(0, order_ref.shape[0], place, 0)


def three_rows(row):
    high = row.astype(bf16)
    rest = row - high.astype(f32)
    middle = rest.astype(bf16)
    low = (rest - middle.astype(f32)).astype(bf16)
    index = lax.broadcasted_iota(jnp.int32, (EXTRA, row.shape[1]), 0)
    zero = jnp.zeros((EXTRA, row.shape[1]), f32)
    rows = jnp.where(index == 0, high.astype(f32), zero)
    rows = jnp.where(index == 1, middle.astype(f32), rows)
    rows = jnp.where(index == 2, low.astype(f32), rows)
    return rows.astype(bf16)


def tile_at(tile):
    return pl.ds(pl.multiple_of(tile * TILE, TILE), TILE)


def block_at(slot):
    return pl.ds(pl.multiple_of(slot * BLOCK, BLOCK), BLOCK)


def tile_lanes(ref, head, slot_ref, tile, rows=slice(None)):
    first, second = slot_ref[2 * tile], slot_ref[2 * tile + 1]
    return jnp.concatenate(
        [ref[head, rows, block_at(first)], ref[head, rows, block_at(second)]], axis=1
    )


def tile_rows(ref, head, slot_ref, tile):
    first, second = slot_ref[2 * tile], slot_ref[2 * tile + 1]
    return jnp.concatenate([ref[head, block_at(first), :], ref[head, block_at(second), :]], axis=0)


def half_at(slot):
    return pl.ds(pl.multiple_of(lax.rem(slot, 2) * BLOCK, BLOCK), BLOCK)


def causal(shape):
    key = lax.broadcasted_iota(jnp.int32, shape, 0)
    query = lax.broadcasted_iota(jnp.int32, shape, 1)
    return key <= query


def gather_kernel(
    parts,
    groups,
    heads,
    x_ref,
    wqkv_ref,
    wout_ref,
    wup_ref,
    wdown_ref,
    small_ref,
    unit_ref,
    full_ref,
    wpair_ref,
    qt_out_ref,
    kt_out_ref,
    vt_out_ref,
    kn_out_ref,
    vn_out_ref,
    wcol_ref,
    gain_ref,
    factor_ref,
    qt_ref,
    kt_ref,
    vt_ref,
    kn_ref,
    vn_ref,
    rows_ref,
    wstage_ref,
    mstage_ref,
    gained_ref,
    mlp_ref,
    wrecv_ref,
    wflip_ref,
    line_sem,
    side_sem,
    keep_sem,
    w_sem,
    lane_sem,
    mlp_sem,
    cross_sem,
    own_sem,
    stage_sem,
    lanes_sem,
    sides_sem,
):
    chips = parts // 2
    here = lax.axis_index("ctx")
    group = lax.axis_index("fsdp")
    core = lax.rem(here, 2)
    chip = here // 2
    other = here + 1 - 2 * core
    width = heads * HD
    group_peers = [lax.rem(group + step, groups) for step in range(1, groups)]

    barrier = pltpu.get_barrier_semaphore()
    pl.semaphore_signal(barrier, inc=1, device_id={"ctx": other})
    for peer in group_peers:
        pl.semaphore_signal(barrier, inc=1, device_id={"fsdp": peer})
    for step in (1, chips - 1):
        peer = lax.rem(chip + step, chips) * 2 + core
        pl.semaphore_signal(barrier, inc=1, device_id={"ctx": peer})
    pl.semaphore_wait(barrier, groups + 2)

    def send(source, target, sems, device):
        return pltpu.make_async_remote_copy(
            src_ref=source,
            dst_ref=target,
            send_sem=sems[0],
            recv_sem=sems[1],
            device_id=device,
        )

    halves = rows_ref.shape[1] // BLOCK

    def line_copy(way, step, piece, part):
        ref = rows_ref.at[2 * piece + core, block_at(part)]
        sems = (line_sem.at[0, way, step, part], line_sem.at[1, way, step, part])
        return send(ref, ref, sems, {"ctx": here + (2 if way else -2)})

    def side_copy(piece, lane, part):
        ref = rows_ref.at[2 * piece + lane, block_at(part)]
        sems = (side_sem.at[0, piece, part], side_sem.at[1, piece, part])
        return send(ref, ref, sems, {"ctx": other})

    def results(slot):
        to = block_at(slot)
        copies = [
            pltpu.make_async_copy(ref.at[:, :, to], out.at[:, :, to], lanes_sem.at[index, slot])
            for index, (ref, out) in enumerate(
                ((qt_ref, qt_out_ref), (kt_ref, kt_out_ref), (vt_ref, vt_out_ref))
            )
        ]
        return copies + [
            pltpu.make_async_copy(ref.at[:, to], out.at[:, to], sides_sem.at[index, slot])
            for index, (ref, out) in enumerate(((kn_ref, kn_out_ref), (vn_ref, vn_out_ref)))
        ]

    def w_copy(peer, source):
        sems = (w_sem.at[0, peer], w_sem.at[1, source])
        return send(gained_ref, wrecv_ref.at[source], sems, {"fsdp": peer})

    def lane_copy(lane):
        ref = wpair_ref.at[lane]
        return send(ref, ref, (lane_sem.at[0], lane_sem.at[1]), {"ctx": other})

    def mlp_copy(peer, source):
        sems = (mlp_sem.at[0, peer], mlp_sem.at[1, source])
        return send(mlp_ref.at[:, core], full_ref.at[:, source, core], sems, {"fsdp": peer})

    def cross_copy(source, lane):
        ref = full_ref.at[:, source, lane]
        sems = (cross_sem.at[0, source], cross_sem.at[1, source])
        return send(ref, ref, sems, {"ctx": other})

    def keep_copy(piece):
        return pltpu.make_async_copy(rows_ref.at[piece], unit_ref.at[piece], keep_sem.at[piece])

    own_copy = pltpu.make_async_copy(mlp_ref, full_ref.at[:, group], own_sem)

    stages = [pltpu.make_async_copy(wqkv_ref, wstage_ref, stage_sem.at[0])] + [
        pltpu.make_async_copy(ref, mstage_ref.at[index], stage_sem.at[index + 1])
        for index, ref in enumerate((wout_ref, wup_ref, wdown_ref))
    ]
    for stage in stages:
        stage.start()
    rows = x_ref[...].astype(f32)
    rows_ref[here] = (rows * rms_scale(rows)).astype(bf16)

    def forward(way, step, piece, part):
        @pl.when((chip < chips - 1) if way else (chip > 0))
        def _():
            line_copy(way, step, piece, part).start()

    for part in range(halves):
        for way in range(2):
            forward(way, 0, chip, part)
        side_copy(chip, core, part).start()
    held = gain_ref.shape[0]
    lanes = -(-held // PAD) * PAD
    gains = jnp.broadcast_to(small_ref[:, :D], (8, D))
    gains = pltpu.roll(gains, lax.rem(D - group * held, D), 1)[:1, :lanes]
    gain_ref[...] = jnp.broadcast_to(gains, (PAD, lanes)).T[:held, :1]
    soft = jnp.log(1.0 + jnp.exp(small_ref[:, 2 * D :])) * (scale_base / math.sqrt(HD) * LOG2E)
    soft = jnp.concatenate([soft, jnp.zeros((1, PAD - HD), f32)], axis=1)
    factor_ref[...] = jnp.broadcast_to(soft, (PAD, PAD)).T[:HD, :1]
    shift = lax.rem(D - here * width, D)
    stages[0].wait()
    for part in range(3):
        turned = pltpu.roll(wstage_ref[:, part * D : (part + 1) * D], shift, 1)
        gained_ref[part] = (turned[:, :width] * gain_ref[...]).astype(bf16)
        wcol_ref[:, part * width : (part + 1) * width] = turned[:, :width].astype(bf16)
    for peer in group_peers:
        w_copy(peer, group).start()
    for index in range(3):
        stages[index + 1].wait()
        mlp_ref[index] = mstage_ref[index].astype(bf16).reshape(mlp_ref.shape[1:])
    own_copy.start()
    keep_copy(here).start()
    wrecv_ref[group] = gained_ref[...]
    for peer in group_peers:
        w_copy(group, peer).wait_recv()
    for peer in group_peers:
        mlp_copy(peer, group).start()
    for part in range(3):
        flipped = wrecv_ref[:, part].reshape(D, width).T
        wflip_ref[part * width : (part + 1) * width] = flipped
    wpair_ref[core] = wflip_ref[...]
    lane_copy(core).start()

    extra_row = lax.broadcasted_iota(jnp.int32, (PAD - HD, BLOCK), 0)
    extra = jnp.where(extra_row < 3, 1.0, 0.0)
    spare = jnp.zeros((PAD - HD, BLOCK), bf16)

    def project(piece, part):
        slot = piece * halves + part
        to = block_at(slot)
        result = dot(wflip_ref[...], rows_ref[piece, block_at(part), :], (1, 1))
        for head in range(heads):
            query, key, value = (
                result[share * width + head * HD : share * width + (head + 1) * HD]
                for share in range(3)
            )
            qt_ref[head, :HD, to] = (query * factor_ref[...]).astype(bf16)
            qt_ref[head, HD:, to] = spare
            kt_ref[head, :, to] = key.astype(bf16)
            vt_ref[head, :HD, to] = value.astype(bf16)
            vt_ref[head, HD:, to] = jnp.ones((EXTRA, BLOCK), bf16)
            kn_ref[head, to, :] = jnp.concatenate([key, extra], axis=0).T.astype(bf16)
            vn_ref[head, to, :] = jnp.concatenate([value, extra], axis=0).T.astype(bf16)
        for copy in results(slot):
            copy.start()

    def visit(index, carry):
        distance, part = index // halves, lax.rem(index, halves)
        for way in range(2):
            piece = chip - distance if way else chip + distance
            valid = (piece >= 0) if way else (piece <= chips - 1)

            @pl.when(valid & (distance > 0))
            def _():
                line_copy(way, distance - 1, piece, part).wait_recv()
                side_copy(piece, core, part).start()
                forward(way, distance, piece, part)

                @pl.when(part == halves - 1)
                def _():
                    keep_copy(2 * piece + core).start()

        for way in range(2):
            piece = chip - distance if way else chip + distance
            valid = (piece >= 0) if way else ((piece <= chips - 1) & (distance > 0))

            @pl.when(valid)
            def _():
                project(2 * piece + core, part)
                side_copy(piece, 1 - core, part).wait_recv()
                project(2 * piece + 1 - core, part)

                @pl.when(part == halves - 1)
                def _():
                    keep_copy(2 * piece + 1 - core).start()

        return carry

    lax.fori_loop(0, chips * halves, visit, 0)

    for peer in group_peers:
        mlp_copy(group, peer).wait_recv()
        cross_copy(peer, core).start()
    for peer in group_peers:
        cross_copy(peer, 1 - core).wait_recv()
        cross_copy(peer, core).wait_send()
        w_copy(peer, group).wait_send()
        mlp_copy(peer, group).wait_send()
    own_copy.wait()
    lane_copy(1 - core).wait_recv()
    lane_copy(core).wait_send()

    def drain(piece, carry):
        keep_copy(2 * piece).wait()
        keep_copy(2 * piece + 1).wait()
        for part in range(halves):
            side_copy(piece, core, part).wait_send()

            @pl.when((piece <= chip) & (chip < chips - 1))
            def _():
                line_copy(1, chip - piece, piece, part).wait_send()

            @pl.when((piece >= chip) & (chip > 0))
            def _():
                line_copy(0, piece - chip, piece, part).wait_send()

        return carry

    lax.fori_loop(0, chips, drain, 0)

    def settle(slot, carry):
        for copy in results(slot):
            copy.wait()
        return carry

    lax.fori_loop(0, 2 * chips * halves, settle, 0)


def gather_rows(parts, groups, heads, rows, w_qkv, w_out, w_up, w_down, small):
    rows_dev = rows.shape[0]
    held = w_qkv.shape[0]
    tokens = parts * rows_dev
    dma = pltpu.SemaphoreType.DMA
    chips = parts // 2
    anywhere = pl.BlockSpec(memory_space=pl.ANY)
    return pl.pallas_call(
        functools.partial(gather_kernel, parts, groups, heads),
        name="gather_rows",
        out_shape=[
            jax.ShapeDtypeStruct((parts, rows_dev, D), bf16),
            jax.ShapeDtypeStruct((3, groups, 2, held // 2, D), bf16),
            jax.ShapeDtypeStruct((2, 3 * heads * HD, D), bf16),
            jax.ShapeDtypeStruct((heads, PAD, tokens), bf16),
            jax.ShapeDtypeStruct((heads, HD, tokens), bf16),
            jax.ShapeDtypeStruct((heads, HD + EXTRA, tokens), bf16),
            jax.ShapeDtypeStruct((heads, tokens, PAD), bf16),
            jax.ShapeDtypeStruct((heads, tokens, PAD), bf16),
            jax.ShapeDtypeStruct((held, 3 * heads * HD), bf16),
            jax.ShapeDtypeStruct((held, 1), f32),
            jax.ShapeDtypeStruct((HD, 1), f32),
        ],
        in_specs=in_vmem(1) + [anywhere] * 4 + in_vmem(1),
        out_specs=[anywhere] * 2 + in_vmem(1) + [anywhere] * 5 + in_vmem(3),
        scratch_shapes=[
            pltpu.VMEM((heads, PAD, tokens), bf16),
            pltpu.VMEM((heads, HD, tokens), bf16),
            pltpu.VMEM((heads, HD + EXTRA, tokens), bf16),
            pltpu.VMEM((heads, tokens, PAD), bf16),
            pltpu.VMEM((heads, tokens, PAD), bf16),
            pltpu.VMEM((parts, rows_dev, D), bf16),
            pltpu.VMEM((held, 3 * D), f32),
            pltpu.VMEM((3, held, D), f32),
            pltpu.VMEM((3, held, heads * HD), bf16),
            pltpu.VMEM((3, 2, held // 2, D), bf16),
            pltpu.VMEM((groups, 3, held, heads * HD), bf16),
            pltpu.VMEM((3 * heads * HD, D), bf16),
            dma((2, 2, chips, rows_dev // BLOCK)),
            dma((2, chips, rows_dev // BLOCK)),
            dma((parts,)),
            dma((2, groups)),
            dma((2,)),
            dma((2, groups)),
            dma((2, groups)),
            dma,
            dma((4,)),
            dma((3, tokens // BLOCK)),
            dma((2, tokens // BLOCK)),
        ],
        compiler_params=pltpu.CompilerParams(
            vmem_limit_bytes=60 * 1024 * 1024, collective_id=2, has_side_effects=True
        ),
    )(rows, w_qkv, w_out, w_up, w_down, small)


def forward_kernel(
    heads,
    order_ref,
    qt_ref,
    kt_ref,
    kn_in_ref,
    vt_in_ref,
    lse_ref,
    ot_ref,
    slot_ref,
    kn_ref,
    vt_ref,
    acc_ref,
    top_ref,
    load_sem,
):
    loads = [
        pltpu.make_async_copy(source, target, load_sem.at[index])
        for index, (source, target) in enumerate(((kn_in_ref, kn_ref), (vt_in_ref, vt_ref)))
    ]
    for load in loads:
        load.start()
    fill_slots(order_ref, slot_ref)
    tokens = kn_ref.shape[1]
    num_tiles = tokens // TILE
    prompt_tiles = num_tiles // 2

    def longest(ref):
        def visit(slot, most):
            rows = [ref[head, :HD, block_at(slot)].astype(f32) for head in range(heads)]
            sums = [jnp.sum(row * row, axis=0, keepdims=True) for row in rows]
            return functools.reduce(jnp.maximum, sums, most)

        return jnp.max(lax.fori_loop(0, tokens // BLOCK, visit, jnp.zeros((1, BLOCK), f32)))

    bounded = longest(qt_ref) * longest(kt_ref) <= SCORE_BOUND * SCORE_BOUND

    for load in loads:
        load.wait()

    def run(shifted):
        def query_tile(tile, carry):
            queries = [tile_lanes(qt_ref, head, slot_ref, tile) for head in range(heads)]
            if shifted:
                top_ref[...] = jnp.full(top_ref.shape, -1e30, f32)
            else:
                top_ref[...] = jnp.zeros(top_ref.shape, f32)
            acc_ref[...] = jnp.zeros(acc_ref.shape, f32)

            def step(key_rows, value_lanes, start, masked):
                scores = [dot(key_rows[head], queries[head][:, start:]) for head in range(heads)]
                if masked:
                    allowed = causal(scores[0].shape)
                    scores = [jnp.where(allowed, score, -1e30) for score in scores]
                if shifted:
                    olds = [top_ref[head, :, start:] for head in range(heads)]
                    tops = [
                        jnp.maximum(old, jnp.max(score, axis=0, keepdims=True))
                        for old, score in zip(olds, scores)
                    ]
                    scores = [score - top for score, top in zip(scores, tops)]
                    for head in range(heads):
                        acc_ref[head, :, start:] *= jnp.exp2(olds[head] - tops[head])
                        top_ref[head, :, start:] = tops[head]
                probs = [jnp.exp2(score).astype(bf16) for score in scores]
                for head in range(heads):
                    acc_ref[head, :, start:] += dot(value_lanes[head], probs[head])

            def full(key_tile, inner):
                step(
                    [tile_rows(kn_ref, head, slot_ref, key_tile) for head in range(heads)],
                    [tile_lanes(vt_ref, head, slot_ref, key_tile) for head in range(heads)],
                    0,
                    False,
                )
                return inner

            lax.fori_loop(0, jnp.minimum(tile, prompt_tiles), full, 0)
            for part in range(TILE // BLOCK):
                block = block_at(slot_ref[tile * (TILE // BLOCK) + part])
                step(
                    [kn_ref[head, block, :] for head in range(heads)],
                    [vt_ref[head, :, block] for head in range(heads)],
                    part * BLOCK,
                    True,
                )
            for head in range(heads):
                acc = acc_ref[head]
                mass = acc[HD : HD + 1]
                mixed = (acc[:HD] / mass).astype(bf16)
                lse_ref[head, :, tile_at(tile)] = top_ref[head] + jnp.log2(mass)
                for part in range(TILE // BLOCK):
                    slot = slot_ref[tile * (TILE // BLOCK) + part]
                    ot_ref[slot // 2, head * HD : (head + 1) * HD, half_at(slot)] = mixed[
                        :, part * BLOCK : (part + 1) * BLOCK
                    ]
            return carry

        lax.fori_loop(0, num_tiles, query_tile, 0)

    @pl.when(bounded)
    def _():
        run(False)

    @pl.when(jnp.logical_not(bounded))
    def _():
        run(True)


def backward_kernel(
    heads,
    order_ref,
    qt_ref,
    kt_in_ref,
    kn_in_ref,
    vn_in_ref,
    lse_ref,
    ot_ref,
    dt_ref,
    factor_ref,
    dqkv_ref,
    dscale_ref,
    slot_ref,
    kt_ref,
    kn_ref,
    vn_ref,
    qa_ref,
    da_ref,
    dq_ref,
    dk_ref,
    dv_ref,
    scale_ref,
    load_sem,
):
    loads = [
        pltpu.make_async_copy(source, target, load_sem.at[index])
        for index, (source, target) in enumerate(
            ((kn_in_ref, kn_ref), (vn_in_ref, vn_ref), (kt_in_ref, kt_ref))
        )
    ]
    for load in loads:
        load.start()
    fill_slots(order_ref, slot_ref)
    tokens = kn_ref.shape[1]
    num_blocks = tokens // BLOCK
    num_tiles = tokens // TILE
    prompt_tiles = num_tiles // 2
    width = heads * HD

    def prepare(block, carry):
        slot = slot_ref[block]
        to = pl.ds(pl.multiple_of(block * BLOCK, BLOCK), BLOCK)
        for head in range(heads):
            rows = slice(head * HD, (head + 1) * HD)
            grad = dt_ref[slot // 2, rows, half_at(slot)]
            mixed = ot_ref[slot // 2, rows, half_at(slot)]
            delta = jnp.sum(grad.astype(f32) * mixed.astype(f32), axis=0, keepdims=True)
            da_ref[head, :HD, to] = grad
            da_ref[head, HD : HD + EXTRA, to] = three_rows(-delta)
            da_ref[head, HD + EXTRA :, to] = jnp.zeros((PAD - HD - EXTRA, BLOCK), bf16)
            qa_ref[head, :HD, to] = qt_ref[head, :HD, block_at(slot)]
            qa_ref[head, HD : HD + EXTRA, to] = three_rows(-lse_ref[head, :, to])
            qa_ref[head, HD + EXTRA :, to] = jnp.zeros((PAD - HD - EXTRA, BLOCK), bf16)
        return carry

    lax.fori_loop(0, num_blocks, prepare, 0)
    dk_ref[...] = jnp.zeros(dk_ref.shape, f32)
    dv_ref[...] = jnp.zeros(dv_ref.shape, f32)
    scale_ref[...] = jnp.zeros(scale_ref.shape, f32)
    for load in loads:
        load.wait()

    def query_tile(tile, carry):
        here = tile_at(tile)
        dq_ref[...] = jnp.zeros(dq_ref.shape, f32)

        def step(keys, key_rows, key_lanes, value_rows, start, masked):
            to = pl.ds(pl.multiple_of(tile * TILE + start, BLOCK), TILE - start)
            queries = [qa_ref[head, :, to] for head in range(heads)]
            grads = [da_ref[head, :, to] for head in range(heads)]
            scores = [dot(key_rows[head], queries[head]) for head in range(heads)]
            spreads = [dot(value_rows[head], grads[head]) for head in range(heads)]
            probs = [jnp.exp2(score) for score in scores]
            if masked:
                allowed = causal(scores[0].shape)
                probs = [jnp.where(allowed, prob, 0.0) for prob in probs]
            dscores = [(prob * spread).astype(bf16) for prob, spread in zip(probs, spreads)]
            for head in range(heads):
                dv_ref[head, :, keys] += dot(grads[head][:HD], probs[head].astype(bf16), (1, 1))
                dk_ref[head, :, keys] += dot(queries[head][:HD], dscores[head], (1, 1))
                dq_ref[head, :, start:] += dot(key_lanes[head], dscores[head])

        def full(key_tile, inner):
            step(
                tile_at(key_tile),
                [tile_rows(kn_ref, head, slot_ref, key_tile) for head in range(heads)],
                [tile_lanes(kt_ref, head, slot_ref, key_tile) for head in range(heads)],
                [tile_rows(vn_ref, head, slot_ref, key_tile) for head in range(heads)],
                0,
                False,
            )
            return inner

        lax.fori_loop(0, jnp.minimum(tile, prompt_tiles), full, 0)
        for part in range(TILE // BLOCK):
            position = tile * (TILE // BLOCK) + part
            block = block_at(slot_ref[position])
            step(
                block_at(position),
                [kn_ref[head, block, :] for head in range(heads)],
                [kt_ref[head, :, block] for head in range(heads)],
                [vn_ref[head, block, :] for head in range(heads)],
                part * BLOCK,
                True,
            )
        for head in range(heads):
            dq = dq_ref[head]
            product = dq * qa_ref[head, :HD, here].astype(f32)
            for lane in range(TILE // PAD):
                scale_ref[head] += product[:, lane * PAD : (lane + 1) * PAD]
            scaled = (dq * (factor_ref[...] * LN2)).astype(bf16)
            for part in range(TILE // BLOCK):
                slot = slot_ref[tile * (TILE // BLOCK) + part]
                dqkv_ref[slot // 2, head * HD : (head + 1) * HD, half_at(slot)] = scaled[
                    :, part * BLOCK : (part + 1) * BLOCK
                ]
        return carry

    lax.fori_loop(0, num_tiles, query_tile, 0)

    def finish(block, carry):
        slot = slot_ref[block]
        owner, to = slot // 2, half_at(slot)
        at = pl.ds(pl.multiple_of(block * BLOCK, BLOCK), BLOCK)
        for head in range(heads):
            row = width + head * HD
            dqkv_ref[owner, row : row + HD, to] = (dk_ref[head, :, at] * LN2).astype(bf16)
            row = 2 * width + head * HD
            dqkv_ref[owner, row : row + HD, to] = dv_ref[head, :, at].astype(bf16)
        return carry

    lax.fori_loop(0, num_blocks, finish, 0)
    sums = functools.reduce(jnp.add, [scale_ref[head] for head in range(heads)])
    sums = jnp.concatenate([sums, jnp.zeros((PAD - HD, PAD), f32)], axis=0).T
    dscale_ref[...] = jnp.sum(sums, axis=0, keepdims=True)


def in_vmem(count):
    return [pl.BlockSpec(memory_space=pltpu.VMEM)] * count


def params():
    return pltpu.CompilerParams(vmem_limit_bytes=60 * 1024 * 1024)


def attention_forward(order, qt, kt, kn, vt, parts):
    heads, tokens = kn.shape[:2]
    return pl.pallas_call(
        functools.partial(forward_kernel, heads),
        name="attention_forward",
        out_shape=[
            jax.ShapeDtypeStruct((heads, 1, tokens), f32),
            jax.ShapeDtypeStruct((parts, heads * HD, tokens // parts), bf16),
        ],
        in_specs=[pl.BlockSpec(memory_space=pltpu.SMEM)]
        + in_vmem(2)
        + [pl.BlockSpec(memory_space=pl.ANY)] * 2,
        out_specs=in_vmem(2),
        scratch_shapes=[
            pltpu.SMEM(order.shape, jnp.int32),
            pltpu.VMEM(kn.shape, bf16),
            pltpu.VMEM(vt.shape, bf16),
            pltpu.VMEM((heads, HD + EXTRA, TILE), f32),
            pltpu.VMEM((heads, 1, TILE), f32),
            pltpu.SemaphoreType.DMA((2,)),
        ],
        compiler_params=params(),
        cost_estimate=attention_cost(heads, tokens, 2),
    )(order, qt, kt, kn, vt)


def attention_cost(heads, tokens, passes):
    pairs = heads * tokens * tokens // 2
    return pl.CostEstimate(
        flops=2 * passes * pairs * BLOCK, bytes_accessed=tokens * D, transcendentals=pairs
    )


def attention_backward(order, kept, mixed, dmixed, factor):
    qt, kt, kn, vn, lse = kept
    heads, tokens = kn.shape[:2]
    return pl.pallas_call(
        functools.partial(backward_kernel, heads),
        name="attention_backward",
        out_shape=[
            jax.ShapeDtypeStruct((mixed.shape[0], 3 * heads * HD, mixed.shape[2]), bf16),
            jax.ShapeDtypeStruct((1, PAD), f32),
        ],
        in_specs=[pl.BlockSpec(memory_space=pltpu.SMEM)]
        + in_vmem(1)
        + [pl.BlockSpec(memory_space=pl.ANY)] * 3
        + in_vmem(4),
        out_specs=in_vmem(2),
        scratch_shapes=[
            pltpu.SMEM(order.shape, jnp.int32),
            pltpu.VMEM(kt.shape, bf16),
            pltpu.VMEM(kn.shape, bf16),
            pltpu.VMEM(vn.shape, bf16),
            pltpu.VMEM((heads, PAD, tokens), bf16),
            pltpu.VMEM((heads, PAD, tokens), bf16),
            pltpu.VMEM((heads, HD, TILE), f32),
            pltpu.VMEM((heads, HD, tokens), f32),
            pltpu.VMEM((heads, HD, tokens), f32),
            pltpu.VMEM((heads, HD, PAD), f32),
            pltpu.SemaphoreType.DMA((3,)),
        ],
        compiler_params=params(),
        cost_estimate=attention_cost(heads, tokens, 5),
    )(order, qt, kt, kn, vn, lse, mixed, dmixed, factor)


def middle_kernel(
    parts,
    groups,
    mixed_ref,
    x_ref,
    dy_ref,
    weights_ref,
    gain_ref,
    *refs,
):
    out_ref, dmid_ref, dmixed_ref, gain_grad_ref = refs[:4]
    chunk_refs = refs[4 : 4 + groups]
    (
        w_ref,
        attn_ref,
        dattn_ref,
        act_ref,
        normed_ref,
        dhidden_ref,
        dbranch_ref,
        grad_ref,
        theirs_ref,
        w_sem,
        attn_sem,
        dattn_sem,
        pair_sem,
    ) = refs[4 + groups :]
    here = lax.axis_index("ctx")
    group = lax.axis_index("fsdp")
    core = lax.rem(here, 2)
    other = here + 1 - 2 * core
    peers = [lax.rem(here + step, parts) for step in range(1, parts)]
    tokens = x_ref.shape[0]
    width = mixed_ref.shape[1]
    held = theirs_ref.shape[2]
    loads = [
        pltpu.make_async_copy(weights_ref.at[index], w_ref.at[index], w_sem.at[index])
        for index in range(3)
    ]
    for load in loads:
        load.start()

    barrier = pltpu.get_barrier_semaphore()
    for peer in peers:
        pl.semaphore_signal(barrier, inc=1, device_id={"ctx": peer})
    pl.semaphore_wait(barrier, parts - 1)

    def lanes(part):
        return pl.ds(pl.multiple_of(part * BLOCK, BLOCK), BLOCK)

    def attn_copy(part, peer, source):
        return pltpu.make_async_remote_copy(
            src_ref=mixed_ref.at[peer, :, lanes(part)],
            dst_ref=attn_ref.at[source, :, lanes(part)],
            send_sem=attn_sem.at[0, part, peer],
            recv_sem=attn_sem.at[1, part, source],
            device_id={"ctx": peer},
        )

    def dattn_copy(part, peer, source):
        return pltpu.make_async_remote_copy(
            src_ref=dattn_ref.at[peer, :, lanes(part)],
            dst_ref=dmixed_ref.at[source, :, lanes(part)],
            send_sem=dattn_sem.at[0, part, peer],
            recv_sem=dattn_sem.at[1, part, source],
            device_id={"ctx": peer},
        )

    def rows_of(owner, lane):
        start = pl.multiple_of((owner * 2 + lane) * held, 16)
        return pl.ds(start, held)

    def pair_copy(index, owner, lane):
        return pltpu.make_async_remote_copy(
            src_ref=grad_ref.at[index, rows_of(owner, lane), :],
            dst_ref=theirs_ref.at[index, owner],
            send_sem=pair_sem.at[0, index, owner],
            recv_sem=pair_sem.at[1, index, owner],
            device_id={"ctx": other},
        )

    for part in range(tokens // BLOCK):
        for peer in peers:
            attn_copy(part, peer, here).start()
    attn_ref[here] = mixed_ref[here]
    gain_grad_ref[...] = jnp.zeros(gain_grad_ref.shape, f32)
    for load in loads:
        load.wait()
    gain = gain_ref[...]

    def layer(part, carry):
        rows = lanes(part)
        for peer in peers:
            attn_copy(part, here, peer).wait_recv()
        attn = attn_ref[:, :, rows].reshape(D, BLOCK)
        mid = x_ref[rows, :].astype(f32) + dot(attn, w_ref[0], (0, 0))
        scale = rms_scale(mid)
        unit = mid * scale
        normed = (unit * gain).astype(bf16)
        normed_ref[rows, :] = normed
        hidden = dot(normed, w_ref[1])
        gate = jax.nn.sigmoid(hidden)
        act = (hidden * gate).astype(bf16)
        act_ref[rows, :] = act
        dy = dy_ref[rows, :]
        dact = dot(dy, w_ref[2], (1, 1))
        dhidden = (dact * gate * (1.0 + hidden * (1.0 - gate))).astype(bf16)
        dhidden_ref[rows, :] = dhidden
        dnormed = dot(dhidden, w_ref[1], (1, 1))
        dunit = dnormed * gain
        dmid = dy.astype(f32) + scale * (
            dunit - unit * jnp.mean(dunit * unit, axis=-1, keepdims=True)
        )
        dmid_ref[rows, :] = dmid
        dbranch = dmid.astype(bf16)
        dbranch_ref[rows, :] = dbranch
        dattn = dot(w_ref[0], dbranch, (1, 1)).astype(bf16).reshape(parts, width, BLOCK)
        dattn_ref[:, :, rows] = dattn
        for peer in peers:
            dattn_copy(part, peer, here).start()
        dmixed_ref[here, :, rows] = dattn_ref[here, :, rows]
        out_ref[rows, :] = (mid + dot(act, w_ref[2])).astype(bf16)
        gain_grad_ref[...] += jnp.sum(dnormed * unit, axis=0, keepdims=True)
        return carry

    lax.fori_loop(0, tokens // BLOCK, layer, 0)

    def down_rows(index, carry):
        rows = lanes(index)
        grad_ref[2, rows, :] = dot(act_ref[:, rows], dy_ref[...], (0, 0)).astype(bf16)
        return carry

    def up_rows(index, carry):
        rows = lanes(index)
        grad_ref[1, rows, :] = dot(normed_ref[:, rows], dhidden_ref[...], (0, 0)).astype(bf16)
        return carry

    def out_rows(index, carry):
        rows = pl.ds(pl.multiple_of(index * width, 16), width)
        grad_ref[0, rows, :] = dot(attn_ref[index], dbranch_ref[...]).astype(bf16)
        return carry

    for index, count, run in (
        (2, D // BLOCK, down_rows),
        (1, D // BLOCK, up_rows),
        (0, parts, out_rows),
    ):
        lax.fori_loop(0, count, run, 0)
        for owner in range(groups):
            pair_copy(index, owner, 1 - core).start()
    for step in range(groups):
        owner = group ^ step
        for index in (2, 1, 0):
            pair_copy(index, owner, core).wait_recv()
            chunk_refs[step][index] = (
                grad_ref[index, rows_of(owner, core), :].astype(f32)
                + theirs_ref[index, owner].astype(f32)
            ).astype(bf16)
    for part in range(tokens // BLOCK):
        for peer in peers:
            dattn_copy(part, here, peer).wait_recv()
            dattn_copy(part, peer, here).wait_send()
            attn_copy(part, peer, here).wait_send()
    for index in range(3):
        for owner in range(groups):
            pair_copy(index, owner, 1 - core).wait_send()


def middle(parts, groups, mixed, rows, cotangent, weights, gain):
    rows_dev = rows.shape[0]
    half = D // groups // 2
    dma = pltpu.SemaphoreType.DMA
    halves = rows_dev // BLOCK
    return pl.pallas_call(
        functools.partial(middle_kernel, parts, groups),
        name="middle",
        out_shape=[
            jax.ShapeDtypeStruct((rows_dev, D), bf16),
            jax.ShapeDtypeStruct((rows_dev, D), f32),
            jax.ShapeDtypeStruct(mixed.shape, bf16),
            jax.ShapeDtypeStruct((1, D), f32),
        ]
        + [jax.ShapeDtypeStruct((3, half, D), bf16)] * groups,
        in_specs=in_vmem(3) + [pl.BlockSpec(memory_space=pl.ANY)] + in_vmem(1),
        out_specs=in_vmem(4 + groups),
        scratch_shapes=[
            pltpu.VMEM((3, D, D), bf16),
            pltpu.VMEM(mixed.shape, bf16),
            pltpu.VMEM(mixed.shape, bf16),
            pltpu.VMEM((rows_dev, D), bf16),
            pltpu.VMEM((rows_dev, D), bf16),
            pltpu.VMEM((rows_dev, D), bf16),
            pltpu.VMEM((rows_dev, D), bf16),
            pltpu.VMEM((3, D, D), bf16),
            pltpu.VMEM((3, groups, half, D), bf16),
            dma((3,)),
            dma((2, halves, parts)),
            dma((2, halves, parts)),
            dma((2, 3, groups)),
        ],
        compiler_params=pltpu.CompilerParams(
            vmem_limit_bytes=60 * 1024 * 1024, collective_id=3, has_side_effects=True
        ),
    )(mixed, rows, cotangent, weights, gain)


def reduce_kernel(
    parts,
    groups,
    dq_in_ref,
    wt_in_ref,
    units_ref,
    wc_ref,
    small_ref,
    *refs,
):
    chunk_in_refs = refs[:groups]
    (
        down_ref,
        up_ref,
        own_ref,
        ugather_ref,
        mgather_ref,
        sgather_ref,
        dq_ref,
        wt_ref,
        chunk_ref,
        held_ref,
        total_ref,
        u_ref,
        usum_ref,
        msum_ref,
        pair_ref,
        sum_ref,
        urecv_ref,
        mlp_ref,
        mrecv_ref,
        part_ref,
        column_ref,
        smine_ref,
        srecv_ref,
        pair_sem,
        sum_sem,
        u_sem,
        m_sem,
        line_sem,
        side_sem,
        small_sem,
        cross_sem,
        load_sem,
        held_sem,
        keep_sem,
    ) = refs[groups:]
    chips = parts // 2
    here = lax.axis_index("ctx")
    group = lax.axis_index("fsdp")
    core = lax.rem(here, 2)
    chip = here // 2
    other = here + 1 - 2 * core
    ctx_peers = [lax.rem(here + step, parts) for step in range(1, parts)]
    chip_peers = [lax.rem(chip + step, chips) for step in range(1, chips)]
    group_peers = [lax.rem(group + step, groups) for step in range(1, groups)]

    loads = [
        pltpu.make_async_copy(ref, chunk_ref.at[index], load_sem.at[index])
        for index, ref in enumerate(chunk_in_refs)
    ]
    loads.append(pltpu.make_async_copy(dq_in_ref, dq_ref, load_sem.at[groups]))
    loads.append(pltpu.make_async_copy(wt_in_ref, wt_ref, load_sem.at[groups + 1]))
    for load in loads:
        load.start()

    def unit_load(piece):
        slot = lax.rem(piece, 2)
        return pltpu.make_async_copy(units_ref.at[piece], held_ref.at[slot], held_sem.at[slot])

    for piece in range(2):
        unit_load(piece).start()

    barrier = pltpu.get_barrier_semaphore()
    for peer in ctx_peers:
        pl.semaphore_signal(barrier, inc=1, device_id={"ctx": peer})
    for peer in group_peers:
        pl.semaphore_signal(barrier, inc=1, device_id={"fsdp": peer})
    pl.semaphore_wait(barrier, parts + groups - 2)

    def send(source, target, sems, device):
        return pltpu.make_async_remote_copy(
            src_ref=source,
            dst_ref=target,
            send_sem=sems[0],
            recv_sem=sems[1],
            device_id=device,
        )

    def pair_copy(index):
        return send(
            dq_in_ref.at[index, 1 - core],
            pair_ref.at[index],
            (pair_sem.at[0, index], pair_sem.at[1, index]),
            {"ctx": other},
        )

    def u_copy(peer, source):
        return send(
            u_ref.at[peer],
            urecv_ref.at[source],
            (u_sem.at[0, peer], u_sem.at[1, source]),
            {"fsdp": peer},
        )

    def m_copy(peer, source):
        return send(
            mlp_ref.at[peer],
            mrecv_ref.at[source],
            (m_sem.at[0, peer], m_sem.at[1, source]),
            {"ctx": 2 * peer + core},
        )

    for index in range(chips):
        pair_copy(index).start()
    for load in loads:
        load.wait()
    share = mlp_ref.shape[2]
    for matrix in range(3):
        total = functools.reduce(jnp.add, [chunk_ref[step, matrix].astype(f32) for step in range(groups)])
        for index in range(chips):
            mlp_ref[index, matrix] = total[index * share : (index + 1) * share].astype(bf16)
    for peer in chip_peers:
        m_copy(peer, chip).start()
    for index in range(chips):
        pair_copy(index).wait_recv()

    rows_half = own_ref.shape[0] // 2

    def partial(target, index):
        rows = pl.ds(pl.multiple_of(index * rows_half, rows_half), rows_half)
        part_ref[rows, :] = dot(dq_ref[target, core, :, rows], wt_ref[core], (0, 0)) + dot(
            pair_ref[target, :, rows], wt_ref[1 - core], (0, 0)
        )
        return rows

    def sum_copy(way, target, index):
        ref = sum_ref.at[way + target, pl.ds(index * rows_half, rows_half)]
        sems = (sum_sem.at[0, way, target, index], sum_sem.at[1, way, target, index])
        return send(ref, ref, sems, {"ctx": here + (2 if way else -2)})

    def reduce_step(step):
        last = step == chips - 2
        for way, target, active, first, out_ref in (
            (0, step - (chips - 1) + chip, step >= chips - 1 - chip, chip == chips - 1, down_ref),
            (1, chips - 1 - step + chip, step >= chip, chip == 0, up_ref),
        ):

            @pl.when(active)
            def _():
                def half(index, carry):
                    rows = partial(target, index)

                    @pl.when(first)
                    def _():
                        sum_ref[way + target, rows] = part_ref[rows, :].astype(bf16)

                    @pl.when(jnp.logical_not(first))
                    def _():
                        sum_copy(way, target, index).wait_recv()
                        sum_ref[way + target, rows] = (
                            part_ref[rows, :] + sum_ref[way + target, rows].astype(f32)
                        ).astype(bf16)

                    if last:
                        out_ref[rows, :] = sum_ref[way + target, rows]
                    else:
                        sum_copy(way, target, index).start()
                    return carry

                lax.fori_loop(0, 2, half, 0)

            if last:

                @pl.when(jnp.logical_not(active))
                def _():
                    out_ref[...] = jnp.zeros(out_ref.shape, bf16)

    gathers = (ugather_ref, mgather_ref)
    sums = (usum_ref, msum_ref)

    def keep_copy(which):
        return pltpu.make_async_copy(sums[which], gathers[which].at[here], keep_sem.at[which])

    def line_copy(which, way, step, piece):
        ref = gathers[which].at[2 * piece + core]
        sems = (line_sem.at[0, which, way, step], line_sem.at[1, which, way, step])
        source = sums[which] if step == 0 else ref
        return send(source, ref, sems, {"ctx": here + (2 if way else -2)})

    def side_copy(which, piece, lane, own=False):
        ref = gathers[which].at[2 * piece + lane]
        sems = (side_sem.at[0, which, piece], side_sem.at[1, which, piece])
        return send(sums[which] if own else ref, ref, sems, {"ctx": other})

    def line_sends(which, step, go):
        @pl.when((chip < chips - 1) & (chip - step >= 0))
        def _():
            go(line_copy(which, 1, step, chip - step))

        @pl.when((chip > 0) & (chip + step <= chips - 1))
        def _():
            go(line_copy(which, 0, step, chip + step))

    def line_receive(which, step):
        @pl.when(chip - 1 - step >= 0)
        def _():
            line_copy(which, 1, step, chip - 1 - step).wait_recv()
            side_copy(which, chip - 1 - step, core).start()

        @pl.when(chip + 1 + step <= chips - 1)
        def _():
            line_copy(which, 0, step, chip + 1 + step).wait_recv()
            side_copy(which, chip + 1 + step, core).start()

    def small_copy(peer, source):
        return send(
            smine_ref,
            srecv_ref.at[source],
            (small_sem.at[0, peer], small_sem.at[1, source]),
            {"ctx": peer},
        )

    def cross_copy(peer, source):
        return send(
            sgather_ref.at[group],
            sgather_ref.at[source],
            (cross_sem.at[0, peer], cross_sem.at[1, source]),
            {"fsdp": peer},
        )

    reduce_step(0)

    total_ref[...] = jnp.zeros(total_ref.shape, f32)

    def accumulate(piece, carry):
        unit_load(piece).wait()
        total_ref[...] += dot(dq_ref[piece // 2, lax.rem(piece, 2)], held_ref[lax.rem(piece, 2)])

        @pl.when(piece + 2 < parts)
        def _():
            unit_load(piece + 2).start()

        return carry

    lax.fori_loop(0, parts, accumulate, 0)
    u_ref[...] = total_ref[...].T.astype(bf16).reshape(u_ref.shape)
    for peer in group_peers:
        u_copy(peer, group).start()

    total = mlp_ref[chip].astype(f32)
    for peer in chip_peers:
        m_copy(chip, peer).wait_recv()
        total = total + mrecv_ref[peer].astype(f32)
    msum_ref[...] = total.astype(bf16)
    keep_copy(1).start()
    side_copy(1, chip, core, True).start()
    line_sends(1, 0, lambda copy: copy.start())

    total = u_ref[group].astype(f32)
    for peer in group_peers:
        u_copy(group, peer).wait_recv()
        total = total + urecv_ref[peer].astype(f32)
    usum_ref[...] = total.astype(bf16)
    keep_copy(0).start()
    side_copy(0, chip, core, True).start()
    line_sends(0, 0, lambda copy: copy.start())
    held = total.shape[0]
    gain = jnp.sum(total * wc_ref[...].astype(f32), axis=1, keepdims=True)
    column_ref[...] = jnp.zeros(column_ref.shape, f32)
    column_ref[:held, :] = jnp.broadcast_to(gain, (held, PAD))
    flat = column_ref[...].T[:1]
    smine_ref[...] = small_ref[...]
    for row in range(column_ref.shape[0] // PAD):
        smine_ref[row : row + 1, :] = flat[:, row * PAD : (row + 1) * PAD]
    for peer in ctx_peers:
        small_copy(peer, here).start()

    for step in range(1, chips):
        if step == 1:
            reduce_step(step)
        for which in range(2):
            line_receive(which, step - 1)
            if step <= chips - 2:
                line_sends(which, step, lambda copy: copy.start())
        if 1 < step <= chips - 2:
            reduce_step(step)
        if step == 1:
            small = smine_ref[...]
            for peer in ctx_peers:
                small_copy(here, peer).wait_recv()
                small = small + srecv_ref[peer]
            sgather_ref[group] = small
            for peer in group_peers:
                cross_copy(peer, group).start()

    for index in range(2):
        rows = partial(chip, index)
        own_ref[rows, :] = part_ref[rows, :].astype(bf16)

    for which in range(2):
        keep_copy(which).wait()
        for piece in range(chips):
            side_copy(which, piece, 1 - core).wait_recv()
            side_copy(which, piece, core).wait_send()
        for step in range(chips - 1):
            line_sends(which, step, lambda copy: copy.wait_send())
    for index in range(chips):
        pair_copy(index).wait_send()
    for peer in group_peers:
        cross_copy(group, peer).wait_recv()
        cross_copy(peer, group).wait_send()
        u_copy(peer, group).wait_send()
    for peer in chip_peers:
        m_copy(peer, chip).wait_send()
    for peer in ctx_peers:
        small_copy(peer, here).wait_send()
    for step in range(chips - 2):

        @pl.when(step >= chips - 1 - chip)
        def _():
            for index in range(2):
                sum_copy(0, step - (chips - 1) + chip, index).wait_send()

        @pl.when(step >= chip)
        def _():
            for index in range(2):
                sum_copy(1, chips - 1 - step + chip, index).wait_send()


def reduce_gradients(parts, groups, dqkv, w_pair, units, w_columns, small, chunks):
    chips = parts // 2
    mlp_shape = (chips, 3, chunks[0].shape[1] // chips, D)
    rows_dev = dqkv.shape[3]
    rows, width = w_columns.shape
    lanes = -(-rows // PAD) * PAD
    dma = pltpu.SemaphoreType.DMA
    anywhere = pl.BlockSpec(memory_space=pl.ANY)
    u_shape = (groups, rows, width)
    return pl.pallas_call(
        functools.partial(reduce_kernel, parts, groups),
        name="reduce_gradients",
        out_shape=[
            jax.ShapeDtypeStruct((rows_dev, D), bf16),
            jax.ShapeDtypeStruct((rows_dev, D), bf16),
            jax.ShapeDtypeStruct((rows_dev, D), bf16),
            jax.ShapeDtypeStruct((parts, rows, width), bf16),
            jax.ShapeDtypeStruct((parts,) + mlp_shape[1:], bf16),
            jax.ShapeDtypeStruct((groups,) + small.shape, f32),
        ],
        in_specs=[anywhere] * 3 + in_vmem(2) + [anywhere] * groups,
        out_specs=in_vmem(3) + [anywhere] * 2 + in_vmem(1),
        scratch_shapes=[
            pltpu.VMEM(dqkv.shape, bf16),
            pltpu.VMEM(w_pair.shape, bf16),
            pltpu.VMEM((groups,) + chunks[0].shape, bf16),
            pltpu.VMEM((2,) + units.shape[1:], bf16),
            pltpu.VMEM((width, D), f32),
            pltpu.VMEM(u_shape, bf16),
            pltpu.VMEM(u_shape[1:], bf16),
            pltpu.VMEM(mlp_shape[1:], bf16),
            pltpu.VMEM((chips,) + dqkv.shape[2:], bf16),
            pltpu.VMEM((chips + 1, rows_dev, D), bf16),
            pltpu.VMEM(u_shape, bf16),
            pltpu.VMEM(mlp_shape, bf16),
            pltpu.VMEM(mlp_shape, bf16),
            pltpu.VMEM((rows_dev, D), f32),
            pltpu.VMEM((lanes, PAD), f32),
            pltpu.VMEM(small.shape, f32),
            pltpu.VMEM((parts,) + small.shape, f32),
            dma((2, chips)),
            dma((2, 2, chips, 2)),
            dma((2, groups)),
            dma((2, chips)),
            dma((2, 2, 2, chips)),
            dma((2, 2, chips)),
            dma((2, parts)),
            dma((2, groups)),
            dma((groups + 2,)),
            dma((2,)),
            dma((2,)),
        ],
        compiler_params=pltpu.CompilerParams(
            vmem_limit_bytes=60 * 1024 * 1024, collective_id=1, has_side_effects=True
        ),
    )(dqkv, w_pair, units, w_columns, small, *chunks)


def update_kernel(rates, qkv_ref, gain_ref, mlp_ref, *refs):
    sets = len(rates)
    parts, rows, width = qkv_ref.shape
    width = width // 3
    for index, rate in enumerate(rates):
        weight, first, second = (ref[...] for ref in refs[3 * index : 3 * index + 3])
        if index == 0:
            pieces = [qkv_ref[part].astype(f32) for part in range(parts)]
            gradient = jnp.concatenate(
                [piece[:, at * width : (at + 1) * width] for at in range(3) for piece in pieces],
                axis=1,
            )
            gradient = gradient * gain_ref[...]
        else:
            gradient = mlp_ref[0, index - 1].astype(f32)
        outs = refs[3 * sets + 4 * index : 3 * sets + 4 * index + 4]
        new, first, second = adamw(weight, first, second, gradient, rate, decay_rate)
        outs[0][...] = new
        outs[1][...] = first
        outs[2][...] = second
        outs[3][...] = new.astype(bf16)


def update(rates, parts, qkv, gain, mlp, *arrays):
    rows = arrays[0].shape[0]
    chips = parts // 2
    step_rows = rows // parts
    if step_rows % 8 == 0:

        def owner(i):
            return (2 * lax.rem(i, chips) + i // chips, 0, 0, 0)

    else:
        step_rows = 32
        mlp = mlp.reshape(chips, 2, 3, rows // parts, D).transpose(2, 1, 0, 3, 4)
        mlp = mlp.reshape(3, rows // step_rows, step_rows, D).transpose(1, 0, 2, 3)

        def owner(i):
            return (i, 0, 0, 0)

    in_specs = [
        pl.BlockSpec((parts, step_rows, qkv.shape[2]), lambda i: (0, i, 0)),
        pl.BlockSpec((step_rows, 1), lambda i: (i, 0)),
        pl.BlockSpec((1, 3, step_rows, D), owner),
    ]
    specs, shapes, moved = [], [], 0
    for array in arrays:
        in_specs.append(pl.BlockSpec((step_rows, array.shape[1]), lambda i: (i, 0)))
    for index in range(len(rates)):
        shape = arrays[3 * index].shape
        shapes += [jax.ShapeDtypeStruct(shape, f32)] * 3 + [jax.ShapeDtypeStruct(shape, bf16)]
        specs += [pl.BlockSpec((step_rows, shape[1]), lambda i: (i, 0))] * 4
        moved += shape[0] * shape[1] * 28
    return pl.pallas_call(
        functools.partial(update_kernel, rates),
        name="update_weights",
        grid=(rows // step_rows,),
        in_specs=in_specs,
        out_specs=specs,
        out_shape=shapes,
        compiler_params=params(),
        cost_estimate=pl.CostEstimate(flops=moved, bytes_accessed=moved, transcendentals=0),
    )(qkv, gain, mlp, *arrays)


def finish_kernel(x_ref, dmid_ref, own_ref, down_ref, up_ref, layer_ref, out_ref, same_ref):
    rows = x_ref[...].astype(f32)
    scale = rms_scale(rows)
    unit = rows * scale
    dunit = own_ref[...].astype(f32) + down_ref[...].astype(f32) + up_ref[...].astype(f32)
    grad = dmid_ref[...] + scale * (
        dunit - unit * jnp.mean(dunit * unit, axis=-1, keepdims=True)
    )
    out_ref[...] = grad.astype(bf16)
    same_ref[...] = layer_ref[...]


def finish(*arrays):
    rows = arrays[0].shape[0]
    spec = pl.BlockSpec((PAD // 2, D), lambda i: (i, 0))
    return pl.pallas_call(
        finish_kernel,
        name="finish",
        grid=(2 * rows // PAD,),
        in_specs=[spec] * len(arrays),
        out_specs=[spec] * 2,
        out_shape=[jax.ShapeDtypeStruct((rows, D), bf16)] * 2,
        compiler_params=params(),
    )(*arrays)


def body(
    parts,
    groups,
    inputs,
    cotangent,
    block_order,
    w_qkv,
    m_qkv,
    v_qkv,
    w_out,
    m_out,
    v_out,
    w_up,
    m_up,
    v_up,
    w_down,
    m_down,
    v_down,
    small_params,
    small_m,
    small_v,
):
    heads = H // parts
    width = heads * HD
    rows_dev = inputs.shape[1]
    tokens = rows_dev * parts
    here = lax.axis_index("ctx")
    order = block_order[0]
    gain_two = small_params[D : 2 * D]
    query_scale = small_params[2 * D :]
    group = lax.axis_index("fsdp")
    rows = w_qkv.shape[0]

    (
        unit_all,
        mlp_full,
        w_pair,
        qt,
        kt,
        vt,
        kn,
        vn,
        w_columns,
        gain_rows,
        factor_two,
    ) = gather_rows(
        parts, groups, heads, inputs[0], w_qkv, w_out, w_up, w_down, small_params[None]
    )
    lse, mixed = attention_forward(order, qt, kt, kn, vt, parts)
    kept = (qt, kt, kn, vn, lse)
    output, dmid, dmixed, gain_two_grad, *chunks = middle(
        parts,
        groups,
        mixed,
        inputs[0],
        cotangent[0],
        mlp_full.reshape(3, D, D),
        gain_two[None],
    )
    for step in range(1, groups):
        swap = [(i, i ^ step) for i in range(groups)]
        chunks[step] = lax.ppermute(chunks[step], "fsdp", swap)
    dqkv, dscale = attention_backward(order, kept, mixed, dmixed, factor_two)
    scale_grad = (
        dscale[0, :HD]
        / factor_two[:, 0]
        * (scale_base / math.sqrt(HD))
        * jax.nn.sigmoid(query_scale)
    )
    lanes = -(-rows // PAD) * PAD
    small_rows = -(-(lanes + D + PAD) // (8 * PAD)) * 8
    small = jnp.concatenate([jnp.zeros((lanes,), f32), gain_two_grad[0], scale_grad])
    small = jnp.pad(small, (0, small_rows * PAD - small.shape[0])).reshape(small_rows, PAD)
    send_down, send_up, own_part, u_all, mlp_all, small_all = reduce_gradients(
        parts,
        groups,
        dqkv.reshape(parts // 2, 2, 3 * width, rows_dev),
        w_pair,
        unit_all,
        w_columns,
        small,
        chunks,
    )
    got_down = lax.ppermute(send_down, "ctx", [(i, i - 2) for i in range(2, parts)])
    got_up = lax.ppermute(send_up, "ctx", [(i, i + 2) for i in range(parts - 2)])
    rate_qkv = qkv_rate_base / math.sqrt(D)
    rate_out = 0.5 / math.sqrt(max(D // 256, 1))
    rate_up = 0.5 / math.sqrt(D)
    rate_down = 0.5 / math.sqrt(FF)
    updated = update(
        (rate_qkv, rate_out, rate_up, rate_down),
        parts,
        u_all,
        gain_rows,
        mlp_all,
        w_qkv,
        m_qkv,
        v_qkv,
        w_out,
        m_out,
        v_out,
        w_up,
        m_up,
        v_up,
        w_down,
        m_down,
        v_down,
    )
    flat = small_all.reshape(groups, small_rows * PAD)
    rest = jnp.sum(flat[:, lanes : lanes + D + HD], axis=0)
    small_total = jnp.concatenate([flat[:, :rows].reshape(D), rest])
    small_set = adamw(small_params, small_m, small_v, small_total, small_rate, 0.0)
    input_grad, output = finish(inputs[0], dmid, own_part, got_down, got_up, output)
    return (
        output[None],
        input_grad[None],
        *updated,
        *small_set,
    )


def solution(mesh):
    rows = P("fsdp", "ctx", None)
    weight = P("fsdp", None)
    return jax.shard_map(
        functools.partial(body, mesh.shape["ctx"], mesh.shape["fsdp"]),
        mesh=mesh,
        in_specs=(rows, rows, weight) + (weight,) * 12 + (P(),) * 3,
        out_specs=(rows, rows) + (weight,) * 16 + (P(),) * 3,
        check_vma=False,
    )
```

```python
import functools
import math

import jax
import jax.numpy as jnp
from jax import lax
from jax.experimental import pallas as pl
from jax.experimental.pallas import tpu as pltpu
from jax.sharding import PartitionSpec as P

D = 1280
H = 16
HD = 80
FF = 1280
BLOCK = 256
CONT = 512
STEP = 3
PAD = 128
EXTRA = 16
TILE = CONT
SCORE_BOUND = 95.0

bf16 = jnp.bfloat16
f32 = jnp.float32

norm_eps = 1e-06
beta_one = 0.5
beta_two = 0.5
adam_eps = 1e-08
decay_rate = 0.1
small_rate = 0.75
qkv_rate_base = 1.0
scale_base = 1.442695
LOG2E = math.log2(math.e)
LN2 = math.log(2.0)


def rms_scale(values):
    return lax.rsqrt(jnp.mean(values * values, axis=-1, keepdims=True) + norm_eps)


def adamw(weight, first, second, gradient, step_rate, decay_on):
    first_new = beta_one * first + (1.0 - beta_one) * gradient
    second_new = beta_two * second + (1.0 - beta_two) * gradient * gradient
    corr_one = 1.0 - beta_one**STEP
    corr_two = 1.0 - beta_two**STEP
    update = first_new / corr_one / (jnp.sqrt(second_new / corr_two) + adam_eps)
    weight_new = weight - step_rate * (update + decay_on * weight)
    return (weight_new, first_new, second_new)


def dot(left, right, contract=(1, 0)):
    return lax.dot_general(
        left, right, (((contract[0],), (contract[1],)), ((), ())), preferred_element_type=f32
    )


def fill_slots(order_ref, slot_ref):
    def place(slot, carry):
        slot_ref[order_ref[slot]] = slot
        return carry

    lax.fori_loop(0, order_ref.shape[0], place, 0)


def three_rows(row):
    high = row.astype(bf16)
    rest = row - high.astype(f32)
    middle = rest.astype(bf16)
    low = (rest - middle.astype(f32)).astype(bf16)
    index = lax.broadcasted_iota(jnp.int32, (EXTRA, row.shape[1]), 0)
    zero = jnp.zeros((EXTRA, row.shape[1]), f32)
    rows = jnp.where(index == 0, high.astype(f32), zero)
    rows = jnp.where(index == 1, middle.astype(f32), rows)
    rows = jnp.where(index == 2, low.astype(f32), rows)
    return rows.astype(bf16)


def tile_at(tile):
    return pl.ds(pl.multiple_of(tile * TILE, TILE), TILE)


def block_at(slot):
    return pl.ds(pl.multiple_of(slot * BLOCK, BLOCK), BLOCK)


def tile_lanes(ref, head, slot_ref, tile, rows=slice(None)):
    first, second = slot_ref[2 * tile], slot_ref[2 * tile + 1]
    return jnp.concatenate(
        [ref[head, rows, block_at(first)], ref[head, rows, block_at(second)]], axis=1
    )


def tile_rows(ref, head, slot_ref, tile):
    first, second = slot_ref[2 * tile], slot_ref[2 * tile + 1]
    return jnp.concatenate([ref[head, block_at(first), :], ref[head, block_at(second), :]], axis=0)


def half_at(slot):
    return pl.ds(pl.multiple_of(lax.rem(slot, 2) * BLOCK, BLOCK), BLOCK)


def causal(shape):
    key = lax.broadcasted_iota(jnp.int32, shape, 0)
    query = lax.broadcasted_iota(jnp.int32, shape, 1)
    return key <= query


def gather_kernel(
    parts,
    groups,
    heads,
    x_ref,
    wqkv_ref,
    wout_ref,
    wup_ref,
    wdown_ref,
    small_ref,
    unit_ref,
    full_ref,
    wpair_ref,
    qt_out_ref,
    kt_out_ref,
    vt_out_ref,
    kn_out_ref,
    vn_out_ref,
    wcol_ref,
    gain_ref,
    factor_ref,
    most_ref,
    qt_ref,
    kt_ref,
    vt_ref,
    kn_ref,
    vn_ref,
    rows_ref,
    wstage_ref,
    mstage_ref,
    gained_ref,
    mlp_ref,
    wrecv_ref,
    wflip_ref,
    line_sem,
    side_sem,
    keep_sem,
    w_sem,
    lane_sem,
    mlp_sem,
    cross_sem,
    own_sem,
    stage_sem,
    lanes_sem,
    sides_sem,
):
    chips = parts // 2
    here = lax.axis_index("ctx")
    group = lax.axis_index("fsdp")
    core = lax.rem(here, 2)
    chip = here // 2
    other = here + 1 - 2 * core
    width = heads * HD
    group_peers = [lax.rem(group + step, groups) for step in range(1, groups)]

    barrier = pltpu.get_barrier_semaphore()
    pl.semaphore_signal(barrier, inc=1, device_id={"ctx": other})
    for peer in group_peers:
        pl.semaphore_signal(barrier, inc=1, device_id={"fsdp": peer})
    for step in (1, chips - 1):
        peer = lax.rem(chip + step, chips) * 2 + core
        pl.semaphore_signal(barrier, inc=1, device_id={"ctx": peer})

    def send(source, target, sems, device):
        return pltpu.make_async_remote_copy(
            src_ref=source,
            dst_ref=target,
            send_sem=sems[0],
            recv_sem=sems[1],
            device_id=device,
        )

    halves = rows_ref.shape[1] // BLOCK

    def line_copy(way, step, piece, part):
        ref = rows_ref.at[2 * piece + core, block_at(part)]
        sems = (line_sem.at[0, way, step, part], line_sem.at[1, way, step, part])
        return send(ref, ref, sems, {"ctx": here + (2 if way else -2)})

    def side_copy(piece, lane, part):
        ref = rows_ref.at[2 * piece + lane, block_at(part)]
        sems = (side_sem.at[0, piece, part], side_sem.at[1, piece, part])
        return send(ref, ref, sems, {"ctx": other})

    def results(slot):
        to = block_at(slot)
        copies = [
            pltpu.make_async_copy(ref.at[:, :, to], out.at[:, :, to], lanes_sem.at[index, slot])
            for index, (ref, out) in enumerate(
                ((qt_ref, qt_out_ref), (kt_ref, kt_out_ref), (vt_ref, vt_out_ref))
            )
        ]
        return copies + [
            pltpu.make_async_copy(ref.at[:, to], out.at[:, to], sides_sem.at[index, slot])
            for index, (ref, out) in enumerate(((kn_ref, kn_out_ref), (vn_ref, vn_out_ref)))
        ]

    def w_copy(peer, source):
        sems = (w_sem.at[0, peer], w_sem.at[1, source])
        return send(gained_ref, wrecv_ref.at[source], sems, {"fsdp": peer})

    def lane_copy(lane):
        ref = wpair_ref.at[lane]
        return send(ref, ref, (lane_sem.at[0], lane_sem.at[1]), {"ctx": other})

    def mlp_copy(peer, source):
        sems = (mlp_sem.at[0, peer], mlp_sem.at[1, source])
        return send(mlp_ref.at[:, core], full_ref.at[:, source, core], sems, {"fsdp": peer})

    def cross_copy(source, lane):
        ref = full_ref.at[:, source, lane]
        sems = (cross_sem.at[0, source], cross_sem.at[1, source])
        return send(ref, ref, sems, {"ctx": other})

    def keep_copy(piece):
        return pltpu.make_async_copy(rows_ref.at[piece], unit_ref.at[piece], keep_sem.at[piece])

    own_copy = pltpu.make_async_copy(mlp_ref, full_ref.at[:, group], own_sem)

    stages = [pltpu.make_async_copy(wqkv_ref, wstage_ref, stage_sem.at[0])] + [
        pltpu.make_async_copy(ref, mstage_ref.at[index], stage_sem.at[index + 1])
        for index, ref in enumerate((wout_ref, wup_ref, wdown_ref))
    ]
    for stage in stages:
        stage.start()
    rows = x_ref[...].astype(f32)
    rows_ref[here] = (rows * rms_scale(rows)).astype(bf16)
    pl.semaphore_wait(barrier, groups + 2)

    def forward(way, step, piece, part):
        @pl.when((chip < chips - 1) if way else (chip > 0))
        def _():
            line_copy(way, step, piece, part).start()

    for part in range(halves):
        for way in range(2):
            forward(way, 0, chip, part)
        side_copy(chip, core, part).start()
    held = gain_ref.shape[0]
    lanes = -(-held // PAD) * PAD
    gains = jnp.broadcast_to(small_ref[:, :D], (8, D))
    gains = pltpu.roll(gains, lax.rem(D - group * held, D), 1)[:1, :lanes]
    gain_ref[...] = jnp.broadcast_to(gains, (PAD, lanes)).T[:held, :1]
    soft = jnp.log(1.0 + jnp.exp(small_ref[:, 2 * D :])) * (scale_base / math.sqrt(HD) * LOG2E)
    soft = jnp.concatenate([soft, jnp.zeros((1, PAD - HD), f32)], axis=1)
    factor_ref[...] = jnp.broadcast_to(soft, (PAD, PAD)).T[:HD, :1]
    shift = lax.rem(D - here * width, D)
    stages[0].wait()
    for part in range(3):
        turned = pltpu.roll(wstage_ref[:, part * D : (part + 1) * D], shift, 1)
        gained_ref[part] = (turned[:, :width] * gain_ref[...]).astype(bf16)
        wcol_ref[:, part * width : (part + 1) * width] = turned[:, :width].astype(bf16)
    for peer in group_peers:
        w_copy(peer, group).start()
    for index in range(3):
        stages[index + 1].wait()
        mlp_ref[index] = mstage_ref[index].astype(bf16).reshape(mlp_ref.shape[1:])
    own_copy.start()
    keep_copy(here).start()
    wrecv_ref[group] = gained_ref[...]
    for peer in group_peers:
        w_copy(group, peer).wait_recv()
    for peer in group_peers:
        mlp_copy(peer, group).start()
    for part in range(3):
        flipped = wrecv_ref[:, part].reshape(D, width).T
        wflip_ref[part * width : (part + 1) * width] = flipped
    wpair_ref[core] = wflip_ref[...]
    lane_copy(core).start()

    extra_row = lax.broadcasted_iota(jnp.int32, (PAD - HD, BLOCK), 0)
    extra = jnp.where(extra_row < 3, 1.0, 0.0)
    spare = jnp.zeros((PAD - HD, BLOCK), bf16)

    most_ref[...] = jnp.zeros(most_ref.shape, f32)

    def project(piece, part):
        slot = piece * halves + part
        to = block_at(slot)
        result = dot(wflip_ref[...], rows_ref[piece, block_at(part), :], (1, 1))
        for head in range(heads):
            query, key, value = (
                result[share * width + head * HD : share * width + (head + 1) * HD]
                for share in range(3)
            )
            query = query * factor_ref[...]
            for row, rows in enumerate((query, key)):
                most_ref[row : row + 1] = jnp.maximum(
                    most_ref[row : row + 1], jnp.sum(rows * rows, axis=0, keepdims=True)
                )
            qt_ref[head, :HD, to] = query.astype(bf16)
            qt_ref[head, HD:, to] = spare
            kt_ref[head, :, to] = key.astype(bf16)
            vt_ref[head, :HD, to] = value.astype(bf16)
            vt_ref[head, HD:, to] = jnp.ones((EXTRA, BLOCK), bf16)
            kn_ref[head, to, :] = jnp.concatenate([key, extra], axis=0).T.astype(bf16)
            vn_ref[head, to, :] = jnp.concatenate([value, extra], axis=0).T.astype(bf16)
        for copy in results(slot):
            copy.start()

    def visit(index, carry):
        distance, part = index // halves, lax.rem(index, halves)
        for way in range(2):
            piece = chip - distance if way else chip + distance
            valid = (piece >= 0) if way else (piece <= chips - 1)

            @pl.when(valid & (distance > 0))
            def _():
                line_copy(way, distance - 1, piece, part).wait_recv()
                side_copy(piece, core, part).start()
                forward(way, distance, piece, part)

                @pl.when(part == halves - 1)
                def _():
                    keep_copy(2 * piece + core).start()

        for way in range(2):
            piece = chip - distance if way else chip + distance
            valid = (piece >= 0) if way else ((piece <= chips - 1) & (distance > 0))

            @pl.when(valid)
            def _():
                project(2 * piece + core, part)
                side_copy(piece, 1 - core, part).wait_recv()
                project(2 * piece + 1 - core, part)

                @pl.when(part == halves - 1)
                def _():
                    keep_copy(2 * piece + 1 - core).start()

        return carry

    lax.fori_loop(0, chips * halves, visit, 0)

    for peer in group_peers:
        mlp_copy(group, peer).wait_recv()
        cross_copy(peer, core).start()
    for peer in group_peers:
        cross_copy(peer, 1 - core).wait_recv()
        cross_copy(peer, core).wait_send()
        w_copy(peer, group).wait_send()
        mlp_copy(peer, group).wait_send()
    own_copy.wait()
    lane_copy(1 - core).wait_recv()
    lane_copy(core).wait_send()

    def drain(piece, carry):
        keep_copy(2 * piece).wait()
        keep_copy(2 * piece + 1).wait()
        for part in range(halves):
            side_copy(piece, core, part).wait_send()

            @pl.when((piece <= chip) & (chip < chips - 1))
            def _():
                line_copy(1, chip - piece, piece, part).wait_send()

            @pl.when((piece >= chip) & (chip > 0))
            def _():
                line_copy(0, piece - chip, piece, part).wait_send()

        return carry

    lax.fori_loop(0, chips, drain, 0)

    def settle(slot, carry):
        for copy in results(slot):
            copy.wait()
        return carry

    lax.fori_loop(0, 2 * chips * halves, settle, 0)


def gather_rows(parts, groups, heads, rows, w_qkv, w_out, w_up, w_down, small):
    rows_dev = rows.shape[0]
    held = w_qkv.shape[0]
    tokens = parts * rows_dev
    dma = pltpu.SemaphoreType.DMA
    chips = parts // 2
    anywhere = pl.BlockSpec(memory_space=pl.ANY)
    return pl.pallas_call(
        functools.partial(gather_kernel, parts, groups, heads),
        name="gather_rows",
        out_shape=[
            jax.ShapeDtypeStruct((parts, rows_dev, D), bf16),
            jax.ShapeDtypeStruct((3, groups, 2, held // 2, D), bf16),
            jax.ShapeDtypeStruct((2, 3 * heads * HD, D), bf16),
            jax.ShapeDtypeStruct((heads, PAD, tokens), bf16),
            jax.ShapeDtypeStruct((heads, HD, tokens), bf16),
            jax.ShapeDtypeStruct((heads, HD + EXTRA, tokens), bf16),
            jax.ShapeDtypeStruct((heads, tokens, PAD), bf16),
            jax.ShapeDtypeStruct((heads, tokens, PAD), bf16),
            jax.ShapeDtypeStruct((held, 3 * heads * HD), bf16),
            jax.ShapeDtypeStruct((held, 1), f32),
            jax.ShapeDtypeStruct((HD, 1), f32),
            jax.ShapeDtypeStruct((8, BLOCK), f32),
        ],
        in_specs=in_vmem(1) + [anywhere] * 4 + in_vmem(1),
        out_specs=[anywhere] * 2 + in_vmem(1) + [anywhere] * 5 + in_vmem(4),
        scratch_shapes=[
            pltpu.VMEM((heads, PAD, tokens), bf16),
            pltpu.VMEM((heads, HD, tokens), bf16),
            pltpu.VMEM((heads, HD + EXTRA, tokens), bf16),
            pltpu.VMEM((heads, tokens, PAD), bf16),
            pltpu.VMEM((heads, tokens, PAD), bf16),
            pltpu.VMEM((parts, rows_dev, D), bf16),
            pltpu.VMEM((held, 3 * D), f32),
            pltpu.VMEM((3, held, D), f32),
            pltpu.VMEM((3, held, heads * HD), bf16),
            pltpu.VMEM((3, 2, held // 2, D), bf16),
            pltpu.VMEM((groups, 3, held, heads * HD), bf16),
            pltpu.VMEM((3 * heads * HD, D), bf16),
            dma((2, 2, chips, rows_dev // BLOCK)),
            dma((2, chips, rows_dev // BLOCK)),
            dma((parts,)),
            dma((2, groups)),
            dma((2,)),
            dma((2, groups)),
            dma((2, groups)),
            dma,
            dma((4,)),
            dma((3, tokens // BLOCK)),
            dma((2, tokens // BLOCK)),
        ],
        compiler_params=pltpu.CompilerParams(
            vmem_limit_bytes=60 * 1024 * 1024, collective_id=2, has_side_effects=True
        ),
    )(rows, w_qkv, w_out, w_up, w_down, small)


def forward_kernel(
    heads,
    order_ref,
    most_ref,
    qt_ref,
    kn_in_ref,
    vt_in_ref,
    lse_ref,
    ot_ref,
    slot_ref,
    kn_ref,
    vt_ref,
    acc_ref,
    top_ref,
    load_sem,
):
    loads = [
        pltpu.make_async_copy(source, target, load_sem.at[index])
        for index, (source, target) in enumerate(((kn_in_ref, kn_ref), (vt_in_ref, vt_ref)))
    ]
    for load in loads:
        load.start()
    fill_slots(order_ref, slot_ref)
    tokens = kn_ref.shape[1]
    num_tiles = tokens // TILE
    prompt_tiles = num_tiles // 2

    bounded = (
        jnp.max(most_ref[0:1]) * jnp.max(most_ref[1:2]) <= SCORE_BOUND * SCORE_BOUND
    )
    for load in loads:
        load.wait()

    def run(shifted):
        def query_tile(tile, carry):
            queries = [tile_lanes(qt_ref, head, slot_ref, tile) for head in range(heads)]
            if shifted:
                top_ref[...] = jnp.full(top_ref.shape, -1e30, f32)
            else:
                top_ref[...] = jnp.zeros(top_ref.shape, f32)
            acc_ref[...] = jnp.zeros(acc_ref.shape, f32)

            def step(key_rows, value_lanes, start, masked):
                scores = [dot(key_rows[head], queries[head][:, start:]) for head in range(heads)]
                if masked:
                    allowed = causal(scores[0].shape)
                    scores = [jnp.where(allowed, score, -1e30) for score in scores]
                if shifted:
                    olds = [top_ref[head, :, start:] for head in range(heads)]
                    tops = [
                        jnp.maximum(old, jnp.max(score, axis=0, keepdims=True))
                        for old, score in zip(olds, scores)
                    ]
                    scores = [score - top for score, top in zip(scores, tops)]
                    for head in range(heads):
                        acc_ref[head, :, start:] *= jnp.exp2(olds[head] - tops[head])
                        top_ref[head, :, start:] = tops[head]
                probs = [jnp.exp2(score).astype(bf16) for score in scores]
                for head in range(heads):
                    acc_ref[head, :, start:] += dot(value_lanes[head], probs[head])

            def full(key_tile, inner):
                step(
                    [tile_rows(kn_ref, head, slot_ref, key_tile) for head in range(heads)],
                    [tile_lanes(vt_ref, head, slot_ref, key_tile) for head in range(heads)],
                    0,
                    False,
                )
                return inner

            lax.fori_loop(0, jnp.minimum(tile, prompt_tiles), full, 0)
            for part in range(TILE // BLOCK):
                block = block_at(slot_ref[tile * (TILE // BLOCK) + part])
                step(
                    [kn_ref[head, block, :] for head in range(heads)],
                    [vt_ref[head, :, block] for head in range(heads)],
                    part * BLOCK,
                    True,
                )
            for head in range(heads):
                acc = acc_ref[head]
                mass = acc[HD : HD + 1]
                mixed = (acc[:HD] / mass).astype(bf16)
                lse_ref[head, :, tile_at(tile)] = top_ref[head] + jnp.log2(mass)
                for part in range(TILE // BLOCK):
                    slot = slot_ref[tile * (TILE // BLOCK) + part]
                    ot_ref[slot // 2, head * HD : (head + 1) * HD, half_at(slot)] = mixed[
                        :, part * BLOCK : (part + 1) * BLOCK
                    ]
            return carry

        lax.fori_loop(0, num_tiles, query_tile, 0)

    @pl.when(bounded)
    def _():
        run(False)

    @pl.when(jnp.logical_not(bounded))
    def _():
        run(True)


def backward_kernel(
    heads,
    order_ref,
    qt_ref,
    kt_in_ref,
    kn_in_ref,
    vn_in_ref,
    lse_ref,
    ot_ref,
    dt_ref,
    factor_ref,
    dqkv_ref,
    dscale_ref,
    slot_ref,
    kt_ref,
    kn_ref,
    vn_ref,
    qa_ref,
    da_ref,
    dq_ref,
    dk_ref,
    dv_ref,
    scale_ref,
    load_sem,
):
    loads = [
        pltpu.make_async_copy(source, target, load_sem.at[index])
        for index, (source, target) in enumerate(
            ((kn_in_ref, kn_ref), (vn_in_ref, vn_ref), (kt_in_ref, kt_ref))
        )
    ]
    for load in loads:
        load.start()
    fill_slots(order_ref, slot_ref)
    tokens = kn_ref.shape[1]
    num_blocks = tokens // BLOCK
    num_tiles = tokens // TILE
    prompt_tiles = num_tiles // 2
    width = heads * HD

    def prepare(block, carry):
        slot = slot_ref[block]
        to = pl.ds(pl.multiple_of(block * BLOCK, BLOCK), BLOCK)
        for head in range(heads):
            rows = slice(head * HD, (head + 1) * HD)
            grad = dt_ref[slot // 2, rows, half_at(slot)]
            mixed = ot_ref[slot // 2, rows, half_at(slot)]
            delta = jnp.sum(grad.astype(f32) * mixed.astype(f32), axis=0, keepdims=True)
            da_ref[head, :HD, to] = grad
            da_ref[head, HD : HD + EXTRA, to] = three_rows(-delta)
            da_ref[head, HD + EXTRA :, to] = jnp.zeros((PAD - HD - EXTRA, BLOCK), bf16)
            qa_ref[head, :HD, to] = qt_ref[head, :HD, block_at(slot)]
            qa_ref[head, HD : HD + EXTRA, to] = three_rows(-lse_ref[head, :, to])
            qa_ref[head, HD + EXTRA :, to] = jnp.zeros((PAD - HD - EXTRA, BLOCK), bf16)
        return carry

    lax.fori_loop(0, num_blocks, prepare, 0)
    dk_ref[...] = jnp.zeros(dk_ref.shape, f32)
    dv_ref[...] = jnp.zeros(dv_ref.shape, f32)
    scale_ref[...] = jnp.zeros(scale_ref.shape, f32)
    for load in loads:
        load.wait()

    def query_tile(tile, carry):
        here = tile_at(tile)
        dq_ref[...] = jnp.zeros(dq_ref.shape, f32)

        def step(keys, key_rows, key_lanes, value_rows, start, masked):
            to = pl.ds(pl.multiple_of(tile * TILE + start, BLOCK), TILE - start)
            queries = [qa_ref[head, :, to] for head in range(heads)]
            grads = [da_ref[head, :, to] for head in range(heads)]
            scores = [dot(key_rows[head], queries[head]) for head in range(heads)]
            spreads = [dot(value_rows[head], grads[head]) for head in range(heads)]
            probs = [jnp.exp2(score) for score in scores]
            if masked:
                allowed = causal(scores[0].shape)
                probs = [jnp.where(allowed, prob, 0.0) for prob in probs]
            dscores = [(prob * spread).astype(bf16) for prob, spread in zip(probs, spreads)]
            for head in range(heads):
                dv_ref[head, :, keys] += dot(grads[head][:HD], probs[head].astype(bf16), (1, 1))
                dk_ref[head, :, keys] += dot(queries[head][:HD], dscores[head], (1, 1))
                dq_ref[head, :, start:] += dot(key_lanes[head], dscores[head])

        def full(key_tile, inner):
            step(
                tile_at(key_tile),
                [tile_rows(kn_ref, head, slot_ref, key_tile) for head in range(heads)],
                [tile_lanes(kt_ref, head, slot_ref, key_tile) for head in range(heads)],
                [tile_rows(vn_ref, head, slot_ref, key_tile) for head in range(heads)],
                0,
                False,
            )
            return inner

        lax.fori_loop(0, jnp.minimum(tile, prompt_tiles), full, 0)
        for part in range(TILE // BLOCK):
            position = tile * (TILE // BLOCK) + part
            block = block_at(slot_ref[position])
            step(
                block_at(position),
                [kn_ref[head, block, :] for head in range(heads)],
                [kt_ref[head, :, block] for head in range(heads)],
                [vn_ref[head, block, :] for head in range(heads)],
                part * BLOCK,
                True,
            )
        for head in range(heads):
            dq = dq_ref[head]
            product = dq * qa_ref[head, :HD, here].astype(f32)
            for lane in range(TILE // PAD):
                scale_ref[head] += product[:, lane * PAD : (lane + 1) * PAD]
            scaled = (dq * (factor_ref[...] * LN2)).astype(bf16)
            for part in range(TILE // BLOCK):
                slot = slot_ref[tile * (TILE // BLOCK) + part]
                dqkv_ref[slot // 2, head * HD : (head + 1) * HD, half_at(slot)] = scaled[
                    :, part * BLOCK : (part + 1) * BLOCK
                ]
        return carry

    lax.fori_loop(0, num_tiles, query_tile, 0)

    def finish(block, carry):
        slot = slot_ref[block]
        owner, to = slot // 2, half_at(slot)
        at = pl.ds(pl.multiple_of(block * BLOCK, BLOCK), BLOCK)
        for head in range(heads):
            row = width + head * HD
            dqkv_ref[owner, row : row + HD, to] = (dk_ref[head, :, at] * LN2).astype(bf16)
            row = 2 * width + head * HD
            dqkv_ref[owner, row : row + HD, to] = dv_ref[head, :, at].astype(bf16)
        return carry

    lax.fori_loop(0, num_blocks, finish, 0)
    sums = functools.reduce(jnp.add, [scale_ref[head] for head in range(heads)])
    sums = jnp.concatenate([sums, jnp.zeros((PAD - HD, PAD), f32)], axis=0).T
    dscale_ref[...] = jnp.sum(sums, axis=0, keepdims=True)


def in_vmem(count):
    return [pl.BlockSpec(memory_space=pltpu.VMEM)] * count


def params():
    return pltpu.CompilerParams(vmem_limit_bytes=60 * 1024 * 1024)


def attention_forward(order, most, qt, kn, vt, parts):
    heads, tokens = kn.shape[:2]
    return pl.pallas_call(
        functools.partial(forward_kernel, heads),
        name="attention_forward",
        out_shape=[
            jax.ShapeDtypeStruct((heads, 1, tokens), f32),
            jax.ShapeDtypeStruct((parts, heads * HD, tokens // parts), bf16),
        ],
        in_specs=[pl.BlockSpec(memory_space=pltpu.SMEM)]
        + in_vmem(2)
        + [pl.BlockSpec(memory_space=pl.ANY)] * 2,
        out_specs=in_vmem(2),
        scratch_shapes=[
            pltpu.SMEM(order.shape, jnp.int32),
            pltpu.VMEM(kn.shape, bf16),
            pltpu.VMEM(vt.shape, bf16),
            pltpu.VMEM((heads, HD + EXTRA, TILE), f32),
            pltpu.VMEM((heads, 1, TILE), f32),
            pltpu.SemaphoreType.DMA((2,)),
        ],
        compiler_params=params(),
        cost_estimate=attention_cost(heads, tokens, 2),
    )(order, most, qt, kn, vt)


def attention_cost(heads, tokens, passes):
    pairs = heads * tokens * tokens // 2
    return pl.CostEstimate(
        flops=2 * passes * pairs * BLOCK, bytes_accessed=tokens * D, transcendentals=pairs
    )


def attention_backward(order, kept, mixed, dmixed, factor):
    qt, kt, kn, vn, lse = kept
    heads, tokens = kn.shape[:2]
    return pl.pallas_call(
        functools.partial(backward_kernel, heads),
        name="attention_backward",
        out_shape=[
            jax.ShapeDtypeStruct((mixed.shape[0], 3 * heads * HD, mixed.shape[2]), bf16),
            jax.ShapeDtypeStruct((1, PAD), f32),
        ],
        in_specs=[pl.BlockSpec(memory_space=pltpu.SMEM)]
        + in_vmem(1)
        + [pl.BlockSpec(memory_space=pl.ANY)] * 3
        + in_vmem(4),
        out_specs=in_vmem(2),
        scratch_shapes=[
            pltpu.SMEM(order.shape, jnp.int32),
            pltpu.VMEM(kt.shape, bf16),
            pltpu.VMEM(kn.shape, bf16),
            pltpu.VMEM(vn.shape, bf16),
            pltpu.VMEM((heads, PAD, tokens), bf16),
            pltpu.VMEM((heads, PAD, tokens), bf16),
            pltpu.VMEM((heads, HD, TILE), f32),
            pltpu.VMEM((heads, HD, tokens), f32),
            pltpu.VMEM((heads, HD, tokens), f32),
            pltpu.VMEM((heads, HD, PAD), f32),
            pltpu.SemaphoreType.DMA((3,)),
        ],
        compiler_params=params(),
        cost_estimate=attention_cost(heads, tokens, 5),
    )(order, qt, kt, kn, vn, lse, mixed, dmixed, factor)


def middle_kernel(
    parts,
    groups,
    mixed_ref,
    x_ref,
    dy_ref,
    weights_ref,
    gain_ref,
    *refs,
):
    out_ref, dmid_ref, dmixed_ref, gain_grad_ref = refs[:4]
    chunk_refs = refs[4 : 4 + groups]
    (
        w_ref,
        attn_ref,
        dattn_ref,
        act_ref,
        normed_ref,
        dhidden_ref,
        dbranch_ref,
        grad_ref,
        theirs_ref,
        w_sem,
        attn_sem,
        dattn_sem,
        pair_sem,
    ) = refs[4 + groups :]
    here = lax.axis_index("ctx")
    group = lax.axis_index("fsdp")
    core = lax.rem(here, 2)
    other = here + 1 - 2 * core
    peers = [lax.rem(here + step, parts) for step in range(1, parts)]
    tokens = x_ref.shape[0]
    width = mixed_ref.shape[1]
    held = theirs_ref.shape[2]
    loads = [
        pltpu.make_async_copy(weights_ref.at[index], w_ref.at[index], w_sem.at[index])
        for index in range(3)
    ]
    for load in loads:
        load.start()

    barrier = pltpu.get_barrier_semaphore()
    for peer in peers:
        pl.semaphore_signal(barrier, inc=1, device_id={"ctx": peer})
    pl.semaphore_wait(barrier, parts - 1)

    def lanes(part):
        return pl.ds(pl.multiple_of(part * BLOCK, BLOCK), BLOCK)

    def attn_copy(part, peer, source):
        return pltpu.make_async_remote_copy(
            src_ref=mixed_ref.at[peer, :, lanes(part)],
            dst_ref=attn_ref.at[source, :, lanes(part)],
            send_sem=attn_sem.at[0, part, peer],
            recv_sem=attn_sem.at[1, part, source],
            device_id={"ctx": peer},
        )

    def dattn_copy(part, peer, source):
        return pltpu.make_async_remote_copy(
            src_ref=dattn_ref.at[peer, :, lanes(part)],
            dst_ref=dmixed_ref.at[source, :, lanes(part)],
            send_sem=dattn_sem.at[0, part, peer],
            recv_sem=dattn_sem.at[1, part, source],
            device_id={"ctx": peer},
        )

    def rows_of(owner, lane):
        start = pl.multiple_of((owner * 2 + lane) * held, 16)
        return pl.ds(start, held)

    def pair_copy(index, owner, lane):
        return pltpu.make_async_remote_copy(
            src_ref=grad_ref.at[index, rows_of(owner, lane), :],
            dst_ref=theirs_ref.at[index, owner],
            send_sem=pair_sem.at[0, index, owner],
            recv_sem=pair_sem.at[1, index, owner],
            device_id={"ctx": other},
        )

    for part in range(tokens // BLOCK):
        for peer in peers:
            attn_copy(part, peer, here).start()
    attn_ref[here] = mixed_ref[here]
    gain_grad_ref[...] = jnp.zeros(gain_grad_ref.shape, f32)
    for load in loads:
        load.wait()
    gain = gain_ref[...]

    def layer(part, carry):
        rows = lanes(part)
        for peer in peers:
            attn_copy(part, here, peer).wait_recv()
        attn = attn_ref[:, :, rows].reshape(D, BLOCK)
        mid = x_ref[rows, :].astype(f32) + dot(attn, w_ref[0], (0, 0))
        scale = rms_scale(mid)
        unit = mid * scale
        normed = (unit * gain).astype(bf16)
        normed_ref[rows, :] = normed
        hidden = dot(normed, w_ref[1])
        gate = jax.nn.sigmoid(hidden)
        act = (hidden * gate).astype(bf16)
        act_ref[rows, :] = act
        dy = dy_ref[rows, :]
        dact = dot(dy, w_ref[2], (1, 1))
        dhidden = (dact * gate * (1.0 + hidden * (1.0 - gate))).astype(bf16)
        dhidden_ref[rows, :] = dhidden
        dnormed = dot(dhidden, w_ref[1], (1, 1))
        dunit = dnormed * gain
        dmid = dy.astype(f32) + scale * (
            dunit - unit * jnp.mean(dunit * unit, axis=-1, keepdims=True)
        )
        dmid_ref[rows, :] = dmid
        dbranch = dmid.astype(bf16)
        dbranch_ref[rows, :] = dbranch
        dattn = dot(w_ref[0], dbranch, (1, 1)).astype(bf16).reshape(parts, width, BLOCK)
        dattn_ref[:, :, rows] = dattn
        for peer in peers:
            dattn_copy(part, peer, here).start()
        dmixed_ref[here, :, rows] = dattn_ref[here, :, rows]
        out_ref[rows, :] = (mid + dot(act, w_ref[2])).astype(bf16)
        gain_grad_ref[...] += jnp.sum(dnormed * unit, axis=0, keepdims=True)
        return carry

    lax.fori_loop(0, tokens // BLOCK, layer, 0)

    def down_rows(index, carry):
        rows = lanes(index)
        grad_ref[2, rows, :] = dot(act_ref[:, rows], dy_ref[...], (0, 0)).astype(bf16)
        return carry

    def up_rows(index, carry):
        rows = lanes(index)
        grad_ref[1, rows, :] = dot(normed_ref[:, rows], dhidden_ref[...], (0, 0)).astype(bf16)
        return carry

    def out_rows(index, carry):
        rows = pl.ds(pl.multiple_of(index * width, 16), width)
        grad_ref[0, rows, :] = dot(attn_ref[index], dbranch_ref[...]).astype(bf16)
        return carry

    for index, count, run in (
        (2, D // BLOCK, down_rows),
        (1, D // BLOCK, up_rows),
        (0, parts, out_rows),
    ):
        lax.fori_loop(0, count, run, 0)
        for owner in range(groups):
            pair_copy(index, owner, 1 - core).start()
    for step in range(groups):
        owner = group ^ step
        for index in (2, 1, 0):
            pair_copy(index, owner, core).wait_recv()
            chunk_refs[step][index] = (
                grad_ref[index, rows_of(owner, core), :].astype(f32)
                + theirs_ref[index, owner].astype(f32)
            ).astype(bf16)
    for part in range(tokens // BLOCK):
        for peer in peers:
            dattn_copy(part, here, peer).wait_recv()
            dattn_copy(part, peer, here).wait_send()
            attn_copy(part, peer, here).wait_send()
    for index in range(3):
        for owner in range(groups):
            pair_copy(index, owner, 1 - core).wait_send()


def middle(parts, groups, mixed, rows, cotangent, weights, gain):
    rows_dev = rows.shape[0]
    half = D // groups // 2
    dma = pltpu.SemaphoreType.DMA
    halves = rows_dev // BLOCK
    return pl.pallas_call(
        functools.partial(middle_kernel, parts, groups),
        name="middle",
        out_shape=[
            jax.ShapeDtypeStruct((rows_dev, D), bf16),
            jax.ShapeDtypeStruct((rows_dev, D), f32),
            jax.ShapeDtypeStruct(mixed.shape, bf16),
            jax.ShapeDtypeStruct((1, D), f32),
        ]
        + [jax.ShapeDtypeStruct((3, half, D), bf16)] * groups,
        in_specs=in_vmem(3) + [pl.BlockSpec(memory_space=pl.ANY)] + in_vmem(1),
        out_specs=in_vmem(4 + groups),
        scratch_shapes=[
            pltpu.VMEM((3, D, D), bf16),
            pltpu.VMEM(mixed.shape, bf16),
            pltpu.VMEM(mixed.shape, bf16),
            pltpu.VMEM((rows_dev, D), bf16),
            pltpu.VMEM((rows_dev, D), bf16),
            pltpu.VMEM((rows_dev, D), bf16),
            pltpu.VMEM((rows_dev, D), bf16),
            pltpu.VMEM((3, D, D), bf16),
            pltpu.VMEM((3, groups, half, D), bf16),
            dma((3,)),
            dma((2, halves, parts)),
            dma((2, halves, parts)),
            dma((2, 3, groups)),
        ],
        compiler_params=pltpu.CompilerParams(
            vmem_limit_bytes=60 * 1024 * 1024, collective_id=3, has_side_effects=True
        ),
    )(mixed, rows, cotangent, weights, gain)


def reduce_kernel(
    parts,
    groups,
    dq_in_ref,
    wt_in_ref,
    units_ref,
    wc_ref,
    small_ref,
    *refs,
):
    chunk_in_refs = refs[:groups]
    (
        down_ref,
        up_ref,
        own_ref,
        ugather_ref,
        mgather_ref,
        sgather_ref,
        dq_ref,
        wt_ref,
        chunk_ref,
        held_ref,
        total_ref,
        u_ref,
        usum_ref,
        msum_ref,
        pair_ref,
        sum_ref,
        urecv_ref,
        mlp_ref,
        mrecv_ref,
        part_ref,
        column_ref,
        smine_ref,
        srecv_ref,
        pair_sem,
        sum_sem,
        u_sem,
        m_sem,
        line_sem,
        side_sem,
        small_sem,
        cross_sem,
        load_sem,
        held_sem,
        keep_sem,
    ) = refs[groups:]
    chips = parts // 2
    here = lax.axis_index("ctx")
    group = lax.axis_index("fsdp")
    core = lax.rem(here, 2)
    chip = here // 2
    other = here + 1 - 2 * core
    ctx_peers = [lax.rem(here + step, parts) for step in range(1, parts)]
    chip_peers = [lax.rem(chip + step, chips) for step in range(1, chips)]
    group_peers = [lax.rem(group + step, groups) for step in range(1, groups)]

    loads = [
        pltpu.make_async_copy(ref, chunk_ref.at[index], load_sem.at[index])
        for index, ref in enumerate(chunk_in_refs)
    ]
    loads.append(pltpu.make_async_copy(dq_in_ref, dq_ref, load_sem.at[groups]))
    loads.append(pltpu.make_async_copy(wt_in_ref, wt_ref, load_sem.at[groups + 1]))
    for load in loads:
        load.start()

    def unit_load(piece):
        slot = lax.rem(piece, 2)
        return pltpu.make_async_copy(units_ref.at[piece], held_ref.at[slot], held_sem.at[slot])

    for piece in range(2):
        unit_load(piece).start()

    barrier = pltpu.get_barrier_semaphore()
    for peer in ctx_peers:
        pl.semaphore_signal(barrier, inc=1, device_id={"ctx": peer})
    for peer in group_peers:
        pl.semaphore_signal(barrier, inc=1, device_id={"fsdp": peer})

    def send(source, target, sems, device):
        return pltpu.make_async_remote_copy(
            src_ref=source,
            dst_ref=target,
            send_sem=sems[0],
            recv_sem=sems[1],
            device_id=device,
        )

    def pair_copy(index):
        return send(
            dq_in_ref.at[index, 1 - core],
            pair_ref.at[index],
            (pair_sem.at[0, index], pair_sem.at[1, index]),
            {"ctx": other},
        )

    def u_copy(peer, source):
        return send(
            u_ref.at[peer],
            urecv_ref.at[source],
            (u_sem.at[0, peer], u_sem.at[1, source]),
            {"fsdp": peer},
        )

    def m_copy(peer, source):
        return send(
            mlp_ref.at[peer],
            mrecv_ref.at[source],
            (m_sem.at[0, peer], m_sem.at[1, source]),
            {"ctx": 2 * peer + core},
        )

    for load in loads[:groups]:
        load.wait()
    share = mlp_ref.shape[2]
    for matrix in range(3):
        total = functools.reduce(
            jnp.add, [chunk_ref[step, matrix].astype(f32) for step in range(groups)]
        )
        for index in range(chips):
            mlp_ref[index, matrix] = total[index * share : (index + 1) * share].astype(bf16)
    pl.semaphore_wait(barrier, parts + groups - 2)
    for peer in chip_peers:
        m_copy(peer, chip).start()
    for index in range(chips):
        pair_copy(index).start()
    for load in loads[groups:]:
        load.wait()

    rows_half = own_ref.shape[0] // 2

    def partial(target, index):
        rows = pl.ds(pl.multiple_of(index * rows_half, rows_half), rows_half)
        part_ref[rows, :] = dot(dq_ref[target, core, :, rows], wt_ref[core], (0, 0)) + dot(
            pair_ref[target, :, rows], wt_ref[1 - core], (0, 0)
        )
        return rows

    def sum_copy(way, target, index):
        ref = sum_ref.at[way + target, pl.ds(index * rows_half, rows_half)]
        sems = (sum_sem.at[0, way, target, index], sum_sem.at[1, way, target, index])
        return send(ref, ref, sems, {"ctx": here + (2 if way else -2)})

    def reduce_step(step):
        last = step == chips - 2
        for way, target, active, first, out_ref in (
            (0, step - (chips - 1) + chip, step >= chips - 1 - chip, chip == chips - 1, down_ref),
            (1, chips - 1 - step + chip, step >= chip, chip == 0, up_ref),
        ):

            @pl.when(active)
            def _():
                def half(index, carry):
                    rows = partial(target, index)

                    @pl.when(first)
                    def _():
                        sum_ref[way + target, rows] = part_ref[rows, :].astype(bf16)

                    @pl.when(jnp.logical_not(first))
                    def _():
                        sum_copy(way, target, index).wait_recv()
                        sum_ref[way + target, rows] = (
                            part_ref[rows, :] + sum_ref[way + target, rows].astype(f32)
                        ).astype(bf16)

                    if last:
                        out_ref[rows, :] = sum_ref[way + target, rows]
                    else:
                        sum_copy(way, target, index).start()
                    return carry

                lax.fori_loop(0, 2, half, 0)

            if last:

                @pl.when(jnp.logical_not(active))
                def _():
                    out_ref[...] = jnp.zeros(out_ref.shape, bf16)

    gathers = (ugather_ref, mgather_ref)
    sums = (usum_ref, msum_ref)

    def keep_copy(which):
        return pltpu.make_async_copy(sums[which], gathers[which].at[here], keep_sem.at[which])

    def line_copy(which, way, step, piece):
        ref = gathers[which].at[2 * piece + core]
        sems = (line_sem.at[0, which, way, step], line_sem.at[1, which, way, step])
        source = sums[which] if step == 0 else ref
        return send(source, ref, sems, {"ctx": here + (2 if way else -2)})

    def side_copy(which, piece, lane, own=False):
        ref = gathers[which].at[2 * piece + lane]
        sems = (side_sem.at[0, which, piece], side_sem.at[1, which, piece])
        return send(sums[which] if own else ref, ref, sems, {"ctx": other})

    def line_sends(which, step, go):
        @pl.when((chip < chips - 1) & (chip - step >= 0))
        def _():
            go(line_copy(which, 1, step, chip - step))

        @pl.when((chip > 0) & (chip + step <= chips - 1))
        def _():
            go(line_copy(which, 0, step, chip + step))

    def line_receive(which, step):
        @pl.when(chip - 1 - step >= 0)
        def _():
            line_copy(which, 1, step, chip - 1 - step).wait_recv()
            side_copy(which, chip - 1 - step, core).start()

        @pl.when(chip + 1 + step <= chips - 1)
        def _():
            line_copy(which, 0, step, chip + 1 + step).wait_recv()
            side_copy(which, chip + 1 + step, core).start()

    def small_copy(peer, source):
        return send(
            smine_ref,
            srecv_ref.at[source],
            (small_sem.at[0, peer], small_sem.at[1, source]),
            {"ctx": peer},
        )

    def cross_copy(peer, source):
        return send(
            sgather_ref.at[group],
            sgather_ref.at[source],
            (cross_sem.at[0, peer], cross_sem.at[1, source]),
            {"fsdp": peer},
        )

    for index in range(chips):
        pair_copy(index).wait_recv()
    reduce_step(0)

    total_ref[...] = jnp.zeros(total_ref.shape, f32)

    def accumulate(piece, carry):
        unit_load(piece).wait()
        total_ref[...] += dot(dq_ref[piece // 2, lax.rem(piece, 2)], held_ref[lax.rem(piece, 2)])

        @pl.when(piece + 2 < parts)
        def _():
            unit_load(piece + 2).start()

        return carry

    lax.fori_loop(0, parts, accumulate, 0)
    u_ref[...] = total_ref[...].T.astype(bf16).reshape(u_ref.shape)
    for peer in group_peers:
        u_copy(peer, group).start()

    total = mlp_ref[chip].astype(f32)
    for peer in chip_peers:
        m_copy(chip, peer).wait_recv()
        total = total + mrecv_ref[peer].astype(f32)
    msum_ref[...] = total.astype(bf16)
    keep_copy(1).start()
    side_copy(1, chip, core, True).start()
    line_sends(1, 0, lambda copy: copy.start())

    total = u_ref[group].astype(f32)
    for peer in group_peers:
        u_copy(group, peer).wait_recv()
        total = total + urecv_ref[peer].astype(f32)
    usum_ref[...] = total.astype(bf16)
    keep_copy(0).start()
    side_copy(0, chip, core, True).start()
    line_sends(0, 0, lambda copy: copy.start())
    held = total.shape[0]
    gain = jnp.sum(total * wc_ref[...].astype(f32), axis=1, keepdims=True)
    column_ref[...] = jnp.zeros(column_ref.shape, f32)
    column_ref[:held, :] = jnp.broadcast_to(gain, (held, PAD))
    flat = column_ref[...].T[:1]
    smine_ref[...] = small_ref[...]
    for row in range(column_ref.shape[0] // PAD):
        smine_ref[row : row + 1, :] = flat[:, row * PAD : (row + 1) * PAD]
    for peer in ctx_peers:
        small_copy(peer, here).start()

    for step in range(1, chips):
        if step == 1:
            reduce_step(step)
        for which in range(2):
            line_receive(which, step - 1)
            if step <= chips - 2:
                line_sends(which, step, lambda copy: copy.start())
        if 1 < step <= chips - 2:
            reduce_step(step)
        if step == 1:
            small = smine_ref[...]
            for peer in ctx_peers:
                small_copy(here, peer).wait_recv()
                small = small + srecv_ref[peer]
            sgather_ref[group] = small
            for peer in group_peers:
                cross_copy(peer, group).start()

    for index in range(2):
        rows = partial(chip, index)
        own_ref[rows, :] = part_ref[rows, :].astype(bf16)

    for which in range(2):
        keep_copy(which).wait()
        for piece in range(chips):
            side_copy(which, piece, 1 - core).wait_recv()
            side_copy(which, piece, core).wait_send()
        for step in range(chips - 1):
            line_sends(which, step, lambda copy: copy.wait_send())
    for index in range(chips):
        pair_copy(index).wait_send()
    for peer in group_peers:
        cross_copy(group, peer).wait_recv()
        cross_copy(peer, group).wait_send()
        u_copy(peer, group).wait_send()
    for peer in chip_peers:
        m_copy(peer, chip).wait_send()
    for peer in ctx_peers:
        small_copy(peer, here).wait_send()
    for step in range(chips - 2):

        @pl.when(step >= chips - 1 - chip)
        def _():
            for index in range(2):
                sum_copy(0, step - (chips - 1) + chip, index).wait_send()

        @pl.when(step >= chip)
        def _():
            for index in range(2):
                sum_copy(1, chips - 1 - step + chip, index).wait_send()


def reduce_gradients(parts, groups, dqkv, w_pair, units, w_columns, small, chunks):
    chips = parts // 2
    mlp_shape = (chips, 3, chunks[0].shape[1] // chips, D)
    rows_dev = dqkv.shape[3]
    rows, width = w_columns.shape
    lanes = -(-rows // PAD) * PAD
    dma = pltpu.SemaphoreType.DMA
    anywhere = pl.BlockSpec(memory_space=pl.ANY)
    u_shape = (groups, rows, width)
    return pl.pallas_call(
        functools.partial(reduce_kernel, parts, groups),
        name="reduce_gradients",
        out_shape=[
            jax.ShapeDtypeStruct((rows_dev, D), bf16),
            jax.ShapeDtypeStruct((rows_dev, D), bf16),
            jax.ShapeDtypeStruct((rows_dev, D), bf16),
            jax.ShapeDtypeStruct((parts, rows, width), bf16),
            jax.ShapeDtypeStruct((parts,) + mlp_shape[1:], bf16),
            jax.ShapeDtypeStruct((groups,) + small.shape, f32),
        ],
        in_specs=[anywhere] * 3 + in_vmem(2) + [anywhere] * groups,
        out_specs=in_vmem(3) + [anywhere] * 2 + in_vmem(1),
        scratch_shapes=[
            pltpu.VMEM(dqkv.shape, bf16),
            pltpu.VMEM(w_pair.shape, bf16),
            pltpu.VMEM((groups,) + chunks[0].shape, bf16),
            pltpu.VMEM((2,) + units.shape[1:], bf16),
            pltpu.VMEM((width, D), f32),
            pltpu.VMEM(u_shape, bf16),
            pltpu.VMEM(u_shape[1:], bf16),
            pltpu.VMEM(mlp_shape[1:], bf16),
            pltpu.VMEM((chips,) + dqkv.shape[2:], bf16),
            pltpu.VMEM((chips + 1, rows_dev, D), bf16),
            pltpu.VMEM(u_shape, bf16),
            pltpu.VMEM(mlp_shape, bf16),
            pltpu.VMEM(mlp_shape, bf16),
            pltpu.VMEM((rows_dev, D), f32),
            pltpu.VMEM((lanes, PAD), f32),
            pltpu.VMEM(small.shape, f32),
            pltpu.VMEM((parts,) + small.shape, f32),
            dma((2, chips)),
            dma((2, 2, chips, 2)),
            dma((2, groups)),
            dma((2, chips)),
            dma((2, 2, 2, chips)),
            dma((2, 2, chips)),
            dma((2, parts)),
            dma((2, groups)),
            dma((groups + 2,)),
            dma((2,)),
            dma((2,)),
        ],
        compiler_params=pltpu.CompilerParams(
            vmem_limit_bytes=60 * 1024 * 1024, collective_id=1, has_side_effects=True
        ),
    )(dqkv, w_pair, units, w_columns, small, *chunks)


def update_kernel(rates, qkv_ref, gain_ref, mlp_ref, *refs):
    sets = len(rates)
    parts, rows, width = qkv_ref.shape
    width = width // 3
    for index, rate in enumerate(rates):
        weight, first, second = (ref[...] for ref in refs[3 * index : 3 * index + 3])
        if index == 0:
            pieces = [qkv_ref[part].astype(f32) for part in range(parts)]
            gradient = jnp.concatenate(
                [piece[:, at * width : (at + 1) * width] for at in range(3) for piece in pieces],
                axis=1,
            )
            gradient = gradient * gain_ref[...]
        else:
            gradient = mlp_ref[0, index - 1].astype(f32)
        outs = refs[3 * sets + 4 * index : 3 * sets + 4 * index + 4]
        new, first, second = adamw(weight, first, second, gradient, rate, decay_rate)
        outs[0][...] = new
        outs[1][...] = first
        outs[2][...] = second
        outs[3][...] = new.astype(bf16)


def update(rates, parts, qkv, gain, mlp, *arrays):
    rows = arrays[0].shape[0]
    chips = parts // 2
    step_rows = rows // parts
    if step_rows % 8 == 0:

        def owner(i):
            return (2 * lax.rem(i, chips) + i // chips, 0, 0, 0)

    else:
        step_rows = 32
        mlp = mlp.reshape(chips, 2, 3, rows // parts, D).transpose(2, 1, 0, 3, 4)
        mlp = mlp.reshape(3, rows // step_rows, step_rows, D).transpose(1, 0, 2, 3)

        def owner(i):
            return (i, 0, 0, 0)

    in_specs = [
        pl.BlockSpec((parts, step_rows, qkv.shape[2]), lambda i: (0, i, 0)),
        pl.BlockSpec((step_rows, 1), lambda i: (i, 0)),
        pl.BlockSpec((1, 3, step_rows, D), owner),
    ]
    specs, shapes, moved = [], [], 0
    for array in arrays:
        in_specs.append(pl.BlockSpec((step_rows, array.shape[1]), lambda i: (i, 0)))
    for index in range(len(rates)):
        shape = arrays[3 * index].shape
        shapes += [jax.ShapeDtypeStruct(shape, f32)] * 3 + [jax.ShapeDtypeStruct(shape, bf16)]
        specs += [pl.BlockSpec((step_rows, shape[1]), lambda i: (i, 0))] * 4
        moved += shape[0] * shape[1] * 28
    return pl.pallas_call(
        functools.partial(update_kernel, rates),
        name="update_weights",
        grid=(rows // step_rows,),
        in_specs=in_specs,
        out_specs=specs,
        out_shape=shapes,
        compiler_params=params(),
        cost_estimate=pl.CostEstimate(flops=moved, bytes_accessed=moved, transcendentals=0),
    )(qkv, gain, mlp, *arrays)


def finish_kernel(down_ref, up_ref, own_ref, x_ref, dmid_ref, layer_ref, out_ref, same_ref):
    here = pl.ds(pl.multiple_of(pl.program_id(0) * PAD, PAD), PAD)
    rows = x_ref[...].astype(f32)
    scale = rms_scale(rows)
    unit = rows * scale
    dunit = (
        own_ref[...].astype(f32) + down_ref[here, :].astype(f32) + up_ref[here, :].astype(f32)
    )
    grad = dmid_ref[...] + scale * (
        dunit - unit * jnp.mean(dunit * unit, axis=-1, keepdims=True)
    )
    out_ref[...] = grad.astype(bf16)
    same_ref[...] = layer_ref[...]


def finish(*arrays):
    rows = arrays[0].shape[0]
    spec = pl.BlockSpec((PAD, D), lambda i: (i, 0))
    return pl.pallas_call(
        finish_kernel,
        name="finish",
        grid=(rows // PAD,),
        in_specs=in_vmem(2) + [spec] * 4,
        out_specs=[spec] * 2,
        out_shape=[jax.ShapeDtypeStruct((rows, D), bf16)] * 2,
        compiler_params=pltpu.CompilerParams(vmem_limit_bytes=40 * 1024 * 1024),
    )(*arrays)


def body(
    parts,
    groups,
    inputs,
    cotangent,
    block_order,
    w_qkv,
    m_qkv,
    v_qkv,
    w_out,
    m_out,
    v_out,
    w_up,
    m_up,
    v_up,
    w_down,
    m_down,
    v_down,
    small_params,
    small_m,
    small_v,
):
    heads = H // parts
    width = heads * HD
    rows_dev = inputs.shape[1]
    tokens = rows_dev * parts
    here = lax.axis_index("ctx")
    order = block_order[0]
    gain_two = small_params[D : 2 * D]
    query_scale = small_params[2 * D :]
    group = lax.axis_index("fsdp")
    rows = w_qkv.shape[0]

    (
        unit_all,
        mlp_full,
        w_pair,
        qt,
        kt,
        vt,
        kn,
        vn,
        w_columns,
        gain_rows,
        factor_two,
        most,
    ) = gather_rows(
        parts, groups, heads, inputs[0], w_qkv, w_out, w_up, w_down, small_params[None]
    )
    lse, mixed = attention_forward(order, most, qt, kn, vt, parts)
    kept = (qt, kt, kn, vn, lse)
    output, dmid, dmixed, gain_two_grad, *chunks = middle(
        parts,
        groups,
        mixed,
        inputs[0],
        cotangent[0],
        mlp_full.reshape(3, D, D),
        gain_two[None],
    )
    for step in range(1, groups):
        swap = [(i, i ^ step) for i in range(groups)]
        chunks[step] = lax.ppermute(chunks[step], "fsdp", swap)
    dqkv, dscale = attention_backward(order, kept, mixed, dmixed, factor_two)
    scale_grad = (
        dscale[0, :HD]
        / factor_two[:, 0]
        * (scale_base / math.sqrt(HD))
        * jax.nn.sigmoid(query_scale)
    )
    lanes = -(-rows // PAD) * PAD
    small_rows = -(-(lanes + D + PAD) // (8 * PAD)) * 8
    small = jnp.concatenate([jnp.zeros((lanes,), f32), gain_two_grad[0], scale_grad])
    small = jnp.pad(small, (0, small_rows * PAD - small.shape[0])).reshape(small_rows, PAD)
    send_down, send_up, own_part, u_all, mlp_all, small_all = reduce_gradients(
        parts,
        groups,
        dqkv.reshape(parts // 2, 2, 3 * width, rows_dev),
        w_pair,
        unit_all,
        w_columns,
        small,
        chunks,
    )
    got_down = lax.ppermute(send_down, "ctx", [(i, i - 2) for i in range(2, parts)])
    got_up = lax.ppermute(send_up, "ctx", [(i, i + 2) for i in range(parts - 2)])
    rate_qkv = qkv_rate_base / math.sqrt(D)
    rate_out = 0.5 / math.sqrt(max(D // 256, 1))
    rate_up = 0.5 / math.sqrt(D)
    rate_down = 0.5 / math.sqrt(FF)
    updated = update(
        (rate_qkv, rate_out, rate_up, rate_down),
        parts,
        u_all,
        gain_rows,
        mlp_all,
        w_qkv,
        m_qkv,
        v_qkv,
        w_out,
        m_out,
        v_out,
        w_up,
        m_up,
        v_up,
        w_down,
        m_down,
        v_down,
    )
    flat = small_all.reshape(groups, small_rows * PAD)
    rest = jnp.sum(flat[:, lanes : lanes + D + HD], axis=0)
    small_total = jnp.concatenate([flat[:, :rows].reshape(D), rest])
    small_set = adamw(small_params, small_m, small_v, small_total, small_rate, 0.0)
    input_grad, output = finish(got_down, got_up, own_part, inputs[0], dmid, output)
    return (
        output[None],
        input_grad[None],
        *updated,
        *small_set,
    )


def solution(mesh):
    rows = P("fsdp", "ctx", None)
    weight = P("fsdp", None)
    return jax.shard_map(
        functools.partial(body, mesh.shape["ctx"], mesh.shape["fsdp"]),
        mesh=mesh,
        in_specs=(rows, rows, weight) + (weight,) * 12 + (P(),) * 3,
        out_specs=(rows, rows) + (weight,) * 16 + (P(),) * 3,
        check_vma=False,
    )
```

```python
import functools
import math

import jax
import jax.numpy as jnp
from jax import lax
from jax.experimental import pallas as pl
from jax.experimental.pallas import tpu as pltpu
from jax.sharding import PartitionSpec as P

D = 1280
H = 16
HD = 80
FF = 1280
BLOCK = 256
CONT = 512
STEP = 3
PAD = 128
EXTRA = 16
TILE = CONT
SCORE_BOUND = 95.0

bf16 = jnp.bfloat16
f32 = jnp.float32

norm_eps = 1e-06
beta_one = 0.5
beta_two = 0.5
adam_eps = 1e-08
decay_rate = 0.1
small_rate = 0.75
qkv_rate_base = 1.0
scale_base = 1.442695
LOG2E = math.log2(math.e)
LN2 = math.log(2.0)


def rms_scale(values):
    return lax.rsqrt(jnp.mean(values * values, axis=-1, keepdims=True) + norm_eps)


def adamw(weight, first, second, gradient, step_rate, decay_on):
    first_new = beta_one * first + (1.0 - beta_one) * gradient
    second_new = beta_two * second + (1.0 - beta_two) * gradient * gradient
    corr_one = 1.0 - beta_one**STEP
    corr_two = 1.0 - beta_two**STEP
    update = first_new / corr_one / (jnp.sqrt(second_new / corr_two) + adam_eps)
    weight_new = weight - step_rate * (update + decay_on * weight)
    return (weight_new, first_new, second_new)


def dot(left, right, contract=(1, 0)):
    return lax.dot_general(
        left, right, (((contract[0],), (contract[1],)), ((), ())), preferred_element_type=f32
    )


def fill_slots(order_ref, slot_ref):
    def place(slot, carry):
        slot_ref[order_ref[slot]] = slot
        return carry

    lax.fori_loop(0, order_ref.shape[0], place, 0)


def three_rows(row):
    high = row.astype(bf16)
    rest = row - high.astype(f32)
    middle = rest.astype(bf16)
    low = (rest - middle.astype(f32)).astype(bf16)
    index = lax.broadcasted_iota(jnp.int32, (EXTRA, row.shape[1]), 0)
    zero = jnp.zeros((EXTRA, row.shape[1]), f32)
    rows = jnp.where(index == 0, high.astype(f32), zero)
    rows = jnp.where(index == 1, middle.astype(f32), rows)
    rows = jnp.where(index == 2, low.astype(f32), rows)
    return rows.astype(bf16)


def tile_at(tile):
    return pl.ds(pl.multiple_of(tile * TILE, TILE), TILE)


def block_at(slot):
    return pl.ds(pl.multiple_of(slot * BLOCK, BLOCK), BLOCK)


def tile_lanes(ref, head, slot_ref, tile, rows=slice(None)):
    first, second = slot_ref[2 * tile], slot_ref[2 * tile + 1]
    return jnp.concatenate(
        [ref[head, rows, block_at(first)], ref[head, rows, block_at(second)]], axis=1
    )


def tile_rows(ref, head, slot_ref, tile):
    first, second = slot_ref[2 * tile], slot_ref[2 * tile + 1]
    return jnp.concatenate([ref[head, block_at(first), :], ref[head, block_at(second), :]], axis=0)


def half_at(slot):
    return pl.ds(pl.multiple_of(lax.rem(slot, 2) * BLOCK, BLOCK), BLOCK)


def causal(shape):
    key = lax.broadcasted_iota(jnp.int32, shape, 0)
    query = lax.broadcasted_iota(jnp.int32, shape, 1)
    return key <= query


def gather_kernel(
    parts,
    groups,
    heads,
    x_ref,
    wqkv_ref,
    wout_ref,
    wup_ref,
    wdown_ref,
    small_ref,
    unit_ref,
    full_ref,
    wpair_ref,
    qt_out_ref,
    kt_out_ref,
    vt_out_ref,
    kn_out_ref,
    vn_out_ref,
    wcol_ref,
    gain_ref,
    factor_ref,
    most_ref,
    qt_ref,
    kt_ref,
    vt_ref,
    kn_ref,
    vn_ref,
    rows_ref,
    wstage_ref,
    mstage_ref,
    gained_ref,
    mlp_ref,
    wrecv_ref,
    wflip_ref,
    line_sem,
    side_sem,
    keep_sem,
    w_sem,
    lane_sem,
    mlp_sem,
    cross_sem,
    own_sem,
    stage_sem,
    lanes_sem,
    sides_sem,
):
    chips = parts // 2
    here = lax.axis_index("ctx")
    group = lax.axis_index("fsdp")
    core = lax.rem(here, 2)
    chip = here // 2
    other = here + 1 - 2 * core
    width = heads * HD
    group_peers = [lax.rem(group + step, groups) for step in range(1, groups)]

    barrier = pltpu.get_barrier_semaphore()
    pl.semaphore_signal(barrier, inc=1, device_id={"ctx": other})
    for peer in group_peers:
        pl.semaphore_signal(barrier, inc=1, device_id={"fsdp": peer})
    for step in (1, chips - 1):
        peer = lax.rem(chip + step, chips) * 2 + core
        pl.semaphore_signal(barrier, inc=1, device_id={"ctx": peer})

    def send(source, target, sems, device):
        return pltpu.make_async_remote_copy(
            src_ref=source,
            dst_ref=target,
            send_sem=sems[0],
            recv_sem=sems[1],
            device_id=device,
        )

    halves = rows_ref.shape[1] // BLOCK

    def line_copy(way, step, piece, part):
        ref = rows_ref.at[2 * piece + core, block_at(part)]
        sems = (line_sem.at[0, way, step, part], line_sem.at[1, way, step, part])
        return send(ref, ref, sems, {"ctx": here + (2 if way else -2)})

    def side_copy(piece, lane, part):
        ref = rows_ref.at[2 * piece + lane, block_at(part)]
        sems = (side_sem.at[0, piece, part], side_sem.at[1, piece, part])
        return send(ref, ref, sems, {"ctx": other})

    def results(slot):
        to = block_at(slot)
        copies = [
            pltpu.make_async_copy(ref.at[:, :, to], out.at[:, :, to], lanes_sem.at[index, slot])
            for index, (ref, out) in enumerate(
                ((qt_ref, qt_out_ref), (kt_ref, kt_out_ref), (vt_ref, vt_out_ref))
            )
        ]
        return copies + [
            pltpu.make_async_copy(ref.at[:, to], out.at[:, to], sides_sem.at[index, slot])
            for index, (ref, out) in enumerate(((kn_ref, kn_out_ref), (vn_ref, vn_out_ref)))
        ]

    def w_copy(peer, source):
        sems = (w_sem.at[0, peer], w_sem.at[1, source])
        return send(gained_ref, wrecv_ref.at[source], sems, {"fsdp": peer})

    def lane_copy(lane):
        ref = wpair_ref.at[lane]
        return send(ref, ref, (lane_sem.at[0], lane_sem.at[1]), {"ctx": other})

    def mlp_copy(peer, source):
        sems = (mlp_sem.at[0, peer], mlp_sem.at[1, source])
        return send(mlp_ref.at[:, core], full_ref.at[:, source, core], sems, {"fsdp": peer})

    def cross_copy(source, lane):
        ref = full_ref.at[:, source, lane]
        sems = (cross_sem.at[0, source], cross_sem.at[1, source])
        return send(ref, ref, sems, {"ctx": other})

    def keep_copy(piece):
        return pltpu.make_async_copy(rows_ref.at[piece], unit_ref.at[piece], keep_sem.at[piece])

    own_copy = pltpu.make_async_copy(mlp_ref, full_ref.at[:, group], own_sem)

    stages = [pltpu.make_async_copy(wqkv_ref, wstage_ref, stage_sem.at[0])] + [
        pltpu.make_async_copy(ref, mstage_ref.at[index], stage_sem.at[index + 1])
        for index, ref in enumerate((wout_ref, wup_ref, wdown_ref))
    ]
    for stage in stages:
        stage.start()
    rows = x_ref[...].astype(f32)
    rows_ref[here] = (rows * rms_scale(rows)).astype(bf16)
    pl.semaphore_wait(barrier, groups + 2)

    def forward(way, step, piece, part):
        @pl.when((chip < chips - 1) if way else (chip > 0))
        def _():
            line_copy(way, step, piece, part).start()

    for part in range(halves):
        for way in range(2):
            forward(way, 0, chip, part)
        side_copy(chip, core, part).start()
    held = gain_ref.shape[0]
    lanes = -(-held // PAD) * PAD
    gains = jnp.broadcast_to(small_ref[:, :D], (8, D))
    gains = pltpu.roll(gains, lax.rem(D - group * held, D), 1)[:1, :lanes]
    gain_ref[...] = jnp.broadcast_to(gains, (PAD, lanes)).T[:held, :1]
    soft = jnp.log(1.0 + jnp.exp(small_ref[:, 2 * D :])) * (scale_base / math.sqrt(HD) * LOG2E)
    soft = jnp.concatenate([soft, jnp.zeros((1, PAD - HD), f32)], axis=1)
    factor_ref[...] = jnp.broadcast_to(soft, (PAD, PAD)).T[:HD, :1]
    shift = lax.rem(D - here * width, D)
    stages[0].wait()
    for part in range(3):
        turned = pltpu.roll(wstage_ref[:, part * D : (part + 1) * D], shift, 1)
        gained_ref[part] = (turned[:, :width] * gain_ref[...]).astype(bf16)
        wcol_ref[:, part * width : (part + 1) * width] = turned[:, :width].astype(bf16)
    for peer in group_peers:
        w_copy(peer, group).start()
    for index in range(3):
        stages[index + 1].wait()
        mlp_ref[index] = mstage_ref[index].astype(bf16).reshape(mlp_ref.shape[1:])
    own_copy.start()
    keep_copy(here).start()
    wrecv_ref[group] = gained_ref[...]
    for peer in group_peers:
        w_copy(group, peer).wait_recv()
    for peer in group_peers:
        mlp_copy(peer, group).start()
    for part in range(3):
        flipped = wrecv_ref[:, part].reshape(D, width).T
        wflip_ref[part * width : (part + 1) * width] = flipped
    wpair_ref[core] = wflip_ref[...]
    lane_copy(core).start()

    extra_row = lax.broadcasted_iota(jnp.int32, (PAD - HD, BLOCK), 0)
    extra = jnp.where(extra_row < 3, 1.0, 0.0)
    spare = jnp.zeros((PAD - HD, BLOCK), bf16)

    most_ref[...] = jnp.zeros(most_ref.shape, f32)

    def project(piece, part):
        slot = piece * halves + part
        to = block_at(slot)
        result = dot(wflip_ref[...], rows_ref[piece, block_at(part), :], (1, 1))
        for head in range(heads):
            query, key, value = (
                result[share * width + head * HD : share * width + (head + 1) * HD]
                for share in range(3)
            )
            query = query * factor_ref[...]
            for row, rows in enumerate((query, key)):
                most_ref[row : row + 1] = jnp.maximum(
                    most_ref[row : row + 1], jnp.sum(rows * rows, axis=0, keepdims=True)
                )
            qt_ref[head, :HD, to] = query.astype(bf16)
            qt_ref[head, HD:, to] = spare
            kt_ref[head, :, to] = key.astype(bf16)
            vt_ref[head, :HD, to] = value.astype(bf16)
            vt_ref[head, HD:, to] = jnp.ones((EXTRA, BLOCK), bf16)
            kn_ref[head, to, :] = jnp.concatenate([key, extra], axis=0).T.astype(bf16)
            vn_ref[head, to, :] = jnp.concatenate([value, extra], axis=0).T.astype(bf16)
        for copy in results(slot):
            copy.start()

    def visit(index, carry):
        distance, part = index // halves, lax.rem(index, halves)
        for way in range(2):
            piece = chip - distance if way else chip + distance
            valid = (piece >= 0) if way else (piece <= chips - 1)

            @pl.when(valid & (distance > 0))
            def _():
                line_copy(way, distance - 1, piece, part).wait_recv()
                side_copy(piece, core, part).start()
                forward(way, distance, piece, part)

                @pl.when(part == halves - 1)
                def _():
                    keep_copy(2 * piece + core).start()

        for way in range(2):
            piece = chip - distance if way else chip + distance
            valid = (piece >= 0) if way else ((piece <= chips - 1) & (distance > 0))

            @pl.when(valid)
            def _():
                project(2 * piece + core, part)
                side_copy(piece, 1 - core, part).wait_recv()
                project(2 * piece + 1 - core, part)

                @pl.when(part == halves - 1)
                def _():
                    keep_copy(2 * piece + 1 - core).start()

        return carry

    lax.fori_loop(0, chips * halves, visit, 0)

    for peer in group_peers:
        mlp_copy(group, peer).wait_recv()
        cross_copy(peer, core).start()
    for peer in group_peers:
        cross_copy(peer, 1 - core).wait_recv()
        cross_copy(peer, core).wait_send()
        w_copy(peer, group).wait_send()
        mlp_copy(peer, group).wait_send()
    own_copy.wait()
    lane_copy(1 - core).wait_recv()
    lane_copy(core).wait_send()

    def drain(piece, carry):
        keep_copy(2 * piece).wait()
        keep_copy(2 * piece + 1).wait()
        for part in range(halves):
            side_copy(piece, core, part).wait_send()

            @pl.when((piece <= chip) & (chip < chips - 1))
            def _():
                line_copy(1, chip - piece, piece, part).wait_send()

            @pl.when((piece >= chip) & (chip > 0))
            def _():
                line_copy(0, piece - chip, piece, part).wait_send()

        return carry

    lax.fori_loop(0, chips, drain, 0)

    def settle(slot, carry):
        for copy in results(slot):
            copy.wait()
        return carry

    lax.fori_loop(0, 2 * chips * halves, settle, 0)


def gather_rows(parts, groups, heads, rows, w_qkv, w_out, w_up, w_down, small):
    rows_dev = rows.shape[0]
    held = w_qkv.shape[0]
    tokens = parts * rows_dev
    dma = pltpu.SemaphoreType.DMA
    chips = parts // 2
    anywhere = pl.BlockSpec(memory_space=pl.ANY)
    return pl.pallas_call(
        functools.partial(gather_kernel, parts, groups, heads),
        name="gather_rows",
        out_shape=[
            jax.ShapeDtypeStruct((parts, rows_dev, D), bf16),
            jax.ShapeDtypeStruct((3, groups, 2, held // 2, D), bf16),
            jax.ShapeDtypeStruct((2, 3 * heads * HD, D), bf16),
            jax.ShapeDtypeStruct((heads, PAD, tokens), bf16),
            jax.ShapeDtypeStruct((heads, HD, tokens), bf16),
            jax.ShapeDtypeStruct((heads, HD + EXTRA, tokens), bf16),
            jax.ShapeDtypeStruct((heads, tokens, PAD), bf16),
            jax.ShapeDtypeStruct((heads, tokens, PAD), bf16),
            jax.ShapeDtypeStruct((held, 3 * heads * HD), bf16),
            jax.ShapeDtypeStruct((held, 1), f32),
            jax.ShapeDtypeStruct((HD, 1), f32),
            jax.ShapeDtypeStruct((8, BLOCK), f32),
        ],
        in_specs=in_vmem(1) + [anywhere] * 4 + in_vmem(1),
        out_specs=[anywhere] * 2 + in_vmem(1) + [anywhere] * 5 + in_vmem(4),
        scratch_shapes=[
            pltpu.VMEM((heads, PAD, tokens), bf16),
            pltpu.VMEM((heads, HD, tokens), bf16),
            pltpu.VMEM((heads, HD + EXTRA, tokens), bf16),
            pltpu.VMEM((heads, tokens, PAD), bf16),
            pltpu.VMEM((heads, tokens, PAD), bf16),
            pltpu.VMEM((parts, rows_dev, D), bf16),
            pltpu.VMEM((held, 3 * D), f32),
            pltpu.VMEM((3, held, D), f32),
            pltpu.VMEM((3, held, heads * HD), bf16),
            pltpu.VMEM((3, 2, held // 2, D), bf16),
            pltpu.VMEM((groups, 3, held, heads * HD), bf16),
            pltpu.VMEM((3 * heads * HD, D), bf16),
            dma((2, 2, chips, rows_dev // BLOCK)),
            dma((2, chips, rows_dev // BLOCK)),
            dma((parts,)),
            dma((2, groups)),
            dma((2,)),
            dma((2, groups)),
            dma((2, groups)),
            dma,
            dma((4,)),
            dma((3, tokens // BLOCK)),
            dma((2, tokens // BLOCK)),
        ],
        compiler_params=pltpu.CompilerParams(
            vmem_limit_bytes=60 * 1024 * 1024, collective_id=2, has_side_effects=True
        ),
    )(rows, w_qkv, w_out, w_up, w_down, small)


def forward_kernel(
    heads,
    order_ref,
    most_ref,
    qt_ref,
    kn_in_ref,
    vt_in_ref,
    lse_ref,
    ot_ref,
    slot_ref,
    kn_ref,
    vt_ref,
    acc_ref,
    top_ref,
    load_sem,
):
    loads = [
        pltpu.make_async_copy(source, target, load_sem.at[index])
        for index, (source, target) in enumerate(((kn_in_ref, kn_ref), (vt_in_ref, vt_ref)))
    ]
    for load in loads:
        load.start()
    fill_slots(order_ref, slot_ref)
    tokens = kn_ref.shape[1]
    num_tiles = tokens // TILE
    prompt_tiles = num_tiles // 2

    bounded = (
        jnp.max(most_ref[0:1]) * jnp.max(most_ref[1:2]) <= SCORE_BOUND * SCORE_BOUND
    )
    for load in loads:
        load.wait()

    def run(shifted):
        def query_tile(tile, carry):
            queries = [tile_lanes(qt_ref, head, slot_ref, tile) for head in range(heads)]
            if shifted:
                top_ref[...] = jnp.full(top_ref.shape, -1e30, f32)
            else:
                top_ref[...] = jnp.zeros(top_ref.shape, f32)
            acc_ref[...] = jnp.zeros(acc_ref.shape, f32)

            def step(key_rows, value_lanes, start, masked):
                scores = [dot(key_rows[head], queries[head][:, start:]) for head in range(heads)]
                if masked:
                    allowed = causal(scores[0].shape)
                    scores = [jnp.where(allowed, score, -1e30) for score in scores]
                if shifted:
                    olds = [top_ref[head, :, start:] for head in range(heads)]
                    tops = [
                        jnp.maximum(old, jnp.max(score, axis=0, keepdims=True))
                        for old, score in zip(olds, scores)
                    ]
                    scores = [score - top for score, top in zip(scores, tops)]
                    for head in range(heads):
                        acc_ref[head, :, start:] *= jnp.exp2(olds[head] - tops[head])
                        top_ref[head, :, start:] = tops[head]
                probs = [jnp.exp2(score).astype(bf16) for score in scores]
                for head in range(heads):
                    acc_ref[head, :, start:] += dot(value_lanes[head], probs[head])

            def full(key_tile, inner):
                step(
                    [tile_rows(kn_ref, head, slot_ref, key_tile) for head in range(heads)],
                    [tile_lanes(vt_ref, head, slot_ref, key_tile) for head in range(heads)],
                    0,
                    False,
                )
                return inner

            lax.fori_loop(0, jnp.minimum(tile, prompt_tiles), full, 0)
            for part in range(TILE // BLOCK):
                block = block_at(slot_ref[tile * (TILE // BLOCK) + part])
                step(
                    [kn_ref[head, block, :] for head in range(heads)],
                    [vt_ref[head, :, block] for head in range(heads)],
                    part * BLOCK,
                    True,
                )
            for head in range(heads):
                acc = acc_ref[head]
                mass = acc[HD : HD + 1]
                mixed = (acc[:HD] / mass).astype(bf16)
                lse_ref[head, :, tile_at(tile)] = top_ref[head] + jnp.log2(mass)
                for part in range(TILE // BLOCK):
                    slot = slot_ref[tile * (TILE // BLOCK) + part]
                    ot_ref[slot // 2, head * HD : (head + 1) * HD, half_at(slot)] = mixed[
                        :, part * BLOCK : (part + 1) * BLOCK
                    ]
            return carry

        lax.fori_loop(0, num_tiles, query_tile, 0)

    @pl.when(bounded)
    def _():
        run(False)

    @pl.when(jnp.logical_not(bounded))
    def _():
        run(True)


def backward_kernel(
    heads,
    order_ref,
    qt_ref,
    kt_in_ref,
    kn_in_ref,
    vn_in_ref,
    lse_ref,
    ot_ref,
    dt_ref,
    factor_ref,
    dqkv_ref,
    dscale_ref,
    slot_ref,
    kt_ref,
    kn_ref,
    vn_ref,
    qa_ref,
    da_ref,
    dq_ref,
    dk_ref,
    dv_ref,
    scale_ref,
    load_sem,
):
    loads = [
        pltpu.make_async_copy(source, target, load_sem.at[index])
        for index, (source, target) in enumerate(
            ((kn_in_ref, kn_ref), (vn_in_ref, vn_ref), (kt_in_ref, kt_ref))
        )
    ]
    for load in loads:
        load.start()
    fill_slots(order_ref, slot_ref)
    tokens = kn_ref.shape[1]
    num_blocks = tokens // BLOCK
    num_tiles = tokens // TILE
    prompt_tiles = num_tiles // 2
    width = heads * HD

    def prepare(block, carry):
        slot = slot_ref[block]
        to = pl.ds(pl.multiple_of(block * BLOCK, BLOCK), BLOCK)
        for head in range(heads):
            rows = slice(head * HD, (head + 1) * HD)
            grad = dt_ref[slot // 2, rows, half_at(slot)]
            mixed = ot_ref[slot // 2, rows, half_at(slot)]
            delta = jnp.sum(grad.astype(f32) * mixed.astype(f32), axis=0, keepdims=True)
            da_ref[head, :HD, to] = grad
            da_ref[head, HD : HD + EXTRA, to] = three_rows(-delta)
            da_ref[head, HD + EXTRA :, to] = jnp.zeros((PAD - HD - EXTRA, BLOCK), bf16)
            qa_ref[head, :HD, to] = qt_ref[head, :HD, block_at(slot)]
            qa_ref[head, HD : HD + EXTRA, to] = three_rows(-lse_ref[head, :, to])
            qa_ref[head, HD + EXTRA :, to] = jnp.zeros((PAD - HD - EXTRA, BLOCK), bf16)
        return carry

    lax.fori_loop(0, num_blocks, prepare, 0)
    dk_ref[...] = jnp.zeros(dk_ref.shape, f32)
    dv_ref[...] = jnp.zeros(dv_ref.shape, f32)
    scale_ref[...] = jnp.zeros(scale_ref.shape, f32)
    for load in loads:
        load.wait()

    def query_tile(tile, carry):
        here = tile_at(tile)
        dq_ref[...] = jnp.zeros(dq_ref.shape, f32)

        def step(keys, key_rows, key_lanes, value_rows, start, masked):
            to = pl.ds(pl.multiple_of(tile * TILE + start, BLOCK), TILE - start)
            queries = [qa_ref[head, :, to] for head in range(heads)]
            grads = [da_ref[head, :, to] for head in range(heads)]
            scores = [dot(key_rows[head], queries[head]) for head in range(heads)]
            spreads = [dot(value_rows[head], grads[head]) for head in range(heads)]
            probs = [jnp.exp2(score) for score in scores]
            if masked:
                allowed = causal(scores[0].shape)
                probs = [jnp.where(allowed, prob, 0.0) for prob in probs]
            dscores = [(prob * spread).astype(bf16) for prob, spread in zip(probs, spreads)]
            for head in range(heads):
                dv_ref[head, :, keys] += dot(grads[head][:HD], probs[head].astype(bf16), (1, 1))
                dk_ref[head, :, keys] += dot(queries[head][:HD], dscores[head], (1, 1))
                dq_ref[head, :, start:] += dot(key_lanes[head], dscores[head])

        def full(key_tile, inner):
            step(
                tile_at(key_tile),
                [tile_rows(kn_ref, head, slot_ref, key_tile) for head in range(heads)],
                [tile_lanes(kt_ref, head, slot_ref, key_tile) for head in range(heads)],
                [tile_rows(vn_ref, head, slot_ref, key_tile) for head in range(heads)],
                0,
                False,
            )
            return inner

        lax.fori_loop(0, jnp.minimum(tile, prompt_tiles), full, 0)
        for part in range(TILE // BLOCK):
            position = tile * (TILE // BLOCK) + part
            block = block_at(slot_ref[position])
            step(
                block_at(position),
                [kn_ref[head, block, :] for head in range(heads)],
                [kt_ref[head, :, block] for head in range(heads)],
                [vn_ref[head, block, :] for head in range(heads)],
                part * BLOCK,
                True,
            )
        for head in range(heads):
            dq = dq_ref[head]
            product = dq * qa_ref[head, :HD, here].astype(f32)
            for lane in range(TILE // PAD):
                scale_ref[head] += product[:, lane * PAD : (lane + 1) * PAD]
            scaled = (dq * (factor_ref[...] * LN2)).astype(bf16)
            for part in range(TILE // BLOCK):
                slot = slot_ref[tile * (TILE // BLOCK) + part]
                dqkv_ref[slot // 2, head * HD : (head + 1) * HD, half_at(slot)] = scaled[
                    :, part * BLOCK : (part + 1) * BLOCK
                ]
        return carry

    lax.fori_loop(0, num_tiles, query_tile, 0)

    def finish(block, carry):
        slot = slot_ref[block]
        owner, to = slot // 2, half_at(slot)
        at = pl.ds(pl.multiple_of(block * BLOCK, BLOCK), BLOCK)
        for head in range(heads):
            row = width + head * HD
            dqkv_ref[owner, row : row + HD, to] = (dk_ref[head, :, at] * LN2).astype(bf16)
            row = 2 * width + head * HD
            dqkv_ref[owner, row : row + HD, to] = dv_ref[head, :, at].astype(bf16)
        return carry

    lax.fori_loop(0, num_blocks, finish, 0)
    sums = functools.reduce(jnp.add, [scale_ref[head] for head in range(heads)])
    sums = jnp.concatenate([sums, jnp.zeros((PAD - HD, PAD), f32)], axis=0).T
    dscale_ref[...] = jnp.sum(sums, axis=0, keepdims=True)


def in_vmem(count):
    return [pl.BlockSpec(memory_space=pltpu.VMEM)] * count


def params(mebibytes):
    return pltpu.CompilerParams(vmem_limit_bytes=mebibytes * 1024 * 1024)


def attention_forward(order, most, qt, kn, vt, parts):
    heads, tokens = kn.shape[:2]
    return pl.pallas_call(
        functools.partial(forward_kernel, heads),
        name="attention_forward",
        out_shape=[
            jax.ShapeDtypeStruct((heads, 1, tokens), f32),
            jax.ShapeDtypeStruct((parts, heads * HD, tokens // parts), bf16),
        ],
        in_specs=[pl.BlockSpec(memory_space=pltpu.SMEM)]
        + in_vmem(2)
        + [pl.BlockSpec(memory_space=pl.ANY)] * 2,
        out_specs=in_vmem(2),
        scratch_shapes=[
            pltpu.SMEM(order.shape, jnp.int32),
            pltpu.VMEM(kn.shape, bf16),
            pltpu.VMEM(vt.shape, bf16),
            pltpu.VMEM((heads, HD + EXTRA, TILE), f32),
            pltpu.VMEM((heads, 1, TILE), f32),
            pltpu.SemaphoreType.DMA((2,)),
        ],
        compiler_params=params(60),
        cost_estimate=attention_cost(heads, tokens, 2),
    )(order, most, qt, kn, vt)


def attention_cost(heads, tokens, passes):
    pairs = heads * tokens * tokens // 2
    return pl.CostEstimate(
        flops=2 * passes * pairs * BLOCK, bytes_accessed=tokens * D, transcendentals=pairs
    )


def attention_backward(order, kept, mixed, dmixed, factor):
    qt, kt, kn, vn, lse = kept
    heads, tokens = kn.shape[:2]
    return pl.pallas_call(
        functools.partial(backward_kernel, heads),
        name="attention_backward",
        out_shape=[
            jax.ShapeDtypeStruct((mixed.shape[0], 3 * heads * HD, mixed.shape[2]), bf16),
            jax.ShapeDtypeStruct((1, PAD), f32),
        ],
        in_specs=[pl.BlockSpec(memory_space=pltpu.SMEM)]
        + in_vmem(1)
        + [pl.BlockSpec(memory_space=pl.ANY)] * 3
        + in_vmem(4),
        out_specs=in_vmem(2),
        scratch_shapes=[
            pltpu.SMEM(order.shape, jnp.int32),
            pltpu.VMEM(kt.shape, bf16),
            pltpu.VMEM(kn.shape, bf16),
            pltpu.VMEM(vn.shape, bf16),
            pltpu.VMEM((heads, PAD, tokens), bf16),
            pltpu.VMEM((heads, PAD, tokens), bf16),
            pltpu.VMEM((heads, HD, TILE), f32),
            pltpu.VMEM((heads, HD, tokens), f32),
            pltpu.VMEM((heads, HD, tokens), f32),
            pltpu.VMEM((heads, HD, PAD), f32),
            pltpu.SemaphoreType.DMA((3,)),
        ],
        compiler_params=params(60),
        cost_estimate=attention_cost(heads, tokens, 5),
    )(order, qt, kt, kn, vn, lse, mixed, dmixed, factor)


def middle_kernel(
    parts,
    groups,
    mixed_ref,
    x_ref,
    dy_ref,
    weights_ref,
    gain_ref,
    *refs,
):
    out_ref, dmid_ref, dmixed_ref, gain_grad_ref = refs[:4]
    chunk_refs = refs[4 : 4 + groups]
    (
        w_ref,
        attn_ref,
        dattn_ref,
        act_ref,
        normed_ref,
        dhidden_ref,
        dbranch_ref,
        grad_ref,
        theirs_ref,
        w_sem,
        attn_sem,
        dattn_sem,
        pair_sem,
    ) = refs[4 + groups :]
    here = lax.axis_index("ctx")
    group = lax.axis_index("fsdp")
    core = lax.rem(here, 2)
    other = here + 1 - 2 * core
    peers = [lax.rem(here + step, parts) for step in range(1, parts)]
    tokens = x_ref.shape[0]
    width = mixed_ref.shape[1]
    held = theirs_ref.shape[2]
    loads = [
        pltpu.make_async_copy(weights_ref.at[index], w_ref.at[index], w_sem.at[index])
        for index in range(3)
    ]
    for load in loads:
        load.start()

    barrier = pltpu.get_barrier_semaphore()
    for peer in peers:
        pl.semaphore_signal(barrier, inc=1, device_id={"ctx": peer})
    pl.semaphore_wait(barrier, parts - 1)

    def lanes(part):
        return pl.ds(pl.multiple_of(part * BLOCK, BLOCK), BLOCK)

    def attn_copy(part, peer, source):
        return pltpu.make_async_remote_copy(
            src_ref=mixed_ref.at[peer, :, lanes(part)],
            dst_ref=attn_ref.at[source, :, lanes(part)],
            send_sem=attn_sem.at[0, part, peer],
            recv_sem=attn_sem.at[1, part, source],
            device_id={"ctx": peer},
        )

    def dattn_copy(part, peer, source):
        return pltpu.make_async_remote_copy(
            src_ref=dattn_ref.at[peer, :, lanes(part)],
            dst_ref=dmixed_ref.at[source, :, lanes(part)],
            send_sem=dattn_sem.at[0, part, peer],
            recv_sem=dattn_sem.at[1, part, source],
            device_id={"ctx": peer},
        )

    def rows_of(owner, lane):
        start = pl.multiple_of((owner * 2 + lane) * held, 16)
        return pl.ds(start, held)

    def pair_copy(index, owner, lane):
        return pltpu.make_async_remote_copy(
            src_ref=grad_ref.at[index, rows_of(owner, lane), :],
            dst_ref=theirs_ref.at[index, owner],
            send_sem=pair_sem.at[0, index, owner],
            recv_sem=pair_sem.at[1, index, owner],
            device_id={"ctx": other},
        )

    for part in range(tokens // BLOCK):
        for peer in peers:
            attn_copy(part, peer, here).start()
    attn_ref[here] = mixed_ref[here]
    gain_grad_ref[...] = jnp.zeros(gain_grad_ref.shape, f32)
    for load in loads:
        load.wait()
    gain = gain_ref[...]

    def layer(part, carry):
        rows = lanes(part)
        for peer in peers:
            attn_copy(part, here, peer).wait_recv()
        attn = attn_ref[:, :, rows].reshape(D, BLOCK)
        mid = x_ref[rows, :].astype(f32) + dot(attn, w_ref[0], (0, 0))
        scale = rms_scale(mid)
        unit = mid * scale
        normed = (unit * gain).astype(bf16)
        normed_ref[rows, :] = normed
        hidden = dot(normed, w_ref[1])
        gate = jax.nn.sigmoid(hidden)
        act = (hidden * gate).astype(bf16)
        act_ref[rows, :] = act
        dy = dy_ref[rows, :]
        dact = dot(dy, w_ref[2], (1, 1))
        dhidden = (dact * gate * (1.0 + hidden * (1.0 - gate))).astype(bf16)
        dhidden_ref[rows, :] = dhidden
        dnormed = dot(dhidden, w_ref[1], (1, 1))
        dunit = dnormed * gain
        dmid = dy.astype(f32) + scale * (
            dunit - unit * jnp.mean(dunit * unit, axis=-1, keepdims=True)
        )
        dmid_ref[rows, :] = dmid
        dbranch = dmid.astype(bf16)
        dbranch_ref[rows, :] = dbranch
        dattn = dot(w_ref[0], dbranch, (1, 1)).astype(bf16).reshape(parts, width, BLOCK)
        dattn_ref[:, :, rows] = dattn
        for peer in peers:
            dattn_copy(part, peer, here).start()
        dmixed_ref[here, :, rows] = dattn_ref[here, :, rows]
        out_ref[rows, :] = (mid + dot(act, w_ref[2])).astype(bf16)
        gain_grad_ref[...] += jnp.sum(dnormed * unit, axis=0, keepdims=True)
        return carry

    lax.fori_loop(0, tokens // BLOCK, layer, 0)

    def down_rows(index, carry):
        rows = lanes(index)
        grad_ref[2, rows, :] = dot(act_ref[:, rows], dy_ref[...], (0, 0)).astype(bf16)
        return carry

    def up_rows(index, carry):
        rows = lanes(index)
        grad_ref[1, rows, :] = dot(normed_ref[:, rows], dhidden_ref[...], (0, 0)).astype(bf16)
        return carry

    def out_rows(index, carry):
        rows = pl.ds(pl.multiple_of(index * width, 16), width)
        grad_ref[0, rows, :] = dot(attn_ref[index], dbranch_ref[...]).astype(bf16)
        return carry

    for index, count, run in (
        (2, D // BLOCK, down_rows),
        (1, D // BLOCK, up_rows),
        (0, parts, out_rows),
    ):
        lax.fori_loop(0, count, run, 0)
        for owner in range(groups):
            pair_copy(index, owner, 1 - core).start()
    for step in range(groups):
        owner = group ^ step
        for index in (2, 1, 0):
            pair_copy(index, owner, core).wait_recv()
            chunk_refs[step][index] = (
                grad_ref[index, rows_of(owner, core), :].astype(f32)
                + theirs_ref[index, owner].astype(f32)
            ).astype(bf16)
    for part in range(tokens // BLOCK):
        for peer in peers:
            dattn_copy(part, here, peer).wait_recv()
            dattn_copy(part, peer, here).wait_send()
            attn_copy(part, peer, here).wait_send()
    for index in range(3):
        for owner in range(groups):
            pair_copy(index, owner, 1 - core).wait_send()


def middle(parts, groups, mixed, rows, cotangent, weights, gain):
    rows_dev = rows.shape[0]
    half = D // groups // 2
    dma = pltpu.SemaphoreType.DMA
    halves = rows_dev // BLOCK
    return pl.pallas_call(
        functools.partial(middle_kernel, parts, groups),
        name="middle",
        out_shape=[
            jax.ShapeDtypeStruct((rows_dev, D), bf16),
            jax.ShapeDtypeStruct((rows_dev, D), f32),
            jax.ShapeDtypeStruct(mixed.shape, bf16),
            jax.ShapeDtypeStruct((1, D), f32),
        ]
        + [jax.ShapeDtypeStruct((3, half, D), bf16)] * groups,
        in_specs=in_vmem(3) + [pl.BlockSpec(memory_space=pl.ANY)] + in_vmem(1),
        out_specs=in_vmem(4 + groups),
        scratch_shapes=[
            pltpu.VMEM((3, D, D), bf16),
            pltpu.VMEM(mixed.shape, bf16),
            pltpu.VMEM(mixed.shape, bf16),
            pltpu.VMEM((rows_dev, D), bf16),
            pltpu.VMEM((rows_dev, D), bf16),
            pltpu.VMEM((rows_dev, D), bf16),
            pltpu.VMEM((rows_dev, D), bf16),
            pltpu.VMEM((3, D, D), bf16),
            pltpu.VMEM((3, groups, half, D), bf16),
            dma((3,)),
            dma((2, halves, parts)),
            dma((2, halves, parts)),
            dma((2, 3, groups)),
        ],
        compiler_params=pltpu.CompilerParams(
            vmem_limit_bytes=60 * 1024 * 1024, collective_id=3, has_side_effects=True
        ),
    )(mixed, rows, cotangent, weights, gain)


def reduce_kernel(
    parts,
    groups,
    dq_in_ref,
    wt_in_ref,
    units_ref,
    wc_ref,
    small_ref,
    *refs,
):
    chunk_in_refs = refs[:groups]
    (
        down_ref,
        up_ref,
        own_ref,
        ugather_ref,
        mgather_ref,
        sgather_ref,
        dq_ref,
        wt_ref,
        chunk_ref,
        held_ref,
        total_ref,
        u_ref,
        usum_ref,
        msum_ref,
        pair_ref,
        sum_ref,
        urecv_ref,
        mlp_ref,
        mrecv_ref,
        part_ref,
        column_ref,
        smine_ref,
        srecv_ref,
        pair_sem,
        sum_sem,
        u_sem,
        m_sem,
        line_sem,
        side_sem,
        small_sem,
        cross_sem,
        load_sem,
        held_sem,
        keep_sem,
    ) = refs[groups:]
    chips = parts // 2
    here = lax.axis_index("ctx")
    group = lax.axis_index("fsdp")
    core = lax.rem(here, 2)
    chip = here // 2
    other = here + 1 - 2 * core
    ctx_peers = [lax.rem(here + step, parts) for step in range(1, parts)]
    chip_peers = [lax.rem(chip + step, chips) for step in range(1, chips)]
    group_peers = [lax.rem(group + step, groups) for step in range(1, groups)]

    loads = [
        pltpu.make_async_copy(ref, chunk_ref.at[index], load_sem.at[index])
        for index, ref in enumerate(chunk_in_refs)
    ]
    loads.append(pltpu.make_async_copy(dq_in_ref, dq_ref, load_sem.at[groups]))
    loads.append(pltpu.make_async_copy(wt_in_ref, wt_ref, load_sem.at[groups + 1]))
    for load in loads:
        load.start()

    def unit_load(piece):
        slot = lax.rem(piece, 2)
        return pltpu.make_async_copy(units_ref.at[piece], held_ref.at[slot], held_sem.at[slot])

    for piece in range(2):
        unit_load(piece).start()

    barrier = pltpu.get_barrier_semaphore()
    for peer in ctx_peers:
        pl.semaphore_signal(barrier, inc=1, device_id={"ctx": peer})
    for peer in group_peers:
        pl.semaphore_signal(barrier, inc=1, device_id={"fsdp": peer})

    def send(source, target, sems, device):
        return pltpu.make_async_remote_copy(
            src_ref=source,
            dst_ref=target,
            send_sem=sems[0],
            recv_sem=sems[1],
            device_id=device,
        )

    def pair_copy(index):
        return send(
            dq_in_ref.at[index, 1 - core],
            pair_ref.at[index],
            (pair_sem.at[0, index], pair_sem.at[1, index]),
            {"ctx": other},
        )

    def u_copy(peer, source):
        return send(
            u_ref.at[peer],
            urecv_ref.at[source],
            (u_sem.at[0, peer], u_sem.at[1, source]),
            {"fsdp": peer},
        )

    def m_copy(peer, source):
        return send(
            mlp_ref.at[peer],
            mrecv_ref.at[source],
            (m_sem.at[0, peer], m_sem.at[1, source]),
            {"ctx": 2 * peer + core},
        )

    for load in loads[:groups]:
        load.wait()
    share = mlp_ref.shape[2]
    for matrix in range(3):
        total = functools.reduce(
            jnp.add, [chunk_ref[step, matrix].astype(f32) for step in range(groups)]
        )
        for index in range(chips):
            mlp_ref[index, matrix] = total[index * share : (index + 1) * share].astype(bf16)
    pl.semaphore_wait(barrier, parts + groups - 2)
    for peer in chip_peers:
        m_copy(peer, chip).start()
    for index in range(chips):
        pair_copy(index).start()
    for load in loads[groups:]:
        load.wait()

    rows_half = own_ref.shape[0] // 2

    def partial(target, index):
        rows = pl.ds(pl.multiple_of(index * rows_half, rows_half), rows_half)
        part_ref[rows, :] = dot(dq_ref[target, core, :, rows], wt_ref[core], (0, 0)) + dot(
            pair_ref[target, :, rows], wt_ref[1 - core], (0, 0)
        )
        return rows

    def sum_copy(way, target, index):
        ref = sum_ref.at[way + target, pl.ds(index * rows_half, rows_half)]
        sems = (sum_sem.at[0, way, target, index], sum_sem.at[1, way, target, index])
        return send(ref, ref, sems, {"ctx": here + (2 if way else -2)})

    def reduce_step(step):
        last = step == chips - 2
        for way, target, active, first, out_ref in (
            (0, step - (chips - 1) + chip, step >= chips - 1 - chip, chip == chips - 1, down_ref),
            (1, chips - 1 - step + chip, step >= chip, chip == 0, up_ref),
        ):

            @pl.when(active)
            def _():
                def half(index, carry):
                    rows = partial(target, index)

                    @pl.when(first)
                    def _():
                        sum_ref[way + target, rows] = part_ref[rows, :].astype(bf16)

                    @pl.when(jnp.logical_not(first))
                    def _():
                        sum_copy(way, target, index).wait_recv()
                        sum_ref[way + target, rows] = (
                            part_ref[rows, :] + sum_ref[way + target, rows].astype(f32)
                        ).astype(bf16)

                    if last:
                        out_ref[rows, :] = sum_ref[way + target, rows]
                    else:
                        sum_copy(way, target, index).start()
                    return carry

                lax.fori_loop(0, 2, half, 0)

            if last:

                @pl.when(jnp.logical_not(active))
                def _():
                    out_ref[...] = jnp.zeros(out_ref.shape, bf16)

    gathers = (ugather_ref, mgather_ref)
    sums = (usum_ref, msum_ref)

    def keep_copy(which):
        return pltpu.make_async_copy(sums[which], gathers[which].at[here], keep_sem.at[which])

    def line_copy(which, way, step, piece):
        ref = gathers[which].at[2 * piece + core]
        sems = (line_sem.at[0, which, way, step], line_sem.at[1, which, way, step])
        source = sums[which] if step == 0 else ref
        return send(source, ref, sems, {"ctx": here + (2 if way else -2)})

    def side_copy(which, piece, lane, own=False):
        ref = gathers[which].at[2 * piece + lane]
        sems = (side_sem.at[0, which, piece], side_sem.at[1, which, piece])
        return send(sums[which] if own else ref, ref, sems, {"ctx": other})

    def line_sends(which, step, go):
        @pl.when((chip < chips - 1) & (chip - step >= 0))
        def _():
            go(line_copy(which, 1, step, chip - step))

        @pl.when((chip > 0) & (chip + step <= chips - 1))
        def _():
            go(line_copy(which, 0, step, chip + step))

    def line_receive(which, step):
        @pl.when(chip - 1 - step >= 0)
        def _():
            line_copy(which, 1, step, chip - 1 - step).wait_recv()
            side_copy(which, chip - 1 - step, core).start()

        @pl.when(chip + 1 + step <= chips - 1)
        def _():
            line_copy(which, 0, step, chip + 1 + step).wait_recv()
            side_copy(which, chip + 1 + step, core).start()

    def small_copy(peer, source):
        return send(
            smine_ref,
            srecv_ref.at[source],
            (small_sem.at[0, peer], small_sem.at[1, source]),
            {"ctx": peer},
        )

    def cross_copy(peer, source):
        return send(
            sgather_ref.at[group],
            sgather_ref.at[source],
            (cross_sem.at[0, peer], cross_sem.at[1, source]),
            {"fsdp": peer},
        )

    for index in range(chips):
        pair_copy(index).wait_recv()
    reduce_step(0)

    total_ref[...] = jnp.zeros(total_ref.shape, f32)

    def accumulate(piece, carry):
        unit_load(piece).wait()
        total_ref[...] += dot(dq_ref[piece // 2, lax.rem(piece, 2)], held_ref[lax.rem(piece, 2)])

        @pl.when(piece + 2 < parts)
        def _():
            unit_load(piece + 2).start()

        return carry

    lax.fori_loop(0, parts, accumulate, 0)
    u_ref[...] = total_ref[...].T.astype(bf16).reshape(u_ref.shape)
    for peer in group_peers:
        u_copy(peer, group).start()

    total = mlp_ref[chip].astype(f32)
    for peer in chip_peers:
        m_copy(chip, peer).wait_recv()
        total = total + mrecv_ref[peer].astype(f32)
    msum_ref[...] = total.astype(bf16)
    keep_copy(1).start()
    side_copy(1, chip, core, True).start()
    line_sends(1, 0, lambda copy: copy.start())

    total = u_ref[group].astype(f32)
    for peer in group_peers:
        u_copy(group, peer).wait_recv()
        total = total + urecv_ref[peer].astype(f32)
    usum_ref[...] = total.astype(bf16)
    keep_copy(0).start()
    side_copy(0, chip, core, True).start()
    line_sends(0, 0, lambda copy: copy.start())
    held = total.shape[0]
    gain = jnp.sum(total * wc_ref[...].astype(f32), axis=1, keepdims=True)
    column_ref[...] = jnp.zeros(column_ref.shape, f32)
    column_ref[:held, :] = jnp.broadcast_to(gain, (held, PAD))
    flat = column_ref[...].T[:1]
    smine_ref[...] = small_ref[...]
    for row in range(column_ref.shape[0] // PAD):
        smine_ref[row : row + 1, :] = flat[:, row * PAD : (row + 1) * PAD]
    for peer in ctx_peers:
        small_copy(peer, here).start()

    for step in range(1, chips):
        if step == 1:
            reduce_step(step)
        for which in range(2):
            line_receive(which, step - 1)
            if step <= chips - 2:
                line_sends(which, step, lambda copy: copy.start())
        if 1 < step <= chips - 2:
            reduce_step(step)
        if step == 1:
            small = smine_ref[...]
            for peer in ctx_peers:
                small_copy(here, peer).wait_recv()
                small = small + srecv_ref[peer]
            sgather_ref[group] = small
            for peer in group_peers:
                cross_copy(peer, group).start()

    for index in range(2):
        rows = partial(chip, index)
        own_ref[rows, :] = part_ref[rows, :].astype(bf16)

    for which in range(2):
        keep_copy(which).wait()
        for piece in range(chips):
            side_copy(which, piece, 1 - core).wait_recv()
            side_copy(which, piece, core).wait_send()
        for step in range(chips - 1):
            line_sends(which, step, lambda copy: copy.wait_send())
    for index in range(chips):
        pair_copy(index).wait_send()
    for peer in group_peers:
        cross_copy(group, peer).wait_recv()
        cross_copy(peer, group).wait_send()
        u_copy(peer, group).wait_send()
    for peer in chip_peers:
        m_copy(peer, chip).wait_send()
    for peer in ctx_peers:
        small_copy(peer, here).wait_send()
    for step in range(chips - 2):

        @pl.when(step >= chips - 1 - chip)
        def _():
            for index in range(2):
                sum_copy(0, step - (chips - 1) + chip, index).wait_send()

        @pl.when(step >= chip)
        def _():
            for index in range(2):
                sum_copy(1, chips - 1 - step + chip, index).wait_send()


def reduce_gradients(parts, groups, dqkv, w_pair, units, w_columns, small, chunks):
    chips = parts // 2
    mlp_shape = (chips, 3, chunks[0].shape[1] // chips, D)
    rows_dev = dqkv.shape[3]
    rows, width = w_columns.shape
    lanes = -(-rows // PAD) * PAD
    dma = pltpu.SemaphoreType.DMA
    anywhere = pl.BlockSpec(memory_space=pl.ANY)
    u_shape = (groups, rows, width)
    return pl.pallas_call(
        functools.partial(reduce_kernel, parts, groups),
        name="reduce_gradients",
        out_shape=[
            jax.ShapeDtypeStruct((rows_dev, D), bf16),
            jax.ShapeDtypeStruct((rows_dev, D), bf16),
            jax.ShapeDtypeStruct((rows_dev, D), bf16),
            jax.ShapeDtypeStruct((parts, rows, width), bf16),
            jax.ShapeDtypeStruct((parts,) + mlp_shape[1:], bf16),
            jax.ShapeDtypeStruct((groups,) + small.shape, f32),
        ],
        in_specs=[anywhere] * 3 + in_vmem(2) + [anywhere] * groups,
        out_specs=in_vmem(3) + [anywhere] * 2 + in_vmem(1),
        scratch_shapes=[
            pltpu.VMEM(dqkv.shape, bf16),
            pltpu.VMEM(w_pair.shape, bf16),
            pltpu.VMEM((groups,) + chunks[0].shape, bf16),
            pltpu.VMEM((2,) + units.shape[1:], bf16),
            pltpu.VMEM((width, D), f32),
            pltpu.VMEM(u_shape, bf16),
            pltpu.VMEM(u_shape[1:], bf16),
            pltpu.VMEM(mlp_shape[1:], bf16),
            pltpu.VMEM((chips,) + dqkv.shape[2:], bf16),
            pltpu.VMEM((chips + 1, rows_dev, D), bf16),
            pltpu.VMEM(u_shape, bf16),
            pltpu.VMEM(mlp_shape, bf16),
            pltpu.VMEM(mlp_shape, bf16),
            pltpu.VMEM((rows_dev, D), f32),
            pltpu.VMEM((lanes, PAD), f32),
            pltpu.VMEM(small.shape, f32),
            pltpu.VMEM((parts,) + small.shape, f32),
            dma((2, chips)),
            dma((2, 2, chips, 2)),
            dma((2, groups)),
            dma((2, chips)),
            dma((2, 2, 2, chips)),
            dma((2, 2, chips)),
            dma((2, parts)),
            dma((2, groups)),
            dma((groups + 2,)),
            dma((2,)),
            dma((2,)),
        ],
        compiler_params=pltpu.CompilerParams(
            vmem_limit_bytes=60 * 1024 * 1024, collective_id=1, has_side_effects=True
        ),
    )(dqkv, w_pair, units, w_columns, small, *chunks)


def update_kernel(rates, qkv_ref, gain_ref, mlp_ref, *refs):
    sets = len(rates)
    parts, rows, width = qkv_ref.shape
    width = width // 3
    for index, rate in enumerate(rates):
        weight, first, second = (ref[...] for ref in refs[3 * index : 3 * index + 3])
        if index == 0:
            pieces = [qkv_ref[part].astype(f32) for part in range(parts)]
            gradient = jnp.concatenate(
                [piece[:, at * width : (at + 1) * width] for at in range(3) for piece in pieces],
                axis=1,
            )
            gradient = gradient * gain_ref[...]
        else:
            gradient = mlp_ref[0, index - 1].astype(f32)
        outs = refs[3 * sets + 4 * index : 3 * sets + 4 * index + 4]
        new, first, second = adamw(weight, first, second, gradient, rate, decay_rate)
        outs[0][...] = new
        outs[1][...] = first
        outs[2][...] = second
        outs[3][...] = new.astype(bf16)


def update(rates, parts, qkv, gain, mlp, *arrays):
    rows = arrays[0].shape[0]
    chips = parts // 2
    step_rows = rows // parts
    if step_rows % 8 == 0:

        def owner(i):
            return (2 * lax.rem(i, chips) + i // chips, 0, 0, 0)

    else:
        step_rows = 32
        mlp = mlp.reshape(chips, 2, 3, rows // parts, D).transpose(2, 1, 0, 3, 4)
        mlp = mlp.reshape(3, rows // step_rows, step_rows, D).transpose(1, 0, 2, 3)

        def owner(i):
            return (i, 0, 0, 0)

    in_specs = [
        pl.BlockSpec((parts, step_rows, qkv.shape[2]), lambda i: (0, i, 0)),
        pl.BlockSpec((step_rows, 1), lambda i: (i, 0)),
        pl.BlockSpec((1, 3, step_rows, D), owner),
    ]
    specs, shapes, moved = [], [], 0
    for array in arrays:
        in_specs.append(pl.BlockSpec((step_rows, array.shape[1]), lambda i: (i, 0)))
    for index in range(len(rates)):
        shape = arrays[3 * index].shape
        shapes += [jax.ShapeDtypeStruct(shape, f32)] * 3 + [jax.ShapeDtypeStruct(shape, bf16)]
        specs += [pl.BlockSpec((step_rows, shape[1]), lambda i: (i, 0))] * 4
        moved += shape[0] * shape[1] * 28
    return pl.pallas_call(
        functools.partial(update_kernel, rates),
        name="update_weights",
        grid=(rows // step_rows,),
        in_specs=in_specs,
        out_specs=specs,
        out_shape=shapes,
        compiler_params=params(55),
        cost_estimate=pl.CostEstimate(flops=moved, bytes_accessed=moved, transcendentals=0),
    )(qkv, gain, mlp, *arrays)


def finish_kernel(down_ref, up_ref, own_ref, x_ref, dmid_ref, layer_ref, out_ref, same_ref):
    here = pl.ds(pl.multiple_of(pl.program_id(0) * PAD, PAD), PAD)
    rows = x_ref[...].astype(f32)
    scale = rms_scale(rows)
    unit = rows * scale
    dunit = (
        own_ref[...].astype(f32) + down_ref[here, :].astype(f32) + up_ref[here, :].astype(f32)
    )
    grad = dmid_ref[...] + scale * (
        dunit - unit * jnp.mean(dunit * unit, axis=-1, keepdims=True)
    )
    out_ref[...] = grad.astype(bf16)
    same_ref[...] = layer_ref[...]


def finish(*arrays):
    rows = arrays[0].shape[0]
    spec = pl.BlockSpec((PAD, D), lambda i: (i, 0))
    return pl.pallas_call(
        finish_kernel,
        name="finish",
        grid=(rows // PAD,),
        in_specs=in_vmem(2) + [spec] * 4,
        out_specs=[spec] * 2,
        out_shape=[jax.ShapeDtypeStruct((rows, D), bf16)] * 2,
        compiler_params=params(40),
    )(*arrays)


def body(
    parts,
    groups,
    inputs,
    cotangent,
    block_order,
    w_qkv,
    m_qkv,
    v_qkv,
    w_out,
    m_out,
    v_out,
    w_up,
    m_up,
    v_up,
    w_down,
    m_down,
    v_down,
    small_params,
    small_m,
    small_v,
):
    heads = H // parts
    width = heads * HD
    rows_dev = inputs.shape[1]
    tokens = rows_dev * parts
    here = lax.axis_index("ctx")
    order = block_order[0]
    gain_two = small_params[D : 2 * D]
    query_scale = small_params[2 * D :]
    group = lax.axis_index("fsdp")
    rows = w_qkv.shape[0]

    (
        unit_all,
        mlp_full,
        w_pair,
        qt,
        kt,
        vt,
        kn,
        vn,
        w_columns,
        gain_rows,
        factor_two,
        most,
    ) = gather_rows(
        parts, groups, heads, inputs[0], w_qkv, w_out, w_up, w_down, small_params[None]
    )
    lse, mixed = attention_forward(order, most, qt, kn, vt, parts)
    kept = (qt, kt, kn, vn, lse)
    output, dmid, dmixed, gain_two_grad, *chunks = middle(
        parts,
        groups,
        mixed,
        inputs[0],
        cotangent[0],
        mlp_full.reshape(3, D, D),
        gain_two[None],
    )
    for step in range(1, groups):
        swap = [(i, i ^ step) for i in range(groups)]
        chunks[step] = lax.ppermute(chunks[step], "fsdp", swap)
    dqkv, dscale = attention_backward(order, kept, mixed, dmixed, factor_two)
    scale_grad = (
        dscale[0, :HD]
        / factor_two[:, 0]
        * (scale_base / math.sqrt(HD))
        * jax.nn.sigmoid(query_scale)
    )
    lanes = -(-rows // PAD) * PAD
    small_rows = -(-(lanes + D + PAD) // (8 * PAD)) * 8
    small = jnp.concatenate([jnp.zeros((lanes,), f32), gain_two_grad[0], scale_grad])
    small = jnp.pad(small, (0, small_rows * PAD - small.shape[0])).reshape(small_rows, PAD)
    send_down, send_up, own_part, u_all, mlp_all, small_all = reduce_gradients(
        parts,
        groups,
        dqkv.reshape(parts // 2, 2, 3 * width, rows_dev),
        w_pair,
        unit_all,
        w_columns,
        small,
        chunks,
    )
    got_down = lax.ppermute(send_down, "ctx", [(i, i - 2) for i in range(2, parts)])
    got_up = lax.ppermute(send_up, "ctx", [(i, i + 2) for i in range(parts - 2)])
    rate_qkv = qkv_rate_base / math.sqrt(D)
    rate_out = 0.5 / math.sqrt(max(D // 256, 1))
    rate_up = 0.5 / math.sqrt(D)
    rate_down = 0.5 / math.sqrt(FF)
    updated = update(
        (rate_qkv, rate_out, rate_up, rate_down),
        parts,
        u_all,
        gain_rows,
        mlp_all,
        w_qkv,
        m_qkv,
        v_qkv,
        w_out,
        m_out,
        v_out,
        w_up,
        m_up,
        v_up,
        w_down,
        m_down,
        v_down,
    )
    flat = small_all.reshape(groups, small_rows * PAD)
    rest = jnp.sum(flat[:, lanes : lanes + D + HD], axis=0)
    small_total = jnp.concatenate([flat[:, :rows].reshape(D), rest])
    small_set = adamw(small_params, small_m, small_v, small_total, small_rate, 0.0)
    input_grad, output = finish(got_down, got_up, own_part, inputs[0], dmid, output)
    return (
        output[None],
        input_grad[None],
        *updated,
        *small_set,
    )


def solution(mesh):
    rows = P("fsdp", "ctx", None)
    weight = P("fsdp", None)
    return jax.shard_map(
        functools.partial(body, mesh.shape["ctx"], mesh.shape["fsdp"]),
        mesh=mesh,
        in_specs=(rows, rows, weight) + (weight,) * 12 + (P(),) * 3,
        out_specs=(rows, rows) + (weight,) * 16 + (P(),) * 3,
        check_vma=False,
    )
```

```python
import functools
import math

import jax
import jax.numpy as jnp
from jax import lax
from jax.experimental import pallas as pl
from jax.experimental.pallas import tpu as pltpu
from jax.sharding import PartitionSpec as P

D = 1280
H = 16
HD = 80
FF = 1280
BLOCK = 256
CONT = 512
STEP = 3
PAD = 128
EXTRA = 16
TILE = CONT
SCORE_BOUND = 95.0

bf16 = jnp.bfloat16
f32 = jnp.float32

norm_eps = 1e-06
beta_one = 0.5
beta_two = 0.5
adam_eps = 1e-08
decay_rate = 0.1
small_rate = 0.75
qkv_rate_base = 1.0
scale_base = 1.442695
LOG2E = math.log2(math.e)
LN2 = math.log(2.0)


def rms_scale(values):
    return lax.rsqrt(jnp.mean(values * values, axis=-1, keepdims=True) + norm_eps)


def adamw(weight, first, second, gradient, step_rate, decay_on):
    first_new = beta_one * first + (1.0 - beta_one) * gradient
    second_new = beta_two * second + (1.0 - beta_two) * gradient * gradient
    corr_one = 1.0 - beta_one**STEP
    corr_two = 1.0 - beta_two**STEP
    update = first_new / corr_one / (jnp.sqrt(second_new / corr_two) + adam_eps)
    weight_new = weight - step_rate * (update + decay_on * weight)
    return (weight_new, first_new, second_new)


def dot(left, right, contract=(1, 0)):
    return lax.dot_general(
        left, right, (((contract[0],), (contract[1],)), ((), ())), preferred_element_type=f32
    )


def fill_slots(order_ref, slot_ref):
    def place(slot, carry):
        slot_ref[order_ref[slot]] = slot
        return carry

    lax.fori_loop(0, order_ref.shape[0], place, 0)


def three_rows(row):
    high = row.astype(bf16)
    rest = row - high.astype(f32)
    middle = rest.astype(bf16)
    low = (rest - middle.astype(f32)).astype(bf16)
    index = lax.broadcasted_iota(jnp.int32, (EXTRA, row.shape[1]), 0)
    zero = jnp.zeros((EXTRA, row.shape[1]), f32)
    rows = jnp.where(index == 0, high.astype(f32), zero)
    rows = jnp.where(index == 1, middle.astype(f32), rows)
    rows = jnp.where(index == 2, low.astype(f32), rows)
    return rows.astype(bf16)


def tile_at(tile):
    return pl.ds(pl.multiple_of(tile * TILE, TILE), TILE)


def block_at(slot):
    return pl.ds(pl.multiple_of(slot * BLOCK, BLOCK), BLOCK)


def tile_lanes(ref, head, slot_ref, tile, rows=slice(None)):
    first, second = slot_ref[2 * tile], slot_ref[2 * tile + 1]
    return jnp.concatenate(
        [ref[head, rows, block_at(first)], ref[head, rows, block_at(second)]], axis=1
    )


def tile_rows(ref, head, slot_ref, tile):
    first, second = slot_ref[2 * tile], slot_ref[2 * tile + 1]
    return jnp.concatenate([ref[head, block_at(first), :], ref[head, block_at(second), :]], axis=0)


def half_at(slot):
    return pl.ds(pl.multiple_of(lax.rem(slot, 2) * BLOCK, BLOCK), BLOCK)


def causal(shape):
    key = lax.broadcasted_iota(jnp.int32, shape, 0)
    query = lax.broadcasted_iota(jnp.int32, shape, 1)
    return key <= query


def gather_kernel(
    parts,
    groups,
    heads,
    x_ref,
    wqkv_ref,
    wout_ref,
    wup_ref,
    wdown_ref,
    small_ref,
    unit_ref,
    full_ref,
    wpair_ref,
    qt_out_ref,
    kt_out_ref,
    vt_out_ref,
    kn_out_ref,
    vn_out_ref,
    wcol_ref,
    gain_ref,
    factor_ref,
    most_ref,
    qt_ref,
    kt_ref,
    vt_ref,
    kn_ref,
    vn_ref,
    rows_ref,
    wstage_ref,
    mstage_ref,
    gained_ref,
    mlp_ref,
    wrecv_ref,
    wflip_ref,
    line_sem,
    side_sem,
    keep_sem,
    w_sem,
    lane_sem,
    mlp_sem,
    cross_sem,
    own_sem,
    stage_sem,
    lanes_sem,
    sides_sem,
):
    chips = parts // 2
    here = lax.axis_index("ctx")
    group = lax.axis_index("fsdp")
    core = lax.rem(here, 2)
    chip = here // 2
    other = here + 1 - 2 * core
    width = heads * HD
    group_peers = [lax.rem(group + step, groups) for step in range(1, groups)]

    barrier = pltpu.get_barrier_semaphore()
    pl.semaphore_signal(barrier, inc=1, device_id={"ctx": other})
    for peer in group_peers:
        pl.semaphore_signal(barrier, inc=1, device_id={"fsdp": peer})
    for step in (1, chips - 1):
        peer = lax.rem(chip + step, chips) * 2 + core
        pl.semaphore_signal(barrier, inc=1, device_id={"ctx": peer})

    def send(source, target, sems, device):
        return pltpu.make_async_remote_copy(
            src_ref=source,
            dst_ref=target,
            send_sem=sems[0],
            recv_sem=sems[1],
            device_id=device,
        )

    halves = rows_ref.shape[1] // BLOCK

    def line_copy(way, step, piece, part):
        ref = rows_ref.at[2 * piece + core, block_at(part)]
        sems = (line_sem.at[0, way, step, part], line_sem.at[1, way, step, part])
        return send(ref, ref, sems, {"ctx": here + (2 if way else -2)})

    def side_copy(piece, lane, part):
        ref = rows_ref.at[2 * piece + lane, block_at(part)]
        sems = (side_sem.at[0, piece, part], side_sem.at[1, piece, part])
        return send(ref, ref, sems, {"ctx": other})

    def results(slot):
        to = block_at(slot)
        copies = [
            pltpu.make_async_copy(ref.at[:, :, to], out.at[:, :, to], lanes_sem.at[index, slot])
            for index, (ref, out) in enumerate(
                ((qt_ref, qt_out_ref), (kt_ref, kt_out_ref), (vt_ref, vt_out_ref))
            )
        ]
        return copies + [
            pltpu.make_async_copy(ref.at[:, to], out.at[:, to], sides_sem.at[index, slot])
            for index, (ref, out) in enumerate(((kn_ref, kn_out_ref), (vn_ref, vn_out_ref)))
        ]

    def w_copy(peer, source):
        sems = (w_sem.at[0, peer], w_sem.at[1, source])
        return send(gained_ref, wrecv_ref.at[source], sems, {"fsdp": peer})

    def lane_copy(lane):
        ref = wpair_ref.at[lane]
        return send(ref, ref, (lane_sem.at[0], lane_sem.at[1]), {"ctx": other})

    def mlp_copy(peer, source):
        sems = (mlp_sem.at[0, peer], mlp_sem.at[1, source])
        return send(mlp_ref.at[:, core], full_ref.at[:, source, core], sems, {"fsdp": peer})

    def cross_copy(source, lane):
        ref = full_ref.at[:, source, lane]
        sems = (cross_sem.at[0, source], cross_sem.at[1, source])
        return send(ref, ref, sems, {"ctx": other})

    def keep_copy(piece):
        return pltpu.make_async_copy(rows_ref.at[piece], unit_ref.at[piece], keep_sem.at[piece])

    own_copy = pltpu.make_async_copy(mlp_ref, full_ref.at[:, group], own_sem)

    stages = [pltpu.make_async_copy(wqkv_ref, wstage_ref, stage_sem.at[0])] + [
        pltpu.make_async_copy(ref, mstage_ref.at[index], stage_sem.at[index + 1])
        for index, ref in enumerate((wout_ref, wup_ref, wdown_ref))
    ]
    for stage in stages:
        stage.start()
    rows = x_ref[...].astype(f32)
    rows_ref[here] = (rows * rms_scale(rows)).astype(bf16)
    pl.semaphore_wait(barrier, groups + 2)

    def forward(way, step, piece, part):
        @pl.when((chip < chips - 1) if way else (chip > 0))
        def _():
            line_copy(way, step, piece, part).start()

    for part in range(halves):
        for way in range(2):
            forward(way, 0, chip, part)
        side_copy(chip, core, part).start()
    held = gain_ref.shape[0]
    lanes = -(-held // PAD) * PAD
    gains = jnp.broadcast_to(small_ref[:D].reshape(1, D), (8, D))
    gains = pltpu.roll(gains, lax.rem(D - group * held, D), 1)[:1, :lanes]
    gain_ref[...] = jnp.broadcast_to(gains, (PAD, lanes)).T[:held, :1]
    scales = small_ref[2 * D :].reshape(1, HD)
    soft = jnp.log(1.0 + jnp.exp(scales)) * (scale_base / math.sqrt(HD) * LOG2E)
    soft = jnp.concatenate([soft, jnp.zeros((1, PAD - HD), f32)], axis=1)
    factor_ref[...] = jnp.broadcast_to(soft, (PAD, PAD)).T[:HD, :1]
    shift = lax.rem(D - here * width, D)
    stages[0].wait()
    for part in range(3):
        turned = pltpu.roll(wstage_ref[:, part * D : (part + 1) * D], shift, 1)
        gained_ref[part] = (turned[:, :width] * gain_ref[...]).astype(bf16)
        wcol_ref[:, part * width : (part + 1) * width] = turned[:, :width].astype(bf16)
    for peer in group_peers:
        w_copy(peer, group).start()
    for index in range(3):
        stages[index + 1].wait()
        mlp_ref[index] = mstage_ref[index].astype(bf16).reshape(mlp_ref.shape[1:])
    own_copy.start()
    keep_copy(here).start()
    wrecv_ref[group] = gained_ref[...]
    for peer in group_peers:
        w_copy(group, peer).wait_recv()
    for peer in group_peers:
        mlp_copy(peer, group).start()
    for part in range(3):
        flipped = wrecv_ref[:, part].reshape(D, width).T
        wflip_ref[part * width : (part + 1) * width] = flipped
    wpair_ref[core] = wflip_ref[...]
    lane_copy(core).start()

    extra_row = lax.broadcasted_iota(jnp.int32, (PAD - HD, BLOCK), 0)
    extra = jnp.where(extra_row < 3, 1.0, 0.0)
    spare = jnp.zeros((PAD - HD, BLOCK), bf16)

    most_ref[...] = jnp.zeros(most_ref.shape, f32)

    def project(piece, part):
        slot = piece * halves + part
        to = block_at(slot)
        result = dot(wflip_ref[...], rows_ref[piece, block_at(part), :], (1, 1))
        for head in range(heads):
            query, key, value = (
                result[share * width + head * HD : share * width + (head + 1) * HD]
                for share in range(3)
            )
            query = query * factor_ref[...]
            for row, rows in enumerate((query, key)):
                most_ref[row : row + 1] = jnp.maximum(
                    most_ref[row : row + 1], jnp.sum(rows * rows, axis=0, keepdims=True)
                )
            qt_ref[head, :HD, to] = query.astype(bf16)
            qt_ref[head, HD:, to] = spare
            kt_ref[head, :, to] = key.astype(bf16)
            vt_ref[head, :HD, to] = value.astype(bf16)
            vt_ref[head, HD:, to] = jnp.ones((EXTRA, BLOCK), bf16)
            kn_ref[head, to, :] = jnp.concatenate([key, extra], axis=0).T.astype(bf16)
            vn_ref[head, to, :] = jnp.concatenate([value, extra], axis=0).T.astype(bf16)
        for copy in results(slot):
            copy.start()

    def visit(index, carry):
        distance, part = index // halves, lax.rem(index, halves)
        for way in range(2):
            piece = chip - distance if way else chip + distance
            valid = (piece >= 0) if way else (piece <= chips - 1)

            @pl.when(valid & (distance > 0))
            def _():
                line_copy(way, distance - 1, piece, part).wait_recv()
                side_copy(piece, core, part).start()
                forward(way, distance, piece, part)

                @pl.when(part == halves - 1)
                def _():
                    keep_copy(2 * piece + core).start()

        for way in range(2):
            piece = chip - distance if way else chip + distance
            valid = (piece >= 0) if way else ((piece <= chips - 1) & (distance > 0))

            @pl.when(valid)
            def _():
                project(2 * piece + core, part)
                side_copy(piece, 1 - core, part).wait_recv()
                project(2 * piece + 1 - core, part)

                @pl.when(part == halves - 1)
                def _():
                    keep_copy(2 * piece + 1 - core).start()

        return carry

    lax.fori_loop(0, chips * halves, visit, 0)

    for peer in group_peers:
        mlp_copy(group, peer).wait_recv()
        cross_copy(peer, core).start()
    for peer in group_peers:
        cross_copy(peer, 1 - core).wait_recv()
        cross_copy(peer, core).wait_send()
        w_copy(peer, group).wait_send()
        mlp_copy(peer, group).wait_send()
    own_copy.wait()
    lane_copy(1 - core).wait_recv()
    lane_copy(core).wait_send()

    def drain(piece, carry):
        keep_copy(2 * piece).wait()
        keep_copy(2 * piece + 1).wait()
        for part in range(halves):
            side_copy(piece, core, part).wait_send()

            @pl.when((piece <= chip) & (chip < chips - 1))
            def _():
                line_copy(1, chip - piece, piece, part).wait_send()

            @pl.when((piece >= chip) & (chip > 0))
            def _():
                line_copy(0, piece - chip, piece, part).wait_send()

        return carry

    lax.fori_loop(0, chips, drain, 0)

    def settle(slot, carry):
        for copy in results(slot):
            copy.wait()
        return carry

    lax.fori_loop(0, 2 * chips * halves, settle, 0)


def gather_rows(parts, groups, heads, rows, w_qkv, w_out, w_up, w_down, small):
    rows_dev = rows.shape[0]
    held = w_qkv.shape[0]
    tokens = parts * rows_dev
    dma = pltpu.SemaphoreType.DMA
    chips = parts // 2
    anywhere = pl.BlockSpec(memory_space=pl.ANY)
    return pl.pallas_call(
        functools.partial(gather_kernel, parts, groups, heads),
        name="gather_rows",
        out_shape=[
            jax.ShapeDtypeStruct((parts, rows_dev, D), bf16),
            jax.ShapeDtypeStruct((3, groups, 2, held // 2, D), bf16),
            jax.ShapeDtypeStruct((2, 3 * heads * HD, D), bf16),
            jax.ShapeDtypeStruct((heads, PAD, tokens), bf16),
            jax.ShapeDtypeStruct((heads, HD, tokens), bf16),
            jax.ShapeDtypeStruct((heads, HD + EXTRA, tokens), bf16),
            jax.ShapeDtypeStruct((heads, tokens, PAD), bf16),
            jax.ShapeDtypeStruct((heads, tokens, PAD), bf16),
            jax.ShapeDtypeStruct((held, 3 * heads * HD), bf16),
            jax.ShapeDtypeStruct((held, 1), f32),
            jax.ShapeDtypeStruct((HD, 1), f32),
            jax.ShapeDtypeStruct((8, BLOCK), f32),
        ],
        in_specs=in_vmem(1) + [anywhere] * 4 + in_vmem(1),
        out_specs=[anywhere] * 2 + in_vmem(1) + [anywhere] * 5 + in_vmem(4),
        scratch_shapes=[
            pltpu.VMEM((heads, PAD, tokens), bf16),
            pltpu.VMEM((heads, HD, tokens), bf16),
            pltpu.VMEM((heads, HD + EXTRA, tokens), bf16),
            pltpu.VMEM((heads, tokens, PAD), bf16),
            pltpu.VMEM((heads, tokens, PAD), bf16),
            pltpu.VMEM((parts, rows_dev, D), bf16),
            pltpu.VMEM((held, 3 * D), f32),
            pltpu.VMEM((3, held, D), f32),
            pltpu.VMEM((3, held, heads * HD), bf16),
            pltpu.VMEM((3, 2, held // 2, D), bf16),
            pltpu.VMEM((groups, 3, held, heads * HD), bf16),
            pltpu.VMEM((3 * heads * HD, D), bf16),
            dma((2, 2, chips, rows_dev // BLOCK)),
            dma((2, chips, rows_dev // BLOCK)),
            dma((parts,)),
            dma((2, groups)),
            dma((2,)),
            dma((2, groups)),
            dma((2, groups)),
            dma,
            dma((4,)),
            dma((3, tokens // BLOCK)),
            dma((2, tokens // BLOCK)),
        ],
        compiler_params=pltpu.CompilerParams(
            vmem_limit_bytes=60 * 1024 * 1024, collective_id=2, has_side_effects=True
        ),
    )(rows, w_qkv, w_out, w_up, w_down, small)


def forward_kernel(
    heads,
    order_ref,
    most_ref,
    qt_ref,
    kn_in_ref,
    vt_in_ref,
    lse_ref,
    ot_ref,
    slot_ref,
    kn_ref,
    vt_ref,
    acc_ref,
    top_ref,
    load_sem,
):
    loads = [
        pltpu.make_async_copy(source, target, load_sem.at[index])
        for index, (source, target) in enumerate(((kn_in_ref, kn_ref), (vt_in_ref, vt_ref)))
    ]
    for load in loads:
        load.start()
    fill_slots(order_ref, slot_ref)
    tokens = kn_ref.shape[1]
    num_tiles = tokens // TILE
    prompt_tiles = num_tiles // 2

    bounded = (
        jnp.max(most_ref[0:1]) * jnp.max(most_ref[1:2]) <= SCORE_BOUND * SCORE_BOUND
    )
    for load in loads:
        load.wait()

    def run(shifted):
        def query_tile(tile, carry):
            queries = [tile_lanes(qt_ref, head, slot_ref, tile) for head in range(heads)]
            if shifted:
                top_ref[...] = jnp.full(top_ref.shape, -1e30, f32)
            else:
                top_ref[...] = jnp.zeros(top_ref.shape, f32)
            acc_ref[...] = jnp.zeros(acc_ref.shape, f32)

            def step(key_rows, value_lanes, start, masked):
                scores = [dot(key_rows[head], queries[head][:, start:]) for head in range(heads)]
                if masked:
                    allowed = causal(scores[0].shape)
                    scores = [jnp.where(allowed, score, -1e30) for score in scores]
                if shifted:
                    olds = [top_ref[head, :, start:] for head in range(heads)]
                    tops = [
                        jnp.maximum(old, jnp.max(score, axis=0, keepdims=True))
                        for old, score in zip(olds, scores)
                    ]
                    scores = [score - top for score, top in zip(scores, tops)]
                    for head in range(heads):
                        acc_ref[head, :, start:] *= jnp.exp2(olds[head] - tops[head])
                        top_ref[head, :, start:] = tops[head]
                probs = [jnp.exp2(score).astype(bf16) for score in scores]
                for head in range(heads):
                    acc_ref[head, :, start:] += dot(value_lanes[head], probs[head])

            def full(key_tile, inner):
                step(
                    [tile_rows(kn_ref, head, slot_ref, key_tile) for head in range(heads)],
                    [tile_lanes(vt_ref, head, slot_ref, key_tile) for head in range(heads)],
                    0,
                    False,
                )
                return inner

            lax.fori_loop(0, jnp.minimum(tile, prompt_tiles), full, 0)
            for part in range(TILE // BLOCK):
                block = block_at(slot_ref[tile * (TILE // BLOCK) + part])
                step(
                    [kn_ref[head, block, :] for head in range(heads)],
                    [vt_ref[head, :, block] for head in range(heads)],
                    part * BLOCK,
                    True,
                )
            for head in range(heads):
                acc = acc_ref[head]
                mass = acc[HD : HD + 1]
                mixed = (acc[:HD] / mass).astype(bf16)
                lse_ref[head, :, tile_at(tile)] = top_ref[head] + jnp.log2(mass)
                for part in range(TILE // BLOCK):
                    slot = slot_ref[tile * (TILE // BLOCK) + part]
                    ot_ref[slot // 2, head * HD : (head + 1) * HD, half_at(slot)] = mixed[
                        :, part * BLOCK : (part + 1) * BLOCK
                    ]
            return carry

        lax.fori_loop(0, num_tiles, query_tile, 0)

    @pl.when(bounded)
    def _():
        run(False)

    @pl.when(jnp.logical_not(bounded))
    def _():
        run(True)


def backward_kernel(
    heads,
    order_ref,
    qt_ref,
    kt_in_ref,
    kn_in_ref,
    vn_in_ref,
    lse_ref,
    ot_ref,
    dt_ref,
    factor_ref,
    dqkv_ref,
    dscale_ref,
    slot_ref,
    kt_ref,
    kn_ref,
    vn_ref,
    qa_ref,
    da_ref,
    dq_ref,
    dk_ref,
    dv_ref,
    scale_ref,
    load_sem,
):
    loads = [
        pltpu.make_async_copy(source, target, load_sem.at[index])
        for index, (source, target) in enumerate(
            ((kn_in_ref, kn_ref), (vn_in_ref, vn_ref), (kt_in_ref, kt_ref))
        )
    ]
    for load in loads:
        load.start()
    fill_slots(order_ref, slot_ref)
    tokens = kn_ref.shape[1]
    num_blocks = tokens // BLOCK
    num_tiles = tokens // TILE
    prompt_tiles = num_tiles // 2
    width = heads * HD

    def prepare(block, carry):
        slot = slot_ref[block]
        to = pl.ds(pl.multiple_of(block * BLOCK, BLOCK), BLOCK)
        for head in range(heads):
            rows = slice(head * HD, (head + 1) * HD)
            grad = dt_ref[slot // 2, rows, half_at(slot)]
            mixed = ot_ref[slot // 2, rows, half_at(slot)]
            delta = jnp.sum(grad.astype(f32) * mixed.astype(f32), axis=0, keepdims=True)
            da_ref[head, :HD, to] = grad
            da_ref[head, HD : HD + EXTRA, to] = three_rows(-delta)
            da_ref[head, HD + EXTRA :, to] = jnp.zeros((PAD - HD - EXTRA, BLOCK), bf16)
            qa_ref[head, :HD, to] = qt_ref[head, :HD, block_at(slot)]
            qa_ref[head, HD : HD + EXTRA, to] = three_rows(-lse_ref[head, :, to])
            qa_ref[head, HD + EXTRA :, to] = jnp.zeros((PAD - HD - EXTRA, BLOCK), bf16)
        return carry

    lax.fori_loop(0, num_blocks, prepare, 0)
    dk_ref[...] = jnp.zeros(dk_ref.shape, f32)
    dv_ref[...] = jnp.zeros(dv_ref.shape, f32)
    scale_ref[...] = jnp.zeros(scale_ref.shape, f32)
    for load in loads:
        load.wait()

    def query_tile(tile, carry):
        here = tile_at(tile)
        dq_ref[...] = jnp.zeros(dq_ref.shape, f32)

        def step(keys, key_rows, key_lanes, value_rows, start, masked):
            to = pl.ds(pl.multiple_of(tile * TILE + start, BLOCK), TILE - start)
            queries = [qa_ref[head, :, to] for head in range(heads)]
            grads = [da_ref[head, :, to] for head in range(heads)]
            scores = [dot(key_rows[head], queries[head]) for head in range(heads)]
            spreads = [dot(value_rows[head], grads[head]) for head in range(heads)]
            probs = [jnp.exp2(score) for score in scores]
            if masked:
                allowed = causal(scores[0].shape)
                probs = [jnp.where(allowed, prob, 0.0) for prob in probs]
            dscores = [(prob * spread).astype(bf16) for prob, spread in zip(probs, spreads)]
            for head in range(heads):
                dv_ref[head, :, keys] += dot(grads[head][:HD], probs[head].astype(bf16), (1, 1))
                dk_ref[head, :, keys] += dot(queries[head][:HD], dscores[head], (1, 1))
                dq_ref[head, :, start:] += dot(key_lanes[head], dscores[head])

        def full(key_tile, inner):
            step(
                tile_at(key_tile),
                [tile_rows(kn_ref, head, slot_ref, key_tile) for head in range(heads)],
                [tile_lanes(kt_ref, head, slot_ref, key_tile) for head in range(heads)],
                [tile_rows(vn_ref, head, slot_ref, key_tile) for head in range(heads)],
                0,
                False,
            )
            return inner

        lax.fori_loop(0, jnp.minimum(tile, prompt_tiles), full, 0)
        for part in range(TILE // BLOCK):
            position = tile * (TILE // BLOCK) + part
            block = block_at(slot_ref[position])
            step(
                block_at(position),
                [kn_ref[head, block, :] for head in range(heads)],
                [kt_ref[head, :, block] for head in range(heads)],
                [vn_ref[head, block, :] for head in range(heads)],
                part * BLOCK,
                True,
            )
        for head in range(heads):
            dq = dq_ref[head]
            product = dq * qa_ref[head, :HD, here].astype(f32)
            for lane in range(TILE // PAD):
                scale_ref[head] += product[:, lane * PAD : (lane + 1) * PAD]
            scaled = (dq * (factor_ref[...] * LN2)).astype(bf16)
            for part in range(TILE // BLOCK):
                slot = slot_ref[tile * (TILE // BLOCK) + part]
                dqkv_ref[slot // 2, head * HD : (head + 1) * HD, half_at(slot)] = scaled[
                    :, part * BLOCK : (part + 1) * BLOCK
                ]
        return carry

    lax.fori_loop(0, num_tiles, query_tile, 0)

    def finish(block, carry):
        slot = slot_ref[block]
        owner, to = slot // 2, half_at(slot)
        at = pl.ds(pl.multiple_of(block * BLOCK, BLOCK), BLOCK)
        for head in range(heads):
            row = width + head * HD
            dqkv_ref[owner, row : row + HD, to] = (dk_ref[head, :, at] * LN2).astype(bf16)
            row = 2 * width + head * HD
            dqkv_ref[owner, row : row + HD, to] = dv_ref[head, :, at].astype(bf16)
        return carry

    lax.fori_loop(0, num_blocks, finish, 0)
    sums = functools.reduce(jnp.add, [scale_ref[head] for head in range(heads)])
    sums = jnp.concatenate([sums, jnp.zeros((PAD - HD, PAD), f32)], axis=0).T
    dscale_ref[...] = jnp.sum(sums, axis=0, keepdims=True)


def in_vmem(count):
    return [pl.BlockSpec(memory_space=pltpu.VMEM)] * count


def params(mebibytes):
    return pltpu.CompilerParams(vmem_limit_bytes=mebibytes * 1024 * 1024)


def attention_forward(order, most, qt, kn, vt, parts):
    heads, tokens = kn.shape[:2]
    return pl.pallas_call(
        functools.partial(forward_kernel, heads),
        name="attention_forward",
        out_shape=[
            jax.ShapeDtypeStruct((heads, 1, tokens), f32),
            jax.ShapeDtypeStruct((parts, heads * HD, tokens // parts), bf16),
        ],
        in_specs=[pl.BlockSpec(memory_space=pltpu.SMEM)]
        + in_vmem(2)
        + [pl.BlockSpec(memory_space=pl.ANY)] * 2,
        out_specs=in_vmem(2),
        scratch_shapes=[
            pltpu.SMEM(order.shape, jnp.int32),
            pltpu.VMEM(kn.shape, bf16),
            pltpu.VMEM(vt.shape, bf16),
            pltpu.VMEM((heads, HD + EXTRA, TILE), f32),
            pltpu.VMEM((heads, 1, TILE), f32),
            pltpu.SemaphoreType.DMA((2,)),
        ],
        compiler_params=params(60),
        cost_estimate=attention_cost(heads, tokens, 2),
    )(order, most, qt, kn, vt)


def attention_cost(heads, tokens, passes):
    pairs = heads * tokens * tokens // 2
    return pl.CostEstimate(
        flops=2 * passes * pairs * BLOCK, bytes_accessed=tokens * D, transcendentals=pairs
    )


def attention_backward(order, kept, mixed, dmixed, factor):
    qt, kt, kn, vn, lse = kept
    heads, tokens = kn.shape[:2]
    return pl.pallas_call(
        functools.partial(backward_kernel, heads),
        name="attention_backward",
        out_shape=[
            jax.ShapeDtypeStruct((mixed.shape[0], 3 * heads * HD, mixed.shape[2]), bf16),
            jax.ShapeDtypeStruct((1, PAD), f32),
        ],
        in_specs=[pl.BlockSpec(memory_space=pltpu.SMEM)]
        + in_vmem(1)
        + [pl.BlockSpec(memory_space=pl.ANY)] * 3
        + in_vmem(4),
        out_specs=in_vmem(2),
        scratch_shapes=[
            pltpu.SMEM(order.shape, jnp.int32),
            pltpu.VMEM(kt.shape, bf16),
            pltpu.VMEM(kn.shape, bf16),
            pltpu.VMEM(vn.shape, bf16),
            pltpu.VMEM((heads, PAD, tokens), bf16),
            pltpu.VMEM((heads, PAD, tokens), bf16),
            pltpu.VMEM((heads, HD, TILE), f32),
            pltpu.VMEM((heads, HD, tokens), f32),
            pltpu.VMEM((heads, HD, tokens), f32),
            pltpu.VMEM((heads, HD, PAD), f32),
            pltpu.SemaphoreType.DMA((3,)),
        ],
        compiler_params=params(60),
        cost_estimate=attention_cost(heads, tokens, 5),
    )(order, qt, kt, kn, vn, lse, mixed, dmixed, factor)


def middle_kernel(
    parts,
    groups,
    mixed_ref,
    x_ref,
    dy_ref,
    weights_ref,
    gain_ref,
    *refs,
):
    out_ref, dmid_ref, dmixed_ref, gain_grad_ref = refs[:4]
    chunk_refs = refs[4 : 4 + groups]
    (
        w_ref,
        attn_ref,
        dattn_ref,
        act_ref,
        normed_ref,
        dhidden_ref,
        dbranch_ref,
        grad_ref,
        theirs_ref,
        w_sem,
        attn_sem,
        dattn_sem,
        pair_sem,
    ) = refs[4 + groups :]
    here = lax.axis_index("ctx")
    group = lax.axis_index("fsdp")
    core = lax.rem(here, 2)
    other = here + 1 - 2 * core
    peers = [lax.rem(here + step, parts) for step in range(1, parts)]
    tokens = x_ref.shape[0]
    width = mixed_ref.shape[1]
    held = theirs_ref.shape[2]
    loads = [
        pltpu.make_async_copy(weights_ref.at[index], w_ref.at[index], w_sem.at[index])
        for index in range(3)
    ]
    for load in loads:
        load.start()

    barrier = pltpu.get_barrier_semaphore()
    for peer in peers:
        pl.semaphore_signal(barrier, inc=1, device_id={"ctx": peer})
    pl.semaphore_wait(barrier, parts - 1)

    def lanes(part):
        return pl.ds(pl.multiple_of(part * BLOCK, BLOCK), BLOCK)

    def attn_copy(part, peer, source):
        return pltpu.make_async_remote_copy(
            src_ref=mixed_ref.at[peer, :, lanes(part)],
            dst_ref=attn_ref.at[source, :, lanes(part)],
            send_sem=attn_sem.at[0, part, peer],
            recv_sem=attn_sem.at[1, part, source],
            device_id={"ctx": peer},
        )

    def dattn_copy(part, peer, source):
        return pltpu.make_async_remote_copy(
            src_ref=dattn_ref.at[peer, :, lanes(part)],
            dst_ref=dmixed_ref.at[source, :, lanes(part)],
            send_sem=dattn_sem.at[0, part, peer],
            recv_sem=dattn_sem.at[1, part, source],
            device_id={"ctx": peer},
        )

    def rows_of(owner, lane):
        start = pl.multiple_of((owner * 2 + lane) * held, 16)
        return pl.ds(start, held)

    def pair_copy(index, owner, lane):
        return pltpu.make_async_remote_copy(
            src_ref=grad_ref.at[index, rows_of(owner, lane), :],
            dst_ref=theirs_ref.at[index, owner],
            send_sem=pair_sem.at[0, index, owner],
            recv_sem=pair_sem.at[1, index, owner],
            device_id={"ctx": other},
        )

    for part in range(tokens // BLOCK):
        for peer in peers:
            attn_copy(part, peer, here).start()
    attn_ref[here] = mixed_ref[here]
    gain_grad_ref[...] = jnp.zeros(gain_grad_ref.shape, f32)
    for load in loads:
        load.wait()
    gain = gain_ref[...]

    def layer(part, carry):
        rows = lanes(part)
        for peer in peers:
            attn_copy(part, here, peer).wait_recv()
        attn = attn_ref[:, :, rows].reshape(D, BLOCK)
        mid = x_ref[rows, :].astype(f32) + dot(attn, w_ref[0], (0, 0))
        scale = rms_scale(mid)
        unit = mid * scale
        normed = (unit * gain).astype(bf16)
        normed_ref[rows, :] = normed
        hidden = dot(normed, w_ref[1])
        gate = jax.nn.sigmoid(hidden)
        act = (hidden * gate).astype(bf16)
        act_ref[rows, :] = act
        dy = dy_ref[rows, :]
        dact = dot(dy, w_ref[2], (1, 1))
        dhidden = (dact * gate * (1.0 + hidden * (1.0 - gate))).astype(bf16)
        dhidden_ref[rows, :] = dhidden
        dnormed = dot(dhidden, w_ref[1], (1, 1))
        dunit = dnormed * gain
        dmid = dy.astype(f32) + scale * (
            dunit - unit * jnp.mean(dunit * unit, axis=-1, keepdims=True)
        )
        dmid_ref[rows, :] = dmid
        dbranch = dmid.astype(bf16)
        dbranch_ref[rows, :] = dbranch
        dattn = dot(w_ref[0], dbranch, (1, 1)).astype(bf16).reshape(parts, width, BLOCK)
        dattn_ref[:, :, rows] = dattn
        for peer in peers:
            dattn_copy(part, peer, here).start()
        dmixed_ref[here, :, rows] = dattn_ref[here, :, rows]
        out_ref[rows, :] = (mid + dot(act, w_ref[2])).astype(bf16)
        gain_grad_ref[...] += jnp.sum(dnormed * unit, axis=0, keepdims=True)
        return carry

    lax.fori_loop(0, tokens // BLOCK, layer, 0)

    def down_rows(index, carry):
        rows = lanes(index)
        grad_ref[2, rows, :] = dot(act_ref[:, rows], dy_ref[...], (0, 0)).astype(bf16)
        return carry

    def up_rows(index, carry):
        rows = lanes(index)
        grad_ref[1, rows, :] = dot(normed_ref[:, rows], dhidden_ref[...], (0, 0)).astype(bf16)
        return carry

    def out_rows(index, carry):
        rows = pl.ds(pl.multiple_of(index * width, 16), width)
        grad_ref[0, rows, :] = dot(attn_ref[index], dbranch_ref[...]).astype(bf16)
        return carry

    for index, count, run in (
        (2, D // BLOCK, down_rows),
        (1, D // BLOCK, up_rows),
        (0, parts, out_rows),
    ):
        lax.fori_loop(0, count, run, 0)
        for owner in range(groups):
            pair_copy(index, owner, 1 - core).start()
    for step in range(groups):
        owner = group ^ step
        for index in (2, 1, 0):
            pair_copy(index, owner, core).wait_recv()
            chunk_refs[step][index] = (
                grad_ref[index, rows_of(owner, core), :].astype(f32)
                + theirs_ref[index, owner].astype(f32)
            ).astype(bf16)
    for part in range(tokens // BLOCK):
        for peer in peers:
            dattn_copy(part, here, peer).wait_recv()
            dattn_copy(part, peer, here).wait_send()
            attn_copy(part, peer, here).wait_send()
    for index in range(3):
        for owner in range(groups):
            pair_copy(index, owner, 1 - core).wait_send()


def middle(parts, groups, mixed, rows, cotangent, weights, gain):
    rows_dev = rows.shape[0]
    half = D // groups // 2
    dma = pltpu.SemaphoreType.DMA
    halves = rows_dev // BLOCK
    return pl.pallas_call(
        functools.partial(middle_kernel, parts, groups),
        name="middle",
        out_shape=[
            jax.ShapeDtypeStruct((rows_dev, D), bf16),
            jax.ShapeDtypeStruct((rows_dev, D), f32),
            jax.ShapeDtypeStruct(mixed.shape, bf16),
            jax.ShapeDtypeStruct((1, D), f32),
        ]
        + [jax.ShapeDtypeStruct((3, half, D), bf16)] * groups,
        in_specs=in_vmem(3) + [pl.BlockSpec(memory_space=pl.ANY)] + in_vmem(1),
        out_specs=in_vmem(4 + groups),
        scratch_shapes=[
            pltpu.VMEM((3, D, D), bf16),
            pltpu.VMEM(mixed.shape, bf16),
            pltpu.VMEM(mixed.shape, bf16),
            pltpu.VMEM((rows_dev, D), bf16),
            pltpu.VMEM((rows_dev, D), bf16),
            pltpu.VMEM((rows_dev, D), bf16),
            pltpu.VMEM((rows_dev, D), bf16),
            pltpu.VMEM((3, D, D), bf16),
            pltpu.VMEM((3, groups, half, D), bf16),
            dma((3,)),
            dma((2, halves, parts)),
            dma((2, halves, parts)),
            dma((2, 3, groups)),
        ],
        compiler_params=pltpu.CompilerParams(
            vmem_limit_bytes=60 * 1024 * 1024, collective_id=3, has_side_effects=True
        ),
    )(mixed, rows, cotangent, weights, gain)


def reduce_kernel(
    parts,
    groups,
    dq_in_ref,
    wt_in_ref,
    units_ref,
    wc_ref,
    small_ref,
    *refs,
):
    chunk_in_refs = refs[:groups]
    (
        down_ref,
        up_ref,
        own_ref,
        ugather_ref,
        mgather_ref,
        sgather_ref,
        dq_ref,
        wt_ref,
        chunk_ref,
        held_ref,
        total_ref,
        u_ref,
        usum_ref,
        msum_ref,
        pair_ref,
        sum_ref,
        urecv_ref,
        mlp_ref,
        mrecv_ref,
        part_ref,
        column_ref,
        smine_ref,
        srecv_ref,
        pair_sem,
        sum_sem,
        u_sem,
        m_sem,
        line_sem,
        side_sem,
        small_sem,
        cross_sem,
        load_sem,
        held_sem,
        keep_sem,
    ) = refs[groups:]
    chips = parts // 2
    here = lax.axis_index("ctx")
    group = lax.axis_index("fsdp")
    core = lax.rem(here, 2)
    chip = here // 2
    other = here + 1 - 2 * core
    ctx_peers = [lax.rem(here + step, parts) for step in range(1, parts)]
    chip_peers = [lax.rem(chip + step, chips) for step in range(1, chips)]
    group_peers = [lax.rem(group + step, groups) for step in range(1, groups)]

    loads = [
        pltpu.make_async_copy(ref, chunk_ref.at[index], load_sem.at[index])
        for index, ref in enumerate(chunk_in_refs)
    ]
    loads.append(pltpu.make_async_copy(dq_in_ref, dq_ref, load_sem.at[groups]))
    loads.append(pltpu.make_async_copy(wt_in_ref, wt_ref, load_sem.at[groups + 1]))
    for load in loads:
        load.start()

    def unit_load(piece):
        slot = lax.rem(piece, 2)
        return pltpu.make_async_copy(units_ref.at[piece], held_ref.at[slot], held_sem.at[slot])

    for piece in range(2):
        unit_load(piece).start()

    barrier = pltpu.get_barrier_semaphore()
    for peer in ctx_peers:
        pl.semaphore_signal(barrier, inc=1, device_id={"ctx": peer})
    for peer in group_peers:
        pl.semaphore_signal(barrier, inc=1, device_id={"fsdp": peer})

    def send(source, target, sems, device):
        return pltpu.make_async_remote_copy(
            src_ref=source,
            dst_ref=target,
            send_sem=sems[0],
            recv_sem=sems[1],
            device_id=device,
        )

    def pair_copy(index):
        return send(
            dq_in_ref.at[index, 1 - core],
            pair_ref.at[index],
            (pair_sem.at[0, index], pair_sem.at[1, index]),
            {"ctx": other},
        )

    def u_copy(peer, source):
        return send(
            u_ref.at[peer],
            urecv_ref.at[source],
            (u_sem.at[0, peer], u_sem.at[1, source]),
            {"fsdp": peer},
        )

    def m_copy(peer, source):
        return send(
            mlp_ref.at[peer],
            mrecv_ref.at[source],
            (m_sem.at[0, peer], m_sem.at[1, source]),
            {"ctx": 2 * peer + core},
        )

    for load in loads[:groups]:
        load.wait()
    share = mlp_ref.shape[2]
    for matrix in range(3):
        total = functools.reduce(
            jnp.add, [chunk_ref[step, matrix].astype(f32) for step in range(groups)]
        )
        for index in range(chips):
            mlp_ref[index, matrix] = total[index * share : (index + 1) * share].astype(bf16)
    pl.semaphore_wait(barrier, parts + groups - 2)
    for peer in chip_peers:
        m_copy(peer, chip).start()
    for index in range(chips):
        pair_copy(index).start()
    for load in loads[groups:]:
        load.wait()

    rows_half = own_ref.shape[0] // 2

    def partial(target, index):
        rows = pl.ds(pl.multiple_of(index * rows_half, rows_half), rows_half)
        part_ref[rows, :] = dot(dq_ref[target, core, :, rows], wt_ref[core], (0, 0)) + dot(
            pair_ref[target, :, rows], wt_ref[1 - core], (0, 0)
        )
        return rows

    def sum_copy(way, target, index):
        ref = sum_ref.at[way + target, pl.ds(index * rows_half, rows_half)]
        sems = (sum_sem.at[0, way, target, index], sum_sem.at[1, way, target, index])
        return send(ref, ref, sems, {"ctx": here + (2 if way else -2)})

    def reduce_step(step):
        last = step == chips - 2
        for way, target, active, first, out_ref in (
            (0, step - (chips - 1) + chip, step >= chips - 1 - chip, chip == chips - 1, down_ref),
            (1, chips - 1 - step + chip, step >= chip, chip == 0, up_ref),
        ):

            @pl.when(active)
            def _():
                def half(index, carry):
                    rows = partial(target, index)

                    @pl.when(first)
                    def _():
                        sum_ref[way + target, rows] = part_ref[rows, :].astype(bf16)

                    @pl.when(jnp.logical_not(first))
                    def _():
                        sum_copy(way, target, index).wait_recv()
                        sum_ref[way + target, rows] = (
                            part_ref[rows, :] + sum_ref[way + target, rows].astype(f32)
                        ).astype(bf16)

                    if last:
                        out_ref[rows, :] = sum_ref[way + target, rows]
                    else:
                        sum_copy(way, target, index).start()
                    return carry

                lax.fori_loop(0, 2, half, 0)

            if last:

                @pl.when(jnp.logical_not(active))
                def _():
                    out_ref[...] = jnp.zeros(out_ref.shape, bf16)

    gathers = (ugather_ref, mgather_ref)
    sums = (usum_ref, msum_ref)

    def keep_copy(which):
        return pltpu.make_async_copy(sums[which], gathers[which].at[here], keep_sem.at[which])

    def line_copy(which, way, step, piece):
        ref = gathers[which].at[2 * piece + core]
        sems = (line_sem.at[0, which, way, step], line_sem.at[1, which, way, step])
        source = sums[which] if step == 0 else ref
        return send(source, ref, sems, {"ctx": here + (2 if way else -2)})

    def side_copy(which, piece, lane, own=False):
        ref = gathers[which].at[2 * piece + lane]
        sems = (side_sem.at[0, which, piece], side_sem.at[1, which, piece])
        return send(sums[which] if own else ref, ref, sems, {"ctx": other})

    def line_sends(which, step, go):
        @pl.when((chip < chips - 1) & (chip - step >= 0))
        def _():
            go(line_copy(which, 1, step, chip - step))

        @pl.when((chip > 0) & (chip + step <= chips - 1))
        def _():
            go(line_copy(which, 0, step, chip + step))

    def line_receive(which, step):
        @pl.when(chip - 1 - step >= 0)
        def _():
            line_copy(which, 1, step, chip - 1 - step).wait_recv()
            side_copy(which, chip - 1 - step, core).start()

        @pl.when(chip + 1 + step <= chips - 1)
        def _():
            line_copy(which, 0, step, chip + 1 + step).wait_recv()
            side_copy(which, chip + 1 + step, core).start()

    def small_copy(peer, source):
        return send(
            smine_ref,
            srecv_ref.at[source],
            (small_sem.at[0, peer], small_sem.at[1, source]),
            {"ctx": peer},
        )

    def cross_copy(peer, source):
        return send(
            sgather_ref.at[group],
            sgather_ref.at[source],
            (cross_sem.at[0, peer], cross_sem.at[1, source]),
            {"fsdp": peer},
        )

    for index in range(chips):
        pair_copy(index).wait_recv()
    reduce_step(0)

    total_ref[...] = jnp.zeros(total_ref.shape, f32)

    def accumulate(piece, carry):
        unit_load(piece).wait()
        total_ref[...] += dot(dq_ref[piece // 2, lax.rem(piece, 2)], held_ref[lax.rem(piece, 2)])

        @pl.when(piece + 2 < parts)
        def _():
            unit_load(piece + 2).start()

        return carry

    lax.fori_loop(0, parts, accumulate, 0)
    u_ref[...] = total_ref[...].T.astype(bf16).reshape(u_ref.shape)
    for peer in group_peers:
        u_copy(peer, group).start()

    total = mlp_ref[chip].astype(f32)
    for peer in chip_peers:
        m_copy(chip, peer).wait_recv()
        total = total + mrecv_ref[peer].astype(f32)
    msum_ref[...] = total.astype(bf16)
    keep_copy(1).start()
    side_copy(1, chip, core, True).start()
    line_sends(1, 0, lambda copy: copy.start())

    total = u_ref[group].astype(f32)
    for peer in group_peers:
        u_copy(group, peer).wait_recv()
        total = total + urecv_ref[peer].astype(f32)
    usum_ref[...] = total.astype(bf16)
    keep_copy(0).start()
    side_copy(0, chip, core, True).start()
    line_sends(0, 0, lambda copy: copy.start())
    held = total.shape[0]
    gain = jnp.sum(total * wc_ref[...].astype(f32), axis=1, keepdims=True)
    column_ref[...] = jnp.zeros(column_ref.shape, f32)
    column_ref[:held, :] = jnp.broadcast_to(gain, (held, PAD))
    flat = column_ref[...].T[:1]
    smine_ref[...] = small_ref[...]
    for row in range(column_ref.shape[0] // PAD):
        smine_ref[row : row + 1, :] = flat[:, row * PAD : (row + 1) * PAD]
    for peer in ctx_peers:
        small_copy(peer, here).start()

    for step in range(1, chips):
        if step == 1:
            reduce_step(step)
        for which in range(2):
            line_receive(which, step - 1)
            if step <= chips - 2:
                line_sends(which, step, lambda copy: copy.start())
        if 1 < step <= chips - 2:
            reduce_step(step)
        if step == 1:
            small = smine_ref[...]
            for peer in ctx_peers:
                small_copy(here, peer).wait_recv()
                small = small + srecv_ref[peer]
            sgather_ref[group] = small
            for peer in group_peers:
                cross_copy(peer, group).start()

    for index in range(2):
        rows = partial(chip, index)
        own_ref[rows, :] = part_ref[rows, :].astype(bf16)

    for which in range(2):
        keep_copy(which).wait()
        for piece in range(chips):
            side_copy(which, piece, 1 - core).wait_recv()
            side_copy(which, piece, core).wait_send()
        for step in range(chips - 1):
            line_sends(which, step, lambda copy: copy.wait_send())
    for index in range(chips):
        pair_copy(index).wait_send()
    for peer in group_peers:
        cross_copy(group, peer).wait_recv()
        cross_copy(peer, group).wait_send()
        u_copy(peer, group).wait_send()
    for peer in chip_peers:
        m_copy(peer, chip).wait_send()
    for peer in ctx_peers:
        small_copy(peer, here).wait_send()
    for step in range(chips - 2):

        @pl.when(step >= chips - 1 - chip)
        def _():
            for index in range(2):
                sum_copy(0, step - (chips - 1) + chip, index).wait_send()

        @pl.when(step >= chip)
        def _():
            for index in range(2):
                sum_copy(1, chips - 1 - step + chip, index).wait_send()


def reduce_gradients(parts, groups, dqkv, w_pair, units, w_columns, small, chunks):
    chips = parts // 2
    mlp_shape = (chips, 3, chunks[0].shape[1] // chips, D)
    rows_dev = dqkv.shape[3]
    rows, width = w_columns.shape
    lanes = -(-rows // PAD) * PAD
    dma = pltpu.SemaphoreType.DMA
    anywhere = pl.BlockSpec(memory_space=pl.ANY)
    u_shape = (groups, rows, width)
    return pl.pallas_call(
        functools.partial(reduce_kernel, parts, groups),
        name="reduce_gradients",
        out_shape=[
            jax.ShapeDtypeStruct((rows_dev, D), bf16),
            jax.ShapeDtypeStruct((rows_dev, D), bf16),
            jax.ShapeDtypeStruct((rows_dev, D), bf16),
            jax.ShapeDtypeStruct((parts, rows, width), bf16),
            jax.ShapeDtypeStruct((parts,) + mlp_shape[1:], bf16),
            jax.ShapeDtypeStruct((groups,) + small.shape, f32),
        ],
        in_specs=[anywhere] * 3 + in_vmem(2) + [anywhere] * groups,
        out_specs=in_vmem(3) + [anywhere] * 2 + in_vmem(1),
        scratch_shapes=[
            pltpu.VMEM(dqkv.shape, bf16),
            pltpu.VMEM(w_pair.shape, bf16),
            pltpu.VMEM((groups,) + chunks[0].shape, bf16),
            pltpu.VMEM((2,) + units.shape[1:], bf16),
            pltpu.VMEM((width, D), f32),
            pltpu.VMEM(u_shape, bf16),
            pltpu.VMEM(u_shape[1:], bf16),
            pltpu.VMEM(mlp_shape[1:], bf16),
            pltpu.VMEM((chips,) + dqkv.shape[2:], bf16),
            pltpu.VMEM((chips + 1, rows_dev, D), bf16),
            pltpu.VMEM(u_shape, bf16),
            pltpu.VMEM(mlp_shape, bf16),
            pltpu.VMEM(mlp_shape, bf16),
            pltpu.VMEM((rows_dev, D), f32),
            pltpu.VMEM((lanes, PAD), f32),
            pltpu.VMEM(small.shape, f32),
            pltpu.VMEM((parts,) + small.shape, f32),
            dma((2, chips)),
            dma((2, 2, chips, 2)),
            dma((2, groups)),
            dma((2, chips)),
            dma((2, 2, 2, chips)),
            dma((2, 2, chips)),
            dma((2, parts)),
            dma((2, groups)),
            dma((groups + 2,)),
            dma((2,)),
            dma((2,)),
        ],
        compiler_params=pltpu.CompilerParams(
            vmem_limit_bytes=60 * 1024 * 1024, collective_id=1, has_side_effects=True
        ),
    )(dqkv, w_pair, units, w_columns, small, *chunks)


def update_kernel(rates, qkv_ref, gain_ref, mlp_ref, *refs):
    sets = len(rates)
    parts, rows, width = qkv_ref.shape
    width = width // 3
    for index, rate in enumerate(rates):
        weight, first, second = (ref[...] for ref in refs[3 * index : 3 * index + 3])
        if index == 0:
            pieces = [qkv_ref[part].astype(f32) for part in range(parts)]
            gradient = jnp.concatenate(
                [piece[:, at * width : (at + 1) * width] for at in range(3) for piece in pieces],
                axis=1,
            )
            gradient = gradient * gain_ref[...]
        else:
            gradient = mlp_ref[0, index - 1].astype(f32)
        outs = refs[3 * sets + 4 * index : 3 * sets + 4 * index + 4]
        new, first, second = adamw(weight, first, second, gradient, rate, decay_rate)
        outs[0][...] = new
        outs[1][...] = first
        outs[2][...] = second
        outs[3][...] = new.astype(bf16)


def update(rates, parts, qkv, gain, mlp, *arrays):
    rows = arrays[0].shape[0]
    chips = parts // 2
    step_rows = rows // parts
    if step_rows % 8 == 0:

        def owner(i):
            return (2 * lax.rem(i, chips) + i // chips, 0, 0, 0)

    else:
        step_rows = 32
        mlp = mlp.reshape(chips, 2, 3, rows // parts, D).transpose(2, 1, 0, 3, 4)
        mlp = mlp.reshape(3, rows // step_rows, step_rows, D).transpose(1, 0, 2, 3)

        def owner(i):
            return (i, 0, 0, 0)

    in_specs = [
        pl.BlockSpec((parts, step_rows, qkv.shape[2]), lambda i: (0, i, 0)),
        pl.BlockSpec((step_rows, 1), lambda i: (i, 0)),
        pl.BlockSpec((1, 3, step_rows, D), owner),
    ]
    specs, shapes, moved = [], [], 0
    for array in arrays:
        in_specs.append(pl.BlockSpec((step_rows, array.shape[1]), lambda i: (i, 0)))
    for index in range(len(rates)):
        shape = arrays[3 * index].shape
        shapes += [jax.ShapeDtypeStruct(shape, f32)] * 3 + [jax.ShapeDtypeStruct(shape, bf16)]
        specs += [pl.BlockSpec((step_rows, shape[1]), lambda i: (i, 0))] * 4
        moved += shape[0] * shape[1] * 28
    return pl.pallas_call(
        functools.partial(update_kernel, rates),
        name="update_weights",
        grid=(rows // step_rows,),
        in_specs=in_specs,
        out_specs=specs,
        out_shape=shapes,
        compiler_params=params(55),
        cost_estimate=pl.CostEstimate(flops=moved, bytes_accessed=moved, transcendentals=0),
    )(qkv, gain, mlp, *arrays)


def finish_kernel(down_ref, up_ref, own_ref, x_ref, dmid_ref, layer_ref, out_ref, same_ref):
    here = pl.ds(pl.multiple_of(pl.program_id(0) * PAD, PAD), PAD)
    rows = x_ref[...].astype(f32)
    scale = rms_scale(rows)
    unit = rows * scale
    dunit = (
        own_ref[...].astype(f32) + down_ref[here, :].astype(f32) + up_ref[here, :].astype(f32)
    )
    grad = dmid_ref[...] + scale * (
        dunit - unit * jnp.mean(dunit * unit, axis=-1, keepdims=True)
    )
    out_ref[...] = grad.astype(bf16)
    same_ref[...] = layer_ref[...]


def finish(*arrays):
    rows = arrays[0].shape[0]
    spec = pl.BlockSpec((PAD, D), lambda i: (i, 0))
    return pl.pallas_call(
        finish_kernel,
        name="finish",
        grid=(rows // PAD,),
        in_specs=in_vmem(2) + [spec] * 4,
        out_specs=[spec] * 2,
        out_shape=[jax.ShapeDtypeStruct((rows, D), bf16)] * 2,
        compiler_params=params(40),
    )(*arrays)


def body(
    parts,
    groups,
    inputs,
    cotangent,
    block_order,
    w_qkv,
    m_qkv,
    v_qkv,
    w_out,
    m_out,
    v_out,
    w_up,
    m_up,
    v_up,
    w_down,
    m_down,
    v_down,
    small_params,
    small_m,
    small_v,
):
    heads = H // parts
    width = heads * HD
    rows_dev = inputs.shape[1]
    tokens = rows_dev * parts
    here = lax.axis_index("ctx")
    order = block_order[0]
    gain_two = small_params[D : 2 * D]
    query_scale = small_params[2 * D :]
    group = lax.axis_index("fsdp")
    rows = w_qkv.shape[0]

    (
        unit_all,
        mlp_full,
        w_pair,
        qt,
        kt,
        vt,
        kn,
        vn,
        w_columns,
        gain_rows,
        factor_two,
        most,
    ) = gather_rows(
        parts, groups, heads, inputs[0], w_qkv, w_out, w_up, w_down, small_params
    )
    lse, mixed = attention_forward(order, most, qt, kn, vt, parts)
    kept = (qt, kt, kn, vn, lse)
    output, dmid, dmixed, gain_two_grad, *chunks = middle(
        parts,
        groups,
        mixed,
        inputs[0],
        cotangent[0],
        mlp_full.reshape(3, D, D),
        gain_two[None],
    )
    for step in range(1, groups):
        swap = [(i, i ^ step) for i in range(groups)]
        chunks[step] = lax.ppermute(chunks[step], "fsdp", swap)
    dqkv, dscale = attention_backward(order, kept, mixed, dmixed, factor_two)
    scale_grad = (
        dscale[0, :HD]
        / factor_two[:, 0]
        * (scale_base / math.sqrt(HD))
        * jax.nn.sigmoid(query_scale)
    )
    lanes = -(-rows // PAD) * PAD
    small_rows = -(-(lanes + D + PAD) // (8 * PAD)) * 8
    small = jnp.concatenate([jnp.zeros((lanes,), f32), gain_two_grad[0], scale_grad])
    small = jnp.pad(small, (0, small_rows * PAD - small.shape[0])).reshape(small_rows, PAD)
    send_down, send_up, own_part, u_all, mlp_all, small_all = reduce_gradients(
        parts,
        groups,
        dqkv.reshape(parts // 2, 2, 3 * width, rows_dev),
        w_pair,
        unit_all,
        w_columns,
        small,
        chunks,
    )
    got_down = lax.ppermute(send_down, "ctx", [(i, i - 2) for i in range(2, parts)])
    got_up = lax.ppermute(send_up, "ctx", [(i, i + 2) for i in range(parts - 2)])
    rate_qkv = qkv_rate_base / math.sqrt(D)
    rate_out = 0.5 / math.sqrt(max(D // 256, 1))
    rate_up = 0.5 / math.sqrt(D)
    rate_down = 0.5 / math.sqrt(FF)
    updated = update(
        (rate_qkv, rate_out, rate_up, rate_down),
        parts,
        u_all,
        gain_rows,
        mlp_all,
        w_qkv,
        m_qkv,
        v_qkv,
        w_out,
        m_out,
        v_out,
        w_up,
        m_up,
        v_up,
        w_down,
        m_down,
        v_down,
    )
    flat = small_all.reshape(groups, small_rows * PAD)
    rest = jnp.sum(flat[:, lanes : lanes + D + HD], axis=0)
    small_total = jnp.concatenate([flat[:, :rows].reshape(D), rest])
    small_set = adamw(small_params, small_m, small_v, small_total, small_rate, 0.0)
    input_grad, output = finish(got_down, got_up, own_part, inputs[0], dmid, output)
    return (
        output[None],
        input_grad[None],
        *updated,
        *small_set,
    )


def solution(mesh):
    rows = P("fsdp", "ctx", None)
    weight = P("fsdp", None)
    return jax.shard_map(
        functools.partial(body, mesh.shape["ctx"], mesh.shape["fsdp"]),
        mesh=mesh,
        in_specs=(rows, rows, weight) + (weight,) * 12 + (P(),) * 3,
        out_specs=(rows, rows) + (weight,) * 16 + (P(),) * 3,
        check_vma=False,
    )
```

```python
import functools
import math

import jax
import jax.numpy as jnp
from jax import lax
from jax.experimental import pallas as pl
from jax.experimental.pallas import tpu as pltpu
from jax.sharding import PartitionSpec as P

D = 1280
H = 16
HD = 80
FF = 1280
BLOCK = 256
CONT = 512
STEP = 3
PAD = 128
EXTRA = 16
TILE = CONT
SCORE_BOUND = 95.0

bf16 = jnp.bfloat16
f32 = jnp.float32

norm_eps = 1e-06
beta_one = 0.5
beta_two = 0.5
adam_eps = 1e-08
decay_rate = 0.1
small_rate = 0.75
qkv_rate_base = 1.0
scale_base = 1.442695
LOG2E = math.log2(math.e)
LN2 = math.log(2.0)


def rms_scale(values):
    return lax.rsqrt(jnp.mean(values * values, axis=-1, keepdims=True) + norm_eps)


def adamw(weight, first, second, gradient, step_rate, decay_on):
    first_new = beta_one * first + (1.0 - beta_one) * gradient
    second_new = beta_two * second + (1.0 - beta_two) * gradient * gradient
    corr_one = 1.0 - beta_one**STEP
    corr_two = 1.0 - beta_two**STEP
    update = first_new / corr_one / (jnp.sqrt(second_new / corr_two) + adam_eps)
    weight_new = weight - step_rate * (update + decay_on * weight)
    return (weight_new, first_new, second_new)


def dot(left, right, contract=(1, 0)):
    return lax.dot_general(
        left, right, (((contract[0],), (contract[1],)), ((), ())), preferred_element_type=f32
    )


def fill_slots(order_ref, slot_ref):
    def place(slot, carry):
        slot_ref[order_ref[slot]] = slot
        return carry

    lax.fori_loop(0, order_ref.shape[0], place, 0)


def three_rows(row):
    high = row.astype(bf16)
    rest = row - high.astype(f32)
    middle = rest.astype(bf16)
    low = (rest - middle.astype(f32)).astype(bf16)
    index = lax.broadcasted_iota(jnp.int32, (EXTRA, row.shape[1]), 0)
    zero = jnp.zeros((EXTRA, row.shape[1]), f32)
    rows = jnp.where(index == 0, high.astype(f32), zero)
    rows = jnp.where(index == 1, middle.astype(f32), rows)
    rows = jnp.where(index == 2, low.astype(f32), rows)
    return rows.astype(bf16)


def tile_at(tile):
    return pl.ds(pl.multiple_of(tile * TILE, TILE), TILE)


def block_at(slot):
    return pl.ds(pl.multiple_of(slot * BLOCK, BLOCK), BLOCK)


def tile_lanes(ref, head, slot_ref, tile, rows=slice(None)):
    first, second = slot_ref[2 * tile], slot_ref[2 * tile + 1]
    return jnp.concatenate(
        [ref[head, rows, block_at(first)], ref[head, rows, block_at(second)]], axis=1
    )


def tile_rows(ref, head, slot_ref, tile):
    first, second = slot_ref[2 * tile], slot_ref[2 * tile + 1]
    return jnp.concatenate([ref[head, block_at(first), :], ref[head, block_at(second), :]], axis=0)


def half_at(slot):
    return pl.ds(pl.multiple_of(lax.rem(slot, 2) * BLOCK, BLOCK), BLOCK)


def causal(shape):
    key = lax.broadcasted_iota(jnp.int32, shape, 0)
    query = lax.broadcasted_iota(jnp.int32, shape, 1)
    return key <= query


def gather_kernel(
    parts,
    groups,
    heads,
    x_ref,
    wqkv_ref,
    wout_ref,
    wup_ref,
    wdown_ref,
    small_ref,
    unit_ref,
    full_ref,
    wpair_ref,
    qt_out_ref,
    kt_out_ref,
    vt_out_ref,
    kn_out_ref,
    vn_out_ref,
    wcol_ref,
    gain_ref,
    factor_ref,
    most_ref,
    qt_ref,
    kt_ref,
    vt_ref,
    kn_ref,
    vn_ref,
    rows_ref,
    wstage_ref,
    mstage_ref,
    gained_ref,
    mlp_ref,
    wrecv_ref,
    wflip_ref,
    line_sem,
    side_sem,
    keep_sem,
    w_sem,
    lane_sem,
    mlp_sem,
    cross_sem,
    own_sem,
    stage_sem,
    lanes_sem,
    sides_sem,
):
    chips = parts // 2
    here = lax.axis_index("ctx")
    group = lax.axis_index("fsdp")
    core = lax.rem(here, 2)
    chip = here // 2
    other = here + 1 - 2 * core
    width = heads * HD
    group_peers = [lax.rem(group + step, groups) for step in range(1, groups)]

    barrier = pltpu.get_barrier_semaphore()
    pl.semaphore_signal(barrier, inc=1, device_id={"ctx": other})
    for peer in group_peers:
        pl.semaphore_signal(barrier, inc=1, device_id={"fsdp": peer})
    for step in (1, chips - 1):
        peer = lax.rem(chip + step, chips) * 2 + core
        pl.semaphore_signal(barrier, inc=1, device_id={"ctx": peer})

    def send(source, target, sems, device):
        return pltpu.make_async_remote_copy(
            src_ref=source,
            dst_ref=target,
            send_sem=sems[0],
            recv_sem=sems[1],
            device_id=device,
        )

    halves = rows_ref.shape[1] // BLOCK

    def line_copy(way, step, piece, part):
        ref = rows_ref.at[2 * piece + core, block_at(part)]
        sems = (line_sem.at[0, way, step, part], line_sem.at[1, way, step, part])
        return send(ref, ref, sems, {"ctx": here + (2 if way else -2)})

    def side_copy(piece, lane, part):
        ref = rows_ref.at[2 * piece + lane, block_at(part)]
        sems = (side_sem.at[0, piece, part], side_sem.at[1, piece, part])
        return send(ref, ref, sems, {"ctx": other})

    def results(slot):
        to = block_at(slot)
        copies = [
            pltpu.make_async_copy(ref.at[:, :, to], out.at[:, :, to], lanes_sem.at[index, slot])
            for index, (ref, out) in enumerate(
                ((qt_ref, qt_out_ref), (kt_ref, kt_out_ref), (vt_ref, vt_out_ref))
            )
        ]
        return copies + [
            pltpu.make_async_copy(ref.at[:, to], out.at[:, to], sides_sem.at[index, slot])
            for index, (ref, out) in enumerate(((kn_ref, kn_out_ref), (vn_ref, vn_out_ref)))
        ]

    def w_copy(peer, source):
        sems = (w_sem.at[0, peer], w_sem.at[1, source])
        return send(gained_ref, wrecv_ref.at[source], sems, {"fsdp": peer})

    def lane_copy(lane):
        ref = wpair_ref.at[lane]
        return send(ref, ref, (lane_sem.at[0], lane_sem.at[1]), {"ctx": other})

    def mlp_copy(peer, source):
        sems = (mlp_sem.at[0, peer], mlp_sem.at[1, source])
        return send(mlp_ref.at[:, core], full_ref.at[:, source, core], sems, {"fsdp": peer})

    def cross_copy(source, lane):
        ref = full_ref.at[:, source, lane]
        sems = (cross_sem.at[0, source], cross_sem.at[1, source])
        return send(ref, ref, sems, {"ctx": other})

    def keep_copy(piece):
        return pltpu.make_async_copy(rows_ref.at[piece], unit_ref.at[piece], keep_sem.at[piece])

    own_copy = pltpu.make_async_copy(mlp_ref, full_ref.at[:, group], own_sem)

    stages = [pltpu.make_async_copy(wqkv_ref, wstage_ref, stage_sem.at[0])] + [
        pltpu.make_async_copy(ref, mstage_ref.at[index], stage_sem.at[index + 1])
        for index, ref in enumerate((wout_ref, wup_ref, wdown_ref))
    ]
    for stage in stages:
        stage.start()
    rows = x_ref[...].astype(f32)
    rows_ref[here] = (rows * rms_scale(rows)).astype(bf16)
    pl.semaphore_wait(barrier, groups + 2)

    def forward(way, step, piece, part):
        @pl.when((chip < chips - 1) if way else (chip > 0))
        def _():
            line_copy(way, step, piece, part).start()

    for part in range(halves):
        for way in range(2):
            forward(way, 0, chip, part)
        side_copy(chip, core, part).start()
    held = gain_ref.shape[0]
    lanes = -(-held // PAD) * PAD
    gains = jnp.broadcast_to(small_ref[:D].reshape(1, D), (8, D))
    gains = pltpu.roll(gains, lax.rem(D - group * held, D), 1)[:1, :lanes]
    gain_ref[...] = jnp.broadcast_to(gains, (PAD, lanes)).T[:held, :1]
    scales = small_ref[2 * D :].reshape(1, HD)
    soft = jnp.log(1.0 + jnp.exp(scales)) * (scale_base / math.sqrt(HD) * LOG2E)
    soft = jnp.concatenate([soft, jnp.zeros((1, PAD - HD), f32)], axis=1)
    factor_ref[...] = jnp.broadcast_to(soft, (PAD, PAD)).T[:HD, :1]
    shift = lax.rem(D - here * width, D)
    stages[0].wait()
    for part in range(3):
        turned = pltpu.roll(wstage_ref[:, part * D : (part + 1) * D], shift, 1)
        gained_ref[part] = (turned[:, :width] * gain_ref[...]).astype(bf16)
        wcol_ref[:, part * width : (part + 1) * width] = turned[:, :width].astype(bf16)
    for peer in group_peers:
        w_copy(peer, group).start()
    for index in range(3):
        stages[index + 1].wait()
        mlp_ref[index] = mstage_ref[index].astype(bf16).reshape(mlp_ref.shape[1:])
    own_copy.start()
    keep_copy(here).start()
    wrecv_ref[group] = gained_ref[...]
    for peer in group_peers:
        w_copy(group, peer).wait_recv()
    for peer in group_peers:
        mlp_copy(peer, group).start()
    for part in range(3):
        flipped = wrecv_ref[:, part].reshape(D, width).T
        wflip_ref[part * width : (part + 1) * width] = flipped
    wpair_ref[core] = wflip_ref[...]
    lane_copy(core).start()

    extra_row = lax.broadcasted_iota(jnp.int32, (PAD - HD, BLOCK), 0)
    extra = jnp.where(extra_row < 3, 1.0, 0.0)
    spare = jnp.zeros((PAD - HD, BLOCK), bf16)

    most_ref[...] = jnp.zeros(most_ref.shape, f32)

    def project(piece, part):
        slot = piece * halves + part
        to = block_at(slot)
        result = dot(wflip_ref[...], rows_ref[piece, block_at(part), :], (1, 1))
        for head in range(heads):
            query, key, value = (
                result[share * width + head * HD : share * width + (head + 1) * HD]
                for share in range(3)
            )
            query = query * factor_ref[...]
            for row, rows in enumerate((query, key)):
                most_ref[row : row + 1] = jnp.maximum(
                    most_ref[row : row + 1], jnp.sum(rows * rows, axis=0, keepdims=True)
                )
            qt_ref[head, :HD, to] = query.astype(bf16)
            qt_ref[head, HD:, to] = spare
            kt_ref[head, :, to] = key.astype(bf16)
            vt_ref[head, :HD, to] = value.astype(bf16)
            vt_ref[head, HD:, to] = jnp.ones((EXTRA, BLOCK), bf16)
            kn_ref[head, to, :] = jnp.concatenate([key, extra], axis=0).T.astype(bf16)
            vn_ref[head, to, :] = jnp.concatenate([value, extra], axis=0).T.astype(bf16)
        for copy in results(slot):
            copy.start()

    def visit(index, carry):
        distance, part = index // halves, lax.rem(index, halves)
        for way in range(2):
            piece = chip - distance if way else chip + distance
            valid = (piece >= 0) if way else (piece <= chips - 1)

            @pl.when(valid & (distance > 0))
            def _():
                line_copy(way, distance - 1, piece, part).wait_recv()
                side_copy(piece, core, part).start()
                forward(way, distance, piece, part)

                @pl.when(part == halves - 1)
                def _():
                    keep_copy(2 * piece + core).start()

        for way in range(2):
            piece = chip - distance if way else chip + distance
            valid = (piece >= 0) if way else ((piece <= chips - 1) & (distance > 0))

            @pl.when(valid)
            def _():
                project(2 * piece + core, part)
                side_copy(piece, 1 - core, part).wait_recv()
                project(2 * piece + 1 - core, part)

                @pl.when(part == halves - 1)
                def _():
                    keep_copy(2 * piece + 1 - core).start()

        return carry

    lax.fori_loop(0, chips * halves, visit, 0)

    for peer in group_peers:
        mlp_copy(group, peer).wait_recv()
        cross_copy(peer, core).start()
    for peer in group_peers:
        cross_copy(peer, 1 - core).wait_recv()
        cross_copy(peer, core).wait_send()
        w_copy(peer, group).wait_send()
        mlp_copy(peer, group).wait_send()
    own_copy.wait()
    lane_copy(1 - core).wait_recv()
    lane_copy(core).wait_send()

    def drain(piece, carry):
        keep_copy(2 * piece).wait()
        keep_copy(2 * piece + 1).wait()
        for part in range(halves):
            side_copy(piece, core, part).wait_send()

            @pl.when((piece <= chip) & (chip < chips - 1))
            def _():
                line_copy(1, chip - piece, piece, part).wait_send()

            @pl.when((piece >= chip) & (chip > 0))
            def _():
                line_copy(0, piece - chip, piece, part).wait_send()

        return carry

    lax.fori_loop(0, chips, drain, 0)

    def settle(slot, carry):
        for copy in results(slot):
            copy.wait()
        return carry

    lax.fori_loop(0, 2 * chips * halves, settle, 0)


def gather_rows(parts, groups, heads, rows, w_qkv, w_out, w_up, w_down, small):
    rows_dev = rows.shape[0]
    held = w_qkv.shape[0]
    tokens = parts * rows_dev
    dma = pltpu.SemaphoreType.DMA
    chips = parts // 2
    anywhere = pl.BlockSpec(memory_space=pl.ANY)
    return pl.pallas_call(
        functools.partial(gather_kernel, parts, groups, heads),
        name="gather_rows",
        out_shape=[
            jax.ShapeDtypeStruct((parts, rows_dev, D), bf16),
            jax.ShapeDtypeStruct((3, groups, 2, held // 2, D), bf16),
            jax.ShapeDtypeStruct((2, 3 * heads * HD, D), bf16),
            jax.ShapeDtypeStruct((heads, PAD, tokens), bf16),
            jax.ShapeDtypeStruct((heads, HD, tokens), bf16),
            jax.ShapeDtypeStruct((heads, HD + EXTRA, tokens), bf16),
            jax.ShapeDtypeStruct((heads, tokens, PAD), bf16),
            jax.ShapeDtypeStruct((heads, tokens, PAD), bf16),
            jax.ShapeDtypeStruct((held, 3 * heads * HD), bf16),
            jax.ShapeDtypeStruct((held, 1), f32),
            jax.ShapeDtypeStruct((HD, 1), f32),
            jax.ShapeDtypeStruct((8, BLOCK), f32),
        ],
        in_specs=in_vmem(1) + [anywhere] * 4 + in_vmem(1),
        out_specs=[anywhere] * 2 + in_vmem(1) + [anywhere] * 5 + in_vmem(4),
        scratch_shapes=[
            pltpu.VMEM((heads, PAD, tokens), bf16),
            pltpu.VMEM((heads, HD, tokens), bf16),
            pltpu.VMEM((heads, HD + EXTRA, tokens), bf16),
            pltpu.VMEM((heads, tokens, PAD), bf16),
            pltpu.VMEM((heads, tokens, PAD), bf16),
            pltpu.VMEM((parts, rows_dev, D), bf16),
            pltpu.VMEM((held, 3 * D), f32),
            pltpu.VMEM((3, held, D), f32),
            pltpu.VMEM((3, held, heads * HD), bf16),
            pltpu.VMEM((3, 2, held // 2, D), bf16),
            pltpu.VMEM((groups, 3, held, heads * HD), bf16),
            pltpu.VMEM((3 * heads * HD, D), bf16),
            dma((2, 2, chips, rows_dev // BLOCK)),
            dma((2, chips, rows_dev // BLOCK)),
            dma((parts,)),
            dma((2, groups)),
            dma((2,)),
            dma((2, groups)),
            dma((2, groups)),
            dma,
            dma((4,)),
            dma((3, tokens // BLOCK)),
            dma((2, tokens // BLOCK)),
        ],
        compiler_params=pltpu.CompilerParams(
            vmem_limit_bytes=60 * 1024 * 1024, collective_id=2, has_side_effects=True
        ),
    )(rows, w_qkv, w_out, w_up, w_down, small)


def forward_kernel(
    heads,
    order_ref,
    most_ref,
    qt_ref,
    kn_in_ref,
    vt_in_ref,
    lse_ref,
    ot_ref,
    slot_ref,
    kn_ref,
    vt_ref,
    acc_ref,
    top_ref,
    load_sem,
):
    loads = [
        pltpu.make_async_copy(source, target, load_sem.at[index])
        for index, (source, target) in enumerate(((kn_in_ref, kn_ref), (vt_in_ref, vt_ref)))
    ]
    for load in loads:
        load.start()
    fill_slots(order_ref, slot_ref)
    tokens = kn_ref.shape[1]
    num_tiles = tokens // TILE
    prompt_tiles = num_tiles // 2

    bounded = (
        jnp.max(most_ref[0:1]) * jnp.max(most_ref[1:2]) <= SCORE_BOUND * SCORE_BOUND
    )
    for load in loads:
        load.wait()

    def run(shifted):
        def query_tile(tile, carry):
            queries = [tile_lanes(qt_ref, head, slot_ref, tile) for head in range(heads)]
            if shifted:
                top_ref[...] = jnp.full(top_ref.shape, -1e30, f32)
            else:
                top_ref[...] = jnp.zeros(top_ref.shape, f32)
            acc_ref[...] = jnp.zeros(acc_ref.shape, f32)

            def step(key_rows, value_lanes, start, masked):
                scores = [dot(key_rows[head], queries[head][:, start:]) for head in range(heads)]
                if masked:
                    allowed = causal(scores[0].shape)
                    scores = [jnp.where(allowed, score, -1e30) for score in scores]
                if shifted:
                    olds = [top_ref[head, :, start:] for head in range(heads)]
                    tops = [
                        jnp.maximum(old, jnp.max(score, axis=0, keepdims=True))
                        for old, score in zip(olds, scores)
                    ]
                    scores = [score - top for score, top in zip(scores, tops)]
                    for head in range(heads):
                        acc_ref[head, :, start:] *= jnp.exp2(olds[head] - tops[head])
                        top_ref[head, :, start:] = tops[head]
                probs = [jnp.exp2(score).astype(bf16) for score in scores]
                for head in range(heads):
                    acc_ref[head, :, start:] += dot(value_lanes[head], probs[head])

            def full(key_tile, inner):
                step(
                    [tile_rows(kn_ref, head, slot_ref, key_tile) for head in range(heads)],
                    [tile_lanes(vt_ref, head, slot_ref, key_tile) for head in range(heads)],
                    0,
                    False,
                )
                return inner

            def double(pair, inner):
                return full(2 * pair + 1, full(2 * pair, inner))

            count = jnp.minimum(tile, prompt_tiles)
            lax.fori_loop(0, count // 2, double, 0)
            lax.fori_loop(count // 2 * 2, count, full, 0)
            for part in range(TILE // BLOCK):
                block = block_at(slot_ref[tile * (TILE // BLOCK) + part])
                step(
                    [kn_ref[head, block, :] for head in range(heads)],
                    [vt_ref[head, :, block] for head in range(heads)],
                    part * BLOCK,
                    True,
                )
            for head in range(heads):
                acc = acc_ref[head]
                mass = acc[HD : HD + 1]
                mixed = (acc[:HD] / mass).astype(bf16)
                lse_ref[head, :, tile_at(tile)] = top_ref[head] + jnp.log2(mass)
                for part in range(TILE // BLOCK):
                    slot = slot_ref[tile * (TILE // BLOCK) + part]
                    ot_ref[slot // 2, head * HD : (head + 1) * HD, half_at(slot)] = mixed[
                        :, part * BLOCK : (part + 1) * BLOCK
                    ]
            return carry

        lax.fori_loop(0, num_tiles, query_tile, 0)

    @pl.when(bounded)
    def _():
        run(False)

    @pl.when(jnp.logical_not(bounded))
    def _():
        run(True)


def backward_kernel(
    heads,
    order_ref,
    qt_ref,
    kt_in_ref,
    kn_in_ref,
    vn_in_ref,
    lse_ref,
    ot_ref,
    dt_ref,
    factor_ref,
    dqkv_ref,
    dscale_ref,
    slot_ref,
    kt_ref,
    kn_ref,
    vn_ref,
    qa_ref,
    da_ref,
    dq_ref,
    dk_ref,
    dv_ref,
    scale_ref,
    load_sem,
):
    loads = [
        pltpu.make_async_copy(source, target, load_sem.at[index])
        for index, (source, target) in enumerate(
            ((kn_in_ref, kn_ref), (vn_in_ref, vn_ref), (kt_in_ref, kt_ref))
        )
    ]
    for load in loads:
        load.start()
    fill_slots(order_ref, slot_ref)
    tokens = kn_ref.shape[1]
    num_blocks = tokens // BLOCK
    num_tiles = tokens // TILE
    prompt_tiles = num_tiles // 2
    width = heads * HD

    def prepare(block, carry):
        slot = slot_ref[block]
        to = pl.ds(pl.multiple_of(block * BLOCK, BLOCK), BLOCK)
        for head in range(heads):
            rows = slice(head * HD, (head + 1) * HD)
            grad = dt_ref[slot // 2, rows, half_at(slot)]
            mixed = ot_ref[slot // 2, rows, half_at(slot)]
            delta = jnp.sum(grad.astype(f32) * mixed.astype(f32), axis=0, keepdims=True)
            da_ref[head, :HD, to] = grad
            da_ref[head, HD : HD + EXTRA, to] = three_rows(-delta)
            da_ref[head, HD + EXTRA :, to] = jnp.zeros((PAD - HD - EXTRA, BLOCK), bf16)
            qa_ref[head, :HD, to] = qt_ref[head, :HD, block_at(slot)]
            qa_ref[head, HD : HD + EXTRA, to] = three_rows(-lse_ref[head, :, to])
            qa_ref[head, HD + EXTRA :, to] = jnp.zeros((PAD - HD - EXTRA, BLOCK), bf16)
        return carry

    lax.fori_loop(0, num_blocks, prepare, 0)
    dk_ref[...] = jnp.zeros(dk_ref.shape, f32)
    dv_ref[...] = jnp.zeros(dv_ref.shape, f32)
    scale_ref[...] = jnp.zeros(scale_ref.shape, f32)
    for load in loads:
        load.wait()

    def query_tile(tile, carry):
        here = tile_at(tile)
        dq_ref[...] = jnp.zeros(dq_ref.shape, f32)

        def step(keys, key_rows, key_lanes, value_rows, start, masked):
            to = pl.ds(pl.multiple_of(tile * TILE + start, BLOCK), TILE - start)
            queries = [qa_ref[head, :, to] for head in range(heads)]
            grads = [da_ref[head, :, to] for head in range(heads)]
            scores = [dot(key_rows[head], queries[head]) for head in range(heads)]
            spreads = [dot(value_rows[head], grads[head]) for head in range(heads)]
            probs = [jnp.exp2(score) for score in scores]
            if masked:
                allowed = causal(scores[0].shape)
                probs = [jnp.where(allowed, prob, 0.0) for prob in probs]
            dscores = [(prob * spread).astype(bf16) for prob, spread in zip(probs, spreads)]
            for head in range(heads):
                dv_ref[head, :, keys] += dot(grads[head][:HD], probs[head].astype(bf16), (1, 1))
                dk_ref[head, :, keys] += dot(queries[head][:HD], dscores[head], (1, 1))
                dq_ref[head, :, start:] += dot(key_lanes[head], dscores[head])

        def full(key_tile, inner):
            step(
                tile_at(key_tile),
                [tile_rows(kn_ref, head, slot_ref, key_tile) for head in range(heads)],
                [tile_lanes(kt_ref, head, slot_ref, key_tile) for head in range(heads)],
                [tile_rows(vn_ref, head, slot_ref, key_tile) for head in range(heads)],
                0,
                False,
            )
            return inner

        def double(pair, inner):
            return full(2 * pair + 1, full(2 * pair, inner))

        count = jnp.minimum(tile, prompt_tiles)
        lax.fori_loop(0, count // 2, double, 0)
        lax.fori_loop(count // 2 * 2, count, full, 0)
        for part in range(TILE // BLOCK):
            position = tile * (TILE // BLOCK) + part
            block = block_at(slot_ref[position])
            step(
                block_at(position),
                [kn_ref[head, block, :] for head in range(heads)],
                [kt_ref[head, :, block] for head in range(heads)],
                [vn_ref[head, block, :] for head in range(heads)],
                part * BLOCK,
                True,
            )
        for head in range(heads):
            dq = dq_ref[head]
            product = dq * qa_ref[head, :HD, here].astype(f32)
            for lane in range(TILE // PAD):
                scale_ref[head] += product[:, lane * PAD : (lane + 1) * PAD]
            scaled = (dq * (factor_ref[...] * LN2)).astype(bf16)
            for part in range(TILE // BLOCK):
                slot = slot_ref[tile * (TILE // BLOCK) + part]
                dqkv_ref[slot // 2, head * HD : (head + 1) * HD, half_at(slot)] = scaled[
                    :, part * BLOCK : (part + 1) * BLOCK
                ]
        return carry

    lax.fori_loop(0, num_tiles, query_tile, 0)

    def finish(block, carry):
        slot = slot_ref[block]
        owner, to = slot // 2, half_at(slot)
        at = pl.ds(pl.multiple_of(block * BLOCK, BLOCK), BLOCK)
        for head in range(heads):
            row = width + head * HD
            dqkv_ref[owner, row : row + HD, to] = (dk_ref[head, :, at] * LN2).astype(bf16)
            row = 2 * width + head * HD
            dqkv_ref[owner, row : row + HD, to] = dv_ref[head, :, at].astype(bf16)
        return carry

    lax.fori_loop(0, num_blocks, finish, 0)
    sums = functools.reduce(jnp.add, [scale_ref[head] for head in range(heads)])
    sums = jnp.concatenate([sums, jnp.zeros((PAD - HD, PAD), f32)], axis=0).T
    dscale_ref[...] = jnp.sum(sums, axis=0, keepdims=True)


def in_vmem(count):
    return [pl.BlockSpec(memory_space=pltpu.VMEM)] * count


def params(mebibytes):
    return pltpu.CompilerParams(vmem_limit_bytes=mebibytes * 1024 * 1024)


def attention_forward(order, most, qt, kn, vt, parts):
    heads, tokens = kn.shape[:2]
    return pl.pallas_call(
        functools.partial(forward_kernel, heads),
        name="attention_forward",
        out_shape=[
            jax.ShapeDtypeStruct((heads, 1, tokens), f32),
            jax.ShapeDtypeStruct((parts, heads * HD, tokens // parts), bf16),
        ],
        in_specs=[pl.BlockSpec(memory_space=pltpu.SMEM)]
        + in_vmem(2)
        + [pl.BlockSpec(memory_space=pl.ANY)] * 2,
        out_specs=in_vmem(2),
        scratch_shapes=[
            pltpu.SMEM(order.shape, jnp.int32),
            pltpu.VMEM(kn.shape, bf16),
            pltpu.VMEM(vt.shape, bf16),
            pltpu.VMEM((heads, HD + EXTRA, TILE), f32),
            pltpu.VMEM((heads, 1, TILE), f32),
            pltpu.SemaphoreType.DMA((2,)),
        ],
        compiler_params=params(60),
        cost_estimate=attention_cost(heads, tokens, 2),
    )(order, most, qt, kn, vt)


def attention_cost(heads, tokens, passes):
    pairs = heads * tokens * tokens // 2
    return pl.CostEstimate(
        flops=2 * passes * pairs * BLOCK, bytes_accessed=tokens * D, transcendentals=pairs
    )


def attention_backward(order, kept, mixed, dmixed, factor):
    qt, kt, kn, vn, lse = kept
    heads, tokens = kn.shape[:2]
    return pl.pallas_call(
        functools.partial(backward_kernel, heads),
        name="attention_backward",
        out_shape=[
            jax.ShapeDtypeStruct((mixed.shape[0], 3 * heads * HD, mixed.shape[2]), bf16),
            jax.ShapeDtypeStruct((1, PAD), f32),
        ],
        in_specs=[pl.BlockSpec(memory_space=pltpu.SMEM)]
        + in_vmem(1)
        + [pl.BlockSpec(memory_space=pl.ANY)] * 3
        + in_vmem(4),
        out_specs=in_vmem(2),
        scratch_shapes=[
            pltpu.SMEM(order.shape, jnp.int32),
            pltpu.VMEM(kt.shape, bf16),
            pltpu.VMEM(kn.shape, bf16),
            pltpu.VMEM(vn.shape, bf16),
            pltpu.VMEM((heads, PAD, tokens), bf16),
            pltpu.VMEM((heads, PAD, tokens), bf16),
            pltpu.VMEM((heads, HD, TILE), f32),
            pltpu.VMEM((heads, HD, tokens), f32),
            pltpu.VMEM((heads, HD, tokens), f32),
            pltpu.VMEM((heads, HD, PAD), f32),
            pltpu.SemaphoreType.DMA((3,)),
        ],
        compiler_params=params(60),
        cost_estimate=attention_cost(heads, tokens, 5),
    )(order, qt, kt, kn, vn, lse, mixed, dmixed, factor)


def middle_kernel(
    parts,
    groups,
    mixed_ref,
    x_ref,
    dy_ref,
    weights_ref,
    gain_ref,
    *refs,
):
    out_ref, dmid_ref, dmixed_ref, gain_grad_ref = refs[:4]
    chunk_refs = refs[4 : 4 + groups]
    (
        w_ref,
        attn_ref,
        dattn_ref,
        act_ref,
        normed_ref,
        dhidden_ref,
        dbranch_ref,
        grad_ref,
        theirs_ref,
        w_sem,
        attn_sem,
        dattn_sem,
        pair_sem,
    ) = refs[4 + groups :]
    here = lax.axis_index("ctx")
    group = lax.axis_index("fsdp")
    core = lax.rem(here, 2)
    other = here + 1 - 2 * core
    peers = [lax.rem(here + step, parts) for step in range(1, parts)]
    tokens = x_ref.shape[0]
    width = mixed_ref.shape[1]
    held = theirs_ref.shape[2]
    loads = [
        pltpu.make_async_copy(weights_ref.at[index], w_ref.at[index], w_sem.at[index])
        for index in range(3)
    ]
    for load in loads:
        load.start()

    barrier = pltpu.get_barrier_semaphore()
    for peer in peers:
        pl.semaphore_signal(barrier, inc=1, device_id={"ctx": peer})
    pl.semaphore_wait(barrier, parts - 1)

    def lanes(part):
        return pl.ds(pl.multiple_of(part * BLOCK, BLOCK), BLOCK)

    def attn_copy(part, peer, source):
        return pltpu.make_async_remote_copy(
            src_ref=mixed_ref.at[peer, :, lanes(part)],
            dst_ref=attn_ref.at[source, :, lanes(part)],
            send_sem=attn_sem.at[0, part, peer],
            recv_sem=attn_sem.at[1, part, source],
            device_id={"ctx": peer},
        )

    def dattn_copy(part, peer, source):
        return pltpu.make_async_remote_copy(
            src_ref=dattn_ref.at[peer, :, lanes(part)],
            dst_ref=dmixed_ref.at[source, :, lanes(part)],
            send_sem=dattn_sem.at[0, part, peer],
            recv_sem=dattn_sem.at[1, part, source],
            device_id={"ctx": peer},
        )

    def rows_of(owner, lane):
        start = pl.multiple_of((owner * 2 + lane) * held, 16)
        return pl.ds(start, held)

    def pair_copy(index, owner, lane):
        return pltpu.make_async_remote_copy(
            src_ref=grad_ref.at[index, rows_of(owner, lane), :],
            dst_ref=theirs_ref.at[index, owner],
            send_sem=pair_sem.at[0, index, owner],
            recv_sem=pair_sem.at[1, index, owner],
            device_id={"ctx": other},
        )

    for part in range(tokens // BLOCK):
        for peer in peers:
            attn_copy(part, peer, here).start()
    attn_ref[here] = mixed_ref[here]
    gain_grad_ref[...] = jnp.zeros(gain_grad_ref.shape, f32)
    for load in loads:
        load.wait()
    gain = gain_ref[...]

    def layer(part, carry):
        rows = lanes(part)
        for peer in peers:
            attn_copy(part, here, peer).wait_recv()
        attn = attn_ref[:, :, rows].reshape(D, BLOCK)
        mid = x_ref[rows, :].astype(f32) + dot(attn, w_ref[0], (0, 0))
        scale = rms_scale(mid)
        unit = mid * scale
        normed = (unit * gain).astype(bf16)
        normed_ref[rows, :] = normed
        hidden = dot(normed, w_ref[1])
        gate = jax.nn.sigmoid(hidden)
        act = (hidden * gate).astype(bf16)
        act_ref[rows, :] = act
        dy = dy_ref[rows, :]
        dact = dot(dy, w_ref[2], (1, 1))
        dhidden = (dact * gate * (1.0 + hidden * (1.0 - gate))).astype(bf16)
        dhidden_ref[rows, :] = dhidden
        dnormed = dot(dhidden, w_ref[1], (1, 1))
        dunit = dnormed * gain
        dmid = dy.astype(f32) + scale * (
            dunit - unit * jnp.mean(dunit * unit, axis=-1, keepdims=True)
        )
        dmid_ref[rows, :] = dmid
        dbranch = dmid.astype(bf16)
        dbranch_ref[rows, :] = dbranch
        dattn = dot(w_ref[0], dbranch, (1, 1)).astype(bf16).reshape(parts, width, BLOCK)
        dattn_ref[:, :, rows] = dattn
        for peer in peers:
            dattn_copy(part, peer, here).start()
        dmixed_ref[here, :, rows] = dattn_ref[here, :, rows]
        out_ref[rows, :] = (mid + dot(act, w_ref[2])).astype(bf16)
        gain_grad_ref[...] += jnp.sum(dnormed * unit, axis=0, keepdims=True)
        return carry

    lax.fori_loop(0, tokens // BLOCK, layer, 0)

    def down_rows(index, carry):
        rows = lanes(index)
        grad_ref[2, rows, :] = dot(act_ref[:, rows], dy_ref[...], (0, 0)).astype(bf16)
        return carry

    def up_rows(index, carry):
        rows = lanes(index)
        grad_ref[1, rows, :] = dot(normed_ref[:, rows], dhidden_ref[...], (0, 0)).astype(bf16)
        return carry

    def out_rows(index, carry):
        rows = pl.ds(pl.multiple_of(index * width, 16), width)
        grad_ref[0, rows, :] = dot(attn_ref[index], dbranch_ref[...]).astype(bf16)
        return carry

    for index, count, run in (
        (2, D // BLOCK, down_rows),
        (1, D // BLOCK, up_rows),
        (0, parts, out_rows),
    ):
        lax.fori_loop(0, count, run, 0)
        for owner in range(groups):
            pair_copy(index, owner, 1 - core).start()
    for step in range(groups):
        owner = group ^ step
        for index in (2, 1, 0):
            pair_copy(index, owner, core).wait_recv()
            chunk_refs[step][index] = (
                grad_ref[index, rows_of(owner, core), :].astype(f32)
                + theirs_ref[index, owner].astype(f32)
            ).astype(bf16)
    for part in range(tokens // BLOCK):
        for peer in peers:
            dattn_copy(part, here, peer).wait_recv()
            dattn_copy(part, peer, here).wait_send()
            attn_copy(part, peer, here).wait_send()
    for index in range(3):
        for owner in range(groups):
            pair_copy(index, owner, 1 - core).wait_send()


def middle(parts, groups, mixed, rows, cotangent, weights, gain):
    rows_dev = rows.shape[0]
    half = D // groups // 2
    dma = pltpu.SemaphoreType.DMA
    halves = rows_dev // BLOCK
    return pl.pallas_call(
        functools.partial(middle_kernel, parts, groups),
        name="middle",
        out_shape=[
            jax.ShapeDtypeStruct((rows_dev, D), bf16),
            jax.ShapeDtypeStruct((rows_dev, D), f32),
            jax.ShapeDtypeStruct(mixed.shape, bf16),
            jax.ShapeDtypeStruct((1, D), f32),
        ]
        + [jax.ShapeDtypeStruct((3, half, D), bf16)] * groups,
        in_specs=in_vmem(3) + [pl.BlockSpec(memory_space=pl.ANY)] + in_vmem(1),
        out_specs=in_vmem(4 + groups),
        scratch_shapes=[
            pltpu.VMEM((3, D, D), bf16),
            pltpu.VMEM(mixed.shape, bf16),
            pltpu.VMEM(mixed.shape, bf16),
            pltpu.VMEM((rows_dev, D), bf16),
            pltpu.VMEM((rows_dev, D), bf16),
            pltpu.VMEM((rows_dev, D), bf16),
            pltpu.VMEM((rows_dev, D), bf16),
            pltpu.VMEM((3, D, D), bf16),
            pltpu.VMEM((3, groups, half, D), bf16),
            dma((3,)),
            dma((2, halves, parts)),
            dma((2, halves, parts)),
            dma((2, 3, groups)),
        ],
        compiler_params=pltpu.CompilerParams(
            vmem_limit_bytes=60 * 1024 * 1024, collective_id=3, has_side_effects=True
        ),
    )(mixed, rows, cotangent, weights, gain)


def reduce_kernel(
    parts,
    groups,
    dq_in_ref,
    wt_in_ref,
    units_ref,
    wc_ref,
    small_ref,
    *refs,
):
    chunk_in_refs = refs[:groups]
    (
        down_ref,
        up_ref,
        own_ref,
        ugather_ref,
        mgather_ref,
        sgather_ref,
        dq_ref,
        wt_ref,
        chunk_ref,
        held_ref,
        total_ref,
        u_ref,
        usum_ref,
        msum_ref,
        pair_ref,
        sum_ref,
        urecv_ref,
        mlp_ref,
        mrecv_ref,
        part_ref,
        column_ref,
        smine_ref,
        srecv_ref,
        pair_sem,
        sum_sem,
        u_sem,
        m_sem,
        line_sem,
        side_sem,
        small_sem,
        cross_sem,
        load_sem,
        held_sem,
        keep_sem,
    ) = refs[groups:]
    chips = parts // 2
    here = lax.axis_index("ctx")
    group = lax.axis_index("fsdp")
    core = lax.rem(here, 2)
    chip = here // 2
    other = here + 1 - 2 * core
    ctx_peers = [lax.rem(here + step, parts) for step in range(1, parts)]
    chip_peers = [lax.rem(chip + step, chips) for step in range(1, chips)]
    group_peers = [lax.rem(group + step, groups) for step in range(1, groups)]

    loads = [
        pltpu.make_async_copy(ref, chunk_ref.at[index], load_sem.at[index])
        for index, ref in enumerate(chunk_in_refs)
    ]
    loads.append(pltpu.make_async_copy(dq_in_ref, dq_ref, load_sem.at[groups]))
    loads.append(pltpu.make_async_copy(wt_in_ref, wt_ref, load_sem.at[groups + 1]))
    for load in loads:
        load.start()

    def unit_load(piece):
        slot = lax.rem(piece, 2)
        return pltpu.make_async_copy(units_ref.at[piece], held_ref.at[slot], held_sem.at[slot])

    for piece in range(2):
        unit_load(piece).start()

    barrier = pltpu.get_barrier_semaphore()
    for peer in ctx_peers:
        pl.semaphore_signal(barrier, inc=1, device_id={"ctx": peer})
    for peer in group_peers:
        pl.semaphore_signal(barrier, inc=1, device_id={"fsdp": peer})

    def send(source, target, sems, device):
        return pltpu.make_async_remote_copy(
            src_ref=source,
            dst_ref=target,
            send_sem=sems[0],
            recv_sem=sems[1],
            device_id=device,
        )

    def pair_copy(index):
        return send(
            dq_in_ref.at[index, 1 - core],
            pair_ref.at[index],
            (pair_sem.at[0, index], pair_sem.at[1, index]),
            {"ctx": other},
        )

    def u_copy(peer, source):
        return send(
            u_ref.at[peer],
            urecv_ref.at[source],
            (u_sem.at[0, peer], u_sem.at[1, source]),
            {"fsdp": peer},
        )

    def m_copy(peer, source):
        return send(
            mlp_ref.at[peer],
            mrecv_ref.at[source],
            (m_sem.at[0, peer], m_sem.at[1, source]),
            {"ctx": 2 * peer + core},
        )

    for load in loads[:groups]:
        load.wait()
    share = mlp_ref.shape[2]
    for matrix in range(3):
        total = functools.reduce(
            jnp.add, [chunk_ref[step, matrix].astype(f32) for step in range(groups)]
        )
        for index in range(chips):
            mlp_ref[index, matrix] = total[index * share : (index + 1) * share].astype(bf16)
    pl.semaphore_wait(barrier, parts + groups - 2)
    for peer in chip_peers:
        m_copy(peer, chip).start()
    for index in range(chips):
        pair_copy(index).start()
    for load in loads[groups:]:
        load.wait()

    rows_half = own_ref.shape[0] // 2

    def partial(target, index):
        rows = pl.ds(pl.multiple_of(index * rows_half, rows_half), rows_half)
        part_ref[rows, :] = dot(dq_ref[target, core, :, rows], wt_ref[core], (0, 0)) + dot(
            pair_ref[target, :, rows], wt_ref[1 - core], (0, 0)
        )
        return rows

    def sum_copy(way, target, index):
        ref = sum_ref.at[way + target, pl.ds(index * rows_half, rows_half)]
        sems = (sum_sem.at[0, way, target, index], sum_sem.at[1, way, target, index])
        return send(ref, ref, sems, {"ctx": here + (2 if way else -2)})

    def reduce_step(step):
        last = step == chips - 2
        for way, target, active, first, out_ref in (
            (0, step - (chips - 1) + chip, step >= chips - 1 - chip, chip == chips - 1, down_ref),
            (1, chips - 1 - step + chip, step >= chip, chip == 0, up_ref),
        ):

            @pl.when(active)
            def _():
                def half(index, carry):
                    rows = partial(target, index)

                    @pl.when(first)
                    def _():
                        sum_ref[way + target, rows] = part_ref[rows, :].astype(bf16)

                    @pl.when(jnp.logical_not(first))
                    def _():
                        sum_copy(way, target, index).wait_recv()
                        sum_ref[way + target, rows] = (
                            part_ref[rows, :] + sum_ref[way + target, rows].astype(f32)
                        ).astype(bf16)

                    if last:
                        out_ref[rows, :] = sum_ref[way + target, rows]
                    else:
                        sum_copy(way, target, index).start()
                    return carry

                lax.fori_loop(0, 2, half, 0)

            if last:

                @pl.when(jnp.logical_not(active))
                def _():
                    out_ref[...] = jnp.zeros(out_ref.shape, bf16)

    gathers = (ugather_ref, mgather_ref)
    sums = (usum_ref, msum_ref)

    def keep_copy(which):
        return pltpu.make_async_copy(sums[which], gathers[which].at[here], keep_sem.at[which])

    def line_copy(which, way, step, piece):
        ref = gathers[which].at[2 * piece + core]
        sems = (line_sem.at[0, which, way, step], line_sem.at[1, which, way, step])
        source = sums[which] if step == 0 else ref
        return send(source, ref, sems, {"ctx": here + (2 if way else -2)})

    def side_copy(which, piece, lane, own=False):
        ref = gathers[which].at[2 * piece + lane]
        sems = (side_sem.at[0, which, piece], side_sem.at[1, which, piece])
        return send(sums[which] if own else ref, ref, sems, {"ctx": other})

    def line_sends(which, step, go):
        @pl.when((chip < chips - 1) & (chip - step >= 0))
        def _():
            go(line_copy(which, 1, step, chip - step))

        @pl.when((chip > 0) & (chip + step <= chips - 1))
        def _():
            go(line_copy(which, 0, step, chip + step))

    def line_receive(which, step):
        @pl.when(chip - 1 - step >= 0)
        def _():
            line_copy(which, 1, step, chip - 1 - step).wait_recv()
            side_copy(which, chip - 1 - step, core).start()

        @pl.when(chip + 1 + step <= chips - 1)
        def _():
            line_copy(which, 0, step, chip + 1 + step).wait_recv()
            side_copy(which, chip + 1 + step, core).start()

    def small_copy(peer, source):
        return send(
            smine_ref,
            srecv_ref.at[source],
            (small_sem.at[0, peer], small_sem.at[1, source]),
            {"ctx": peer},
        )

    def cross_copy(peer, source):
        return send(
            sgather_ref.at[group],
            sgather_ref.at[source],
            (cross_sem.at[0, peer], cross_sem.at[1, source]),
            {"fsdp": peer},
        )

    for index in range(chips):
        pair_copy(index).wait_recv()
    reduce_step(0)

    total_ref[...] = jnp.zeros(total_ref.shape, f32)

    def accumulate(piece, carry):
        unit_load(piece).wait()
        total_ref[...] += dot(dq_ref[piece // 2, lax.rem(piece, 2)], held_ref[lax.rem(piece, 2)])

        @pl.when(piece + 2 < parts)
        def _():
            unit_load(piece + 2).start()

        return carry

    lax.fori_loop(0, parts, accumulate, 0)
    u_ref[...] = total_ref[...].T.astype(bf16).reshape(u_ref.shape)
    for peer in group_peers:
        u_copy(peer, group).start()

    total = mlp_ref[chip].astype(f32)
    for peer in chip_peers:
        m_copy(chip, peer).wait_recv()
        total = total + mrecv_ref[peer].astype(f32)
    msum_ref[...] = total.astype(bf16)
    keep_copy(1).start()
    side_copy(1, chip, core, True).start()
    line_sends(1, 0, lambda copy: copy.start())

    total = u_ref[group].astype(f32)
    for peer in group_peers:
        u_copy(group, peer).wait_recv()
        total = total + urecv_ref[peer].astype(f32)
    usum_ref[...] = total.astype(bf16)
    keep_copy(0).start()
    side_copy(0, chip, core, True).start()
    line_sends(0, 0, lambda copy: copy.start())
    held = total.shape[0]
    gain = jnp.sum(total * wc_ref[...].astype(f32), axis=1, keepdims=True)
    column_ref[...] = jnp.zeros(column_ref.shape, f32)
    column_ref[:held, :] = jnp.broadcast_to(gain, (held, PAD))
    flat = column_ref[...].T[:1]
    smine_ref[...] = small_ref[...]
    for row in range(column_ref.shape[0] // PAD):
        smine_ref[row : row + 1, :] = flat[:, row * PAD : (row + 1) * PAD]
    for peer in ctx_peers:
        small_copy(peer, here).start()

    for step in range(1, chips):
        if step == 1:
            reduce_step(step)
        for which in range(2):
            line_receive(which, step - 1)
            if step <= chips - 2:
                line_sends(which, step, lambda copy: copy.start())
        if 1 < step <= chips - 2:
            reduce_step(step)
        if step == 1:
            small = smine_ref[...]
            for peer in ctx_peers:
                small_copy(here, peer).wait_recv()
                small = small + srecv_ref[peer]
            sgather_ref[group] = small
            for peer in group_peers:
                cross_copy(peer, group).start()

    for index in range(2):
        rows = partial(chip, index)
        own_ref[rows, :] = part_ref[rows, :].astype(bf16)

    for which in range(2):
        keep_copy(which).wait()
        for piece in range(chips):
            side_copy(which, piece, 1 - core).wait_recv()
            side_copy(which, piece, core).wait_send()
        for step in range(chips - 1):
            line_sends(which, step, lambda copy: copy.wait_send())
    for index in range(chips):
        pair_copy(index).wait_send()
    for peer in group_peers:
        cross_copy(group, peer).wait_recv()
        cross_copy(peer, group).wait_send()
        u_copy(peer, group).wait_send()
    for peer in chip_peers:
        m_copy(peer, chip).wait_send()
    for peer in ctx_peers:
        small_copy(peer, here).wait_send()
    for step in range(chips - 2):

        @pl.when(step >= chips - 1 - chip)
        def _():
            for index in range(2):
                sum_copy(0, step - (chips - 1) + chip, index).wait_send()

        @pl.when(step >= chip)
        def _():
            for index in range(2):
                sum_copy(1, chips - 1 - step + chip, index).wait_send()


def reduce_gradients(parts, groups, dqkv, w_pair, units, w_columns, small, chunks):
    chips = parts // 2
    mlp_shape = (chips, 3, chunks[0].shape[1] // chips, D)
    rows_dev = dqkv.shape[3]
    rows, width = w_columns.shape
    lanes = -(-rows // PAD) * PAD
    dma = pltpu.SemaphoreType.DMA
    anywhere = pl.BlockSpec(memory_space=pl.ANY)
    u_shape = (groups, rows, width)
    return pl.pallas_call(
        functools.partial(reduce_kernel, parts, groups),
        name="reduce_gradients",
        out_shape=[
            jax.ShapeDtypeStruct((rows_dev, D), bf16),
            jax.ShapeDtypeStruct((rows_dev, D), bf16),
            jax.ShapeDtypeStruct((rows_dev, D), bf16),
            jax.ShapeDtypeStruct((parts, rows, width), bf16),
            jax.ShapeDtypeStruct((parts,) + mlp_shape[1:], bf16),
            jax.ShapeDtypeStruct((groups,) + small.shape, f32),
        ],
        in_specs=[anywhere] * 3 + in_vmem(2) + [anywhere] * groups,
        out_specs=in_vmem(3) + [anywhere] * 2 + in_vmem(1),
        scratch_shapes=[
            pltpu.VMEM(dqkv.shape, bf16),
            pltpu.VMEM(w_pair.shape, bf16),
            pltpu.VMEM((groups,) + chunks[0].shape, bf16),
            pltpu.VMEM((2,) + units.shape[1:], bf16),
            pltpu.VMEM((width, D), f32),
            pltpu.VMEM(u_shape, bf16),
            pltpu.VMEM(u_shape[1:], bf16),
            pltpu.VMEM(mlp_shape[1:], bf16),
            pltpu.VMEM((chips,) + dqkv.shape[2:], bf16),
            pltpu.VMEM((chips + 1, rows_dev, D), bf16),
            pltpu.VMEM(u_shape, bf16),
            pltpu.VMEM(mlp_shape, bf16),
            pltpu.VMEM(mlp_shape, bf16),
            pltpu.VMEM((rows_dev, D), f32),
            pltpu.VMEM((lanes, PAD), f32),
            pltpu.VMEM(small.shape, f32),
            pltpu.VMEM((parts,) + small.shape, f32),
            dma((2, chips)),
            dma((2, 2, chips, 2)),
            dma((2, groups)),
            dma((2, chips)),
            dma((2, 2, 2, chips)),
            dma((2, 2, chips)),
            dma((2, parts)),
            dma((2, groups)),
            dma((groups + 2,)),
            dma((2,)),
            dma((2,)),
        ],
        compiler_params=pltpu.CompilerParams(
            vmem_limit_bytes=60 * 1024 * 1024, collective_id=1, has_side_effects=True
        ),
    )(dqkv, w_pair, units, w_columns, small, *chunks)


def update_kernel(rates, qkv_ref, gain_ref, mlp_ref, *refs):
    sets = len(rates)
    parts, rows, width = qkv_ref.shape
    width = width // 3
    for index, rate in enumerate(rates):
        weight, first, second = (ref[...] for ref in refs[3 * index : 3 * index + 3])
        if index == 0:
            pieces = [qkv_ref[part].astype(f32) for part in range(parts)]
            gradient = jnp.concatenate(
                [piece[:, at * width : (at + 1) * width] for at in range(3) for piece in pieces],
                axis=1,
            )
            gradient = gradient * gain_ref[...]
        else:
            gradient = mlp_ref[0, index - 1].astype(f32)
        outs = refs[3 * sets + 4 * index : 3 * sets + 4 * index + 4]
        new, first, second = adamw(weight, first, second, gradient, rate, decay_rate)
        outs[0][...] = new
        outs[1][...] = first
        outs[2][...] = second
        outs[3][...] = new.astype(bf16)


def update(rates, parts, qkv, gain, mlp, *arrays):
    rows = arrays[0].shape[0]
    chips = parts // 2
    step_rows = rows // parts
    if step_rows % 8 == 0:

        def owner(i):
            return (2 * lax.rem(i, chips) + i // chips, 0, 0, 0)

    else:
        step_rows = 32
        mlp = mlp.reshape(chips, 2, 3, rows // parts, D).transpose(2, 1, 0, 3, 4)
        mlp = mlp.reshape(3, rows // step_rows, step_rows, D).transpose(1, 0, 2, 3)

        def owner(i):
            return (i, 0, 0, 0)

    in_specs = [
        pl.BlockSpec((parts, step_rows, qkv.shape[2]), lambda i: (0, i, 0)),
        pl.BlockSpec((step_rows, 1), lambda i: (i, 0)),
        pl.BlockSpec((1, 3, step_rows, D), owner),
    ]
    specs, shapes, moved = [], [], 0
    for array in arrays:
        in_specs.append(pl.BlockSpec((step_rows, array.shape[1]), lambda i: (i, 0)))
    for index in range(len(rates)):
        shape = arrays[3 * index].shape
        shapes += [jax.ShapeDtypeStruct(shape, f32)] * 3 + [jax.ShapeDtypeStruct(shape, bf16)]
        specs += [pl.BlockSpec((step_rows, shape[1]), lambda i: (i, 0))] * 4
        moved += shape[0] * shape[1] * 28
    return pl.pallas_call(
        functools.partial(update_kernel, rates),
        name="update_weights",
        grid=(rows // step_rows,),
        in_specs=in_specs,
        out_specs=specs,
        out_shape=shapes,
        compiler_params=params(55),
        cost_estimate=pl.CostEstimate(flops=moved, bytes_accessed=moved, transcendentals=0),
    )(qkv, gain, mlp, *arrays)


def finish_kernel(down_ref, up_ref, own_ref, x_ref, dmid_ref, layer_ref, out_ref, same_ref):
    here = pl.ds(pl.multiple_of(pl.program_id(0) * PAD, PAD), PAD)
    rows = x_ref[...].astype(f32)
    scale = rms_scale(rows)
    unit = rows * scale
    dunit = (
        own_ref[...].astype(f32) + down_ref[here, :].astype(f32) + up_ref[here, :].astype(f32)
    )
    grad = dmid_ref[...] + scale * (
        dunit - unit * jnp.mean(dunit * unit, axis=-1, keepdims=True)
    )
    out_ref[...] = grad.astype(bf16)
    same_ref[...] = layer_ref[...]


def finish(*arrays):
    rows = arrays[0].shape[0]
    spec = pl.BlockSpec((PAD, D), lambda i: (i, 0))
    return pl.pallas_call(
        finish_kernel,
        name="finish",
        grid=(rows // PAD,),
        in_specs=in_vmem(2) + [spec] * 4,
        out_specs=[spec] * 2,
        out_shape=[jax.ShapeDtypeStruct((rows, D), bf16)] * 2,
        compiler_params=params(40),
    )(*arrays)


def body(
    parts,
    groups,
    inputs,
    cotangent,
    block_order,
    w_qkv,
    m_qkv,
    v_qkv,
    w_out,
    m_out,
    v_out,
    w_up,
    m_up,
    v_up,
    w_down,
    m_down,
    v_down,
    small_params,
    small_m,
    small_v,
):
    heads = H // parts
    width = heads * HD
    rows_dev = inputs.shape[1]
    tokens = rows_dev * parts
    here = lax.axis_index("ctx")
    order = block_order[0]
    gain_two = small_params[D : 2 * D]
    query_scale = small_params[2 * D :]
    group = lax.axis_index("fsdp")
    rows = w_qkv.shape[0]

    (
        unit_all,
        mlp_full,
        w_pair,
        qt,
        kt,
        vt,
        kn,
        vn,
        w_columns,
        gain_rows,
        factor_two,
        most,
    ) = gather_rows(
        parts, groups, heads, inputs[0], w_qkv, w_out, w_up, w_down, small_params
    )
    lse, mixed = attention_forward(order, most, qt, kn, vt, parts)
    kept = (qt, kt, kn, vn, lse)
    output, dmid, dmixed, gain_two_grad, *chunks = middle(
        parts,
        groups,
        mixed,
        inputs[0],
        cotangent[0],
        mlp_full.reshape(3, D, D),
        gain_two[None],
    )
    for step in range(1, groups):
        swap = [(i, i ^ step) for i in range(groups)]
        chunks[step] = lax.ppermute(chunks[step], "fsdp", swap)
    dqkv, dscale = attention_backward(order, kept, mixed, dmixed, factor_two)
    scale_grad = (
        dscale[0, :HD]
        / factor_two[:, 0]
        * (scale_base / math.sqrt(HD))
        * jax.nn.sigmoid(query_scale)
    )
    lanes = -(-rows // PAD) * PAD
    small_rows = -(-(lanes + D + PAD) // (8 * PAD)) * 8
    small = jnp.concatenate([jnp.zeros((lanes,), f32), gain_two_grad[0], scale_grad])
    small = jnp.pad(small, (0, small_rows * PAD - small.shape[0])).reshape(small_rows, PAD)
    send_down, send_up, own_part, u_all, mlp_all, small_all = reduce_gradients(
        parts,
        groups,
        dqkv.reshape(parts // 2, 2, 3 * width, rows_dev),
        w_pair,
        unit_all,
        w_columns,
        small,
        chunks,
    )
    got_down = lax.ppermute(send_down, "ctx", [(i, i - 2) for i in range(2, parts)])
    got_up = lax.ppermute(send_up, "ctx", [(i, i + 2) for i in range(parts - 2)])
    rate_qkv = qkv_rate_base / math.sqrt(D)
    rate_out = 0.5 / math.sqrt(max(D // 256, 1))
    rate_up = 0.5 / math.sqrt(D)
    rate_down = 0.5 / math.sqrt(FF)
    updated = update(
        (rate_qkv, rate_out, rate_up, rate_down),
        parts,
        u_all,
        gain_rows,
        mlp_all,
        w_qkv,
        m_qkv,
        v_qkv,
        w_out,
        m_out,
        v_out,
        w_up,
        m_up,
        v_up,
        w_down,
        m_down,
        v_down,
    )
    flat = small_all.reshape(groups, small_rows * PAD)
    rest = jnp.sum(flat[:, lanes : lanes + D + HD], axis=0)
    small_total = jnp.concatenate([flat[:, :rows].reshape(D), rest])
    small_set = adamw(small_params, small_m, small_v, small_total, small_rate, 0.0)
    input_grad, output = finish(got_down, got_up, own_part, inputs[0], dmid, output)
    return (
        output[None],
        input_grad[None],
        *updated,
        *small_set,
    )


def solution(mesh):
    rows = P("fsdp", "ctx", None)
    weight = P("fsdp", None)
    return jax.shard_map(
        functools.partial(body, mesh.shape["ctx"], mesh.shape["fsdp"]),
        mesh=mesh,
        in_specs=(rows, rows, weight) + (weight,) * 12 + (P(),) * 3,
        out_specs=(rows, rows) + (weight,) * 16 + (P(),) * 3,
        check_vma=False,
    )
```
